32 devices in a mesh: rows: 4 (over y, core), seq: 8 (over z, x).
Axes of the slice: x: 2, y: 2, z: 4, core: 2. Of those that a mesh axis runs over, the one named last changes fastest.
Arguments:
- block_in: float32 [8, 256, 8, 768], P('rows', None, 'seq'), may hold values from -12 to 12
- segment_ids: int32 [8, 256, 8], P('rows', None, 'seq'), may hold values from 0 to 15, as said below
- valid_mask: int32 [8, 256, 8], P('rows', None, 'seq'), may hold values 0 or 1
- cotangent: float32 [8, 256, 8, 768], P('rows', None, 'seq'), may hold values from -6 to 6
- gain_mix: float32 [768], replicated, may hold values from 0.5 to 1.5
- in_proj: bfloat16 [768, 2304], replicated, may hold values from -0.21875 to 0.21875
- short_taps: float32 [3, 2304], replicated, may hold values from -3 to 3
- long_kernel: float32 [256, 8, 768], P(None, 'seq'), may hold values from -0.3125 to 0.3125
- skip_gain: float32 [768], replicated, may hold values from -3 to 3
- out_proj: bfloat16 [768, 768], replicated, may hold values from -0.21875 to 0.21875
- gain_mlp: float32 [768], replicated, may hold values from 0.5 to 1.5
- up_proj: bfloat16 [768, 3072], replicated, may hold values from -0.21875 to 0.21875
- down_proj: bfloat16 [3072, 768], replicated, may hold values from -0.15625 to 0.15625
Outputs:
- block_out: float32 [8, 256, 8, 768], P('rows', None, 'seq')
- grad_input: float32 [8, 256, 8, 768], P('rows', None, 'seq')
- grad_gain_mix: float32 [768], replicated
- grad_in_proj: float32 [768, 2304], P('seq')
- grad_short_taps: float32 [3, 2304], replicated
- grad_long_kernel: float32 [256, 8, 768], P(None, 'seq')
- grad_skip_gain: float32 [768], replicated
- grad_out_proj: float32 [768, 768], P('seq')
- grad_gain_mlp: float32 [768], replicated
- grad_up_proj: float32 [768, 3072], P('seq')
- grad_down_proj: float32 [3072, 768], P('seq')
- rms_stats: float32 [3], replicated
The draws below stay inside these ranges and needn't reach their ends.
Inputs may be any that keep to these rules, and one draw needn't show every extreme that they name: `segment_ids`: within a row non-decreasing along t = b * 8 + p, starting at 0 and rising by at most one per position.
All inputs are finite; a program needn't handle non-finite values. No bound on the sum of `valid_mask` on one device may be relied on, other than what follows from the above.
Results may differ from the reference program's by a relative error of at most 0.015.
Values may be sent and summed in bfloat16 or wider, within the bound.
A program may use at most 256 MiB of HBM per device.

```python
import jax
import jax.numpy as jnp
from jax import lax

D = 768
FF = 3072
LENGTH = 2048
BLK = 256
ROWS = 8
N_SEQ = 8


def draw_block_in(key, part):
    key = jax.random.fold_in(key, 11)
    key_main = jax.random.fold_in(key, 0)
    ramp = 1.0 + 2.0 * jnp.arange(LENGTH, dtype=jnp.float32) / (LENGTH - 1)
    base = jnp.clip(jax.random.normal(key_main, (ROWS, LENGTH, D), jnp.float32), -4.0, 4.0)
    values = base * ramp[None, :, None]
    return values.reshape(ROWS, BLK, LENGTH // BLK, D)


def draw_segment_ids(key, part):
    key = jax.random.fold_in(key, 12)
    cuts = jax.random.randint(key, (ROWS, 15), 1, LENGTH)
    places = jnp.arange(LENGTH, dtype=jnp.int32)
    starts = jnp.any(places[None, None, :] == cuts[:, :, None], axis=1).astype(jnp.int32)
    ids = jnp.cumsum(starts, axis=1).astype(jnp.int32)
    return ids.reshape(ROWS, BLK, LENGTH // BLK)


def touch_ends(drawn, own_key, low, top_value):
    longest = drawn.shape.index(max(drawn.shape))
    spots = []
    for shift in (0, 1):
        where = [jax.random.randint(jax.random.fold_in(own_key, axis), (), 0, length) for axis, length in enumerate(drawn.shape)]
        where[longest] = (where[longest] + shift) % drawn.shape[longest]
        spots.append(tuple(where))
    return drawn.at[spots[0]].set(low).at[spots[1]].set(top_value)


def shard_levels(key, extent, cuts, least, largest):
    level = 1.0
    for axis_at, shards_of in cuts:
        draws = jax.random.uniform(jax.random.fold_in(jax.random.fold_in(key, 6), axis_at), (shards_of,), jnp.float32, least / len(cuts), largest / len(cuts))
        level = level * jnp.repeat(jnp.exp(draws), extent[axis_at] // shards_of).reshape((-1,) + (1,) * (len(extent) - 1 - axis_at))
    return level


def scatter_about(own_key, dims, scale, most, cuts=(), kind=jnp.bfloat16):
    values = scale * jax.random.normal(own_key, dims, jnp.float32)
    if cuts:
        values = values * shard_levels(own_key, dims, cuts, -0.22, 0.18)
    return jnp.clip(values, -most, most).astype(kind)


def setup_inputs(seed: int = 0) -> dict:
    arg_keys = jax.random.split(jax.random.key(seed), 14)
    block_in = draw_block_in(jax.random.fold_in(arg_keys[13], 71), 0)
    segment_ids = draw_segment_ids(jax.random.fold_in(arg_keys[13], 71), 0)
    valid_mask = touch_ends((jax.random.randint(arg_keys[2], (ROWS, BLK, N_SEQ), 0, 8) < 7).astype(jnp.int32), jax.random.fold_in(arg_keys[2], 1), 0, 1)
    cotangent = scatter_about(arg_keys[3], (ROWS, BLK, N_SEQ, D), 1.0, 6.0, ((0, 4), (2, 8)), jnp.float32)
    gain_mix = jnp.clip(1.0 + 0.1 * jax.random.normal(arg_keys[4], (D,), jnp.float32), 0.5, 1.5)
    in_proj = scatter_about(arg_keys[5], (D, 3 * D), D ** -0.5, 0.21875)
    short_taps = scatter_about(arg_keys[6], (3, 3 * D), 0.6, 3.0, (), jnp.float32)
    long_kernel = scatter_about(arg_keys[7], (BLK, N_SEQ, D), (LENGTH ** -0.5), 0.3125, ((1, 8),), jnp.float32)
    skip_gain = scatter_about(arg_keys[8], (D,), 0.5, 3.0, (), jnp.float32)
    out_proj = scatter_about(arg_keys[9], (D, D), D ** -0.5, 0.21875)
    gain_mlp = jnp.clip(1.0 + 0.1 * jax.random.normal(arg_keys[10], (D,), jnp.float32), 0.5, 1.5)
    up_proj = scatter_about(arg_keys[11], (D, FF), D ** -0.5, 0.21875)
    down_proj = scatter_about(arg_keys[12], (FF, D), (FF // 2) ** -0.5, 0.15625)
    return dict(block_in=block_in, segment_ids=segment_ids, valid_mask=valid_mask, cotangent=cotangent, gain_mix=gain_mix, in_proj=in_proj, short_taps=short_taps, long_kernel=long_kernel, skip_gain=skip_gain, out_proj=out_proj, gain_mlp=gain_mlp, up_proj=up_proj, down_proj=down_proj)


EPS = 1e-05
THRESH = 0.003
HIGH = lax.Precision.HIGHEST

@jax.custom_vjp
def low(v):
    return lax.optimization_barrier(v.astype(jnp.bfloat16)).astype(jnp.float32)

@jax.custom_vjp
def low_back(v):
    return v

def low_keep(v):
    return (low(v), None)

def low_pass(kept, grad):
    return (grad,)

def back_keep(v):
    return (v, None)

def back_low(kept, grad):
    return (low(grad),)
low.defvjp(low_keep, low_pass)
low_back.defvjp(back_keep, back_low)

def norm_scale(value, gain):
    return value * lax.rsqrt(lax.optimization_barrier(jnp.mean(value * value, axis=-1, keepdims=True)) + EPS) * gain

def long_conv(signal, taps_eff):
    spec_len = 2 * signal.shape[0]
    spectrum = jnp.fft.rfft(signal, n=spec_len, axis=0) * jnp.fft.rfft(taps_eff, n=spec_len, axis=0)
    return jnp.fft.irfft(spectrum, n=spec_len, axis=0)[:signal.shape[0]]

def row_forward(params, row_in, row_seg, row_mask):
    gain_mix, in_proj, short_taps, long_kernel, skip_gain, out_proj, gain_mlp, up_proj, down_proj = params
    width = row_in.shape[1]
    normed_one = low(norm_scale(row_in, gain_mix))
    proj = low_back(low(jnp.dot(normed_one, in_proj, precision=HIGH)))
    same_one = jnp.concatenate([jnp.zeros((1,), jnp.float32), (row_seg[1:] == row_seg[:-1]).astype(jnp.float32)])[:, None]
    same_two = jnp.concatenate([jnp.zeros((2,), jnp.float32), (row_seg[2:] == row_seg[:-2]).astype(jnp.float32)])[:, None]
    proj_one = jnp.concatenate([jnp.zeros((1, 3 * width), jnp.float32), proj[:-1]], axis=0)
    proj_two = jnp.concatenate([jnp.zeros((2, 3 * width), jnp.float32), proj[:-2]], axis=0)
    conv_short = short_taps[0] * proj + short_taps[1] * proj_one * same_one + short_taps[2] * proj_two * same_two
    query = conv_short[:, :width]
    keys = conv_short[:, width:2 * width]
    values = conv_short[:, 2 * width:]
    mask_col = row_mask.astype(jnp.float32)[:, None]
    gated = keys * values * mask_col
    taps_eff = long_kernel - THRESH * jnp.tanh(long_kernel / THRESH)
    long_out = long_conv(gated, taps_eff) + skip_gain * gated
    mixer_low = low(query * long_out)
    mixer_out = low_back(jnp.dot(mixer_low, out_proj, precision=HIGH))
    resid_mid = row_in + mixer_out
    normed_two = low(norm_scale(resid_mid, gain_mlp))
    up_val = low_back(jnp.dot(normed_two, up_proj, precision=HIGH))
    act_low = low(jax.nn.gelu(up_val))
    mlp_out = low_back(jnp.dot(act_low, down_proj, precision=HIGH))
    row_out = resid_mid + mlp_out
    extras = (jnp.sum(mask_col * mixer_out * mixer_out), jnp.sum(mask_col * mlp_out * mlp_out))
    return (row_out, extras)

def reference(block_in, segment_ids, valid_mask, cotangent, gain_mix, in_proj, short_taps, long_kernel, skip_gain, out_proj, gain_mlp, up_proj, down_proj):
    params = (gain_mix, in_proj.astype(jnp.float32), short_taps, long_kernel.reshape(LENGTH, D), skip_gain, out_proj.astype(jnp.float32), gain_mlp, up_proj.astype(jnp.float32), down_proj.astype(jnp.float32))
    rows_in = block_in.reshape(ROWS, LENGTH, D)
    seg_rows = segment_ids.reshape(ROWS, LENGTH)
    mask_rows = valid_mask.reshape(ROWS, LENGTH)
    cot_rows = cotangent.reshape(ROWS, LENGTH, D)

    def one_row(carry, slices):
        grads_sum, stat_sum = carry
        row_in, row_seg, row_mask, row_cot = slices

        def apply_row(params_in, row_value):
            return row_forward(params_in, row_value, row_seg, row_mask)
        row_out, pull_back, extras = jax.vjp(apply_row, params, row_in, has_aux=True)
        grad_params, grad_row = pull_back(row_cot)
        mask_col = row_mask.astype(jnp.float32)[:, None]
        stats = jnp.stack([jnp.sum(mask_col * row_out * row_out), extras[0], extras[1], jnp.sum(row_mask.astype(jnp.float32))])
        grads_sum = jax.tree.map(lambda running, fresh: running + fresh, grads_sum, grad_params)
        return ((grads_sum, stat_sum + stats), (row_out, grad_row))
    start = (jax.tree.map(jnp.zeros_like, params), jnp.zeros((4,), jnp.float32))
    (grads, stats), (outs_all, grads_in) = lax.scan(one_row, start, (rows_in, seg_rows, mask_rows, cot_rows))
    counted = jnp.maximum(stats[3], 1.0)
    rms_stats = jnp.sqrt(stats[:3] / (counted * D))
    return (outs_all.reshape(block_in.shape), grads_in.reshape(block_in.shape), grads[0], grads[1], grads[2], grads[3].reshape(BLK, LENGTH // BLK, D), grads[4], grads[5], grads[6], grads[7], grads[8], rms_stats)
```

```python
import functools
import math

import jax
import jax.numpy as jnp
import numpy as np
from jax import lax
from jax.experimental import pallas as pl
from jax.experimental.pallas import tpu as pltpu
from jax.sharding import PartitionSpec as P

EPS = 1e-05
THRESH = 0.003
HIGH = lax.Precision.HIGHEST


def shortened(x):

    def short(part):
        return part.astype(jnp.bfloat16) if part.dtype == jnp.float32 else part

    return jax.tree.map(short, x)


def passed_along(block, axis, distance):
    devices = range(lax.axis_size(axis))
    route = [((i - distance) % len(devices), i) for i in devices]
    return lax.ppermute(block, axis, route)


def norm_scale(value, gain):
    return value * lax.rsqrt(jnp.mean(value * value, axis=-1, keepdims=True) + EPS) * gain


def angle_tables(left_count, right_count, period):
    left_idx = jnp.arange(left_count, dtype=jnp.int32)[:, None]
    right_idx = jnp.arange(right_count, dtype=jnp.int32)[None, :]
    phase = (left_idx * right_idx % period).astype(jnp.float32) * (2.0 * math.pi / period)
    return (jnp.cos(phase), jnp.sin(phase))


def twiddle_tables(shard_index, spec_len, whole_len):
    turned = shard_index * jnp.arange(spec_len, dtype=jnp.int32) % whole_len
    phase = turned.astype(jnp.float32) * (2.0 * math.pi / whole_len)
    return (jnp.cos(phase)[None, :, None], jnp.sin(phase)[None, :, None])


def local_forward(signal, shard_index, whole_len):
    blocks = signal.shape[1]
    cos_table, sin_table = angle_tables(blocks, 2 * blocks, 2 * blocks)
    real_part = jnp.einsum("rjd,jk->rkd", signal, cos_table, precision=HIGH)
    imag_part = -jnp.einsum("rjd,jk->rkd", signal, sin_table, precision=HIGH)
    cos_twid, sin_twid = twiddle_tables(shard_index, 2 * blocks, whole_len)
    out_real = real_part * cos_twid + imag_part * sin_twid
    out_imag = imag_part * cos_twid - real_part * sin_twid
    return (out_real[:, :, None, :], out_imag[:, :, None, :])


def cross_section(real_part, imag_part, direction):
    count = real_part.shape[2]
    cos_table, sin_table = angle_tables(count, count, count)
    re_cos = jnp.einsum("rcpd,pm->rcmd", real_part, cos_table, precision=HIGH)
    re_sin = jnp.einsum("rcpd,pm->rcmd", real_part, sin_table, precision=HIGH)
    im_cos = jnp.einsum("rcpd,pm->rcmd", imag_part, cos_table, precision=HIGH)
    im_sin = jnp.einsum("rcpd,pm->rcmd", imag_part, sin_table, precision=HIGH)
    return (re_cos - direction * im_sin, im_cos + direction * re_sin)


def local_inverse(real_part, imag_part, shard_index, whole_len):
    real_part = real_part[:, :, 0, :]
    imag_part = imag_part[:, :, 0, :]
    spec_len = real_part.shape[1]
    cos_twid, sin_twid = twiddle_tables(shard_index, spec_len, whole_len)
    turned_re = real_part * cos_twid - imag_part * sin_twid
    turned_im = imag_part * cos_twid + real_part * sin_twid
    cos_table, sin_table = angle_tables(spec_len, spec_len // 2, spec_len)
    result = jnp.einsum("rkd,kj->rjd", turned_re, cos_table, precision=HIGH)
    result = result - jnp.einsum("rkd,kj->rjd", turned_im, sin_table, precision=HIGH)
    return result / whole_len


def earlier(members, at_start):
    received = jax.tree.map(
        lambda part, own: part.astype(own.dtype),
        passed_along(shortened(members), "seq", 1),
        members,
    )
    placed = []
    for member in received:
        rolled = jnp.concatenate([jnp.zeros_like(member[:, :1]), member[:, :-1]], axis=1)
        placed.append(jnp.where(at_start, rolled, member))
    return tuple(placed)


def later(member, at_end):
    received = passed_along(member.astype(jnp.bfloat16), "seq", -1).astype(member.dtype)
    rolled = jnp.concatenate([received[:, 1:], jnp.zeros_like(received[:, :1])], axis=1)
    return jnp.where(at_end, rolled, received)


def times_trans(left, right):
    return lax.dot_general(
        left, right, (((1,), (1,)), ((), ())), preferred_element_type=jnp.float32
    )


def trans_times(left, right):
    return lax.dot_general(
        left, right, (((0,), (0,)), ((), ())), preferred_element_type=jnp.float32
    )


def general_local(
    block_in,
    segment_ids,
    valid_mask,
    cotangent,
    gain_mix,
    in_proj,
    short_taps,
    long_kernel,
    skip_gain,
    out_proj,
    gain_mlp,
    up_proj,
    down_proj,
):
    batch_rows = block_in.shape[0]
    blocks = block_in.shape[1]
    width = block_in.shape[3]
    shard_count = lax.axis_size("seq")
    shard_index = lax.axis_index("seq")
    whole_len = 2 * blocks * shard_count
    tokens = batch_rows * blocks
    at_start = shard_index == 0
    at_end = shard_index == shard_count - 1
    flat_in = block_in.reshape(tokens, width)
    mask_rows = valid_mask[:, :, 0].astype(jnp.float32)[:, :, None]
    normed_one = norm_scale(flat_in, gain_mix).astype(jnp.bfloat16)
    proj_low = jnp.dot(normed_one, in_proj, preferred_element_type=jnp.float32).astype(jnp.bfloat16)
    proj_low = proj_low.reshape(batch_rows, blocks, 3 * width)
    seg_low = segment_ids[:, :, 0].astype(jnp.bfloat16)[:, :, None]
    prev_one = earlier((proj_low, seg_low), at_start)
    prev_two = earlier(prev_one, at_start)
    same_one = (prev_one[1] == seg_low).astype(jnp.float32)
    same_two = (prev_two[1] == seg_low).astype(jnp.float32)
    proj_now = proj_low.astype(jnp.float32)
    proj_one = prev_one[0].astype(jnp.float32)
    proj_two = prev_two[0].astype(jnp.float32)
    conv_short = (
        short_taps[0] * proj_now
        + short_taps[1] * proj_one * same_one
        + short_taps[2] * proj_two * same_two
    )
    query = conv_short[:, :, :width]
    keys = conv_short[:, :, width : 2 * width]
    values = conv_short[:, :, 2 * width :]
    gated = keys * values * mask_rows
    raw_taps = long_kernel[:, 0, :]
    taps_eff = raw_taps - THRESH * jnp.tanh(raw_taps / THRESH)
    kern_re, kern_im = local_forward(taps_eff[None], shard_index, whole_len)
    kern_re, kern_im = (
        lax.all_to_all(
            kern_re.astype(jnp.bfloat16), "seq", split_axis=1, concat_axis=2, tiled=True
        ).astype(kern_re.dtype),
        lax.all_to_all(
            kern_im.astype(jnp.bfloat16), "seq", split_axis=1, concat_axis=2, tiled=True
        ).astype(kern_im.dtype),
    )
    kern_re, kern_im = cross_section(kern_re, kern_im, -1.0)
    gate_re, gate_im = local_forward(gated, shard_index, whole_len)
    gate_re, gate_im = (
        lax.all_to_all(
            gate_re.astype(jnp.bfloat16), "seq", split_axis=1, concat_axis=2, tiled=True
        ).astype(gate_re.dtype),
        lax.all_to_all(
            gate_im.astype(jnp.bfloat16), "seq", split_axis=1, concat_axis=2, tiled=True
        ).astype(gate_im.dtype),
    )
    gate_re, gate_im = cross_section(gate_re, gate_im, -1.0)
    prod_re = gate_re * kern_re - gate_im * kern_im
    prod_im = gate_re * kern_im + gate_im * kern_re
    prod_re, prod_im = cross_section(prod_re, prod_im, 1.0)
    prod_re, prod_im = (
        lax.all_to_all(
            prod_re.astype(jnp.bfloat16), "seq", split_axis=2, concat_axis=1, tiled=True
        ).astype(prod_re.dtype),
        lax.all_to_all(
            prod_im.astype(jnp.bfloat16), "seq", split_axis=2, concat_axis=1, tiled=True
        ).astype(prod_im.dtype),
    )
    long_out = local_inverse(prod_re, prod_im, shard_index, whole_len) + skip_gain * gated
    mixer_low = (query * long_out).reshape(tokens, width).astype(jnp.bfloat16)
    mixer_out = jnp.dot(mixer_low, out_proj, preferred_element_type=jnp.float32)
    resid_mid = flat_in + mixer_out
    normed_two = norm_scale(resid_mid, gain_mlp).astype(jnp.bfloat16)
    up_val = jnp.dot(normed_two, up_proj, preferred_element_type=jnp.float32)
    act_low = jax.nn.gelu(up_val).astype(jnp.bfloat16)
    mlp_out = jnp.dot(act_low, down_proj, preferred_element_type=jnp.float32)
    flat_out = resid_mid + mlp_out
    grad_out = cotangent.reshape(tokens, width)
    grad_mlp = grad_out.astype(jnp.bfloat16)
    grad_down = trans_times(act_low, grad_mlp)
    grad_act = times_trans(grad_mlp, down_proj)
    unused_val, gelu_back = jax.vjp(jax.nn.gelu, up_val)
    grad_upval = gelu_back(grad_act)[0].astype(jnp.bfloat16)
    grad_up = trans_times(normed_two, grad_upval)
    grad_norm_two = times_trans(grad_upval, up_proj)
    unused_two, norm_back_two = jax.vjp(norm_scale, resid_mid, gain_mlp)
    grad_resid, grad_gain_two = norm_back_two(grad_norm_two)
    grad_mid = grad_out + grad_resid
    grad_mix = grad_mid.astype(jnp.bfloat16)
    grad_outp = trans_times(mixer_low, grad_mix)
    grad_prod = times_trans(grad_mix, out_proj).reshape(batch_rows, blocks, width)
    grad_query = grad_prod * long_out
    grad_long = grad_prod * query
    back_re, back_im = local_forward(grad_long, shard_index, whole_len)
    back_re, back_im = (
        lax.all_to_all(
            back_re.astype(jnp.bfloat16), "seq", split_axis=1, concat_axis=2, tiled=True
        ).astype(back_re.dtype),
        lax.all_to_all(
            back_im.astype(jnp.bfloat16), "seq", split_axis=1, concat_axis=2, tiled=True
        ).astype(back_im.dtype),
    )
    back_re, back_im = cross_section(back_re, back_im, -1.0)
    sig_re = kern_re * back_re + kern_im * back_im
    sig_im = kern_re * back_im - kern_im * back_re
    tap_re = jnp.sum(gate_re * back_re + gate_im * back_im, axis=0, keepdims=True)
    tap_im = jnp.sum(gate_re * back_im - gate_im * back_re, axis=0, keepdims=True)
    sig_re, sig_im = cross_section(sig_re, sig_im, 1.0)
    tap_re, tap_im = cross_section(tap_re, tap_im, 1.0)
    sig_re, sig_im, tap_re, tap_im = (
        lax.all_to_all(
            sig_re.astype(jnp.bfloat16), "seq", split_axis=2, concat_axis=1, tiled=True
        ).astype(sig_re.dtype),
        lax.all_to_all(
            sig_im.astype(jnp.bfloat16), "seq", split_axis=2, concat_axis=1, tiled=True
        ).astype(sig_im.dtype),
        lax.all_to_all(
            tap_re.astype(jnp.bfloat16), "seq", split_axis=2, concat_axis=1, tiled=True
        ).astype(tap_re.dtype),
        lax.all_to_all(
            tap_im.astype(jnp.bfloat16), "seq", split_axis=2, concat_axis=1, tiled=True
        ).astype(tap_im.dtype),
    )
    grad_gated = local_inverse(sig_re, sig_im, shard_index, whole_len) + skip_gain * grad_long
    grad_taps_eff = local_inverse(tap_re, tap_im, shard_index, whole_len)[0]
    tanh_val = jnp.tanh(raw_taps / THRESH)
    grad_kernel = (grad_taps_eff * tanh_val * tanh_val)[:, None, :]
    grad_kernel = lax.psum(grad_kernel.astype(jnp.bfloat16), "rows").astype(jnp.float32)
    grad_skip = jnp.sum(grad_long * gated, axis=(0, 1))
    grad_short = jnp.concatenate(
        [grad_query, grad_gated * values * mask_rows, grad_gated * keys * mask_rows], axis=2
    )
    grad_tap_rows = jnp.stack(
        [
            jnp.sum(grad_short * proj_now, axis=(0, 1)),
            jnp.sum(grad_short * proj_one * same_one, axis=(0, 1)),
            jnp.sum(grad_short * proj_two * same_two, axis=(0, 1)),
        ]
    )
    inner_term = short_taps[1] * grad_short * same_one + later(
        short_taps[2] * grad_short * same_two, at_end
    )
    grad_proj = short_taps[0] * grad_short + later(inner_term, at_end)
    grad_proj = grad_proj.reshape(tokens, 3 * width).astype(jnp.bfloat16)
    grad_inp = trans_times(normed_one, grad_proj)
    grad_norm_one = times_trans(grad_proj, in_proj)
    unused_one, norm_back_one = jax.vjp(norm_scale, flat_in, gain_mix)
    grad_first, grad_gain_one = norm_back_one(grad_norm_one)
    grad_flat = grad_mid + grad_first
    mask_flat = mask_rows.reshape(tokens, 1)
    stat_sums = jnp.stack(
        [
            jnp.sum(mask_flat * flat_out * flat_out),
            jnp.sum(mask_flat * mixer_out * mixer_out),
            jnp.sum(mask_flat * mlp_out * mlp_out),
            jnp.sum(mask_flat),
        ]
    )
    grad_gain_one, grad_gain_two, grad_tap_rows, grad_skip, stat_sums = lax.psum(
        (grad_gain_one, grad_gain_two, grad_tap_rows, grad_skip, stat_sums), ("rows", "seq")
    )
    rms_stats = jnp.sqrt(stat_sums[:3] / (jnp.maximum(stat_sums[3], 1.0) * width))
    shares = (
        lax.psum_scatter(grad_inp, "seq", scatter_dimension=0, tiled=True),
        lax.psum_scatter(grad_outp, "seq", scatter_dimension=0, tiled=True),
        lax.psum_scatter(grad_up, "seq", scatter_dimension=0, tiled=True),
        lax.psum_scatter(grad_down, "seq", scatter_dimension=0, tiled=True),
    )
    grad_inp, grad_outp, grad_up, grad_down = (
        lax.psum(shares[0].astype(jnp.bfloat16), "rows").astype(jnp.float32),
        lax.psum(shares[1].astype(jnp.bfloat16), "rows").astype(jnp.float32),
        lax.psum(shares[2].astype(jnp.bfloat16), "rows").astype(jnp.float32),
        lax.psum(shares[3].astype(jnp.bfloat16), "rows").astype(jnp.float32),
    )
    return (
        flat_out.reshape(block_in.shape),
        grad_flat.reshape(block_in.shape),
        grad_gain_one,
        grad_inp,
        grad_tap_rows,
        grad_kernel,
        grad_skip,
        grad_outp,
        grad_gain_two,
        grad_up,
        grad_down,
        rms_stats,
    )


MESH = pl.DeviceIdType.MESH
F32 = jnp.float32
BF16 = jnp.bfloat16
VMEM_BYTES = 60 * 1024 * 1024
ROOT_HALF = math.sqrt(0.5)
C0 = math.sqrt(2.0 / math.pi)
C1 = 0.044715


def dot_nn(a, b):
    return lax.dot_general(a, b, (((1,), (0,)), ((), ())), preferred_element_type=F32)


def dot_nt(a, b):
    return lax.dot_general(a, b, (((1,), (1,)), ((), ())), preferred_element_type=F32)


def fft_points(re, im, sign):
    n = len(re)
    if n == 1:
        return re, im
    even_r, even_i = fft_points(re[0::2], im[0::2], sign)
    odd_r, odd_i = fft_points(re[1::2], im[1::2], sign)
    out_r, out_i = [None] * n, [None] * n
    for k in range(n // 2):
        if k == 0:
            turn_r, turn_i = odd_r[0], odd_i[0]
        elif 4 * k == n:
            if sign > 0:
                out_r[k], out_i[k] = even_r[k] - odd_i[k], even_i[k] + odd_r[k]
                out_r[k + n // 2], out_i[k + n // 2] = even_r[k] + odd_i[k], even_i[k] - odd_r[k]
            else:
                out_r[k], out_i[k] = even_r[k] + odd_i[k], even_i[k] - odd_r[k]
                out_r[k + n // 2], out_i[k + n // 2] = even_r[k] - odd_i[k], even_i[k] + odd_r[k]
            continue
        else:
            cos, sin = math.cos(2 * math.pi * k / n), sign * math.sin(2 * math.pi * k / n)
            turn_r = cos * odd_r[k] - sin * odd_i[k]
            turn_i = cos * odd_i[k] + sin * odd_r[k]
        out_r[k], out_i[k] = even_r[k] + turn_r, even_i[k] + turn_i
        out_r[k + n // 2], out_i[k + n // 2] = even_r[k] - turn_r, even_i[k] - turn_i
    return out_r, out_i


def spectrum_tables(blocks, phases):
    length = blocks * phases
    b = np.arange(blocks)[:, None]
    k = np.arange(blocks)[None, :]
    angle = 2.0 * np.pi * b * (2 * k + 1) / (4.0 * blocks)
    forward = np.concatenate([np.cos(angle), -np.sin(angle)], axis=1)
    inverse = np.concatenate([np.cos(angle).T, -np.sin(angle).T], axis=0) / length
    p = np.arange(phases)[:, None]
    turn = 2.0 * np.pi * p * (2 * k + 1) / (4.0 * length)
    turns = np.stack([np.cos(turn), np.sin(turn)], axis=1)[:, :, None, :]
    turns = np.broadcast_to(turns, (phases, 2, 8, blocks))
    return (
        jnp.asarray(forward, BF16),
        jnp.asarray(inverse, BF16),
        jnp.asarray(turns, F32),
    )


def greet(n):
    me = lax.axis_index("seq")
    barrier = pltpu.get_barrier_semaphore()
    for j in range(1, n):
        pl.semaphore_signal(
            barrier, inc=1, device_id={"seq": lax.rem(me + j, n)}, device_id_type=MESH
        )
    return barrier


def all_peers(n, start):
    me = lax.axis_index("seq")
    for j in range(1, n):
        start(lax.rem(me + j, n), j)


def to_peer(src, dst, send_sem, recv_sem, peer):
    return pltpu.make_async_remote_copy(
        src_ref=src,
        dst_ref=dst,
        send_sem=send_sem,
        recv_sem=recv_sem,
        device_id={"seq": peer},
        device_id_type=MESH,
    )


def in_kernel(
    n, x, w, gain, taps, marks,
    got, got_taps, got_marks, turned,
    sent, sent_taps, normed, send_sem, recv_sem, small_send, small_recv,
):
    me = lax.axis_index("seq")
    rows, blocks = got.shape[0], got.shape[4]
    width = x.shape[1]
    each = width // n
    mine = pl.ds(pl.multiple_of(me * each, each), each)
    barrier = greet(n)
    raw = taps[...]
    sent_taps[...] = (raw - THRESH * jnp.tanh(raw * (1.0 / THRESH))).T.astype(BF16)
    pl.semaphore_wait(barrier, n - 1)

    def small_copies(peer, j):
        part = pl.ds(pl.multiple_of(peer * each, each), each)
        return (
            to_peer(marks, got_marks.at[me], small_send.at[0, j], small_recv.at[0, me], peer),
            to_peer(sent_taps.at[part], got_taps.at[me], small_send.at[1, j], small_recv.at[1, me], peer),
        )

    def start_small(peer, j):
        for copy in small_copies(peer, j):
            copy.start()

    all_peers(n, start_small)
    got_marks[me] = marks[...]
    got_taps[me] = sent_taps[mine]
    for at in range(0, x.shape[0], 128):
        part = x[at:at + 128, :]
        scale = lax.rsqrt(jnp.mean(part * part, axis=-1, keepdims=True) + EPS)
        normed[at:at + 128, :] = (part * scale * gain[...]).astype(BF16)

    def big_copy(r, c, peer, j):
        part = pl.ds(pl.multiple_of(peer * each, each), each)
        return to_peer(
            sent.at[r, c, part], got.at[r, c, me + 2],
            send_sem.at[r, c, j], recv_sem.at[r, c, me], peer,
        )

    for r in range(rows):
        tokens = normed[r * blocks:(r + 1) * blocks, :]
        for c in (1, 2, 0):
            for at in range(0, width, 256):
                piece = dot_nn(tokens, w[:, c * width + at:c * width + at + 256])
                sent[r, c, at:at + 256, :] = piece.T.astype(BF16)
            all_peers(n, lambda peer, j: big_copy(r, c, peer, j).start())
            got[r, c, me + 2] = sent[r, c, mine]
    for r in range(rows):
        tokens = normed[r * blocks:(r + 1) * blocks, :]
        turned[r] = tokens.T

    def wait_small(peer, j):
        part = pl.ds(pl.multiple_of(peer * each, each), each)
        to_peer(marks, got_marks.at[peer], small_send.at[0, j], small_recv.at[0, peer], peer).wait()
        to_peer(sent_taps.at[part], got_taps.at[peer], small_send.at[1, j], small_recv.at[1, peer], peer).wait()

    all_peers(n, wait_small)
    for r in range(rows):
        for c in (1, 2, 0):
            def wait_big(peer, j):
                part = pl.ds(pl.multiple_of(peer * each, each), each)
                to_peer(
                    sent.at[r, c, part], got.at[r, c, peer + 2],
                    send_sem.at[r, c, j], recv_sem.at[r, c, peer], peer,
                ).wait()

            all_peers(n, wait_big)
            for slot in range(2):
                before = got[r, c, n + slot].astype(F32)
                got[r, c, slot] = pltpu.roll(before, 1, 1).astype(BF16)


def short_conv(got, cols, same, r, c, p, rows):
    now = got[r, c, p + 2, rows, :].astype(F32)
    one = got[r, c, p + 1, rows, :].astype(F32) * same[0, p, r:r + 1, :]
    two = got[r, c, p, rows, :].astype(F32) * same[1, p, r:r + 1, :]
    value = cols[3 * c, rows, :] * now + cols[3 * c + 1, rows, :] * one + cols[3 * c + 2, rows, :] * two
    return value, (now, one, two)


def spread_cols(cols_in, cols):
    shape = cols.shape[1:]
    for i in range(cols.shape[0]):
        cols[i] = jnp.broadcast_to(cols_in[:, i:i + 1], shape)


def to_frequency(source, table, spec):
    for at in range(0, source.shape[0], 256):
        spec[at:at + 256, :] = dot_nn(source[at:at + 256, :].astype(BF16), table[...])


def load_phases(spec, n, each, at, lane, half):
    re = [spec[pl.ds(p * each + at, 8), lane:lane + 128] for p in range(n)]
    im = [spec[pl.ds(p * each + at, 8), half + lane:half + lane + 128] for p in range(n)]
    return re, im


def turn_phases(re, im, turns, lane, sign):
    out_r, out_i = [re[0]], [im[0]]
    for p in range(1, len(re)):
        cos = turns[p, 0, :, lane:lane + 128]
        sin = turns[p, 1, :, lane:lane + 128]
        if sign > 0:
            out_r.append(re[p] * cos - im[p] * sin)
            out_i.append(im[p] * cos + re[p] * sin)
        else:
            out_r.append(re[p] * cos + im[p] * sin)
            out_i.append(im[p] * cos - re[p] * sin)
    return out_r, out_i


def over_groups(each, blocks, body):
    for lane in range(0, blocks, 128):
        def step(g, carry):
            body(pl.multiple_of(g * 8, 8), lane)
            return carry
        lax.fori_loop(0, each // 8, step, 0)


def conv_kernel(
    n, got, got_taps, got_marks, cols_in, table, inverse, turns,
    mixed, same, spec_taps, spec_gate, gated, long_out,
    cols, spec, sent, send_sem, recv_sem,
):
    me = lax.axis_index("seq")
    rows, each, blocks = got.shape[0], got.shape[3], got.shape[4]
    mine = pl.ds(pl.multiple_of(me * each, each), each)
    barrier = greet(n)
    spread_cols(cols_in, cols)
    first_lane = lax.broadcasted_iota(jnp.int32, (rows, blocks), 1) == 0
    seg = [got_marks[p, 0:rows, :] for p in range(n)]
    mask = [got_marks[p, rows:2 * rows, :].astype(F32) for p in range(n)]
    wrapped = [pltpu.roll(seg[n - 2], 1, 1), pltpu.roll(seg[n - 1], 1, 1)]
    before = wrapped + seg
    for p in range(n):
        one = (before[p + 1] == seg[p]).astype(F32)
        two = (before[p] == seg[p]).astype(F32)
        if p < 1:
            one = jnp.where(first_lane, 0.0, one)
        if p < 2:
            two = jnp.where(first_lane, 0.0, two)
        same[0, p] = one
        same[1, p] = two
        same[2, p] = mask[p]
        if p < 2:
            same[0, n + p] = pltpu.roll(one, blocks - 1, 1)
            same[1, n + p] = pltpu.roll(two, blocks - 1, 1)
            same[2, n + p] = jnp.zeros_like(one)

    for p in range(n):
        spec[p * each:(p + 1) * each, :] = dot_nn(got_taps[p], table[...])

    def taps_group(at, lane):
        re, im = load_phases(spec, n, each, at, lane, blocks)
        re, im = turn_phases(re, im, turns, lane, -1)
        re, im = fft_points(re, im, -1)
        for k in range(n):
            spec_taps[k, 0, pl.ds(at, 8), lane:lane + 128] = re[k]
            spec_taps[k, 1, pl.ds(at, 8), lane:lane + 128] = im[k]

    over_groups(each, blocks, taps_group)
    pl.semaphore_wait(barrier, n - 1)

    for r in range(rows):
        def gate_step(p, carry):
            for at in range(0, each, 32):
                part = pl.ds(at, 32)
                keys, _ = short_conv(got, cols, same, r, 1, p, part)
                values, _ = short_conv(got, cols, same, r, 2, p, part)
                gated[r, p, part, :] = keys * values * same[2, p, r:r + 1, :]
            return carry

        lax.fori_loop(0, n, gate_step, 0)
        for p in range(n):
            spec[p * each:(p + 1) * each, :] = dot_nn(gated[r, p].astype(BF16), table[...])

        def product_group(at, lane):
            re, im = load_phases(spec, n, each, at, lane, blocks)
            re, im = turn_phases(re, im, turns, lane, -1)
            re, im = fft_points(re, im, -1)
            out_r, out_i = [], []
            for k in range(n):
                spec_gate[r, k, 0, pl.ds(at, 8), lane:lane + 128] = re[k]
                spec_gate[r, k, 1, pl.ds(at, 8), lane:lane + 128] = im[k]
                tap_r = spec_taps[k, 0, pl.ds(at, 8), lane:lane + 128]
                tap_i = spec_taps[k, 1, pl.ds(at, 8), lane:lane + 128]
                out_r.append(re[k] * tap_r - im[k] * tap_i)
                out_i.append(re[k] * tap_i + im[k] * tap_r)
            re, im = fft_points(out_r, out_i, 1)
            re, im = turn_phases(re, im, turns, lane, 1)
            for p in range(n):
                spec[pl.ds(p * each + at, 8), lane:lane + 128] = re[p]
                spec[pl.ds(p * each + at, 8), blocks + lane:blocks + lane + 128] = im[p]

        over_groups(each, blocks, product_group)
        for p in range(n):
            long_out[r, p] = dot_nn(spec[p * each:(p + 1) * each, :].astype(BF16), inverse[...])

        def mix_step(p, carry):
            for at in range(0, each, 32):
                part = pl.ds(at, 32)
                query, _ = short_conv(got, cols, same, r, 0, p, part)
                total = long_out[r, p, part, :] + cols[9, part, :] * gated[r, p, part, :]
                long_out[r, p, part, :] = total
                sent[r, p, part, :] = (query * total).astype(BF16)
            return carry

        lax.fori_loop(0, n, mix_step, 0)
        all_peers(n, lambda peer, j: to_peer(
            sent.at[r, peer], mixed.at[r, mine], send_sem.at[r, j], recv_sem.at[r, me], peer,
        ).start())
        mixed[r, mine] = sent[r, me]

    for r in range(rows):
        def wait(peer, j):
            part = pl.ds(pl.multiple_of(peer * each, each), each)
            to_peer(
                sent.at[r, peer], mixed.at[r, part], send_sem.at[r, j], recv_sem.at[r, peer], peer,
            ).wait()

        all_peers(n, wait)


def mlp_kernel(
    n, chunk, mixed, x, cot, mask_col, w_out, gain, w_up, w_down,
    out, back, mid, share_up, share_down, share_out, gain_sum, stats,
    resid, normed, act, grad_act, acc_out, acc_back, turned, turned_cot, mix_back, sent, send_sem, recv_sem,
):
    me = lax.axis_index("seq")
    rows, blocks = mixed.shape[0], mixed.shape[2]
    width, hidden = w_up.shape
    each = width // n
    mine = pl.ds(pl.multiple_of(me * each, each), each)
    barrier = greet(n)
    gain_sum[...] = jnp.zeros_like(gain_sum)
    stat_out = jnp.zeros((1, width), F32)
    stat_mix = jnp.zeros((1, width), F32)
    stat_mlp = jnp.zeros((1, width), F32)
    for r in range(rows):
        tokens = slice(r * blocks, (r + 1) * blocks)
        mask = mask_col[tokens, :]
        mixer = dot_nn(mixed[r].T, w_out[...])
        stat_mix += jnp.sum(mixer * mixer * mask, axis=0, keepdims=True)
        middle = x[tokens, :] + mixer
        resid[...] = middle
        scale = lax.rsqrt(jnp.mean(middle * middle, axis=-1, keepdims=True) + EPS)
        normed[...] = (middle * scale * gain[...]).astype(BF16)
        turned[:, tokens] = normed[...].T
        cot_low = cot[tokens, :].astype(BF16)
        turned_cot[:, tokens] = cot_low.T
        acc_out[...] = jnp.zeros_like(acc_out)
        acc_back[...] = jnp.zeros_like(acc_back)

        def hidden_step(j, carry):
            cols = pl.ds(pl.multiple_of(j * chunk, chunk), chunk)
            up = dot_nn(normed[...], w_up[:, cols])
            square = up * up
            tanh = jnp.tanh(up * (C0 + (C0 * C1) * square))
            half = 0.5 * (1.0 + tanh)
            act_low = (up * half).astype(BF16)
            slope = half + (0.5 * up) * (1.0 - tanh * tanh) * (C0 + (3.0 * C0 * C1) * square)
            act[tokens, cols] = act_low
            acc_out[...] += dot_nn(act_low, w_down[cols, :])
            grad = dot_nt(cot[tokens, :].astype(BF16), w_down[cols, :])
            grad_low = (grad * slope).astype(BF16)
            grad_act[tokens, cols] = grad_low
            acc_back[...] += dot_nt(grad_low, w_up[:, cols])
            return carry

        lax.fori_loop(0, hidden // chunk, hidden_step, 0)
        middle = resid[...]
        mlp = acc_out[...]
        stat_mlp += jnp.sum(mlp * mlp * mask, axis=0, keepdims=True)
        whole = middle + mlp
        stat_out += jnp.sum(whole * whole * mask, axis=0, keepdims=True)
        out[tokens, :] = whole
        scale = lax.rsqrt(jnp.mean(middle * middle, axis=-1, keepdims=True) + EPS)
        grad = acc_back[...]
        gain_sum[...] += jnp.sum(grad * middle * scale, axis=0, keepdims=True)
        scaled = grad * gain[...]
        shift = jnp.mean(scaled * middle, axis=-1, keepdims=True) * (scale * scale * scale)
        grad_mid = cot[tokens, :] + scaled * scale - middle * shift
        mid[tokens, :] = grad_mid
        mix_back[r] = grad_mid.astype(BF16)
        sent[r] = dot_nt(w_out[...], mix_back[r]).astype(BF16)
        if r == 0:
            pl.semaphore_wait(barrier, n - 1)

        def start(peer, j):
            part = pl.ds(pl.multiple_of(peer * each, each), each)
            to_peer(
                sent.at[r, part], back.at[r, me], send_sem.at[r, j], recv_sem.at[r, me], peer,
            ).start()

        all_peers(n, start)
        back[r, me] = sent[r, mine]

    stats[0:1, :] = stat_out
    stats[1:2, :] = stat_mix
    stats[2:3, :] = stat_mlp
    stats[3:4, :] = jnp.broadcast_to(
        jnp.sum(mask_col[...], axis=0, keepdims=True) * (1.0 / width), (1, width)
    )
    stats[4:8, :] = jnp.zeros((4, width), F32)
    share_out[...] = sum(dot_nn(mixed[r], mix_back[r]) for r in range(rows)).astype(BF16)

    def weight_step(j, carry):
        cols = pl.ds(pl.multiple_of(j * chunk, chunk), chunk)
        share_up[:, cols] = dot_nn(turned[...], grad_act[:, cols]).astype(BF16)
        share_down[:, cols] = dot_nn(turned_cot[...], act[:, cols]).astype(BF16)
        return carry

    lax.fori_loop(0, hidden // chunk, weight_step, 0)
    for r in range(rows):
        def wait(peer, j):
            part = pl.ds(pl.multiple_of(peer * each, each), each)
            to_peer(
                sent.at[r, part], back.at[r, peer], send_sem.at[r, j], recv_sem.at[r, peer], peer,
            ).wait()

        all_peers(n, wait)


def back_kernel(
    n, back, got, same, spec_taps, spec_gate, gated, long_out, cols_in, table, inverse, turns,
    got_back, grad_taps, col_sums,
    cols, sums, spec, spec_sum, grad_long, short, sent, send_sem, recv_sem,
):
    me = lax.axis_index("seq")
    rows, each, blocks = got.shape[0], got.shape[3], got.shape[4]
    mine = pl.ds(pl.multiple_of(me * each, each), each)
    barrier = greet(n)
    spread_cols(cols_in, cols)
    sums[...] = jnp.zeros_like(sums)
    spec_sum[...] = jnp.zeros_like(spec_sum)

    def tap_sums(c, part, grad, inputs):
        for i in range(3):
            sums[3 * c + i, part, :] += grad * inputs[i]

    def spread_back(r, c):
        for slot in range(2):
            short[c, n + slot] = pltpu.roll(short[c, slot], blocks - 1, 1)

        def step(p, carry):
            for at in range(0, each, 32):
                part = pl.ds(at, 32)
                value = cols[3 * c, part, :] * short[c, p, part, :]
                value += cols[3 * c + 1, part, :] * (short[c, p + 1, part, :] * same[0, p + 1, r:r + 1, :])
                value += cols[3 * c + 2, part, :] * (short[c, p + 2, part, :] * same[1, p + 2, r:r + 1, :])
                sent[r, c, p, part, :] = value.astype(BF16)
            return carry

        lax.fori_loop(0, n, step, 0)
        all_peers(n, lambda peer, j: to_peer(
            sent.at[r, c, peer], got_back.at[r, c, mine], send_sem.at[r, c, j], recv_sem.at[r, c, me], peer,
        ).start())
        got_back[r, c, mine] = sent[r, c, me]

    for r in range(rows):
        def query_step(p, carry):
            for at in range(0, each, 32):
                part = pl.ds(at, 32)
                grad = back[r, p, part, :].astype(F32)
                query, inputs = short_conv(got, cols, same, r, 0, p, part)
                grad_query = grad * long_out[r, p, part, :]
                value = grad * query
                grad_long[p, part, :] = value
                short[0, p, part, :] = grad_query
                tap_sums(0, part, grad_query, inputs)
                sums[9, part, :] += value * gated[r, p, part, :]
            return carry

        lax.fori_loop(0, n, query_step, 0)
        if r == 0:
            pl.semaphore_wait(barrier, n - 1)
        spread_back(r, 0)
        for p in range(n):
            spec[p * each:(p + 1) * each, :] = dot_nn(grad_long[p].astype(BF16), table[...])

        def product_group(at, lane):
            re, im = load_phases(spec, n, each, at, lane, blocks)
            re, im = turn_phases(re, im, turns, lane, -1)
            re, im = fft_points(re, im, -1)
            out_r, out_i = [], []
            for k in range(n):
                here = (pl.ds(at, 8), slice(lane, lane + 128))
                tap_r, tap_i = spec_taps[(k, 0) + here], spec_taps[(k, 1) + here]
                gate_r, gate_i = spec_gate[(r, k, 0) + here], spec_gate[(r, k, 1) + here]
                spec_sum[(k, 0) + here] += gate_r * re[k] + gate_i * im[k]
                spec_sum[(k, 1) + here] += gate_r * im[k] - gate_i * re[k]
                out_r.append(tap_r * re[k] + tap_i * im[k])
                out_i.append(tap_r * im[k] - tap_i * re[k])
            re, im = fft_points(out_r, out_i, 1)
            re, im = turn_phases(re, im, turns, lane, 1)
            for p in range(n):
                spec[pl.ds(p * each + at, 8), lane:lane + 128] = re[p]
                spec[pl.ds(p * each + at, 8), blocks + lane:blocks + lane + 128] = im[p]

        over_groups(each, blocks, product_group)
        for p in range(n):
            short[0, p] = dot_nn(spec[p * each:(p + 1) * each, :].astype(BF16), inverse[...])

        def gate_step(p, carry):
            for at in range(0, each, 32):
                part = pl.ds(at, 32)
                keys, key_inputs = short_conv(got, cols, same, r, 1, p, part)
                values, value_inputs = short_conv(got, cols, same, r, 2, p, part)
                grad = short[0, p, part, :] + cols[9, part, :] * grad_long[p, part, :]
                grad = grad * same[2, p, r:r + 1, :]
                grad_keys = grad * values
                grad_values = grad * keys
                short[1, p, part, :] = grad_keys
                short[2, p, part, :] = grad_values
                tap_sums(1, part, grad_keys, key_inputs)
                tap_sums(2, part, grad_values, value_inputs)
            return carry

        lax.fori_loop(0, n, gate_step, 0)
        spread_back(r, 1)
        spread_back(r, 2)

    def taps_group(at, lane):
        here = (pl.ds(at, 8), slice(lane, lane + 128))
        re = [spec_sum[(k, 0) + here] for k in range(n)]
        im = [spec_sum[(k, 1) + here] for k in range(n)]
        re, im = fft_points(re, im, 1)
        re, im = turn_phases(re, im, turns, lane, 1)
        for p in range(n):
            spec[pl.ds(p * each + at, 8), lane:lane + 128] = re[p]
            spec[pl.ds(p * each + at, 8), blocks + lane:blocks + lane + 128] = im[p]

    over_groups(each, blocks, taps_group)
    for p in range(n):
        grad_taps[p] = dot_nn(spec[p * each:(p + 1) * each, :].astype(BF16), inverse[...])
    lanes = lax.broadcasted_iota(jnp.int32, col_sums.shape, 1)
    total = jnp.zeros(col_sums.shape, F32)
    for i in range(sums.shape[0]):
        total = jnp.where(lanes == i, jnp.sum(sums[i], axis=-1, keepdims=True), total)
    col_sums[...] = total
    for r in range(rows):
        for c in range(3):
            def wait(peer, j):
                part = pl.ds(pl.multiple_of(peer * each, each), each)
                to_peer(
                    sent.at[r, c, peer], got_back.at[r, c, part], send_sem.at[r, c, j], recv_sem.at[r, c, peer], peer,
                ).wait()

            all_peers(n, wait)


def final_kernel(got_back, turned, w_in, x, mid, gain, grad_in, share_in, gain_sum):
    rows, parts, width, blocks = got_back.shape
    gain_sum[...] = jnp.zeros_like(gain_sum)
    for r in range(rows):
        tokens = slice(r * blocks, (r + 1) * blocks)
        grad = sum(
            dot_nn(w_in[:, c * width:(c + 1) * width], got_back[r, c]) for c in range(parts)
        ).T
        value = x[tokens, :]
        scale = lax.rsqrt(jnp.mean(value * value, axis=-1, keepdims=True) + EPS)
        gain_sum[...] += jnp.sum(grad * value * scale, axis=0, keepdims=True)
        scaled = grad * gain[...]
        shift = jnp.mean(scaled * value, axis=-1, keepdims=True) * (scale * scale * scale)
        grad_in[tokens, :] = mid[tokens, :] + scaled * scale - value * shift
    for c in range(parts):
        for at in range(0, width, 256):
            share_in[:, c * width + at:c * width + at + 256] = sum(
                dot_nt(turned[r], got_back[r, c, at:at + 256, :]) for r in range(rows)
            ).astype(BF16)


def vmem(count):
    return [pl.BlockSpec(memory_space=pltpu.VMEM)] * count


def call(body, outs, scratch, inputs, collective_id=None):
    extra = {}
    if collective_id is not None:
        extra = dict(collective_id=collective_id, has_side_effects=True)
    return pl.pallas_call(
        body,
        out_shape=tuple(jax.ShapeDtypeStruct(*out) for out in outs),
        in_specs=vmem(len(inputs)),
        out_specs=tuple(vmem(len(outs))),
        scratch_shapes=scratch,
        compiler_params=pltpu.CompilerParams(vmem_limit_bytes=VMEM_BYTES, **extra),
    )(*inputs)


def local(
    block_in, segment_ids, valid_mask, cotangent, gain_mix, in_proj, short_taps, long_kernel,
    skip_gain, out_proj, gain_mlp, up_proj, down_proj,
):
    rows, blocks, _, width = block_in.shape
    hidden = up_proj.shape[1]
    n = lax.axis_size("seq")
    me = lax.axis_index("seq")
    each = width // n
    tokens = rows * blocks
    x = block_in.reshape(tokens, width)
    cot = cotangent.reshape(tokens, width)
    raw = long_kernel[:, 0, :]
    marks = jnp.concatenate(
        [segment_ids[:, :, 0], valid_mask[:, :, 0], jnp.zeros((8 - 2 * rows, blocks), jnp.int32)]
    )
    own = lax.dynamic_slice_in_dim(
        jnp.concatenate([short_taps.reshape(3, 3, width), jnp.broadcast_to(skip_gain, (1, 3, width))]),
        me * each, each, axis=2,
    )
    cols_in = jnp.concatenate([own[:3, c] for c in range(3)] + [own[3, :1]]).T
    cols_in = jnp.pad(cols_in, ((0, 0), (0, 128 - cols_in.shape[1])))
    table, inverse, turns = spectrum_tables(blocks, n)
    dma = pltpu.SemaphoreType.DMA

    got, got_taps, got_marks, turned = call(
        functools.partial(in_kernel, n),
        [
            ((rows, 3, n + 2, each, blocks), BF16),
            ((n, each, blocks), BF16),
            ((n,) + marks.shape, jnp.int32),
            ((rows, width, blocks), BF16),
        ],
        [
            pltpu.VMEM((rows, 3, width, blocks), BF16),
            pltpu.VMEM((width, blocks), BF16),
            pltpu.VMEM((tokens, width), BF16),
            dma((rows, 3, n)), dma((rows, 3, n)), dma((2, n)), dma((2, n)),
        ],
        (x, in_proj, gain_mix[None], raw, marks),
        1,
    )
    mixed, same, spec_taps, spec_gate, gated, long_out = call(
        functools.partial(conv_kernel, n),
        [
            ((rows, width, blocks), BF16),
            ((3, n + 2, rows, blocks), F32),
            ((n, 2, each, blocks), F32),
            ((rows, n, 2, each, blocks), F32),
            ((rows, n, each, blocks), F32),
            ((rows, n, each, blocks), F32),
        ],
        [
            pltpu.VMEM((10, each, blocks), F32),
            pltpu.VMEM((width, 2 * blocks), F32),
            pltpu.VMEM((rows, n, each, blocks), BF16),
            dma((rows, n)), dma((rows, n)),
        ],
        (got, got_taps, got_marks, cols_in, table, inverse, turns),
        2,
    )
    mask_col = valid_mask[:, :, 0].astype(F32).reshape(tokens, 1)
    chunk = 512
    block_out, back, mid, share_up, share_down, share_out, gain_two, stats = call(
        functools.partial(mlp_kernel, n, chunk),
        [
            ((tokens, width), F32),
            ((rows, n, each, blocks), BF16),
            ((tokens, width), F32),
            ((width, hidden), BF16),
            ((width, hidden), BF16),
            ((width, width), BF16),
            ((1, width), F32),
            ((8, width), F32),
        ],
        [
            pltpu.VMEM((blocks, width), F32),
            pltpu.VMEM((blocks, width), BF16),
            pltpu.VMEM((tokens, hidden), BF16),
            pltpu.VMEM((tokens, hidden), BF16),
            pltpu.VMEM((blocks, width), F32),
            pltpu.VMEM((blocks, width), F32),
            pltpu.VMEM((width, tokens), BF16),
            pltpu.VMEM((width, tokens), BF16),
            pltpu.VMEM((rows, blocks, width), BF16),
            pltpu.VMEM((rows, width, blocks), BF16),
            dma((rows, n)), dma((rows, n)),
        ],
        (mixed, x, cot, mask_col, out_proj, gain_mlp[None], up_proj, down_proj),
        3,
    )
    got_back, grad_taps, col_sums = call(
        functools.partial(back_kernel, n),
        [
            ((rows, 3, width, blocks), BF16),
            ((n, each, blocks), F32),
            ((each, 128), F32),
        ],
        [
            pltpu.VMEM((10, each, blocks), F32),
            pltpu.VMEM((10, each, blocks), F32),
            pltpu.VMEM((width, 2 * blocks), F32),
            pltpu.VMEM((n, 2, each, blocks), F32),
            pltpu.VMEM((n, each, blocks), F32),
            pltpu.VMEM((3, n + 2, each, blocks), F32),
            pltpu.VMEM((rows, 3, n, each, blocks), BF16),
            dma((rows, 3, n)), dma((rows, 3, n)),
        ],
        (back, got, same, spec_taps, spec_gate, gated, long_out, cols_in, table, inverse, turns),
        4,
    )
    grad_flat, share_in, gain_one = call(
        final_kernel,
        [((tokens, width), F32), ((width, 3 * width), BF16), ((1, width), F32)],
        [],
        (got_back, turned, in_proj, x, mid, gain_mix[None]),
    )

    def summed(share):
        quarter = lax.psum_scatter(share, "rows", scatter_dimension=1, tiled=True)
        own_rows = lax.psum_scatter(quarter, "seq", scatter_dimension=0, tiled=True)
        return lax.all_gather(own_rows, "rows", axis=1, tiled=True).astype(F32)

    grad_up = summed(share_up)
    grad_out = summed(share_out)
    grad_inp = summed(share_in)
    quarter = lax.psum_scatter(share_down, "rows", scatter_dimension=0, tiled=True)
    own_cols = lax.psum_scatter(quarter, "seq", scatter_dimension=1, tiled=True)
    grad_down = lax.all_gather(own_cols, "rows", axis=0, tiled=True).T.astype(F32)

    taps_back = lax.all_to_all(grad_taps.astype(BF16), "seq", split_axis=0, concat_axis=0, tiled=True)
    taps_back = lax.psum(taps_back.reshape(width, blocks), "rows").T.astype(F32)
    tanh = jnp.tanh(raw / THRESH)
    grad_kernel = (taps_back * tanh * tanh)[:, None, :]

    spread = lax.dynamic_update_slice_in_dim(
        jnp.zeros((10, width), F32), col_sums[:, :10].T, me * each, axis=1
    )
    gain_one, gain_two, stats, spread = lax.psum(
        (gain_one, gain_two, jnp.sum(stats, axis=1), spread), ("rows", "seq")
    )
    grad_tap_rows = jnp.transpose(spread[:9].reshape(3, 3, width), (1, 0, 2)).reshape(3, 3 * width)
    rms_stats = jnp.sqrt(stats[:3] / (jnp.maximum(stats[3], 1.0) * width))
    return (
        block_out.reshape(block_in.shape),
        grad_flat.reshape(block_in.shape),
        gain_one[0],
        grad_inp,
        grad_tap_rows,
        grad_kernel,
        spread[9],
        grad_out,
        gain_two[0],
        grad_up,
        grad_down,
        rms_stats,
    )


def chosen(block_in, *rest):
    rows, blocks, _, width = block_in.shape
    n = lax.axis_size("seq")
    fits = blocks % 256 == 0 and width % (32 * n) == 0 and n == 8 and 2 * rows <= 8
    return (local if fits else general_local)(block_in, *rest)


def solution(mesh):
    return jax.shard_map(
        chosen,
        mesh=mesh,
        in_specs=(
            P("rows", None, "seq", None),
            P("rows", None, "seq"),
            P("rows", None, "seq"),
            P("rows", None, "seq", None),
            P(),
            P(),
            P(),
            P(None, "seq", None),
            P(),
            P(),
            P(),
            P(),
            P(),
        ),
        out_specs=(
            P("rows", None, "seq", None),
            P("rows", None, "seq", None),
            P(),
            P("seq", None),
            P(),
            P(None, "seq", None),
            P(),
            P("seq", None),
            P(),
            P("seq", None),
            P("seq", None),
            P(),
        ),
        check_vma=False,
    )
```

```python
import functools
import math

import jax
import jax.numpy as jnp
import numpy as np
from jax import lax
from jax.experimental import pallas as pl
from jax.experimental.pallas import tpu as pltpu
from jax.sharding import PartitionSpec as P

EPS = 1e-05
THRESH = 0.003
HIGH = lax.Precision.HIGHEST


def shortened(x):

    def short(part):
        return part.astype(jnp.bfloat16) if part.dtype == jnp.float32 else part

    return jax.tree.map(short, x)


def passed_along(block, axis, distance):
    devices = range(lax.axis_size(axis))
    route = [((i - distance) % len(devices), i) for i in devices]
    return lax.ppermute(block, axis, route)


def norm_scale(value, gain):
    return value * lax.rsqrt(jnp.mean(value * value, axis=-1, keepdims=True) + EPS) * gain


def angle_tables(left_count, right_count, period):
    left_idx = jnp.arange(left_count, dtype=jnp.int32)[:, None]
    right_idx = jnp.arange(right_count, dtype=jnp.int32)[None, :]
    phase = (left_idx * right_idx % period).astype(jnp.float32) * (2.0 * math.pi / period)
    return (jnp.cos(phase), jnp.sin(phase))


def twiddle_tables(shard_index, spec_len, whole_len):
    turned = shard_index * jnp.arange(spec_len, dtype=jnp.int32) % whole_len
    phase = turned.astype(jnp.float32) * (2.0 * math.pi / whole_len)
    return (jnp.cos(phase)[None, :, None], jnp.sin(phase)[None, :, None])


def local_forward(signal, shard_index, whole_len):
    blocks = signal.shape[1]
    cos_table, sin_table = angle_tables(blocks, 2 * blocks, 2 * blocks)
    real_part = jnp.einsum("rjd,jk->rkd", signal, cos_table, precision=HIGH)
    imag_part = -jnp.einsum("rjd,jk->rkd", signal, sin_table, precision=HIGH)
    cos_twid, sin_twid = twiddle_tables(shard_index, 2 * blocks, whole_len)
    out_real = real_part * cos_twid + imag_part * sin_twid
    out_imag = imag_part * cos_twid - real_part * sin_twid
    return (out_real[:, :, None, :], out_imag[:, :, None, :])


def cross_section(real_part, imag_part, direction):
    count = real_part.shape[2]
    cos_table, sin_table = angle_tables(count, count, count)
    re_cos = jnp.einsum("rcpd,pm->rcmd", real_part, cos_table, precision=HIGH)
    re_sin = jnp.einsum("rcpd,pm->rcmd", real_part, sin_table, precision=HIGH)
    im_cos = jnp.einsum("rcpd,pm->rcmd", imag_part, cos_table, precision=HIGH)
    im_sin = jnp.einsum("rcpd,pm->rcmd", imag_part, sin_table, precision=HIGH)
    return (re_cos - direction * im_sin, im_cos + direction * re_sin)


def local_inverse(real_part, imag_part, shard_index, whole_len):
    real_part = real_part[:, :, 0, :]
    imag_part = imag_part[:, :, 0, :]
    spec_len = real_part.shape[1]
    cos_twid, sin_twid = twiddle_tables(shard_index, spec_len, whole_len)
    turned_re = real_part * cos_twid - imag_part * sin_twid
    turned_im = imag_part * cos_twid + real_part * sin_twid
    cos_table, sin_table = angle_tables(spec_len, spec_len // 2, spec_len)
    result = jnp.einsum("rkd,kj->rjd", turned_re, cos_table, precision=HIGH)
    result = result - jnp.einsum("rkd,kj->rjd", turned_im, sin_table, precision=HIGH)
    return result / whole_len


def earlier(members, at_start):
    received = jax.tree.map(
        lambda part, own: part.astype(own.dtype),
        passed_along(shortened(members), "seq", 1),
        members,
    )
    placed = []
    for member in received:
        rolled = jnp.concatenate([jnp.zeros_like(member[:, :1]), member[:, :-1]], axis=1)
        placed.append(jnp.where(at_start, rolled, member))
    return tuple(placed)


def later(member, at_end):
    received = passed_along(member.astype(jnp.bfloat16), "seq", -1).astype(member.dtype)
    rolled = jnp.concatenate([received[:, 1:], jnp.zeros_like(received[:, :1])], axis=1)
    return jnp.where(at_end, rolled, received)


def times_trans(left, right):
    return lax.dot_general(
        left, right, (((1,), (1,)), ((), ())), preferred_element_type=jnp.float32
    )


def trans_times(left, right):
    return lax.dot_general(
        left, right, (((0,), (0,)), ((), ())), preferred_element_type=jnp.float32
    )


def general_local(
    block_in,
    segment_ids,
    valid_mask,
    cotangent,
    gain_mix,
    in_proj,
    short_taps,
    long_kernel,
    skip_gain,
    out_proj,
    gain_mlp,
    up_proj,
    down_proj,
):
    batch_rows = block_in.shape[0]
    blocks = block_in.shape[1]
    width = block_in.shape[3]
    shard_count = lax.axis_size("seq")
    shard_index = lax.axis_index("seq")
    whole_len = 2 * blocks * shard_count
    tokens = batch_rows * blocks
    at_start = shard_index == 0
    at_end = shard_index == shard_count - 1
    flat_in = block_in.reshape(tokens, width)
    mask_rows = valid_mask[:, :, 0].astype(jnp.float32)[:, :, None]
    normed_one = norm_scale(flat_in, gain_mix).astype(jnp.bfloat16)
    proj_low = jnp.dot(normed_one, in_proj, preferred_element_type=jnp.float32).astype(jnp.bfloat16)
    proj_low = proj_low.reshape(batch_rows, blocks, 3 * width)
    seg_low = segment_ids[:, :, 0].astype(jnp.bfloat16)[:, :, None]
    prev_one = earlier((proj_low, seg_low), at_start)
    prev_two = earlier(prev_one, at_start)
    same_one = (prev_one[1] == seg_low).astype(jnp.float32)
    same_two = (prev_two[1] == seg_low).astype(jnp.float32)
    proj_now = proj_low.astype(jnp.float32)
    proj_one = prev_one[0].astype(jnp.float32)
    proj_two = prev_two[0].astype(jnp.float32)
    conv_short = (
        short_taps[0] * proj_now
        + short_taps[1] * proj_one * same_one
        + short_taps[2] * proj_two * same_two
    )
    query = conv_short[:, :, :width]
    keys = conv_short[:, :, width : 2 * width]
    values = conv_short[:, :, 2 * width :]
    gated = keys * values * mask_rows
    raw_taps = long_kernel[:, 0, :]
    taps_eff = raw_taps - THRESH * jnp.tanh(raw_taps / THRESH)
    kern_re, kern_im = local_forward(taps_eff[None], shard_index, whole_len)
    kern_re, kern_im = (
        lax.all_to_all(
            kern_re.astype(jnp.bfloat16), "seq", split_axis=1, concat_axis=2, tiled=True
        ).astype(kern_re.dtype),
        lax.all_to_all(
            kern_im.astype(jnp.bfloat16), "seq", split_axis=1, concat_axis=2, tiled=True
        ).astype(kern_im.dtype),
    )
    kern_re, kern_im = cross_section(kern_re, kern_im, -1.0)
    gate_re, gate_im = local_forward(gated, shard_index, whole_len)
    gate_re, gate_im = (
        lax.all_to_all(
            gate_re.astype(jnp.bfloat16), "seq", split_axis=1, concat_axis=2, tiled=True
        ).astype(gate_re.dtype),
        lax.all_to_all(
            gate_im.astype(jnp.bfloat16), "seq", split_axis=1, concat_axis=2, tiled=True
        ).astype(gate_im.dtype),
    )
    gate_re, gate_im = cross_section(gate_re, gate_im, -1.0)
    prod_re = gate_re * kern_re - gate_im * kern_im
    prod_im = gate_re * kern_im + gate_im * kern_re
    prod_re, prod_im = cross_section(prod_re, prod_im, 1.0)
    prod_re, prod_im = (
        lax.all_to_all(
            prod_re.astype(jnp.bfloat16), "seq", split_axis=2, concat_axis=1, tiled=True
        ).astype(prod_re.dtype),
        lax.all_to_all(
            prod_im.astype(jnp.bfloat16), "seq", split_axis=2, concat_axis=1, tiled=True
        ).astype(prod_im.dtype),
    )
    long_out = local_inverse(prod_re, prod_im, shard_index, whole_len) + skip_gain * gated
    mixer_low = (query * long_out).reshape(tokens, width).astype(jnp.bfloat16)
    mixer_out = jnp.dot(mixer_low, out_proj, preferred_element_type=jnp.float32)
    resid_mid = flat_in + mixer_out
    normed_two = norm_scale(resid_mid, gain_mlp).astype(jnp.bfloat16)
    up_val = jnp.dot(normed_two, up_proj, preferred_element_type=jnp.float32)
    act_low = jax.nn.gelu(up_val).astype(jnp.bfloat16)
    mlp_out = jnp.dot(act_low, down_proj, preferred_element_type=jnp.float32)
    flat_out = resid_mid + mlp_out
    grad_out = cotangent.reshape(tokens, width)
    grad_mlp = grad_out.astype(jnp.bfloat16)
    grad_down = trans_times(act_low, grad_mlp)
    grad_act = times_trans(grad_mlp, down_proj)
    unused_val, gelu_back = jax.vjp(jax.nn.gelu, up_val)
    grad_upval = gelu_back(grad_act)[0].astype(jnp.bfloat16)
    grad_up = trans_times(normed_two, grad_upval)
    grad_norm_two = times_trans(grad_upval, up_proj)
    unused_two, norm_back_two = jax.vjp(norm_scale, resid_mid, gain_mlp)
    grad_resid, grad_gain_two = norm_back_two(grad_norm_two)
    grad_mid = grad_out + grad_resid
    grad_mix = grad_mid.astype(jnp.bfloat16)
    grad_outp = trans_times(mixer_low, grad_mix)
    grad_prod = times_trans(grad_mix, out_proj).reshape(batch_rows, blocks, width)
    grad_query = grad_prod * long_out
    grad_long = grad_prod * query
    back_re, back_im = local_forward(grad_long, shard_index, whole_len)
    back_re, back_im = (
        lax.all_to_all(
            back_re.astype(jnp.bfloat16), "seq", split_axis=1, concat_axis=2, tiled=True
        ).astype(back_re.dtype),
        lax.all_to_all(
            back_im.astype(jnp.bfloat16), "seq", split_axis=1, concat_axis=2, tiled=True
        ).astype(back_im.dtype),
    )
    back_re, back_im = cross_section(back_re, back_im, -1.0)
    sig_re = kern_re * back_re + kern_im * back_im
    sig_im = kern_re * back_im - kern_im * back_re
    tap_re = jnp.sum(gate_re * back_re + gate_im * back_im, axis=0, keepdims=True)
    tap_im = jnp.sum(gate_re * back_im - gate_im * back_re, axis=0, keepdims=True)
    sig_re, sig_im = cross_section(sig_re, sig_im, 1.0)
    tap_re, tap_im = cross_section(tap_re, tap_im, 1.0)
    sig_re, sig_im, tap_re, tap_im = (
        lax.all_to_all(
            sig_re.astype(jnp.bfloat16), "seq", split_axis=2, concat_axis=1, tiled=True
        ).astype(sig_re.dtype),
        lax.all_to_all(
            sig_im.astype(jnp.bfloat16), "seq", split_axis=2, concat_axis=1, tiled=True
        ).astype(sig_im.dtype),
        lax.all_to_all(
            tap_re.astype(jnp.bfloat16), "seq", split_axis=2, concat_axis=1, tiled=True
        ).astype(tap_re.dtype),
        lax.all_to_all(
            tap_im.astype(jnp.bfloat16), "seq", split_axis=2, concat_axis=1, tiled=True
        ).astype(tap_im.dtype),
    )
    grad_gated = local_inverse(sig_re, sig_im, shard_index, whole_len) + skip_gain * grad_long
    grad_taps_eff = local_inverse(tap_re, tap_im, shard_index, whole_len)[0]
    tanh_val = jnp.tanh(raw_taps / THRESH)
    grad_kernel = (grad_taps_eff * tanh_val * tanh_val)[:, None, :]
    grad_kernel = lax.psum(grad_kernel.astype(jnp.bfloat16), "rows").astype(jnp.float32)
    grad_skip = jnp.sum(grad_long * gated, axis=(0, 1))
    grad_short = jnp.concatenate(
        [grad_query, grad_gated * values * mask_rows, grad_gated * keys * mask_rows], axis=2
    )
    grad_tap_rows = jnp.stack(
        [
            jnp.sum(grad_short * proj_now, axis=(0, 1)),
            jnp.sum(grad_short * proj_one * same_one, axis=(0, 1)),
            jnp.sum(grad_short * proj_two * same_two, axis=(0, 1)),
        ]
    )
    inner_term = short_taps[1] * grad_short * same_one + later(
        short_taps[2] * grad_short * same_two, at_end
    )
    grad_proj = short_taps[0] * grad_short + later(inner_term, at_end)
    grad_proj = grad_proj.reshape(tokens, 3 * width).astype(jnp.bfloat16)
    grad_inp = trans_times(normed_one, grad_proj)
    grad_norm_one = times_trans(grad_proj, in_proj)
    unused_one, norm_back_one = jax.vjp(norm_scale, flat_in, gain_mix)
    grad_first, grad_gain_one = norm_back_one(grad_norm_one)
    grad_flat = grad_mid + grad_first
    mask_flat = mask_rows.reshape(tokens, 1)
    stat_sums = jnp.stack(
        [
            jnp.sum(mask_flat * flat_out * flat_out),
            jnp.sum(mask_flat * mixer_out * mixer_out),
            jnp.sum(mask_flat * mlp_out * mlp_out),
            jnp.sum(mask_flat),
        ]
    )
    grad_gain_one, grad_gain_two, grad_tap_rows, grad_skip, stat_sums = lax.psum(
        (grad_gain_one, grad_gain_two, grad_tap_rows, grad_skip, stat_sums), ("rows", "seq")
    )
    rms_stats = jnp.sqrt(stat_sums[:3] / (jnp.maximum(stat_sums[3], 1.0) * width))
    shares = (
        lax.psum_scatter(grad_inp, "seq", scatter_dimension=0, tiled=True),
        lax.psum_scatter(grad_outp, "seq", scatter_dimension=0, tiled=True),
        lax.psum_scatter(grad_up, "seq", scatter_dimension=0, tiled=True),
        lax.psum_scatter(grad_down, "seq", scatter_dimension=0, tiled=True),
    )
    grad_inp, grad_outp, grad_up, grad_down = (
        lax.psum(shares[0].astype(jnp.bfloat16), "rows").astype(jnp.float32),
        lax.psum(shares[1].astype(jnp.bfloat16), "rows").astype(jnp.float32),
        lax.psum(shares[2].astype(jnp.bfloat16), "rows").astype(jnp.float32),
        lax.psum(shares[3].astype(jnp.bfloat16), "rows").astype(jnp.float32),
    )
    return (
        flat_out.reshape(block_in.shape),
        grad_flat.reshape(block_in.shape),
        grad_gain_one,
        grad_inp,
        grad_tap_rows,
        grad_kernel,
        grad_skip,
        grad_outp,
        grad_gain_two,
        grad_up,
        grad_down,
        rms_stats,
    )


MESH = pl.DeviceIdType.MESH
F32 = jnp.float32
BF16 = jnp.bfloat16
VMEM_BYTES = 63 * 1024 * 1024
ROOT_HALF = math.sqrt(0.5)
C0 = math.sqrt(2.0 / math.pi)
C1 = 0.044715


def dot_nn(a, b):
    return lax.dot_general(a, b, (((1,), (0,)), ((), ())), preferred_element_type=F32)


def dot_nt(a, b):
    return lax.dot_general(a, b, (((1,), (1,)), ((), ())), preferred_element_type=F32)


def fft_points(re, im, sign):
    n = len(re)
    if n == 1:
        return re, im
    even_r, even_i = fft_points(re[0::2], im[0::2], sign)
    odd_r, odd_i = fft_points(re[1::2], im[1::2], sign)
    out_r, out_i = [None] * n, [None] * n
    for k in range(n // 2):
        if k == 0:
            turn_r, turn_i = odd_r[0], odd_i[0]
        elif 4 * k == n:
            if sign > 0:
                out_r[k], out_i[k] = even_r[k] - odd_i[k], even_i[k] + odd_r[k]
                out_r[k + n // 2], out_i[k + n // 2] = even_r[k] + odd_i[k], even_i[k] - odd_r[k]
            else:
                out_r[k], out_i[k] = even_r[k] + odd_i[k], even_i[k] - odd_r[k]
                out_r[k + n // 2], out_i[k + n // 2] = even_r[k] - odd_i[k], even_i[k] + odd_r[k]
            continue
        else:
            cos, sin = math.cos(2 * math.pi * k / n), sign * math.sin(2 * math.pi * k / n)
            turn_r = cos * odd_r[k] - sin * odd_i[k]
            turn_i = cos * odd_i[k] + sin * odd_r[k]
        out_r[k], out_i[k] = even_r[k] + turn_r, even_i[k] + turn_i
        out_r[k + n // 2], out_i[k + n // 2] = even_r[k] - turn_r, even_i[k] - turn_i
    return out_r, out_i


def spectrum_tables(blocks, phases):
    length = blocks * phases
    b = np.arange(blocks)[:, None]
    k = np.arange(blocks)[None, :]
    angle = 2.0 * np.pi * b * (2 * k + 1) / (4.0 * blocks)
    forward = np.concatenate([np.cos(angle), -np.sin(angle)], axis=1)
    inverse = np.concatenate([np.cos(angle).T, -np.sin(angle).T], axis=0) / length
    p = np.arange(phases)[:, None]
    turn = 2.0 * np.pi * p * (2 * k + 1) / (4.0 * length)
    turns = np.stack([np.cos(turn), np.sin(turn)], axis=1)[:, :, None, :]
    turns = np.broadcast_to(turns, (phases, 2, 8, blocks))
    return (
        jnp.asarray(forward, BF16),
        jnp.asarray(inverse, BF16),
        jnp.asarray(turns, F32),
    )


def greet(n):
    me = lax.axis_index("seq")
    barrier = pltpu.get_barrier_semaphore()
    for j in range(1, n):
        pl.semaphore_signal(
            barrier, inc=1, device_id={"seq": lax.rem(me + j, n)}, device_id_type=MESH
        )
    return barrier


def all_peers(n, start):
    me = lax.axis_index("seq")
    for j in range(1, n):
        start(lax.rem(me + j, n), j)


def to_peer(src, dst, send_sem, recv_sem, peer):
    return pltpu.make_async_remote_copy(
        src_ref=src,
        dst_ref=dst,
        send_sem=send_sem,
        recv_sem=recv_sem,
        device_id={"seq": peer},
        device_id_type=MESH,
    )


def in_kernel(
    n, x, w, gain, taps, marks,
    got, got_taps, got_marks, turned,
    sent, sent_taps, normed, send_sem, recv_sem, small_send, small_recv,
):
    me = lax.axis_index("seq")
    rows, blocks = got.shape[0], got.shape[4]
    width = x.shape[1]
    each = width // n
    mine = pl.ds(pl.multiple_of(me * each, each), each)
    barrier = greet(n)
    raw = taps[...]
    sent_taps[...] = (raw - THRESH * jnp.tanh(raw * (1.0 / THRESH))).T.astype(BF16)
    pl.semaphore_wait(barrier, n - 1)

    def small_copies(peer, j):
        part = pl.ds(pl.multiple_of(peer * each, each), each)
        return (
            to_peer(marks, got_marks.at[me], small_send.at[0, j], small_recv.at[0, me], peer),
            to_peer(sent_taps.at[part], got_taps.at[me], small_send.at[1, j], small_recv.at[1, me], peer),
        )

    def start_small(peer, j):
        for copy in small_copies(peer, j):
            copy.start()

    all_peers(n, start_small)
    got_marks[me] = marks[...]
    got_taps[me] = sent_taps[mine]
    for at in range(0, x.shape[0], 128):
        part = x[at:at + 128, :]
        scale = lax.rsqrt(jnp.mean(part * part, axis=-1, keepdims=True) + EPS)
        normed[at:at + 128, :] = (part * scale * gain[...]).astype(BF16)

    def big_copy(r, c, peer, j):
        part = pl.ds(pl.multiple_of(peer * each, each), each)
        return to_peer(
            sent.at[r, c, part], got.at[r, c, me + 2],
            send_sem.at[r, c, j], recv_sem.at[r, c, me], peer,
        )

    for r in range(rows):
        tokens = normed[r * blocks:(r + 1) * blocks, :]
        for c in (1, 2, 0):
            for at in range(0, width, 256):
                piece = dot_nn(tokens, w[:, c * width + at:c * width + at + 256])
                sent[r, c, at:at + 256, :] = piece.T.astype(BF16)
            all_peers(n, lambda peer, j: big_copy(r, c, peer, j).start())
            got[r, c, me + 2] = sent[r, c, mine]
    for r in range(rows):
        tokens = normed[r * blocks:(r + 1) * blocks, :]
        turned[r] = tokens.T

    def wait_small(peer, j):
        part = pl.ds(pl.multiple_of(peer * each, each), each)
        to_peer(marks, got_marks.at[peer], small_send.at[0, j], small_recv.at[0, peer], peer).wait()
        to_peer(sent_taps.at[part], got_taps.at[peer], small_send.at[1, j], small_recv.at[1, peer], peer).wait()

    all_peers(n, wait_small)
    for r in range(rows):
        for c in (1, 2, 0):
            def wait_big(peer, j):
                part = pl.ds(pl.multiple_of(peer * each, each), each)
                to_peer(
                    sent.at[r, c, part], got.at[r, c, peer + 2],
                    send_sem.at[r, c, j], recv_sem.at[r, c, peer], peer,
                ).wait()

            all_peers(n, wait_big)
            for slot in range(2):
                before = got[r, c, n + slot].astype(F32)
                got[r, c, slot] = pltpu.roll(before, 1, 1).astype(BF16)


def short_conv(got, cols, same, r, c, p, rows):
    now = got[r, c, p + 2, rows, :].astype(F32)
    one = got[r, c, p + 1, rows, :].astype(F32) * same[0, p, r:r + 1, :]
    two = got[r, c, p, rows, :].astype(F32) * same[1, p, r:r + 1, :]
    value = cols[3 * c, rows, :] * now + cols[3 * c + 1, rows, :] * one + cols[3 * c + 2, rows, :] * two
    return value, (now, one, two)


def folded(value):
    return sum(value[:, at:at + 128] for at in range(0, value.shape[1], 128))


def spread_cols(cols_in, cols):
    shape = cols.shape[1:]
    for i in range(cols.shape[0]):
        cols[i] = jnp.broadcast_to(cols_in[:, i:i + 1], shape)


def to_frequency(source, table, spec):
    for at in range(0, source.shape[0], 256):
        spec[at:at + 256, :] = dot_nn(source[at:at + 256, :].astype(BF16), table[...])


def load_phases(spec, n, each, at, lane, half):
    re = [spec[pl.ds(p * each + at, 8), lane:lane + 128] for p in range(n)]
    im = [spec[pl.ds(p * each + at, 8), half + lane:half + lane + 128] for p in range(n)]
    return re, im


def turn_phases(re, im, turns, lane, sign):
    out_r, out_i = [re[0]], [im[0]]
    for p in range(1, len(re)):
        cos = turns[p, 0, :, lane:lane + 128]
        sin = turns[p, 1, :, lane:lane + 128]
        if sign > 0:
            out_r.append(re[p] * cos - im[p] * sin)
            out_i.append(im[p] * cos + re[p] * sin)
        else:
            out_r.append(re[p] * cos + im[p] * sin)
            out_i.append(im[p] * cos - re[p] * sin)
    return out_r, out_i


def over_groups(each, blocks, body):
    for lane in range(0, blocks, 128):
        def step(g, carry):
            body(pl.multiple_of(g * 8, 8), lane)
            return carry
        lax.fori_loop(0, each // 8, step, 0)


def conv_kernel(
    n, got, got_taps, got_marks, cols_in, table, inverse, turns,
    mixed, same, spec_taps, spec_gate, gated, long_out,
    cols, spec, sent, send_sem, recv_sem,
):
    me = lax.axis_index("seq")
    rows, each, blocks = got.shape[0], got.shape[3], got.shape[4]
    mine = pl.ds(pl.multiple_of(me * each, each), each)
    barrier = greet(n)
    spread_cols(cols_in, cols)
    first_lane = lax.broadcasted_iota(jnp.int32, (rows, blocks), 1) == 0
    seg = [got_marks[p, 0:rows, :] for p in range(n)]
    mask = [got_marks[p, rows:2 * rows, :].astype(F32) for p in range(n)]
    wrapped = [pltpu.roll(seg[n - 2], 1, 1), pltpu.roll(seg[n - 1], 1, 1)]
    before = wrapped + seg
    for p in range(n):
        one = (before[p + 1] == seg[p]).astype(F32)
        two = (before[p] == seg[p]).astype(F32)
        if p < 1:
            one = jnp.where(first_lane, 0.0, one)
        if p < 2:
            two = jnp.where(first_lane, 0.0, two)
        same[0, p] = one
        same[1, p] = two
        same[2, p] = mask[p]
        if p < 2:
            same[0, n + p] = pltpu.roll(one, blocks - 1, 1)
            same[1, n + p] = pltpu.roll(two, blocks - 1, 1)
            same[2, n + p] = jnp.zeros_like(one)

    for p in range(n):
        spec[p * each:(p + 1) * each, :] = dot_nn(got_taps[p], table[...])

    def taps_group(at, lane):
        re, im = load_phases(spec, n, each, at, lane, blocks)
        re, im = turn_phases(re, im, turns, lane, -1)
        re, im = fft_points(re, im, -1)
        for k in range(n):
            spec_taps[k, 0, pl.ds(at, 8), lane:lane + 128] = re[k]
            spec_taps[k, 1, pl.ds(at, 8), lane:lane + 128] = im[k]

    over_groups(each, blocks, taps_group)
    pl.semaphore_wait(barrier, n - 1)

    for r in range(rows):
        def gate_step(p, carry):
            for at in range(0, each, 32):
                part = pl.ds(at, 32)
                keys, _ = short_conv(got, cols, same, r, 1, p, part)
                values, _ = short_conv(got, cols, same, r, 2, p, part)
                gated[r, p, part, :] = keys * values * same[2, p, r:r + 1, :]
            return carry

        lax.fori_loop(0, n, gate_step, 0)
        for p in range(n):
            spec[p * each:(p + 1) * each, :] = dot_nn(gated[r, p].astype(BF16), table[...])

        def product_group(at, lane):
            re, im = load_phases(spec, n, each, at, lane, blocks)
            re, im = turn_phases(re, im, turns, lane, -1)
            re, im = fft_points(re, im, -1)
            out_r, out_i = [], []
            for k in range(n):
                spec_gate[r, k, 0, pl.ds(at, 8), lane:lane + 128] = re[k]
                spec_gate[r, k, 1, pl.ds(at, 8), lane:lane + 128] = im[k]
                tap_r = spec_taps[k, 0, pl.ds(at, 8), lane:lane + 128]
                tap_i = spec_taps[k, 1, pl.ds(at, 8), lane:lane + 128]
                out_r.append(re[k] * tap_r - im[k] * tap_i)
                out_i.append(re[k] * tap_i + im[k] * tap_r)
            re, im = fft_points(out_r, out_i, 1)
            re, im = turn_phases(re, im, turns, lane, 1)
            for p in range(n):
                spec[pl.ds(p * each + at, 8), lane:lane + 128] = re[p]
                spec[pl.ds(p * each + at, 8), blocks + lane:blocks + lane + 128] = im[p]

        over_groups(each, blocks, product_group)
        for p in range(n):
            long_out[r, p] = dot_nn(spec[p * each:(p + 1) * each, :].astype(BF16), inverse[...])

        def mix_step(p, carry):
            for at in range(0, each, 32):
                part = pl.ds(at, 32)
                query, _ = short_conv(got, cols, same, r, 0, p, part)
                total = long_out[r, p, part, :] + cols[9, part, :] * gated[r, p, part, :]
                long_out[r, p, part, :] = total
                sent[r, p, part, :] = (query * total).astype(BF16)
            return carry

        lax.fori_loop(0, n, mix_step, 0)
        all_peers(n, lambda peer, j: to_peer(
            sent.at[r, peer], mixed.at[r, mine], send_sem.at[r, j], recv_sem.at[r, me], peer,
        ).start())
        mixed[r, mine] = sent[r, me]

    for r in range(rows):
        def wait(peer, j):
            part = pl.ds(pl.multiple_of(peer * each, each), each)
            to_peer(
                sent.at[r, peer], mixed.at[r, part], send_sem.at[r, j], recv_sem.at[r, peer], peer,
            ).wait()

        all_peers(n, wait)


def mlp_kernel(
    n, chunk, mixed, x, cot, mask_col, w_out, gain, w_up, w_down,
    out, back, mid, share_up, share_down, share_out, gain_sum, stats,
    resid, normed, act, grad_act, acc_out, acc_back, turned, turned_cot, mix_back, sent, send_sem, recv_sem,
):
    me = lax.axis_index("seq")
    rows, blocks = mixed.shape[0], mixed.shape[2]
    width, hidden = w_up.shape
    each = width // n
    mine = pl.ds(pl.multiple_of(me * each, each), each)
    barrier = greet(n)
    gain_sum[...] = jnp.zeros_like(gain_sum)
    stat_out = jnp.zeros((1, width), F32)
    stat_mix = jnp.zeros((1, width), F32)
    stat_mlp = jnp.zeros((1, width), F32)
    for r in range(rows):
        tokens = slice(r * blocks, (r + 1) * blocks)
        mask = mask_col[tokens, :]
        mixer = dot_nn(mixed[r].T, w_out[...])
        stat_mix += jnp.sum(mixer * mixer * mask, axis=0, keepdims=True)
        middle = x[tokens, :] + mixer
        resid[...] = middle
        scale = lax.rsqrt(jnp.mean(middle * middle, axis=-1, keepdims=True) + EPS)
        normed[...] = (middle * scale * gain[...]).astype(BF16)
        turned[:, tokens] = normed[...].T
        cot_low = cot[tokens, :].astype(BF16)
        turned_cot[:, tokens] = cot_low.T
        acc_out[...] = jnp.zeros_like(acc_out)
        acc_back[...] = jnp.zeros_like(acc_back)

        def hidden_step(j, carry):
            cols = pl.ds(pl.multiple_of(j * chunk, chunk), chunk)
            up = dot_nn(normed[...], w_up[:, cols])
            square = up * up
            tanh = jnp.tanh(up * (C0 + (C0 * C1) * square))
            half = 0.5 * (1.0 + tanh)
            act_low = (up * half).astype(BF16)
            slope = half + (0.5 * up) * (1.0 - tanh * tanh) * (C0 + (3.0 * C0 * C1) * square)
            act[tokens, cols] = act_low
            acc_out[...] += dot_nn(act_low, w_down[cols, :])
            grad = dot_nt(cot[tokens, :].astype(BF16), w_down[cols, :])
            grad_low = (grad * slope).astype(BF16)
            grad_act[tokens, cols] = grad_low
            acc_back[...] += dot_nt(grad_low, w_up[:, cols])
            return carry

        lax.fori_loop(0, hidden // chunk, hidden_step, 0)
        middle = resid[...]
        mlp = acc_out[...]
        stat_mlp += jnp.sum(mlp * mlp * mask, axis=0, keepdims=True)
        whole = middle + mlp
        stat_out += jnp.sum(whole * whole * mask, axis=0, keepdims=True)
        out[tokens, :] = whole
        scale = lax.rsqrt(jnp.mean(middle * middle, axis=-1, keepdims=True) + EPS)
        grad = acc_back[...]
        gain_sum[...] += jnp.sum(grad * middle * scale, axis=0, keepdims=True)
        scaled = grad * gain[...]
        shift = jnp.mean(scaled * middle, axis=-1, keepdims=True) * (scale * scale * scale)
        grad_mid = cot[tokens, :] + scaled * scale - middle * shift
        mid[tokens, :] = grad_mid
        mix_back[r] = grad_mid.astype(BF16)
        sent[r] = dot_nt(w_out[...], mix_back[r]).astype(BF16)
        if r == 0:
            pl.semaphore_wait(barrier, n - 1)

        def start(peer, j):
            part = pl.ds(pl.multiple_of(peer * each, each), each)
            to_peer(
                sent.at[r, part], back.at[r, me], send_sem.at[r, j], recv_sem.at[r, me], peer,
            ).start()

        all_peers(n, start)
        back[r, me] = sent[r, mine]

    stats[0:1, :] = stat_out
    stats[1:2, :] = stat_mix
    stats[2:3, :] = stat_mlp
    stats[3:4, :] = jnp.broadcast_to(
        jnp.sum(mask_col[...], axis=0, keepdims=True) * (1.0 / width), (1, width)
    )
    stats[4:8, :] = jnp.zeros((4, width), F32)
    side = each // 2

    def put_rows(share, half, lanes, value):
        for s in range(n):
            for core in range(2):
                low = (2 * s + core) * side
                share[s // 4, (s // 2) % 2, s % 2, core, half, :, lanes] = value[low:low + side]

    for half in range(2):
        low = half * (width // 2)
        value = sum(dot_nn(mixed[r], mix_back[r, :, low:low + width // 2]) for r in range(rows)).astype(BF16)
        put_rows(share_out, half, slice(None), value)
        for low in range(0, hidden // 2, chunk):
            cols = slice(half * (hidden // 2) + low, half * (hidden // 2) + low + chunk)
            put_rows(share_up, half, slice(low, low + chunk), dot_nn(turned[...], grad_act[:, cols]).astype(BF16))
    span = hidden // n
    quarter = width // 4
    for s in range(n):
        value = dot_nn(turned_cot[...], act[:, s * span:(s + 1) * span]).astype(BF16)
        for core in range(2):
            for half in range(2):
                low = (2 * core + half) * quarter
                share_down[s // 4, (s // 2) % 2, s % 2, core, half] = value[low:low + quarter]
    for r in range(rows):
        def wait(peer, j):
            part = pl.ds(pl.multiple_of(peer * each, each), each)
            to_peer(
                sent.at[r, part], back.at[r, peer], send_sem.at[r, j], recv_sem.at[r, peer], peer,
            ).wait()

        all_peers(n, wait)


def place():
    row, seq = lax.axis_index("rows"), lax.axis_index("seq")
    return lax.div(row, 2), lax.rem(row, 2), lax.div(seq, 4), lax.rem(lax.div(seq, 2), 2), lax.rem(seq, 2)


def partner(axis):
    y, c, zh, zl, x = place()
    if axis == "core":
        return {"rows": 2 * y + 1 - c}
    if axis == "y":
        return {"rows": 2 * (1 - y) + c}
    if axis == "x":
        return {"seq": 4 * zh + 2 * zl + 1 - x}
    if axis == "zl":
        return {"seq": 4 * zh + 2 * (1 - zl) + x}
    return {"seq": 4 * (1 - zh) + 2 * zl + x}


def exchange(src, dst, send_sem, recv_sem, axis):
    return pltpu.make_async_remote_copy(
        src_ref=src, dst_ref=dst, send_sem=send_sem, recv_sem=recv_sem,
        device_id=partner(axis), device_id_type=MESH,
    )


ALL = slice(None)


class Tree:
    def __init__(self, order, share, own, parts, gathered, sems):
        self.order = ("core",) + order + ("zl", "zh", "back_y", "back_core")
        self.share, self.own, self.parts, self.gathered, self.sems = share, own, parts, gathered, sems
        self.started = []

    def copies(self, step):
        y, c, zh, zl, x = place()
        axis = self.order[step]
        parts, gathered = self.parts, self.gathered
        own = self.share.at[:, :, :, c] if self.own is None else self.own
        second = self.order[1]
        if axis == "core":
            src, dst = self.share.at[:, :, :, 1 - c], parts[0]
        elif axis == "y":
            src = own.at[:, :, :, 1 - y] if second == "y" else own.at[:, :, x, 1 - y]
            dst = parts[step]
        elif axis == "x":
            src = own.at[:, :, 1 - x] if second == "x" else own.at[:, :, 1 - x, y]
            dst = parts[step]
        elif axis == "zl":
            src, dst = own.at[:, 1 - zl, x, y], parts[3]
        elif axis == "zh":
            src, dst = own.at[1 - zh, zl, x, y], parts[4]
        elif axis == "back_y":
            src = dst = gathered.at[c, y]
        else:
            src = dst = gathered.at[c]
        return exchange(src, dst, self.sems.at[0, step], self.sems.at[1, step], axis.replace("back_", ""))

    def start(self, step):
        self.copies(step).start()
        self.started.append(step)

    def mine(self, a, b, d, e):
        c = place()[1]
        return (self.share, (a, b, d, c, e)) if self.own is None else (self.own, (a, b, d, e))

    def add(self, where, part):
        rows = self.share.shape[-2]
        size = 48 if rows % 48 == 0 else rows
        own, where = self.mine(*where)

        def body(i, carry):
            here = pl.ds(pl.multiple_of(i * size, size), size)
            own[where + (here, ALL)] = own[where + (here, ALL)] + part[0][part[1] + (here, ALL)]
            return carry

        lax.fori_loop(0, rows // size, body, 0)

    def finish(self, step):
        y, c, zh, zl, x = place()
        axis = self.order[step]
        self.copies(step).wait_recv()
        second = self.order[1]
        two = range(2)
        if axis == "core":
            for a in two:
                for b in two:
                    for d in two:
                        for e in two:
                            self.add((a, b, d, e), (self.parts[0], (a, b, d, e)))
        elif axis in ("x", "y"):
            for a in two:
                for b in two:
                    if step == 2:
                        self.add((a, b, x, y), (self.parts[2], (a, b)))
                    else:
                        for d in two:
                            self.add((a, b, d, y) if second == "y" else (a, b, x, d), (self.parts[1], (a, b, d)))
        elif axis == "zl":
            for a in two:
                self.add((a, zl, x, y), (self.parts[3], (a,)))
        elif axis == "zh":
            own, where = self.mine(zh, zl, x, y)
            self.gathered[c, y] = own[where] + self.parts[4][...]
        if step + 1 < len(self.order):
            self.start(step + 1)

    def drain(self):
        for step in self.started:
            self.copies(step).wait_send()


def tree_scratch(r, l):
    shapes = [(2, 2, 2, 2, r, l)] * 2 + [(2, 2, 2, r, l), (2, 2, r, l), (2, r, l), (r, l), (2, 2, r, l)]
    return [pltpu.VMEM(shape, BF16) for shape in shapes] + [pltpu.SemaphoreType.DMA((2, 7))]


def tail_kernel(
    n, back, got, same, spec_taps, spec_gate, gated, long_out, cols_in, table, inverse, turns,
    share_up, share_down, share_out, w_in_far, turned_far, x_far, mid_far, gain, raw_far, sums_two, stats,
    grad_flat, grad_in, grad_out, grad_up, grad_down, grad_kernel, vector_sums, channel_sums,
    got_back, sent, send_sem, recv_sem, fetch_sem,
    tap_own, tap_got, tap_half, tap_part, tap_all, tap_sems, tap_send, tap_recv,
    vector_got, channel_got, vector_sems,
    *tree_refs,
):
    me = lax.axis_index("seq")
    y, c, zh, zl, xbit = place()
    rows, each, blocks = got.shape[0], got.shape[3], got.shape[4]
    width = n * each
    mine = pl.ds(pl.multiple_of(me * each, each), each)
    barrier = greet(n)
    for axis in ("core", "y"):
        pl.semaphore_signal(barrier, inc=1, device_id=partner(axis), device_id_type=MESH)

    trees, at = {}, 0
    specs = (("up", share_up, ("y", "x"), True), ("down", share_down, ("x", "y"), True), ("out", share_out, ("y", "x"), True))
    for i, (name, share, order, far) in enumerate(specs):
        own, parts, gathered, sems = tree_refs[at], tree_refs[at + 1:at + 6], tree_refs[at + 6], tree_refs[at + 7]
        trees[name] = Tree(order, share, own, parts, gathered, sems)
        at += 8
    for name, order in (("in0", ("y", "x")), ("in1", ("x", "y")), ("in2", ("y", "x"))):
        parts = tree_refs[at:at + 5]
        trees[name] = Tree(order, None, None, parts, tree_refs[at + 5], tree_refs[at + 6])
        at += 7

    fetches = [
        pltpu.make_async_copy(src, dst, fetch_sem.at[i])
        for i, (src, dst) in enumerate(
            [(trees[name].share.at[:, :, :, c], trees[name].own) for name in ("up", "down", "out")]
            + [(mid_far, grad_flat), (raw_far, grad_kernel)]
        )
    ]
    for copy in fetches:
        copy.start()
    side = each // 2

    def tap_core():
        return exchange(tap_own.at[1 - c], tap_got, tap_sems.at[0, 0], tap_sems.at[1, 0], "core")

    def tap_y():
        return exchange(tap_own.at[c, 1 - y], tap_half, tap_sems.at[0, 1], tap_sems.at[1, 1], "y")

    def wait_back(r, k):
        def wait(peer, j):
            part = pl.ds(pl.multiple_of(peer * each, each), each)
            to_peer(
                sent.at[r, k, peer], got_back.at[r, k, part], send_sem.at[r, k, j], recv_sem.at[r, k, peer], peer,
            ).wait()

        all_peers(n, wait)

    def conv_phase(cols, sums, spec, spec_sum, grad_long, short):
        spread_cols(cols_in, cols)
        sums[...] = jnp.zeros_like(sums)
        spec_sum[...] = jnp.zeros_like(spec_sum)
        pl.semaphore_wait(barrier, n + 1)
        for name in ("up", "down", "out"):
            trees[name].start(0)

        def tap_sums(part_at, p_part, grad, inputs):
            for i in range(3):
                sums[3 * part_at + i, p_part, :] += folded(grad * inputs[i])

        def spread_back(r, k):
            for slot in range(2):
                short[k, n + slot] = pltpu.roll(short[k, slot], blocks - 1, 1)

            def step(p, carry):
                for low in range(0, each, 32):
                    part = pl.ds(low, 32)
                    value = cols[3 * k, part, :] * short[k, p, part, :]
                    value += cols[3 * k + 1, part, :] * (short[k, p + 1, part, :] * same[0, p + 1, r:r + 1, :])
                    value += cols[3 * k + 2, part, :] * (short[k, p + 2, part, :] * same[1, p + 2, r:r + 1, :])
                    sent[r, k, p, part, :] = value.astype(BF16)
                return carry

            lax.fori_loop(0, n, step, 0)
            all_peers(n, lambda peer, j: to_peer(
                sent.at[r, k, peer], got_back.at[r, k, mine], send_sem.at[r, k, j], recv_sem.at[r, k, me], peer,
            ).start())
            got_back[r, k, mine] = sent[r, k, me]

        for r in range(rows):
            def query_step(p, carry):
                for low in range(0, each, 32):
                    part = pl.ds(low, 32)
                    grad = back[r, p, part, :].astype(F32)
                    query, inputs = short_conv(got, cols, same, r, 0, p, part)
                    grad_query = grad * long_out[r, p, part, :]
                    value = grad * query
                    grad_long[r, p, part, :] = value.astype(BF16)
                    short[0, p, part, :] = grad_query
                    tap_sums(0, part, grad_query, inputs)
                    sums[9, part, :] += folded(value * gated[r, p, part, :])
                return carry

            lax.fori_loop(0, n, query_step, 0)
            spread_back(r, 0)

        for i, name in enumerate(("up", "down", "out")):
            fetches[i].wait()
            trees[name].finish(0)

        for r in range(rows):
            for p in range(n):
                spec[p * each:(p + 1) * each, :] = dot_nn(grad_long[r, p], table[...])

            def product_group(at, lane):
                re, im = load_phases(spec, n, each, at, lane, blocks)
                re, im = turn_phases(re, im, turns, lane, -1)
                re, im = fft_points(re, im, -1)
                out_r, out_i = [], []
                for k in range(n):
                    here = (pl.ds(at, 8), slice(lane, lane + 128))
                    tap_r, tap_i = spec_taps[(k, 0) + here], spec_taps[(k, 1) + here]
                    gate_r, gate_i = spec_gate[(r, k, 0) + here], spec_gate[(r, k, 1) + here]
                    spec_sum[(k, 0) + here] += gate_r * re[k] + gate_i * im[k]
                    spec_sum[(k, 1) + here] += gate_r * im[k] - gate_i * re[k]
                    out_r.append(tap_r * re[k] + tap_i * im[k])
                    out_i.append(tap_r * im[k] - tap_i * re[k])
                re, im = fft_points(out_r, out_i, 1)
                re, im = turn_phases(re, im, turns, lane, 1)
                for p in range(n):
                    spec[pl.ds(p * each + at, 8), lane:lane + 128] = re[p]
                    spec[pl.ds(p * each + at, 8), blocks + lane:blocks + lane + 128] = im[p]

            over_groups(each, blocks, product_group)
            for p in range(n):
                short[0, p] = dot_nn(spec[p * each:(p + 1) * each, :].astype(BF16), inverse[...])

            def gate_step(p, carry):
                for low in range(0, each, 32):
                    part = pl.ds(low, 32)
                    keys, key_inputs = short_conv(got, cols, same, r, 1, p, part)
                    values, value_inputs = short_conv(got, cols, same, r, 2, p, part)
                    grad = short[0, p, part, :] + cols[9, part, :] * grad_long[r, p, part, :].astype(F32)
                    grad = grad * same[2, p, r:r + 1, :]
                    grad_keys = grad * values
                    grad_values = grad * keys
                    short[1, p, part, :] = grad_keys
                    short[2, p, part, :] = grad_values
                    tap_sums(1, part, grad_keys, key_inputs)
                    tap_sums(2, part, grad_values, value_inputs)
                return carry

            lax.fori_loop(0, n, gate_step, 0)
            spread_back(r, 1)
            spread_back(r, 2)

        def taps_group(at, lane):
            here = (pl.ds(at, 8), slice(lane, lane + 128))
            re = [spec_sum[(k, 0) + here] for k in range(n)]
            im = [spec_sum[(k, 1) + here] for k in range(n)]
            re, im = fft_points(re, im, 1)
            re, im = turn_phases(re, im, turns, lane, 1)
            for p in range(n):
                spec[pl.ds(p * each + at, 8), lane:lane + 128] = re[p]
                spec[pl.ds(p * each + at, 8), blocks + lane:blocks + lane + 128] = im[p]

        over_groups(each, blocks, taps_group)
        for p in range(n):
            piece = dot_nn(spec[p * each:(p + 1) * each, :].astype(BF16), inverse[...]).astype(BF16)
            for half in range(2):
                tap_own[half, p // 4, p % 4] = piece[half * side:(half + 1) * side]

        tap_core().start()
        lanes = lax.broadcasted_iota(jnp.int32, (each, 128), 1)
        total = jnp.zeros((each, 128), F32)
        for i in range(10):
            total = jnp.where(lanes == i, jnp.sum(sums[i], axis=-1, keepdims=True), total)
        channel_sums[...] = jnp.zeros_like(channel_sums)
        channel_sums[me, :, 0:each] = total.T[0:16, :]

        for name in ("up", "down", "out"):
            trees[name].finish(1)

        tap_core().wait_recv()
        for half in range(2):
            for q in range(4):
                tap_own[c, half, q] = tap_own[c, half, q] + tap_got[half, q]
        tap_y().start()

    pl.run_scoped(
        conv_phase,
        pltpu.VMEM((10, each, blocks), F32),
        pltpu.VMEM((10, each, 128), F32),
        pltpu.VMEM((width, 2 * blocks), F32),
        pltpu.VMEM((n, 2, each, blocks), F32),
        pltpu.VMEM((rows, n, each, blocks), BF16),
        pltpu.VMEM((3, n + 2, each, blocks), F32),
    )

    def in_phase(w_in, turned, x, spec, share0, share1, share2):
        for k, share in enumerate((share0, share1, share2)):
            trees["in%d" % k].share = share
        near = [
            pltpu.make_async_copy(src, dst, fetch_sem.at[5 + i])
            for i, (src, dst) in enumerate(((w_in_far, w_in), (turned_far, turned), (x_far, x)))
        ]
        for copy in near:
            copy.start()
        for copy in near + fetches[3:]:
            copy.wait()

        def weight_part(k):
            for r in range(rows):
                wait_back(r, k)
            share = trees["in%d" % k].share
            for half in range(2):
                low = half * (width // 2)
                value = sum(dot_nt(turned[r], got_back[r, k, low:low + width // 2, :]) for r in range(rows)).astype(BF16)
                for s in range(n):
                    for core in range(2):
                        block = (2 * s + core) * side
                        share[s // 4, (s // 2) % 2, s % 2, core, half] = value[block:block + side]
            trees["in%d" % k].start(0)
            for r in range(rows):
                value = dot_nn(w_in[:, k * width:(k + 1) * width], got_back[r, k])
                if k == 0:
                    spec[:, r * blocks:(r + 1) * blocks] = value
                else:
                    spec[:, r * blocks:(r + 1) * blocks] += value

        weight_part(0)
        for name in ("up", "down", "out"):
            trees[name].finish(2)
        trees["in0"].finish(0)

        tap_y().wait_recv()
        for q in range(4):
            tap_part[q] = tap_own[c, y, q] + tap_half[q]

        def tap_copy(src_q, there):
            peer = 4 * y + src_q
            return to_peer(tap_part.at[src_q], tap_all.at[c, there], tap_send.at[src_q], tap_recv.at[there], peer)

        for q in range(4):
            @pl.when(4 * y + q != me)
            def _():
                tap_copy(q, me).start()

            @pl.when(4 * y + q == me)
            def _():
                tap_all[c, me] = tap_part[q]

        for name in ("up", "down", "out"):
            trees[name].finish(3)
        weight_part(1)
        trees["in0"].finish(1)
        trees["in1"].finish(0)
        for name in ("up", "down", "out"):
            trees[name].finish(4)

        home = zh == y

        @pl.when(home)
        def _():
            for j in range(1, n):
                peer = lax.rem(me + j, n)
                pltpu.make_async_remote_copy(
                    src_ref=tap_part.at[0], dst_ref=tap_all.at[c, peer], send_sem=tap_send.at[0], recv_sem=tap_recv.at[peer],
                    device_id={"seq": peer}, device_id_type=MESH,
                ).wait_recv()
            exchange(tap_all.at[c], tap_all.at[c], tap_sems.at[0, 2], tap_sems.at[1, 2], "y").start()

        for name in ("up", "down", "out"):
            trees[name].finish(5)

        weight_part(2)
        trees["in0"].finish(2)
        trees["in1"].finish(1)
        trees["in2"].finish(0)

        vector_sums[0:1, :] = jnp.zeros((1, width), F32)
        for r in range(rows):
            tokens = slice(r * blocks, (r + 1) * blocks)
            grad = spec[:, r * blocks:(r + 1) * blocks].T
            value = x[tokens, :]
            scale = lax.rsqrt(jnp.mean(value * value, axis=-1, keepdims=True) + EPS)
            vector_sums[0:1, :] += jnp.sum(grad * value * scale, axis=0, keepdims=True)
            scaled = grad * gain[...]
            shift = jnp.mean(scaled * value, axis=-1, keepdims=True) * (scale * scale * scale)
            grad_flat[tokens, :] = grad_flat[tokens, :] + scaled * scale - value * shift
        vector_sums[1:2, :] = sums_two[...]
        vector_sums[2:6, :] = stats[0:4, :]
        vector_sums[6:8, :] = jnp.zeros((2, width), F32)

        def vector_copies(step):
            axis = ("core", "y", "x", "zl", "zh")[step]
            return (
                exchange(vector_sums, vector_got.at[step], vector_sems.at[0, step], vector_sems.at[1, step], axis),
                exchange(channel_sums, channel_got.at[step], vector_sems.at[2, step], vector_sems.at[3, step], axis),
            )

        def vector_finish(step):
            for copy in vector_copies(step):
                copy.wait()
            vector_sums[...] += vector_got[step]
            channel_sums[...] += channel_got[step]
            if step < 4:
                for copy in vector_copies(step + 1):
                    copy.start()

        for copy in vector_copies(0):
            copy.start()

        @pl.when(jnp.logical_not(home))
        def _():
            exchange(tap_all.at[c], tap_all.at[c], tap_sems.at[0, 2], tap_sems.at[1, 2], "y").wait_recv()

        exchange(tap_all.at[c], tap_all.at[c], tap_sems.at[0, 3], tap_sems.at[1, 3], "core").start()
        trees["in0"].finish(3)
        trees["in1"].finish(2)
        vector_finish(0)
        trees["in2"].finish(1)
        for name in ("up", "down", "out"):
            trees[name].finish(6)
        for half in range(2):
            for core in range(2):
                place_rows = slice(core * side, (core + 1) * side)
                for tree, target in ((trees["up"], grad_up), (trees["out"], grad_out)):
                    l = tree.share.shape[-1]
                    target[place_rows, half * l:(half + 1) * l] = tree.gathered[core, half].astype(F32)
        grad_down[...] = trees["down"].gathered[...].reshape(width, grad_down.shape[0]).astype(F32).T
        trees["in0"].finish(4)
        vector_finish(1)
        trees["in1"].finish(3)
        trees["in2"].finish(2)
        exchange(tap_all.at[c], tap_all.at[c], tap_sems.at[0, 3], tap_sems.at[1, 3], "core").wait_recv()
        tanh = jnp.tanh(grad_kernel[...] * (1.0 / THRESH))
        kernel_grad = jnp.concatenate(
            [tap_all[core, s] for s in range(n) for core in range(2)], axis=0
        ).astype(F32).T
        grad_kernel[...] = kernel_grad * tanh * tanh
        vector_finish(2)
        trees["in0"].finish(5)
        trees["in1"].finish(4)
        trees["in2"].finish(3)
        vector_finish(3)
        trees["in0"].finish(6)
        trees["in1"].finish(5)
        trees["in2"].finish(4)
        vector_finish(4)
        trees["in1"].finish(6)
        trees["in2"].finish(5)
        trees["in2"].finish(6)
        for k in range(3):
            tree = trees["in%d" % k]
            l = tree.share.shape[-1]
            for half in range(2):
                for core in range(2):
                    low = k * width + half * l
                    grad_in[core * side:(core + 1) * side, low:low + l] = tree.gathered[core, half].astype(F32)

        for tree in trees.values():
            tree.drain()
        tap_core().wait_send()
        tap_y().wait_send()
        for q in range(4):
            @pl.when(4 * y + q != me)
            def _():
                tap_copy(q, me).wait_send()

        @pl.when(home)
        def _():
            exchange(tap_all.at[c], tap_all.at[c], tap_sems.at[0, 2], tap_sems.at[1, 2], "y").wait_send()

        exchange(tap_all.at[c], tap_all.at[c], tap_sems.at[0, 3], tap_sems.at[1, 3], "core").wait_send()


    pl.run_scoped(
        in_phase,
        pltpu.VMEM(w_in_far.shape, BF16),
        pltpu.VMEM(turned_far.shape, BF16),
        pltpu.VMEM(x_far.shape, F32),
        pltpu.VMEM((width, 2 * blocks), F32),
        *[pltpu.VMEM((2, 2, 2, 2, 2, side, width // 2), BF16)] * 3,
    )


def vmem(count):
    return [pl.BlockSpec(memory_space=pltpu.VMEM)] * count


def call(body, outs, scratch, inputs, collective_id=None, far=()):
    extra = {}
    if collective_id is not None:
        extra = dict(collective_id=collective_id, has_side_effects=True)
    return pl.pallas_call(
        body,
        out_shape=tuple(jax.ShapeDtypeStruct(*out) for out in outs),
        in_specs=[pl.BlockSpec(memory_space=pl.ANY if i in far else pltpu.VMEM) for i in range(len(inputs))],
        out_specs=tuple(vmem(len(outs))),
        scratch_shapes=scratch,
        compiler_params=pltpu.CompilerParams(vmem_limit_bytes=VMEM_BYTES, **extra),
    )(*inputs)


def local(
    block_in, segment_ids, valid_mask, cotangent, gain_mix, in_proj, short_taps, long_kernel,
    skip_gain, out_proj, gain_mlp, up_proj, down_proj,
):
    rows, blocks, _, width = block_in.shape
    hidden = up_proj.shape[1]
    n = lax.axis_size("seq")
    me = lax.axis_index("seq")
    each = width // n
    tokens = rows * blocks
    x = block_in.reshape(tokens, width)
    cot = cotangent.reshape(tokens, width)
    raw = long_kernel[:, 0, :]
    marks = jnp.concatenate(
        [segment_ids[:, :, 0], valid_mask[:, :, 0], jnp.zeros((8 - 2 * rows, blocks), jnp.int32)]
    )
    own = lax.dynamic_slice_in_dim(
        jnp.concatenate([short_taps.reshape(3, 3, width), jnp.broadcast_to(skip_gain, (1, 3, width))]),
        me * each, each, axis=2,
    )
    cols_in = jnp.concatenate([own[:3, c] for c in range(3)] + [own[3, :1]]).T
    cols_in = jnp.pad(cols_in, ((0, 0), (0, 128 - cols_in.shape[1])))
    table, inverse, turns = spectrum_tables(blocks, n)
    dma = pltpu.SemaphoreType.DMA

    got, got_taps, got_marks, turned = call(
        functools.partial(in_kernel, n),
        [
            ((rows, 3, n + 2, each, blocks), BF16),
            ((n, each, blocks), BF16),
            ((n,) + marks.shape, jnp.int32),
            ((rows, width, blocks), BF16),
        ],
        [
            pltpu.VMEM((rows, 3, width, blocks), BF16),
            pltpu.VMEM((width, blocks), BF16),
            pltpu.VMEM((tokens, width), BF16),
            dma((rows, 3, n)), dma((rows, 3, n)), dma((2, n)), dma((2, n)),
        ],
        (x, in_proj, gain_mix[None], raw, marks),
        1,
    )
    mixed, same, spec_taps, spec_gate, gated, long_out = call(
        functools.partial(conv_kernel, n),
        [
            ((rows, width, blocks), BF16),
            ((3, n + 2, rows, blocks), F32),
            ((n, 2, each, blocks), F32),
            ((rows, n, 2, each, blocks), F32),
            ((rows, n, each, blocks), F32),
            ((rows, n, each, blocks), F32),
        ],
        [
            pltpu.VMEM((10, each, blocks), F32),
            pltpu.VMEM((width, 2 * blocks), F32),
            pltpu.VMEM((rows, n, each, blocks), BF16),
            dma((rows, n)), dma((rows, n)),
        ],
        (got, got_taps, got_marks, cols_in, table, inverse, turns),
        2,
    )
    mask_col = valid_mask[:, :, 0].astype(F32).reshape(tokens, 1)
    chunk = 512
    side = each // 2
    bits = (2, 2, 2, 2, 2)
    up_shape = bits + (side, hidden // 2)
    down_shape = bits + (width // 4, hidden // n)
    out_shape = bits + (side, width // 2)
    block_out, back, mid, share_up, share_down, share_out, gain_two, stats = call(
        functools.partial(mlp_kernel, n, chunk),
        [
            ((tokens, width), F32),
            ((rows, n, each, blocks), BF16),
            ((tokens, width), F32),
            (up_shape, BF16),
            (down_shape, BF16),
            (out_shape, BF16),
            ((1, width), F32),
            ((8, width), F32),
        ],
        [
            pltpu.VMEM((blocks, width), F32),
            pltpu.VMEM((blocks, width), BF16),
            pltpu.VMEM((tokens, hidden), BF16),
            pltpu.VMEM((tokens, hidden), BF16),
            pltpu.VMEM((blocks, width), F32),
            pltpu.VMEM((blocks, width), F32),
            pltpu.VMEM((width, tokens), BF16),
            pltpu.VMEM((width, tokens), BF16),
            pltpu.VMEM((rows, blocks, width), BF16),
            pltpu.VMEM((rows, width, blocks), BF16),
            dma((rows, n)), dma((rows, n)),
        ],
        (mixed, x, cot, mask_col, out_proj, gain_mlp[None], up_proj, down_proj),
        3,
    )
    half_taps = (4, side, blocks)
    trees = []
    for shape in (up_shape, down_shape, out_shape):
        trees += tree_scratch(*shape[5:])
    for _ in range(3):
        trees += tree_scratch(*out_shape[5:])[1:]
    grad_flat, grad_inp, grad_out, grad_up, grad_down, grad_kernel, vectors, channels = call(
        functools.partial(tail_kernel, n),
        [
            ((tokens, width), F32),
            ((each, 3 * width), F32),
            ((each, width), F32),
            ((each, hidden), F32),
            ((hidden // n, width), F32),
            ((blocks, width), F32),
            ((8, width), F32),
            ((n, 16, 128), F32),
        ],
        [
            pltpu.VMEM((rows, 3, width, blocks), BF16),
            pltpu.VMEM((rows, 3, n, each, blocks), BF16),
            dma((rows, 3, n)), dma((rows, 3, n)),
            dma((8,)),
            pltpu.VMEM((2, 2) + half_taps, BF16),
            pltpu.VMEM((2,) + half_taps, BF16),
            pltpu.VMEM(half_taps, BF16),
            pltpu.VMEM(half_taps, BF16),
            pltpu.VMEM((2, n, side, blocks), BF16),
            dma((2, 4)), dma((4,)), dma((n,)),
            pltpu.VMEM((5, 8, width), F32),
            pltpu.VMEM((5, n, 16, 128), F32),
            dma((4, 5)),
        ] + trees,
        (
            back, got, same, spec_taps, spec_gate, gated, long_out, cols_in, table, inverse, turns,
            share_up, share_down, share_out, in_proj, turned, x, mid, gain_mix[None], raw, gain_two, stats,
        ),
        4,
        far=(11, 12, 13, 14, 15, 16, 17, 19),
    )

    stats = jnp.sum(vectors[2:6], axis=1)
    spread = jnp.transpose(channels[:, :10, :each], (1, 0, 2)).reshape(10, width)
    grad_tap_rows = jnp.transpose(spread[:9].reshape(3, 3, width), (1, 0, 2)).reshape(3, 3 * width)
    rms_stats = jnp.sqrt(stats[:3] / (jnp.maximum(stats[3], 1.0) * width))
    return (
        block_out.reshape(block_in.shape),
        grad_flat.reshape(block_in.shape),
        vectors[0],
        grad_inp,
        grad_tap_rows,
        grad_kernel[:, None, :],
        spread[9],
        grad_out,
        vectors[1],
        grad_up,
        grad_down,
        rms_stats,
    )


def chosen(block_in, *rest):
    rows, blocks, _, width = block_in.shape
    n = lax.axis_size("seq")
    fits = blocks % 256 == 0 and width % (32 * n) == 0 and n == 8 and 2 * rows <= 8
    return (local if fits else general_local)(block_in, *rest)


def solution(mesh):
    return jax.shard_map(
        chosen,
        mesh=mesh,
        in_specs=(
            P("rows", None, "seq", None),
            P("rows", None, "seq"),
            P("rows", None, "seq"),
            P("rows", None, "seq", None),
            P(),
            P(),
            P(),
            P(None, "seq", None),
            P(),
            P(),
            P(),
            P(),
            P(),
        ),
        out_specs=(
            P("rows", None, "seq", None),
            P("rows", None, "seq", None),
            P(),
            P("seq", None),
            P(),
            P(None, "seq", None),
            P(),
            P("seq", None),
            P(),
            P("seq", None),
            P("seq", None),
            P(),
        ),
        check_vma=False,
    )
```

```python
import functools
import math

import jax
import jax.numpy as jnp
import numpy as np
from jax import lax
from jax.experimental import pallas as pl
from jax.experimental.pallas import tpu as pltpu
from jax.sharding import PartitionSpec as P

EPS = 1e-05
THRESH = 0.003
HIGH = lax.Precision.HIGHEST


def shortened(x):

    def short(part):
        return part.astype(jnp.bfloat16) if part.dtype == jnp.float32 else part

    return jax.tree.map(short, x)


def passed_along(block, axis, distance):
    devices = range(lax.axis_size(axis))
    route = [((i - distance) % len(devices), i) for i in devices]
    return lax.ppermute(block, axis, route)


def norm_scale(value, gain):
    return value * lax.rsqrt(jnp.mean(value * value, axis=-1, keepdims=True) + EPS) * gain


def angle_tables(left_count, right_count, period):
    left_idx = jnp.arange(left_count, dtype=jnp.int32)[:, None]
    right_idx = jnp.arange(right_count, dtype=jnp.int32)[None, :]
    phase = (left_idx * right_idx % period).astype(jnp.float32) * (2.0 * math.pi / period)
    return (jnp.cos(phase), jnp.sin(phase))


def twiddle_tables(shard_index, spec_len, whole_len):
    turned = shard_index * jnp.arange(spec_len, dtype=jnp.int32) % whole_len
    phase = turned.astype(jnp.float32) * (2.0 * math.pi / whole_len)
    return (jnp.cos(phase)[None, :, None], jnp.sin(phase)[None, :, None])


def local_forward(signal, shard_index, whole_len):
    blocks = signal.shape[1]
    cos_table, sin_table = angle_tables(blocks, 2 * blocks, 2 * blocks)
    real_part = jnp.einsum("rjd,jk->rkd", signal, cos_table, precision=HIGH)
    imag_part = -jnp.einsum("rjd,jk->rkd", signal, sin_table, precision=HIGH)
    cos_twid, sin_twid = twiddle_tables(shard_index, 2 * blocks, whole_len)
    out_real = real_part * cos_twid + imag_part * sin_twid
    out_imag = imag_part * cos_twid - real_part * sin_twid
    return (out_real[:, :, None, :], out_imag[:, :, None, :])


def cross_section(real_part, imag_part, direction):
    count = real_part.shape[2]
    cos_table, sin_table = angle_tables(count, count, count)
    re_cos = jnp.einsum("rcpd,pm->rcmd", real_part, cos_table, precision=HIGH)
    re_sin = jnp.einsum("rcpd,pm->rcmd", real_part, sin_table, precision=HIGH)
    im_cos = jnp.einsum("rcpd,pm->rcmd", imag_part, cos_table, precision=HIGH)
    im_sin = jnp.einsum("rcpd,pm->rcmd", imag_part, sin_table, precision=HIGH)
    return (re_cos - direction * im_sin, im_cos + direction * re_sin)


def local_inverse(real_part, imag_part, shard_index, whole_len):
    real_part = real_part[:, :, 0, :]
    imag_part = imag_part[:, :, 0, :]
    spec_len = real_part.shape[1]
    cos_twid, sin_twid = twiddle_tables(shard_index, spec_len, whole_len)
    turned_re = real_part * cos_twid - imag_part * sin_twid
    turned_im = imag_part * cos_twid + real_part * sin_twid
    cos_table, sin_table = angle_tables(spec_len, spec_len // 2, spec_len)
    result = jnp.einsum("rkd,kj->rjd", turned_re, cos_table, precision=HIGH)
    result = result - jnp.einsum("rkd,kj->rjd", turned_im, sin_table, precision=HIGH)
    return result / whole_len


def earlier(members, at_start):
    received = jax.tree.map(
        lambda part, own: part.astype(own.dtype),
        passed_along(shortened(members), "seq", 1),
        members,
    )
    placed = []
    for member in received:
        rolled = jnp.concatenate([jnp.zeros_like(member[:, :1]), member[:, :-1]], axis=1)
        placed.append(jnp.where(at_start, rolled, member))
    return tuple(placed)


def later(member, at_end):
    received = passed_along(member.astype(jnp.bfloat16), "seq", -1).astype(member.dtype)
    rolled = jnp.concatenate([received[:, 1:], jnp.zeros_like(received[:, :1])], axis=1)
    return jnp.where(at_end, rolled, received)


def times_trans(left, right):
    return lax.dot_general(
        left, right, (((1,), (1,)), ((), ())), preferred_element_type=jnp.float32
    )


def trans_times(left, right):
    return lax.dot_general(
        left, right, (((0,), (0,)), ((), ())), preferred_element_type=jnp.float32
    )


def general_local(
    block_in,
    segment_ids,
    valid_mask,
    cotangent,
    gain_mix,
    in_proj,
    short_taps,
    long_kernel,
    skip_gain,
    out_proj,
    gain_mlp,
    up_proj,
    down_proj,
):
    batch_rows = block_in.shape[0]
    blocks = block_in.shape[1]
    width = block_in.shape[3]
    shard_count = lax.axis_size("seq")
    shard_index = lax.axis_index("seq")
    whole_len = 2 * blocks * shard_count
    tokens = batch_rows * blocks
    at_start = shard_index == 0
    at_end = shard_index == shard_count - 1
    flat_in = block_in.reshape(tokens, width)
    mask_rows = valid_mask[:, :, 0].astype(jnp.float32)[:, :, None]
    normed_one = norm_scale(flat_in, gain_mix).astype(jnp.bfloat16)
    proj_low = jnp.dot(normed_one, in_proj, preferred_element_type=jnp.float32).astype(jnp.bfloat16)
    proj_low = proj_low.reshape(batch_rows, blocks, 3 * width)
    seg_low = segment_ids[:, :, 0].astype(jnp.bfloat16)[:, :, None]
    prev_one = earlier((proj_low, seg_low), at_start)
    prev_two = earlier(prev_one, at_start)
    same_one = (prev_one[1] == seg_low).astype(jnp.float32)
    same_two = (prev_two[1] == seg_low).astype(jnp.float32)
    proj_now = proj_low.astype(jnp.float32)
    proj_one = prev_one[0].astype(jnp.float32)
    proj_two = prev_two[0].astype(jnp.float32)
    conv_short = (
        short_taps[0] * proj_now
        + short_taps[1] * proj_one * same_one
        + short_taps[2] * proj_two * same_two
    )
    query = conv_short[:, :, :width]
    keys = conv_short[:, :, width : 2 * width]
    values = conv_short[:, :, 2 * width :]
    gated = keys * values * mask_rows
    raw_taps = long_kernel[:, 0, :]
    taps_eff = raw_taps - THRESH * jnp.tanh(raw_taps / THRESH)
    kern_re, kern_im = local_forward(taps_eff[None], shard_index, whole_len)
    kern_re, kern_im = (
        lax.all_to_all(
            kern_re.astype(jnp.bfloat16), "seq", split_axis=1, concat_axis=2, tiled=True
        ).astype(kern_re.dtype),
        lax.all_to_all(
            kern_im.astype(jnp.bfloat16), "seq", split_axis=1, concat_axis=2, tiled=True
        ).astype(kern_im.dtype),
    )
    kern_re, kern_im = cross_section(kern_re, kern_im, -1.0)
    gate_re, gate_im = local_forward(gated, shard_index, whole_len)
    gate_re, gate_im = (
        lax.all_to_all(
            gate_re.astype(jnp.bfloat16), "seq", split_axis=1, concat_axis=2, tiled=True
        ).astype(gate_re.dtype),
        lax.all_to_all(
            gate_im.astype(jnp.bfloat16), "seq", split_axis=1, concat_axis=2, tiled=True
        ).astype(gate_im.dtype),
    )
    gate_re, gate_im = cross_section(gate_re, gate_im, -1.0)
    prod_re = gate_re * kern_re - gate_im * kern_im
    prod_im = gate_re * kern_im + gate_im * kern_re
    prod_re, prod_im = cross_section(prod_re, prod_im, 1.0)
    prod_re, prod_im = (
        lax.all_to_all(
            prod_re.astype(jnp.bfloat16), "seq", split_axis=2, concat_axis=1, tiled=True
        ).astype(prod_re.dtype),
        lax.all_to_all(
            prod_im.astype(jnp.bfloat16), "seq", split_axis=2, concat_axis=1, tiled=True
        ).astype(prod_im.dtype),
    )
    long_out = local_inverse(prod_re, prod_im, shard_index, whole_len) + skip_gain * gated
    mixer_low = (query * long_out).reshape(tokens, width).astype(jnp.bfloat16)
    mixer_out = jnp.dot(mixer_low, out_proj, preferred_element_type=jnp.float32)
    resid_mid = flat_in + mixer_out
    normed_two = norm_scale(resid_mid, gain_mlp).astype(jnp.bfloat16)
    up_val = jnp.dot(normed_two, up_proj, preferred_element_type=jnp.float32)
    act_low = jax.nn.gelu(up_val).astype(jnp.bfloat16)
    mlp_out = jnp.dot(act_low, down_proj, preferred_element_type=jnp.float32)
    flat_out = resid_mid + mlp_out
    grad_out = cotangent.reshape(tokens, width)
    grad_mlp = grad_out.astype(jnp.bfloat16)
    grad_down = trans_times(act_low, grad_mlp)
    grad_act = times_trans(grad_mlp, down_proj)
    unused_val, gelu_back = jax.vjp(jax.nn.gelu, up_val)
    grad_upval = gelu_back(grad_act)[0].astype(jnp.bfloat16)
    grad_up = trans_times(normed_two, grad_upval)
    grad_norm_two = times_trans(grad_upval, up_proj)
    unused_two, norm_back_two = jax.vjp(norm_scale, resid_mid, gain_mlp)
    grad_resid, grad_gain_two = norm_back_two(grad_norm_two)
    grad_mid = grad_out + grad_resid
    grad_mix = grad_mid.astype(jnp.bfloat16)
    grad_outp = trans_times(mixer_low, grad_mix)
    grad_prod = times_trans(grad_mix, out_proj).reshape(batch_rows, blocks, width)
    grad_query = grad_prod * long_out
    grad_long = grad_prod * query
    back_re, back_im = local_forward(grad_long, shard_index, whole_len)
    back_re, back_im = (
        lax.all_to_all(
            back_re.astype(jnp.bfloat16), "seq", split_axis=1, concat_axis=2, tiled=True
        ).astype(back_re.dtype),
        lax.all_to_all(
            back_im.astype(jnp.bfloat16), "seq", split_axis=1, concat_axis=2, tiled=True
        ).astype(back_im.dtype),
    )
    back_re, back_im = cross_section(back_re, back_im, -1.0)
    sig_re = kern_re * back_re + kern_im * back_im
    sig_im = kern_re * back_im - kern_im * back_re
    tap_re = jnp.sum(gate_re * back_re + gate_im * back_im, axis=0, keepdims=True)
    tap_im = jnp.sum(gate_re * back_im - gate_im * back_re, axis=0, keepdims=True)
    sig_re, sig_im = cross_section(sig_re, sig_im, 1.0)
    tap_re, tap_im = cross_section(tap_re, tap_im, 1.0)
    sig_re, sig_im, tap_re, tap_im = (
        lax.all_to_all(
            sig_re.astype(jnp.bfloat16), "seq", split_axis=2, concat_axis=1, tiled=True
        ).astype(sig_re.dtype),
        lax.all_to_all(
            sig_im.astype(jnp.bfloat16), "seq", split_axis=2, concat_axis=1, tiled=True
        ).astype(sig_im.dtype),
        lax.all_to_all(
            tap_re.astype(jnp.bfloat16), "seq", split_axis=2, concat_axis=1, tiled=True
        ).astype(tap_re.dtype),
        lax.all_to_all(
            tap_im.astype(jnp.bfloat16), "seq", split_axis=2, concat_axis=1, tiled=True
        ).astype(tap_im.dtype),
    )
    grad_gated = local_inverse(sig_re, sig_im, shard_index, whole_len) + skip_gain * grad_long
    grad_taps_eff = local_inverse(tap_re, tap_im, shard_index, whole_len)[0]
    tanh_val = jnp.tanh(raw_taps / THRESH)
    grad_kernel = (grad_taps_eff * tanh_val * tanh_val)[:, None, :]
    grad_kernel = lax.psum(grad_kernel.astype(jnp.bfloat16), "rows").astype(jnp.float32)
    grad_skip = jnp.sum(grad_long * gated, axis=(0, 1))
    grad_short = jnp.concatenate(
        [grad_query, grad_gated * values * mask_rows, grad_gated * keys * mask_rows], axis=2
    )
    grad_tap_rows = jnp.stack(
        [
            jnp.sum(grad_short * proj_now, axis=(0, 1)),
            jnp.sum(grad_short * proj_one * same_one, axis=(0, 1)),
            jnp.sum(grad_short * proj_two * same_two, axis=(0, 1)),
        ]
    )
    inner_term = short_taps[1] * grad_short * same_one + later(
        short_taps[2] * grad_short * same_two, at_end
    )
    grad_proj = short_taps[0] * grad_short + later(inner_term, at_end)
    grad_proj = grad_proj.reshape(tokens, 3 * width).astype(jnp.bfloat16)
    grad_inp = trans_times(normed_one, grad_proj)
    grad_norm_one = times_trans(grad_proj, in_proj)
    unused_one, norm_back_one = jax.vjp(norm_scale, flat_in, gain_mix)
    grad_first, grad_gain_one = norm_back_one(grad_norm_one)
    grad_flat = grad_mid + grad_first
    mask_flat = mask_rows.reshape(tokens, 1)
    stat_sums = jnp.stack(
        [
            jnp.sum(mask_flat * flat_out * flat_out),
            jnp.sum(mask_flat * mixer_out * mixer_out),
            jnp.sum(mask_flat * mlp_out * mlp_out),
            jnp.sum(mask_flat),
        ]
    )
    grad_gain_one, grad_gain_two, grad_tap_rows, grad_skip, stat_sums = lax.psum(
        (grad_gain_one, grad_gain_two, grad_tap_rows, grad_skip, stat_sums), ("rows", "seq")
    )
    rms_stats = jnp.sqrt(stat_sums[:3] / (jnp.maximum(stat_sums[3], 1.0) * width))
    shares = (
        lax.psum_scatter(grad_inp, "seq", scatter_dimension=0, tiled=True),
        lax.psum_scatter(grad_outp, "seq", scatter_dimension=0, tiled=True),
        lax.psum_scatter(grad_up, "seq", scatter_dimension=0, tiled=True),
        lax.psum_scatter(grad_down, "seq", scatter_dimension=0, tiled=True),
    )
    grad_inp, grad_outp, grad_up, grad_down = (
        lax.psum(shares[0].astype(jnp.bfloat16), "rows").astype(jnp.float32),
        lax.psum(shares[1].astype(jnp.bfloat16), "rows").astype(jnp.float32),
        lax.psum(shares[2].astype(jnp.bfloat16), "rows").astype(jnp.float32),
        lax.psum(shares[3].astype(jnp.bfloat16), "rows").astype(jnp.float32),
    )
    return (
        flat_out.reshape(block_in.shape),
        grad_flat.reshape(block_in.shape),
        grad_gain_one,
        grad_inp,
        grad_tap_rows,
        grad_kernel,
        grad_skip,
        grad_outp,
        grad_gain_two,
        grad_up,
        grad_down,
        rms_stats,
    )


MESH = pl.DeviceIdType.MESH
F32 = jnp.float32
BF16 = jnp.bfloat16
VMEM_BYTES = 62 * 1024 * 1024
C0 = math.sqrt(2.0 / math.pi)
C1 = 0.044715
ALL = slice(None)


def dot_nn(a, b):
    return lax.dot_general(a, b, (((1,), (0,)), ((), ())), preferred_element_type=F32)


def dot_nt(a, b):
    return lax.dot_general(a, b, (((1,), (1,)), ((), ())), preferred_element_type=F32)


def fft_points(re, im, sign):
    n = len(re)
    if n == 1:
        return re, im
    even_r, even_i = fft_points(re[0::2], im[0::2], sign)
    odd_r, odd_i = fft_points(re[1::2], im[1::2], sign)
    out_r, out_i = [None] * n, [None] * n
    for k in range(n // 2):
        if k == 0:
            turn_r, turn_i = odd_r[0], odd_i[0]
        elif 4 * k == n:
            if sign > 0:
                out_r[k], out_i[k] = even_r[k] - odd_i[k], even_i[k] + odd_r[k]
                out_r[k + n // 2], out_i[k + n // 2] = even_r[k] + odd_i[k], even_i[k] - odd_r[k]
            else:
                out_r[k], out_i[k] = even_r[k] + odd_i[k], even_i[k] - odd_r[k]
                out_r[k + n // 2], out_i[k + n // 2] = even_r[k] - odd_i[k], even_i[k] + odd_r[k]
            continue
        else:
            cos, sin = math.cos(2 * math.pi * k / n), sign * math.sin(2 * math.pi * k / n)
            turn_r = cos * odd_r[k] - sin * odd_i[k]
            turn_i = cos * odd_i[k] + sin * odd_r[k]
        out_r[k], out_i[k] = even_r[k] + turn_r, even_i[k] + turn_i
        out_r[k + n // 2], out_i[k + n // 2] = even_r[k] - turn_r, even_i[k] - turn_i
    return out_r, out_i


def spectrum_tables(blocks, n):
    lane = np.arange(blocks)
    span = blocks // n
    place_in = n * (lane % span) + lane // span
    angle = 2.0 * np.pi * place_in[:, None] * np.arange(blocks)[None, :] / blocks
    cos, sin = np.cos(angle), np.sin(angle)
    table = np.block([[cos, -sin], [sin, cos]])
    turn = 2.0 * np.pi * place_in[None, :] * (2.0 * np.arange(n)[:, None] + 0.5) / (2.0 * blocks * n)
    turns = np.stack([np.cos(turn), np.sin(turn)], axis=1)[:, :, None, :]
    return jnp.asarray(table, BF16), jnp.asarray(np.broadcast_to(turns, (n, 2, 8, blocks)), F32)


def place():
    row, seq = lax.axis_index("rows"), lax.axis_index("seq")
    return lax.div(row, 2), lax.rem(row, 2), lax.div(seq, 4), lax.rem(lax.div(seq, 2), 2), lax.rem(seq, 2)


def partner(axis):
    y, c, zh, zl, x = place()
    if axis == "core":
        return {"rows": 2 * y + 1 - c}
    if axis == "y":
        return {"rows": 2 * (1 - y) + c}
    if axis == "x":
        return {"seq": 4 * zh + 2 * zl + 1 - x}
    if axis == "zl":
        return {"seq": 4 * zh + 2 * (1 - zl) + x}
    return {"seq": 4 * (1 - zh) + 2 * zl + x}


def remote(src, dst, send_sem, recv_sem, target):
    return pltpu.make_async_remote_copy(
        src_ref=src, dst_ref=dst, send_sem=send_sem, recv_sem=recv_sem, device_id=target, device_id_type=MESH,
    )


def exchange(src, dst, send_sem, recv_sem, axis):
    return remote(src, dst, send_sem, recv_sem, partner(axis))


def greet(n):
    me = lax.axis_index("seq")
    barrier = pltpu.get_barrier_semaphore()
    for j in range(1, n):
        pl.semaphore_signal(barrier, inc=1, device_id={"seq": lax.rem(me + j, n)}, device_id_type=MESH)
    for axis in ("core", "y"):
        pl.semaphore_signal(barrier, inc=1, device_id=partner(axis), device_id_type=MESH)
    return barrier, n + 1


def aligned(index, size):
    return pl.ds(pl.multiple_of(index * size, size), size)


class Post:
    def __init__(self, n, source, target, sems):
        self.n, self.source, self.target, self.sems = n, source, target, sems

    def copies(self, sender):
        me = lax.axis_index("seq")
        for j in range(1, self.n):
            peer = lax.rem(me + j, self.n)
            come = sender(peer, me)
            yield remote(
                self.source(peer), self.target(come), self.sems.at[0, j], self.sems.at[1, come], {"seq": peer}
            )

    def start(self):
        me = lax.axis_index("seq")
        for copy in self.copies(lambda peer, me: me):
            copy.start()
        self.target(me)[...] = self.source(me)[...]

    def arrive(self):
        for copy in self.copies(lambda peer, me: peer):
            copy.wait_recv()

    def drain(self):
        for copy in self.copies(lambda peer, me: me):
            copy.wait_send()


def over_groups(each, blocks, body):
    for lane in range(0, blocks, 128):
        def step(g, carry):
            body(pl.multiple_of(g * 16, 16), lane)
            return carry
        lax.fori_loop(0, each // 16, step, 0)


def matmul_rows(out, left, right, size=256):
    for at in range(0, out.shape[0], size):
        out[at:at + size, :] = left(at, size, right)


def to_spectrum(n, source, table, turns, fin, spec):
    each, blocks = spec.shape[0] // n, spec.shape[1] // 2

    def group(at, lane):
        loaded = [source(d, pl.ds(at, 16), pl.ds(lane, 128)).astype(F32) for d in range(n)]
        halves = []
        for half in (0, 8):
            re, im = [], []
            for d in range(n):
                value = loaded[d][half:half + 8]
                angle = 2.0 * math.pi * d / (4.0 * n)
                re.append(value * math.cos(angle))
                im.append(value * -math.sin(angle))
            re, im = fft_points(re, im, -1)
            turned = []
            for k in range(n):
                cos, sin = turns[k, 0, :, lane:lane + 128], turns[k, 1, :, lane:lane + 128]
                turned.append((re[k] * cos + im[k] * sin, im[k] * cos - re[k] * sin))
            halves.append(turned)
        for k in range(n):
            for part in range(2):
                value = jnp.concatenate([halves[0][k][part], halves[1][k][part]], axis=0)
                fin[pl.ds(k * each + at, 16), part * blocks + lane:part * blocks + lane + 128] = value.astype(BF16)

    over_groups(each, blocks, group)
    for at in range(0, spec.shape[0], 256):
        spec[at:at + 256, :] = dot_nn(fin[at:at + 256, :], table[...])


def from_spectrum(n, fin, table, turns, spec, store):
    each, blocks = spec.shape[0] // n, spec.shape[1] // 2
    for at in range(0, spec.shape[0], 256):
        spec[at:at + 256, :] = dot_nt(fin[at:at + 256, :], table[...])
    scale = 1.0 / (n * blocks)

    def group(at, lane):
        halves = []
        for half in (0, 8):
            re, im = [], []
            for k in range(n):
                rows = pl.ds(k * each + at + half, 8)
                cos, sin = turns[k, 0, :, lane:lane + 128], turns[k, 1, :, lane:lane + 128]
                old_r, old_i = spec[rows, lane:lane + 128], spec[rows, blocks + lane:blocks + lane + 128]
                re.append(old_r * cos - old_i * sin)
                im.append(old_i * cos + old_r * sin)
            re, im = fft_points(re, im, 1)
            out = []
            for d in range(n):
                angle = 2.0 * math.pi * d / (4.0 * n)
                out.append(re[d] * (scale * math.cos(angle)) - im[d] * (scale * math.sin(angle)))
            halves.append(out)
        for d in range(n):
            store(d, pl.ds(at, 16), pl.ds(lane, 128), jnp.concatenate([halves[0][d], halves[1][d]], axis=0))

    over_groups(each, blocks, group)


def over_rows(total, size, body):
    def step(i, carry):
        body(aligned(i, size))
        return carry
    lax.fori_loop(0, total // size, step, 0)


def over_lanes(width, body):
    def step(i, carry):
        body(aligned(i, 128))
        return carry
    lax.fori_loop(0, width // 128, step, 0)


def front_kernel(
    n, chunk,
    x_far, cot_far, taps_far, marks_in, gain_one, gain_two, w_in_far, w_out_far, w_up_far, w_down_far, weights, table, turns,
    seen_out, proj_out, turned_out, saved_out, same_out, spec_taps_out, spec_gate_out, back_out,
    share_up_out, share_down_out, share_out_out, vectors,
    marks, mark_ends, marks_got, mark_ends_got, x_sent, cot_sent, ends, ends_sent, ends_got, ends_wide,
    taps_sent, taps_chunk, taps_turned, taps_got,
    seen, cot, query, saved, same, spec_gate, gate_sent, gate_got, long_sent, long_got, back_sent, back_got,
    w_out, w_up, w_down, fetch, keep, x_sems, mark_sems, cot_sems, end_sems, tap_sems, gate_sems, long_sems, back_sems,
):
    me = lax.axis_index("seq")
    y, c, zh, zl, xbit = place()
    rows, blocks, width = x_sent.shape
    hidden = w_up.shape[1]
    each, span = width // n, blocks // n
    ext = blocks + 2 * span
    wide = width // 128
    barrier, told = greet(n)

    fetch_out = pltpu.make_async_copy(w_out_far, w_out, fetch.at[0])
    fetch_up = pltpu.make_async_copy(w_up_far, w_up, fetch.at[1])
    fetch_down = pltpu.make_async_copy(w_down_far, w_down, fetch.at[2])
    posts_x = [
        Post(n, lambda d, r=r: x_sent.at[r, aligned(d, span)], lambda p, r=r: seen.at[r, p + 2], x_sems.at[r])
        for r in range(rows)
    ]
    posts_cot = [
        Post(n, lambda d, r=r: cot_sent.at[r, aligned(d, span)], lambda p, r=r: cot.at[r, p], cot_sems.at[r])
        for r in range(rows)
    ]
    post_marks = Post(n, lambda d: marks.at[aligned(d, span)], lambda p: marks_got.at[p + 2], mark_sems)
    posts_gate = [
        Post(n, lambda e, r=r: gate_sent.at[r, aligned(e, each)], lambda d, r=r: gate_got.at[r, d], gate_sems.at[r])
        for r in range(rows)
    ]
    posts_long = [
        Post(n, lambda d, r=r: long_sent.at[r, d], lambda e, r=r: long_got.at[r, aligned(e, each)], long_sems.at[r])
        for r in range(rows)
    ]
    posts_back = [
        Post(n, lambda e, r=r: back_sent.at[r, aligned(e, each)], lambda d, r=r: back_got.at[r, d], back_sems.at[r])
        for r in range(rows)
    ]

    def end_copies(j, slot, peer):
        return (
            remote(ends_sent, ends_got.at[slot], end_sems.at[0, j], end_sems.at[2, slot], {"seq": peer}),
            remote(mark_ends, mark_ends_got.at[slot], end_sems.at[1, j], end_sems.at[3, slot], {"seq": peer}),
        )

    def tap_hop_one(xd):
        target = 4 * y + 2 * c + xd
        return remote(taps_sent.at[y, c, xd], taps_chunk.at[me], tap_sems.at[0, xd], tap_sems.at[1, me], {"seq": target})

    def tap_hop_two(j, slot, peer):
        return remote(
            taps_turned.at[aligned(peer, each)], taps_got.at[y, c, slot], tap_sems.at[2, j], tap_sems.at[3, slot], {"seq": peer}
        )

    def tap_core():
        return exchange(taps_got.at[y, c], taps_got.at[y, c], tap_sems.at[4, 0], tap_sems.at[4, 1], "core")

    def tap_y():
        return exchange(taps_got.at[y], taps_got.at[y], tap_sems.at[4, 2], tap_sems.at[4, 3], "y")

    chosen_chunk = jnp.logical_and(zh == y, zl == c)
    sends_ends = me >= n - 2

    def front(x, cot_in, taps, w_in, normed, turned, proj, gate_wide, fin, spec, spec_taps):
        first = [
            pltpu.make_async_copy(src, dst, fetch.at[3 + i])
            for i, (src, dst) in enumerate(((x_far, x), (taps_far, taps), (w_in_far, w_in), (cot_far, cot_in)))
        ]
        for copy in first + [fetch_out, fetch_up, fetch_down]:
            copy.start()
        marks[...] = jnp.zeros_like(marks)
        marks[:, 0:8] = marks_in[...].T
        first[0].wait()

        def narrow(source, r, target):
            for j in range(wide):
                target[r, :, j * 128:(j + 1) * 128] = source[pl.ds(r * blocks * wide + j, blocks, stride=wide), :].astype(BF16)

        narrow(x, 0, x_sent)
        pl.semaphore_wait(barrier, told)
        posts_x[0].start()
        post_marks.start()
        ends[...] = jnp.zeros_like(ends)
        for r in range(rows):
            for d in range(1, n):
                at = (r * blocks + d * span - 1) * wide
                for j in range(wide):
                    ends[r * n + d:r * n + d + 1, j * 128:(j + 1) * 128] = x[at + j:at + j + 1, :]
        ends_sent[...] = ends[...].astype(BF16)
        mark_ends[0:1, :] = jnp.full((1, 128), -1.0, F32)
        for d in range(1, n):
            mark_ends[d:d + 1, :] = marks[d * span - 1:d * span, :]

        @pl.when(sends_ends)
        def _():
            for j in range(1, n):
                for copy in end_copies(j, me - (n - 2), lax.rem(me + j, n)):
                    copy.start()
            ends_got[me - (n - 2)] = ends_sent[...]
            mark_ends_got[me - (n - 2)] = mark_ends[...]

        narrow(x, 1, x_sent)
        posts_x[1].start()
        first[1].wait()
        for j in range(wide):
            raw = taps[pl.ds(j, blocks, stride=wide), :]
            low = (raw - THRESH * jnp.tanh(raw * (1.0 / THRESH))).astype(BF16)
            for d in range(n):
                taps_sent[d // 4, (d // 2) % 2, d % 2, :, j * 128:(j + 1) * 128] = low[d * span:(d + 1) * span]
        for xd in range(2):
            target = 4 * y + 2 * c + xd

            @pl.when(target != me)
            def _():
                tap_hop_one(xd).start()

            @pl.when(target == me)
            def _():
                taps_chunk[me] = taps_sent[y, c, xd]

        first[3].wait()
        for r in range(rows):
            narrow(cot_in, r, cot_sent)

        for slot in range(2):
            @pl.when(me != n - 2 + slot)
            def _():
                for copy in end_copies(0, slot, n - 2 + slot):
                    copy.wait_recv()
        ends_wide[...] = ends_got[...].astype(F32)
        post_marks.arrive()
        top = lax.broadcasted_iota(jnp.int32, (span, 128), 0) == 0
        for slot in range(2):
            moved = pltpu.roll(marks_got[n + slot], 1, 0)
            marks_got[slot] = jnp.where(top, mark_ends_got[slot, pl.ds(me, 1), :], moved)
        first[2].wait()

        def chunk_row(r):
            posts_x[r].arrive()
            top_row = lax.broadcasted_iota(jnp.int32, (span, width), 0) == 0
            for slot in range(2):
                moved = pltpu.roll(seen[r, n + slot].astype(F32), 1, 0)
                seen[r, slot] = jnp.where(top_row, ends_wide[slot, pl.ds(r * n + me, 1), :], moved).astype(BF16)
            marked = marks_got[...].reshape(ext, 128)
            seg = marked[:, r:r + 1]
            now, one, two = seg[2 * span:], seg[span:ext - span], seg[:blocks]
            same[0, r] = jnp.broadcast_to((now == one).astype(F32), (blocks, 128))
            same[1, r] = jnp.broadcast_to((now == two).astype(F32), (blocks, 128))
            same[2, r] = jnp.broadcast_to(marked[2 * span:, rows + r:rows + r + 1], (blocks, 128))
            for p in range(n + 2):
                value = seen[r, p].astype(F32)
                scale = lax.rsqrt(jnp.mean(value * value, axis=-1, keepdims=True) + EPS)
                normed[r, p * span:(p + 1) * span, :] = (value * scale * gain_one[...]).astype(BF16)
            for k in (1, 2, 0):
                for at in range(0, width, 256):
                    cols = slice(k * width + at, k * width + at + 256)
                    proj[r, k, :, at:at + 256] = dot_nn(normed[r], w_in[:, cols]).astype(BF16)

            def lanes_step(lanes):
                for p in range(n):
                    here = slice(p * span, (p + 1) * span)
                    one_mask, two_mask, mask = same[0, r, here, :], same[1, r, here, :], same[2, r, here, :]
                    value = []
                    for k in range(3):
                        total = weights[3 * k:3 * k + 1, lanes] * proj[r, k, (p + 2) * span:(p + 3) * span, lanes].astype(F32)
                        total += weights[3 * k + 1:3 * k + 2, lanes] * (proj[r, k, (p + 1) * span:(p + 2) * span, lanes].astype(F32) * one_mask)
                        total += weights[3 * k + 2:3 * k + 3, lanes] * (proj[r, k, p * span:(p + 1) * span, lanes].astype(F32) * two_mask)
                        value.append(total)
                    query[r, here, lanes] = value[0].astype(BF16)
                    keys, values = value[1] * mask, value[2] * mask
                    gate = value[1] * values
                    saved[0, r, here, lanes] = keys.astype(BF16)
                    saved[1, r, here, lanes] = values.astype(BF16)
                    saved[2, r, here, lanes] = gate.astype(BF16)
                    gate_wide[here, lanes] = gate

            over_lanes(width, lanes_step)
            gate_sent[r] = gate_wide[...].T.astype(BF16)
            posts_gate[r].start()

        chunk_row(0)

        @pl.when(chosen_chunk)
        def _():
            for p in range(n):
                @pl.when(me != p)
                def _():
                    remote(taps_sent.at[y, c, 0], taps_chunk.at[p], tap_sems.at[0, 0], tap_sems.at[1, p], {"seq": p}).wait_recv()
            taps_turned[...] = taps_chunk[...].reshape(blocks, width).astype(F32).T.astype(BF16)
            for j in range(1, n):
                tap_hop_two(j, xbit, lax.rem(me + j, n)).start()
            taps_got[y, c, xbit] = taps_turned[aligned(me, each)]

        chunk_row(1)
        for xd in range(2):
            @pl.when(4 * y + 2 * c + xd != me)
            def _():
                tap_hop_two(0, xd, 4 * y + 2 * c + xd).wait_recv()
        tap_core().start()
        for r in range(rows):
            posts_cot[r].start()
        for r in range(rows):
            turned[:, r * ext:(r + 1) * ext] = normed[r].T
        tap_core().wait_recv()
        tap_y().start()
        keeps = [
            pltpu.make_async_copy(src, dst, keep.at[i])
            for i, (src, dst) in enumerate(((seen, seen_out), (proj, proj_out), (turned, turned_out)))
        ]
        for copy in keeps:
            copy.start()
        tap_y().wait_recv()
        to_spectrum(n, lambda d, at, lanes: taps_got[d // 4, (d // 2) % 2, d % 2, at, lanes], table, turns, fin, spec)
        spec_taps[...] = spec[...]
        keeps.append(pltpu.make_async_copy(spec_taps, spec_taps_out, keep.at[3]))
        keeps[3].start()

        for r in range(rows):
            posts_gate[r].arrive()
            to_spectrum(n, lambda d, at, lanes: gate_got[r, d, at, lanes], table, turns, fin, spec)

            def product(part):
                re, im = spec[part, 0:blocks], spec[part, blocks:2 * blocks]
                tap_r, tap_i = spec_taps[part, 0:blocks], spec_taps[part, blocks:2 * blocks]
                spec_gate[r, part, 0:blocks] = re.astype(BF16)
                spec_gate[r, part, blocks:2 * blocks] = im.astype(BF16)
                fin[part, 0:blocks] = (re * tap_r - im * tap_i).astype(BF16)
                fin[part, blocks:2 * blocks] = (re * tap_i + im * tap_r).astype(BF16)

            over_rows(width, 32, product)

            def store(d, at, lanes, value):
                long_sent[r, d, at, lanes] = value.astype(BF16)

            from_spectrum(n, fin, table, turns, spec, store)
            posts_long[r].start()
        for copy in keeps:
            copy.wait()

    pl.run_scoped(
        front,
        pltpu.VMEM(x_far.shape, F32),
        pltpu.VMEM(cot_far.shape, F32),
        pltpu.VMEM(taps_far.shape, F32),
        pltpu.VMEM(w_in_far.shape, BF16),
        pltpu.VMEM((rows, ext, width), BF16),
        pltpu.VMEM((width, rows * ext), BF16),
        pltpu.VMEM((rows, 3, ext, width), BF16),
        pltpu.VMEM((blocks, width), F32),
        pltpu.VMEM((width, 2 * blocks), BF16),
        pltpu.VMEM((width, 2 * blocks), F32),
        pltpu.VMEM((width, 2 * blocks), F32),
    )
    later_keeps = [
        pltpu.make_async_copy(spec_gate, spec_gate_out, keep.at[4]),
        pltpu.make_async_copy(same, same_out, keep.at[5]),
    ]
    for copy in later_keeps:
        copy.start()

    def middle(act, grad_act, resid, long_out, acc_out, acc_back, normed, turned, turned_cot, mixed, mix_back, up, down, out):
        vectors[...] = jnp.zeros_like(vectors)
        fetch_out.wait()
        for r in range(rows):
            tokens = slice(r * blocks, (r + 1) * blocks)
            posts_long[r].arrive()
            gated = saved[2, r].astype(F32)
            long_out[...] = long_got[r].astype(F32).T + weights[9:10, :] * gated
            low = (query[r].astype(F32) * long_out[...]).astype(BF16)
            mixer = dot_nn(low, w_out[...])
            mixed[r] = low.T
            mask = same[2, r, :, 0:1]
            vectors[1:2, :] += jnp.sum(mixer * mixer * mask, axis=0, keepdims=True)
            values = seen[r, 2:n + 2].reshape(blocks, width).astype(F32)
            state = values + mixer
            resid[...] = state
            scale = lax.rsqrt(jnp.mean(state * state, axis=-1, keepdims=True) + EPS)
            normed[...] = (state * scale * gain_two[...]).astype(BF16)
            acc_out[...] = mixer
            acc_back[...] = jnp.zeros_like(acc_back)
            if r == 0:
                fetch_up.wait()
                fetch_down.wait()
            posts_cot[r].arrive()

            def hidden_step(j, carry):
                cols = aligned(j, chunk)
                up_val = dot_nn(normed[...], w_up[:, cols])
                square = up_val * up_val
                tanh = jnp.tanh(up_val * (C0 + (C0 * C1) * square))
                half = 0.5 * (1.0 + tanh)
                act_low = (up_val * half).astype(BF16)
                slope = half + (0.5 * up_val) * (1.0 - tanh * tanh) * (C0 + (3.0 * C0 * C1) * square)
                act[tokens, cols] = act_low
                acc_out[...] += dot_nn(act_low, w_down[cols, :])
                grad = dot_nt(cot[r].reshape(blocks, width), w_down[cols, :])
                grad_low = (grad * slope).astype(BF16)
                grad_act[tokens, cols] = grad_low
                acc_back[...] += dot_nt(grad_low, w_up[:, cols])
                return carry

            lax.fori_loop(0, hidden // chunk, hidden_step, 0)
            state = resid[...]
            scale = lax.rsqrt(jnp.mean(state * state, axis=-1, keepdims=True) + EPS)
            grad = acc_back[...]
            vectors[4:5, :] += jnp.sum(grad * state * scale, axis=0, keepdims=True)
            scaled = grad * gain_two[...]
            shift = jnp.mean(scaled * state, axis=-1, keepdims=True) * (scale * scale * scale)
            change = scaled * scale - state * shift
            saved[5, r] = change.astype(BF16)
            mix_back[r] = (cot[r].reshape(blocks, width).astype(F32) + change).astype(BF16)
            grad_prod = dot_nt(mix_back[r], w_out[...])
            grad_long = grad_prod * query[r].astype(F32)
            back_sent[r] = grad_long.T.astype(BF16)
            posts_back[r].start()
            saved[3, r] = grad_long.astype(BF16)
            saved[4, r] = (grad_prod * long_out[...]).astype(BF16)
            vectors[5:6, :] += jnp.sum(grad_long * saved[2, r].astype(F32), axis=0, keepdims=True)
            both = acc_out[...]
            saved[6, r] = both.astype(BF16)
            mixer = state - seen[r, 2:n + 2].reshape(blocks, width).astype(F32)
            mlp = both - mixer
            vectors[2:3, :] += jnp.sum(mlp * mlp * mask, axis=0, keepdims=True)
            whole = state + mlp
            vectors[0:1, :] += jnp.sum(whole * whole * mask, axis=0, keepdims=True)
            vectors[3:4, :] += jnp.broadcast_to(jnp.sum(mask, axis=0, keepdims=True) * (1.0 / width), (1, width))
            turned[:, tokens] = normed[...].T
            turned_cot[:, tokens] = cot[r].reshape(blocks, width).T

        kept = [pltpu.make_async_copy(saved, saved_out, keep.at[6])]
        kept[0].start()
        side, quarter, part = each // 2, width // 4, hidden // n

        def put_rows(share, half, lanes, value):
            for s in range(n):
                for core in range(2):
                    low = (2 * s + core) * side
                    share[s // 4, (s // 2) % 2, s % 2, core, half, :, lanes] = value[low:low + side]

        for half in range(2):
            for low in range(0, hidden // 2, chunk):
                cols = slice(half * (hidden // 2) + low, half * (hidden // 2) + low + chunk)
                put_rows(up, half, slice(low, low + chunk), dot_nn(turned[...], grad_act[:, cols]).astype(BF16))
        kept.append(pltpu.make_async_copy(up, share_up_out, keep.at[7]))
        kept[-1].start()
        for s in range(n):
            value = dot_nn(turned_cot[...], act[:, s * part:(s + 1) * part]).astype(BF16)
            for core in range(2):
                for half in range(2):
                    low = (2 * core + half) * quarter
                    down[s // 4, (s // 2) % 2, s % 2, core, half] = value[low:low + quarter]
        kept.append(pltpu.make_async_copy(down, share_down_out, keep.at[8]))
        kept[-1].start()
        for half in range(2):
            low = half * (width // 2)
            value = sum(dot_nn(mixed[r], mix_back[r, :, low:low + width // 2]) for r in range(rows)).astype(BF16)
            put_rows(out, half, ALL, value)
        kept.append(pltpu.make_async_copy(out, share_out_out, keep.at[9]))
        kept[-1].start()
        for r in range(rows):
            posts_back[r].arrive()
        kept.append(pltpu.make_async_copy(back_got, back_out, keep.at[10]))
        kept[-1].start()
        for copy in kept:
            copy.wait()

    pl.run_scoped(
        middle,
        pltpu.VMEM((rows * blocks, hidden), BF16),
        pltpu.VMEM((rows * blocks, hidden), BF16),
        pltpu.VMEM((blocks, width), F32),
        pltpu.VMEM((blocks, width), F32),
        pltpu.VMEM((blocks, width), F32),
        pltpu.VMEM((blocks, width), F32),
        pltpu.VMEM((blocks, width), BF16),
        pltpu.VMEM((width, rows * blocks), BF16),
        pltpu.VMEM((width, rows * blocks), BF16),
        pltpu.VMEM((rows, width, blocks), BF16),
        pltpu.VMEM((rows, blocks, width), BF16),
        pltpu.VMEM(share_up_out.shape, BF16),
        pltpu.VMEM(share_down_out.shape, BF16),
        pltpu.VMEM(share_out_out.shape, BF16),
    )
    for copy in later_keeps:
        copy.wait()
    for post in posts_x + posts_cot + [post_marks] + posts_gate + posts_long + posts_back:
        post.drain()

    @pl.when(sends_ends)
    def _():
        for j in range(1, n):
            for copy in end_copies(j, me - (n - 2), lax.rem(me + j, n)):
                copy.wait_send()

    for xd in range(2):
        @pl.when(4 * y + 2 * c + xd != me)
        def _():
            tap_hop_one(xd).wait_send()

    @pl.when(chosen_chunk)
    def _():
        for j in range(1, n):
            tap_hop_two(j, xbit, lax.rem(me + j, n)).wait_send()

    tap_core().wait_send()
    tap_y().wait_send()


class Tree:
    def __init__(self, order, share, own, parts, gathered, sems):
        self.order = ("core",) + order + ("zl", "zh", "back_y", "back_core")
        self.share, self.own, self.parts, self.gathered, self.sems = share, own, parts, gathered, sems
        self.started = []

    def copies(self, step):
        y, c, zh, zl, x = place()
        axis = self.order[step]
        parts, gathered = self.parts, self.gathered
        own = self.share.at[:, :, :, c] if self.own is None else self.own
        second = self.order[1]
        if axis == "core":
            src, dst = self.share.at[:, :, :, 1 - c], parts[0]
        elif axis == "y":
            src = own.at[:, :, :, 1 - y] if second == "y" else own.at[:, :, x, 1 - y]
            dst = parts[step]
        elif axis == "x":
            src = own.at[:, :, 1 - x] if second == "x" else own.at[:, :, 1 - x, y]
            dst = parts[step]
        elif axis == "zl":
            src, dst = own.at[:, 1 - zl, x, y], parts[3]
        elif axis == "zh":
            src, dst = own.at[1 - zh, zl, x, y], parts[4]
        elif axis == "back_y":
            src = dst = gathered.at[c, y]
        else:
            src = dst = gathered.at[c]
        return exchange(src, dst, self.sems.at[0, step], self.sems.at[1, step], axis.replace("back_", ""))

    def start(self, step):
        self.copies(step).start()
        self.started.append(step)

    def mine(self, a, b, d, e):
        c = place()[1]
        return (self.share, (a, b, d, c, e)) if self.own is None else (self.own, (a, b, d, e))

    def add(self, where, part):
        rows = self.share.shape[-2]
        size = 48 if rows % 48 == 0 else rows
        own, where = self.mine(*where)

        def body(i, carry):
            here = aligned(i, size)
            own[where + (here, ALL)] = own[where + (here, ALL)] + part[0][part[1] + (here, ALL)]
            return carry

        lax.fori_loop(0, rows // size, body, 0)

    def finish(self, step):
        y, c, zh, zl, x = place()
        axis = self.order[step]
        self.copies(step).wait_recv()
        second = self.order[1]
        two = range(2)
        if axis == "core":
            for a in two:
                for b in two:
                    for d in two:
                        for e in two:
                            self.add((a, b, d, e), (self.parts[0], (a, b, d, e)))
        elif axis in ("x", "y"):
            for a in two:
                for b in two:
                    if step == 2:
                        self.add((a, b, x, y), (self.parts[2], (a, b)))
                    else:
                        for d in two:
                            self.add((a, b, d, y) if second == "y" else (a, b, x, d), (self.parts[1], (a, b, d)))
        elif axis == "zl":
            for a in two:
                self.add((a, zl, x, y), (self.parts[3], (a,)))
        elif axis == "zh":
            own, where = self.mine(zh, zl, x, y)
            self.gathered[c, y] = own[where] + self.parts[4][...]
        if step + 1 < len(self.order):
            self.start(step + 1)

    def drain(self):
        for step in self.started:
            self.copies(step).wait_send()


def tree_scratch(r, l):
    shapes = [(2, 2, 2, 2, r, l)] * 2 + [(2, 2, 2, r, l), (2, 2, r, l), (2, r, l), (r, l), (2, 2, r, l)]
    return [pltpu.VMEM(shape, BF16) for shape in shapes] + [pltpu.SemaphoreType.DMA((2, 7))]


def back_kernel(
    n,
    back_far, spec_taps_far, spec_gate_far, table, turns, share_up, share_down, share_out, saved_far, proj_far, turned_far,
    seen_far, same_far, w_in_far, weights, gain_one, sums_in, x_far, cot_far, taps_far,
    out, grad_flat, grad_in, grad_out, grad_up, grad_down, grad_kernel, vectors,
    gate_sent, gate_got, out_got, grad_sent, grad_got, end_got, out_sems, gate_sems, grad_sems, end_sems, fetch,
    tap_own, tap_one, tap_two, tap_rows, tap_cols, tap_home, tap_sems, tap_send, tap_recv,
    vector_got, vector_sems,
    *tree_refs,
):
    me = lax.axis_index("seq")
    y, c, zh, zl, xbit = place()
    rows, blocks, width = gate_got.shape[0], gate_got.shape[2], gate_got.shape[1]
    each, span = width // n, blocks // n
    ext, wide, side = blocks + 2 * span, width // 128, each // 2
    barrier, told = greet(n)

    trees, at = {}, 0
    for name, share, order in (("up", share_up, ("y", "x")), ("down", share_down, ("x", "y")), ("out", share_out, ("y", "x"))):
        trees[name] = Tree(order, share, tree_refs[at], tree_refs[at + 1:at + 6], tree_refs[at + 6], tree_refs[at + 7])
        at += 8
    for name, order in (("in0", ("y", "x")), ("in1", ("x", "y")), ("in2", ("y", "x"))):
        trees[name] = Tree(order, None, None, tree_refs[at:at + 5], tree_refs[at + 5], tree_refs[at + 6])
        at += 7
    early = ("up", "down", "out")

    posts_out = [
        Post(n, lambda p, r=r: saved_far.at[6, r, aligned(p, span)], lambda d, r=r: out_got.at[r, aligned(d, span)], out_sems.at[r])
        for r in range(rows)
    ]
    posts_gate = [
        Post(n, lambda d, r=r: gate_sent.at[r, d], lambda e, r=r: gate_got.at[r, aligned(e, each)], gate_sems.at[r])
        for r in range(rows)
    ]
    posts_grad = [
        Post(n, lambda p, r=r: grad_sent.at[r, p + 2], lambda d, r=r: grad_got.at[r, aligned(d, span)], grad_sems.at[r])
        for r in range(rows)
    ]
    tall = 16

    def end_copy(r, slot, sender):
        return remote(
            grad_sent.at[r, slot, 0:tall], end_got.at[r, sender], end_sems.at[0, r, slot], end_sems.at[1, r, sender], {"seq": n - 2 + slot}
        )

    def tap_core():
        return exchange(tap_own.at[:, 1 - c], tap_one, tap_sems.at[0, 0], tap_sems.at[1, 0], "core")

    def tap_y():
        return exchange(tap_own.at[1 - y, c], tap_two, tap_sems.at[0, 1], tap_sems.at[1, 1], "y")

    def tap_hop_one(xd):
        target = 4 * y + 2 * c + xd
        return remote(tap_own.at[y, c, xd], tap_rows.at[aligned(me, each)], tap_send.at[0, xd], tap_recv.at[0, me], {"seq": target})

    def tap_hop_two(j, slot, peer):
        return remote(tap_cols.at[peer], tap_home.at[y, c, slot], tap_send.at[1, j], tap_recv.at[1, slot], {"seq": peer})

    def tap_back_core():
        return exchange(tap_home.at[y, c], tap_home.at[y, c], tap_sems.at[0, 2], tap_sems.at[1, 2], "core")

    def tap_back_y():
        return exchange(tap_home.at[y], tap_home.at[y], tap_sems.at[0, 3], tap_sems.at[1, 3], "y")

    chosen_chunk = jnp.logical_and(zh == y, zl == c)
    own_halves = [
        pltpu.make_async_copy(trees[name].share.at[:, :, :, c], trees[name].own, fetch.at[i]) for i, name in enumerate(early)
    ]

    def conv_phase(back, spec_taps, spec_gate, fin, spec, spec_sum):
        near = [
            pltpu.make_async_copy(src, dst, fetch.at[3 + i])
            for i, (src, dst) in enumerate(((back_far, back), (spec_taps_far, spec_taps), (spec_gate_far, spec_gate)))
        ]
        for copy in near + own_halves:
            copy.start()
        pl.semaphore_wait(barrier, told)
        for name in early:
            trees[name].start(0)
        for copy in near:
            copy.wait()
        for r in range(rows):
            to_spectrum(n, lambda d, at, lanes: back[r, d, at, lanes], table, turns, fin, spec)

            def product(part):
                re, im = spec[part, 0:blocks], spec[part, blocks:2 * blocks]
                tap_r, tap_i = spec_taps[part, 0:blocks], spec_taps[part, blocks:2 * blocks]
                gate_r, gate_i = spec_gate[r, part, 0:blocks].astype(F32), spec_gate[r, part, blocks:2 * blocks].astype(F32)
                sum_r, sum_i = gate_r * re + gate_i * im, gate_r * im - gate_i * re
                if r == 0:
                    spec_sum[part, 0:blocks] = sum_r
                    spec_sum[part, blocks:2 * blocks] = sum_i
                else:
                    spec_sum[part, 0:blocks] += sum_r
                    spec_sum[part, blocks:2 * blocks] += sum_i
                fin[part, 0:blocks] = (tap_r * re + tap_i * im).astype(BF16)
                fin[part, blocks:2 * blocks] = (tap_r * im - tap_i * re).astype(BF16)

            over_rows(width, 32, product)

            def store(d, at, lanes, value):
                gate_sent[r, d, at, lanes] = value.astype(BF16)

            from_spectrum(n, fin, table, turns, spec, store)
            posts_gate[r].start()
            if r == 0:
                for i, name in enumerate(early):
                    own_halves[i].wait()
                    trees[name].finish(0)
        for at in range(0, width, 256):
            fin[at:at + 256, :] = spec_sum[at:at + 256, :].astype(BF16)

        def store_taps(d, at, lanes, value):
            tap_own[d // 4, (d // 2) % 2, d % 2, at, lanes] = value.astype(BF16)

        from_spectrum(n, fin, table, turns, spec, store_taps)
        tap_core().start()

    pl.run_scoped(
        conv_phase,
        pltpu.VMEM((rows, n, each, blocks), BF16),
        pltpu.VMEM((width, 2 * blocks), F32),
        pltpu.VMEM((rows, width, 2 * blocks), BF16),
        pltpu.VMEM((width, 2 * blocks), BF16),
        pltpu.VMEM((width, 2 * blocks), F32),
        pltpu.VMEM((width, 2 * blocks), F32),
    )

    def token_phase(saved, proj, turned, seen, same, w_in, gate_back, grad_proj, sums, share0, share1, share2):
        for k, share in enumerate((share0, share1, share2)):
            trees["in%d" % k].share = share
        near = [
            pltpu.make_async_copy(src, dst, fetch.at[6 + i])
            for i, (src, dst) in enumerate((
                (saved_far.at[0:6], saved), (proj_far, proj), (same_far, same), (w_in_far, w_in), (seen_far, seen),
                (turned_far, turned), (x_far, out), (cot_far, grad_flat), (taps_far, grad_kernel),
            ))
        ]
        for copy in near:
            copy.start()
        for post in posts_out:
            for copy in post.copies(lambda peer, me: me):
                copy.start()
        own_out = [
            pltpu.make_async_copy(post.source(me), post.target(me), fetch.at[15 + r]) for r, post in enumerate(posts_out)
        ]
        for copy in own_out:
            copy.start()
        sums[...] = jnp.zeros_like(sums)
        tap_core().wait_recv()
        for a in range(2):
            for xd in range(2):
                tap_own[a, c, xd] = tap_own[a, c, xd] + tap_one[a, xd]
        tap_y().start()
        trees["up"].finish(1)
        trees["out"].finish(1)
        trees["down"].finish(1)
        for copy in near[:3]:
            copy.wait()
        last_row = lax.broadcasted_iota(jnp.int32, (span, 128), 0) == span - 1
        first_row = lax.broadcasted_iota(jnp.int32, (span, 128), 0) == 0

        def token_row(r):
            posts_gate[r].arrive()
            gate_back[...] = gate_got[r].astype(F32).T

            def lanes_step(lanes):
                skip = weights[9:10, lanes]
                for k in range(3):
                    taps = [weights[3 * k + i:3 * k + i + 1, lanes] for i in range(3)]
                    grads, ends = [], []
                    total = [jnp.zeros((span, 128), F32) for _ in range(3)]
                    for p in range(n + 2):
                        if p < n:
                            here = slice(p * span, (p + 1) * span)
                            if k == 0:
                                grad = saved[4, r, here, lanes].astype(F32)
                            else:
                                grad = gate_back[here, lanes] + skip * saved[3, r, here, lanes].astype(F32)
                                grad = grad * saved[2 - k, r, here, lanes].astype(F32)
                            one = grad * same[0, r, here, :]
                            two = grad * same[1, r, here, :]
                            grads.append((grad, one, two))
                            total[0] += grad * proj[r, k, (p + 2) * span:(p + 3) * span, lanes].astype(F32)
                            total[1] += one * proj[r, k, (p + 1) * span:(p + 2) * span, lanes].astype(F32)
                            total[2] += two * proj[r, k, p * span:(p + 1) * span, lanes].astype(F32)
                        value = jnp.zeros((span, 128), F32)
                        if p >= 2:
                            value += taps[0] * grads[p - 2][0]
                        if 1 <= p <= n:
                            value += taps[1] * grads[p - 1][1]
                        if p < n:
                            value += taps[2] * grads[p][2]
                        if p < 2:
                            ends.append(value)
                            value = jnp.where(first_row, value, 0.0)
                        if p >= n:
                            value += jnp.where(last_row, 0.0, pltpu.roll(ends[p - n], span - 1, 0))
                        grad_proj[r, p * span:(p + 1) * span, pl.ds(pl.multiple_of(lanes.start + k * width, 128), 128)] = value.astype(BF16)
                    for i in range(3):
                        folded = total[i][0:8] + total[i][8:16] + total[i][16:24] + total[i][24:32]
                        sums[3 * k + i, :, lanes] += folded

            over_lanes(width, lanes_step)

        def grad_row(r):
            grad = dot_nt(grad_proj[r], w_in[...])
            value = seen[r].reshape(ext, width).astype(F32)
            scale = lax.rsqrt(jnp.mean(value * value, axis=-1, keepdims=True) + EPS)
            vectors[10:11, :] += jnp.sum(grad * value * scale, axis=0, keepdims=True)
            scaled = grad * gain_one[...]
            shift = jnp.mean(scaled * value, axis=-1, keepdims=True) * (scale * scale * scale)
            change = scaled * scale - value * shift
            for p in range(n + 2):
                block = change[p * span:(p + 1) * span]
                if p >= 2:
                    block += saved[5, r, (p - 2) * span:(p - 1) * span, :].astype(F32)
                grad_sent[r, p] = block.astype(BF16)
            posts_grad[r].start()
            for slot in range(2):
                @pl.when(me != n - 2 + slot)
                def _():
                    end_copy(r, slot, me).start()

                @pl.when(me == n - 2 + slot)
                def _():
                    end_got[r, me] = grad_sent[r, slot, 0:tall]

        def weight_part(k):
            share = trees["in%d" % k].share
            both = grad_proj[...].reshape(rows * ext, 3 * width)
            for half in range(2):
                low = k * width + half * (width // 2)
                value = dot_nn(turned[...], both[:, low:low + width // 2]).astype(BF16)
                for s in range(n):
                    for core in range(2):
                        block = (2 * s + core) * side
                        share[s // 4, (s // 2) % 2, s % 2, core, half] = value[block:block + side]
            trees["in%d" % k].start(0)

        vectors[...] = jnp.zeros_like(vectors)
        token_row(0)
        for copy in near[3:5]:
            copy.wait()
        trees["up"].finish(2)
        trees["out"].finish(2)
        grad_row(0)
        tap_y().wait_recv()
        for xd in range(2):
            tap_own[y, c, xd] = tap_own[y, c, xd] + tap_two[xd]
        for xd in range(2):
            @pl.when(4 * y + 2 * c + xd != me)
            def _():
                tap_hop_one(xd).start()

            @pl.when(4 * y + 2 * c + xd == me)
            def _():
                tap_rows[aligned(me, each)] = tap_own[y, c, xd]

        token_row(1)
        trees["down"].finish(2)
        near[5].wait()
        for k in range(3):
            weight_part(k)
        trees["up"].finish(3)
        trees["out"].finish(3)
        trees["in0"].finish(0)
        trees["in1"].finish(0)
        trees["in2"].finish(0)
        grad_row(1)
        trees["down"].finish(3)
        trees["up"].finish(4)
        trees["out"].finish(4)

        @pl.when(chosen_chunk)
        def _():
            for e in range(n):
                @pl.when(me != e)
                def _():
                    remote(tap_own.at[y, c, 0], tap_rows.at[e * each:(e + 1) * each], tap_send.at[0, 0], tap_recv.at[0, e], {"seq": e}).wait_recv()
            tap_cols[...] = tap_rows[...].astype(F32).T.astype(BF16).reshape(tap_cols.shape)
            for j in range(1, n):
                tap_hop_two(j, xbit, lax.rem(me + j, n)).start()
            tap_home[y, c, xbit] = tap_cols[me]

        vectors[0:9, :] = jnp.concatenate([jnp.sum(sums[i], axis=0, keepdims=True) for i in range(9)], axis=0)
        vectors[9:10, :] = sums_in[5:6, :]
        vectors[11:12, :] = sums_in[4:5, :]
        vectors[12:16, :] = sums_in[0:4, :]

        def vector_copy(step):
            axis = ("core", "y", "x", "zl", "zh")[step]
            return exchange(vectors, vector_got.at[step], vector_sems.at[0, step], vector_sems.at[1, step], axis)

        def vector_finish(step):
            vector_copy(step).wait()
            vectors[...] += vector_got[step]
            if step < 4:
                vector_copy(step + 1).start()

        vector_copy(0).start()
        trees["in0"].finish(1)
        trees["in1"].finish(1)
        trees["down"].finish(4)
        trees["up"].finish(5)
        trees["out"].finish(5)
        vector_finish(0)
        trees["in2"].finish(1)
        for xd in range(2):
            @pl.when(4 * y + 2 * c + xd != me)
            def _():
                tap_hop_two(0, xd, 4 * y + 2 * c + xd).wait_recv()
        tap_back_core().start()
        trees["in0"].finish(2)
        trees["in1"].finish(2)
        trees["down"].finish(5)
        for copy in own_out + near[6:8]:
            copy.wait()

        def home(target, r, block):
            for d in range(n):
                value = block(d)
                for j in range(wide):
                    place_at = pl.ds((r * blocks + d * span) * wide + j, span, stride=wide)
                    target[place_at, :] += value[:, j * 128:(j + 1) * 128]

        for r in range(rows):
            posts_out[r].arrive()
            home(out, r, lambda d: out_got[r, d * span:(d + 1) * span, :].astype(F32))
        vector_finish(1)
        trees["in2"].finish(2)
        trees["in0"].finish(3)
        trees["in1"].finish(3)
        tap_back_core().wait_recv()
        tap_back_y().start()
        trees["up"].finish(6)
        trees["out"].finish(6)
        trees["down"].finish(6)
        vector_finish(2)
        trees["in2"].finish(3)
        trees["in0"].finish(4)
        trees["in1"].finish(4)
        for half in range(2):
            for core in range(2):
                place_rows = slice(core * side, (core + 1) * side)
                for tree, target in ((trees["up"], grad_up), (trees["out"], grad_out)):
                    l = tree.share.shape[-1]
                    target[place_rows, half * l:(half + 1) * l] = tree.gathered[core, half].astype(F32)
        grad_down[...] = trees["down"].gathered[...].reshape(width, grad_down.shape[0]).astype(F32).T
        vector_finish(3)
        trees["in2"].finish(4)
        trees["in0"].finish(5)
        trees["in1"].finish(5)
        for r in range(rows):
            posts_grad[r].arrive()

            @pl.when(me >= n - 2)
            def _():
                for d in range(n):
                    @pl.when(me != d)
                    def _():
                        end_copy(r, 0, d).wait_recv()

            keep_end = (me >= n - 2).astype(F32)
            low_row = lax.broadcasted_iota(jnp.int32, (span, width), 0) == span - 1

            def block(d):
                value = grad_got[r, d * span:(d + 1) * span, :].astype(F32)
                if d + 1 < n:
                    end = jnp.where(me >= n - 2, end_got[r, d + 1, 0:8, :].astype(F32)[0:1, :], 0.0)
                    value = value + jnp.where(low_row, end, 0.0)
                return value

            home(grad_flat, r, block)
        vector_finish(4)
        trees["in2"].finish(5)
        trees["in0"].finish(6)
        trees["in1"].finish(6)
        tap_back_y().wait_recv()
        near[8].wait()
        for d in range(n):
            value = tap_home[d // 4, (d // 2) % 2, d % 2].astype(F32)
            for j in range(wide):
                place_at = pl.ds(d * span * wide + j, span, stride=wide)
                tanh = jnp.tanh(grad_kernel[place_at, :] * (1.0 / THRESH))
                grad_kernel[place_at, :] = value[:, j * 128:(j + 1) * 128] * (tanh * tanh)
        trees["in2"].finish(6)
        for k in range(3):
            tree = trees["in%d" % k]
            l = tree.share.shape[-1]
            for half in range(2):
                for core in range(2):
                    low = k * width + half * l
                    grad_in[core * side:(core + 1) * side, low:low + l] = tree.gathered[core, half].astype(F32)

        for tree in trees.values():
            tree.drain()
        for post in posts_out + posts_gate + posts_grad:
            post.drain()
        for r in range(rows):
            for slot in range(2):
                @pl.when(me != n - 2 + slot)
                def _():
                    end_copy(r, slot, me).wait_send()
        tap_core().wait_send()
        tap_y().wait_send()
        for xd in range(2):
            @pl.when(4 * y + 2 * c + xd != me)
            def _():
                tap_hop_one(xd).wait_send()

        @pl.when(chosen_chunk)
        def _():
            for j in range(1, n):
                tap_hop_two(j, xbit, lax.rem(me + j, n)).wait_send()

        tap_back_core().wait_send()
        tap_back_y().wait_send()

    pl.run_scoped(
        token_phase,
        pltpu.VMEM((6, rows, blocks, width), BF16),
        pltpu.VMEM(proj_far.shape, BF16),
        pltpu.VMEM(turned_far.shape, BF16),
        pltpu.VMEM(seen_far.shape, BF16),
        pltpu.VMEM(same_far.shape, F32),
        pltpu.VMEM(w_in_far.shape, BF16),
        pltpu.VMEM((blocks, width), F32),
        pltpu.VMEM((rows, ext, 3 * width), BF16),
        pltpu.VMEM((9, 8, width), F32),
        *[pltpu.VMEM((2, 2, 2, 2, 2, side, width // 2), BF16)] * 3,
    )


def call(body, outs, scratch, inputs, collective_id, far=(), far_outs=()):
    return pl.pallas_call(
        body,
        out_shape=tuple(jax.ShapeDtypeStruct(*out) for out in outs),
        in_specs=[pl.BlockSpec(memory_space=pl.ANY if i in far else pltpu.VMEM) for i in range(len(inputs))],
        out_specs=tuple(pl.BlockSpec(memory_space=pl.ANY if i in far_outs else pltpu.VMEM) for i in range(len(outs))),
        scratch_shapes=scratch,
        compiler_params=pltpu.CompilerParams(
            vmem_limit_bytes=VMEM_BYTES, collective_id=collective_id, has_side_effects=True
        ),
    )(*inputs)


def local(
    block_in, segment_ids, valid_mask, cotangent, gain_mix, in_proj, short_taps, long_kernel,
    skip_gain, out_proj, gain_mlp, up_proj, down_proj,
):
    rows, blocks, _, width = block_in.shape
    hidden = up_proj.shape[1]
    n = lax.axis_size("seq")
    each, span = width // n, blocks // n
    tokens, ext = rows * blocks, blocks + 2 * span
    side, wide = each // 2, width // 128
    chunk = 512
    x = block_in.reshape(tokens * wide, 128)
    cot = cotangent.reshape(tokens * wide, 128)
    raw = long_kernel.reshape(blocks * wide, 128)
    marks = jnp.concatenate(
        [segment_ids[:, :, 0], valid_mask[:, :, 0], jnp.zeros((8 - 2 * rows, blocks), jnp.int32)]
    ).astype(F32)
    weights = jnp.concatenate([
        short_taps.reshape(3, 3, width).transpose(1, 0, 2).reshape(9, width), skip_gain[None], jnp.zeros((6, width), F32),
    ])
    table, turns = spectrum_tables(blocks, n)
    dma = pltpu.SemaphoreType.DMA
    bits = (2, 2, 2, 2, 2)
    up_shape = bits + (side, hidden // 2)
    down_shape = bits + (width // 4, hidden // n)
    out_shape = bits + (side, width // 2)
    low = lambda *shape: pltpu.VMEM(shape, BF16)
    full = lambda *shape: pltpu.VMEM(shape, F32)

    (seen, proj, turned, saved, same, spec_taps, spec_gate, back, share_up, share_down, share_out, sums) = call(
        functools.partial(front_kernel, n, chunk),
        [
            ((rows, n + 2, span, width), BF16),
            ((rows, 3, ext, width), BF16),
            ((width, rows * ext), BF16),
            ((7, rows, blocks, width), BF16),
            ((3, rows, blocks, 128), F32),
            ((width, 2 * blocks), F32),
            ((rows, width, 2 * blocks), BF16),
            ((rows, n, each, blocks), BF16),
            (up_shape, BF16),
            (down_shape, BF16),
            (out_shape, BF16),
            ((8, width), F32),
        ],
        [
            full(blocks, 128), full(n, 128), full(n + 2, span, 128), full(2, n, 128),
            low(rows, blocks, width), low(rows, blocks, width),
            full(2 * n, width), low(2 * n, width), low(2, 2 * n, width), full(2, 2 * n, width),
            low(2, 2, 2, span, width), low(n, span, width), low(width, blocks), low(2, 2, 2, each, blocks),
            low(rows, n + 2, span, width), low(rows, n, span, width), low(rows, blocks, width), low(7, rows, blocks, width),
            full(3, rows, blocks, 128), low(rows, width, 2 * blocks),
            low(rows, width, blocks), low(rows, n, each, blocks), low(rows, n, each, blocks), low(rows, width, blocks),
            low(rows, width, blocks), low(rows, n, each, blocks),
            low(width, width), low(width, hidden), low(hidden, width),
            dma((7,)), dma((11,)),
            dma((rows, 2, n)), dma((2, n)), dma((rows, 2, n)), dma((4, n)), dma((5, n)),
            dma((rows, 2, n)), dma((rows, 2, n)), dma((rows, 2, n)),
        ],
        (x, cot, raw, marks, gain_mix[None], gain_mlp[None], in_proj, out_proj, up_proj, down_proj, weights, table, turns),
        1,
        far=(0, 1, 2, 6, 7, 8, 9),
        far_outs=range(11),
    )

    trees = []
    for shape in (up_shape, down_shape, out_shape):
        trees += tree_scratch(*shape[5:])
    for _ in range(3):
        trees += tree_scratch(*out_shape[5:])[1:]
    block_out, grad_flat, grad_inp, grad_out, grad_up, grad_down, grad_kernel, vectors = call(
        functools.partial(back_kernel, n),
        [
            (x.shape, F32),
            (x.shape, F32),
            ((each, 3 * width), F32),
            ((each, width), F32),
            ((each, hidden), F32),
            ((hidden // n, width), F32),
            (raw.shape, F32),
            ((16, width), F32),
        ],
        [
            low(rows, n, each, blocks), low(rows, width, blocks), low(rows, blocks, width),
            low(rows, n + 2, span, width), low(rows, blocks, width), low(rows, n, 16, width),
            dma((rows, 2, n)), dma((rows, 2, n)), dma((rows, 2, n)), dma((2, rows, n)), dma((17,)),
            low(2, 2, 2, each, blocks), low(2, 2, each, blocks), low(2, each, blocks),
            low(width, blocks), low(n, span, width), low(2, 2, 2, span, width),
            dma((2, 4)), dma((2, n)), dma((2, n)),
            full(5, 16, width), dma((2, 5)),
        ] + trees,
        (
            back, spec_taps, spec_gate, table, turns, share_up, share_down, share_out, saved, proj, turned,
            seen, same, in_proj, weights, gain_mix[None], sums, x, cot, raw,
        ),
        2,
        far=(0, 1, 2, 5, 6, 7, 8, 9, 10, 11, 12, 13, 17, 18, 19),
    )

    stats = jnp.sum(vectors[12:16], axis=1)
    grad_tap_rows = jnp.transpose(vectors[:9].reshape(3, 3, width), (1, 0, 2)).reshape(3, 3 * width)
    rms_stats = jnp.sqrt(stats[:3] / (jnp.maximum(stats[3], 1.0) * width))
    return (
        block_out.reshape(block_in.shape),
        grad_flat.reshape(block_in.shape),
        vectors[10],
        grad_inp,
        grad_tap_rows,
        grad_kernel.reshape(long_kernel.shape),
        vectors[9],
        grad_out,
        vectors[11],
        grad_up,
        grad_down,
        rms_stats,
    )


def chosen(block_in, *rest):
    rows, blocks, _, width = block_in.shape
    n = lax.axis_size("seq")
    fits = blocks % (32 * n) == 0 and width % (32 * n) == 0 and n == 8 and rows == 2 and lax.axis_size("rows") == 4
    return (local if fits else general_local)(block_in, *rest)


def solution(mesh):
    return jax.shard_map(
        chosen,
        mesh=mesh,
        in_specs=(
            P("rows", None, "seq", None),
            P("rows", None, "seq"),
            P("rows", None, "seq"),
            P("rows", None, "seq", None),
            P(),
            P(),
            P(),
            P(None, "seq", None),
            P(),
            P(),
            P(),
            P(),
            P(),
        ),
        out_specs=(
            P("rows", None, "seq", None),
            P("rows", None, "seq", None),
            P(),
            P("seq", None),
            P(),
            P(None, "seq", None),
            P(),
            P("seq", None),
            P(),
            P("seq", None),
            P("seq", None),
            P(),
        ),
        check_vma=False,
    )
```

```python
import functools
import math

import jax
import jax.numpy as jnp
import numpy as np
from jax import lax
from jax.experimental import pallas as pl
from jax.experimental.pallas import tpu as pltpu
from jax.sharding import PartitionSpec as P

EPS = 1e-05
THRESH = 0.003
HIGH = lax.Precision.HIGHEST


def shortened(x):

    def short(part):
        return part.astype(jnp.bfloat16) if part.dtype == jnp.float32 else part

    return jax.tree.map(short, x)


def passed_along(block, axis, distance):
    devices = range(lax.axis_size(axis))
    route = [((i - distance) % len(devices), i) for i in devices]
    return lax.ppermute(block, axis, route)


def norm_scale(value, gain):
    return value * lax.rsqrt(jnp.mean(value * value, axis=-1, keepdims=True) + EPS) * gain


def angle_tables(left_count, right_count, period):
    left_idx = jnp.arange(left_count, dtype=jnp.int32)[:, None]
    right_idx = jnp.arange(right_count, dtype=jnp.int32)[None, :]
    phase = (left_idx * right_idx % period).astype(jnp.float32) * (2.0 * math.pi / period)
    return (jnp.cos(phase), jnp.sin(phase))


def twiddle_tables(shard_index, spec_len, whole_len):
    turned = shard_index * jnp.arange(spec_len, dtype=jnp.int32) % whole_len
    phase = turned.astype(jnp.float32) * (2.0 * math.pi / whole_len)
    return (jnp.cos(phase)[None, :, None], jnp.sin(phase)[None, :, None])


def local_forward(signal, shard_index, whole_len):
    blocks = signal.shape[1]
    cos_table, sin_table = angle_tables(blocks, 2 * blocks, 2 * blocks)
    real_part = jnp.einsum("rjd,jk->rkd", signal, cos_table, precision=HIGH)
    imag_part = -jnp.einsum("rjd,jk->rkd", signal, sin_table, precision=HIGH)
    cos_twid, sin_twid = twiddle_tables(shard_index, 2 * blocks, whole_len)
    out_real = real_part * cos_twid + imag_part * sin_twid
    out_imag = imag_part * cos_twid - real_part * sin_twid
    return (out_real[:, :, None, :], out_imag[:, :, None, :])


def cross_section(real_part, imag_part, direction):
    count = real_part.shape[2]
    cos_table, sin_table = angle_tables(count, count, count)
    re_cos = jnp.einsum("rcpd,pm->rcmd", real_part, cos_table, precision=HIGH)
    re_sin = jnp.einsum("rcpd,pm->rcmd", real_part, sin_table, precision=HIGH)
    im_cos = jnp.einsum("rcpd,pm->rcmd", imag_part, cos_table, precision=HIGH)
    im_sin = jnp.einsum("rcpd,pm->rcmd", imag_part, sin_table, precision=HIGH)
    return (re_cos - direction * im_sin, im_cos + direction * re_sin)


def local_inverse(real_part, imag_part, shard_index, whole_len):
    real_part = real_part[:, :, 0, :]
    imag_part = imag_part[:, :, 0, :]
    spec_len = real_part.shape[1]
    cos_twid, sin_twid = twiddle_tables(shard_index, spec_len, whole_len)
    turned_re = real_part * cos_twid - imag_part * sin_twid
    turned_im = imag_part * cos_twid + real_part * sin_twid
    cos_table, sin_table = angle_tables(spec_len, spec_len // 2, spec_len)
    result = jnp.einsum("rkd,kj->rjd", turned_re, cos_table, precision=HIGH)
    result = result - jnp.einsum("rkd,kj->rjd", turned_im, sin_table, precision=HIGH)
    return result / whole_len


def earlier(members, at_start):
    received = jax.tree.map(
        lambda part, own: part.astype(own.dtype),
        passed_along(shortened(members), "seq", 1),
        members,
    )
    placed = []
    for member in received:
        rolled = jnp.concatenate([jnp.zeros_like(member[:, :1]), member[:, :-1]], axis=1)
        placed.append(jnp.where(at_start, rolled, member))
    return tuple(placed)


def later(member, at_end):
    received = passed_along(member.astype(jnp.bfloat16), "seq", -1).astype(member.dtype)
    rolled = jnp.concatenate([received[:, 1:], jnp.zeros_like(received[:, :1])], axis=1)
    return jnp.where(at_end, rolled, received)


def times_trans(left, right):
    return lax.dot_general(
        left, right, (((1,), (1,)), ((), ())), preferred_element_type=jnp.float32
    )


def trans_times(left, right):
    return lax.dot_general(
        left, right, (((0,), (0,)), ((), ())), preferred_element_type=jnp.float32
    )


def general_local(
    block_in,
    segment_ids,
    valid_mask,
    cotangent,
    gain_mix,
    in_proj,
    short_taps,
    long_kernel,
    skip_gain,
    out_proj,
    gain_mlp,
    up_proj,
    down_proj,
):
    batch_rows = block_in.shape[0]
    blocks = block_in.shape[1]
    width = block_in.shape[3]
    shard_count = lax.axis_size("seq")
    shard_index = lax.axis_index("seq")
    whole_len = 2 * blocks * shard_count
    tokens = batch_rows * blocks
    at_start = shard_index == 0
    at_end = shard_index == shard_count - 1
    flat_in = block_in.reshape(tokens, width)
    mask_rows = valid_mask[:, :, 0].astype(jnp.float32)[:, :, None]
    normed_one = norm_scale(flat_in, gain_mix).astype(jnp.bfloat16)
    proj_low = jnp.dot(normed_one, in_proj, preferred_element_type=jnp.float32).astype(jnp.bfloat16)
    proj_low = proj_low.reshape(batch_rows, blocks, 3 * width)
    seg_low = segment_ids[:, :, 0].astype(jnp.bfloat16)[:, :, None]
    prev_one = earlier((proj_low, seg_low), at_start)
    prev_two = earlier(prev_one, at_start)
    same_one = (prev_one[1] == seg_low).astype(jnp.float32)
    same_two = (prev_two[1] == seg_low).astype(jnp.float32)
    proj_now = proj_low.astype(jnp.float32)
    proj_one = prev_one[0].astype(jnp.float32)
    proj_two = prev_two[0].astype(jnp.float32)
    conv_short = (
        short_taps[0] * proj_now
        + short_taps[1] * proj_one * same_one
        + short_taps[2] * proj_two * same_two
    )
    query = conv_short[:, :, :width]
    keys = conv_short[:, :, width : 2 * width]
    values = conv_short[:, :, 2 * width :]
    gated = keys * values * mask_rows
    raw_taps = long_kernel[:, 0, :]
    taps_eff = raw_taps - THRESH * jnp.tanh(raw_taps / THRESH)
    kern_re, kern_im = local_forward(taps_eff[None], shard_index, whole_len)
    kern_re, kern_im = (
        lax.all_to_all(
            kern_re.astype(jnp.bfloat16), "seq", split_axis=1, concat_axis=2, tiled=True
        ).astype(kern_re.dtype),
        lax.all_to_all(
            kern_im.astype(jnp.bfloat16), "seq", split_axis=1, concat_axis=2, tiled=True
        ).astype(kern_im.dtype),
    )
    kern_re, kern_im = cross_section(kern_re, kern_im, -1.0)
    gate_re, gate_im = local_forward(gated, shard_index, whole_len)
    gate_re, gate_im = (
        lax.all_to_all(
            gate_re.astype(jnp.bfloat16), "seq", split_axis=1, concat_axis=2, tiled=True
        ).astype(gate_re.dtype),
        lax.all_to_all(
            gate_im.astype(jnp.bfloat16), "seq", split_axis=1, concat_axis=2, tiled=True
        ).astype(gate_im.dtype),
    )
    gate_re, gate_im = cross_section(gate_re, gate_im, -1.0)
    prod_re = gate_re * kern_re - gate_im * kern_im
    prod_im = gate_re * kern_im + gate_im * kern_re
    prod_re, prod_im = cross_section(prod_re, prod_im, 1.0)
    prod_re, prod_im = (
        lax.all_to_all(
            prod_re.astype(jnp.bfloat16), "seq", split_axis=2, concat_axis=1, tiled=True
        ).astype(prod_re.dtype),
        lax.all_to_all(
            prod_im.astype(jnp.bfloat16), "seq", split_axis=2, concat_axis=1, tiled=True
        ).astype(prod_im.dtype),
    )
    long_out = local_inverse(prod_re, prod_im, shard_index, whole_len) + skip_gain * gated
    mixer_low = (query * long_out).reshape(tokens, width).astype(jnp.bfloat16)
    mixer_out = jnp.dot(mixer_low, out_proj, preferred_element_type=jnp.float32)
    resid_mid = flat_in + mixer_out
    normed_two = norm_scale(resid_mid, gain_mlp).astype(jnp.bfloat16)
    up_val = jnp.dot(normed_two, up_proj, preferred_element_type=jnp.float32)
    act_low = jax.nn.gelu(up_val).astype(jnp.bfloat16)
    mlp_out = jnp.dot(act_low, down_proj, preferred_element_type=jnp.float32)
    flat_out = resid_mid + mlp_out
    grad_out = cotangent.reshape(tokens, width)
    grad_mlp = grad_out.astype(jnp.bfloat16)
    grad_down = trans_times(act_low, grad_mlp)
    grad_act = times_trans(grad_mlp, down_proj)
    unused_val, gelu_back = jax.vjp(jax.nn.gelu, up_val)
    grad_upval = gelu_back(grad_act)[0].astype(jnp.bfloat16)
    grad_up = trans_times(normed_two, grad_upval)
    grad_norm_two = times_trans(grad_upval, up_proj)
    unused_two, norm_back_two = jax.vjp(norm_scale, resid_mid, gain_mlp)
    grad_resid, grad_gain_two = norm_back_two(grad_norm_two)
    grad_mid = grad_out + grad_resid
    grad_mix = grad_mid.astype(jnp.bfloat16)
    grad_outp = trans_times(mixer_low, grad_mix)
    grad_prod = times_trans(grad_mix, out_proj).reshape(batch_rows, blocks, width)
    grad_query = grad_prod * long_out
    grad_long = grad_prod * query
    back_re, back_im = local_forward(grad_long, shard_index, whole_len)
    back_re, back_im = (
        lax.all_to_all(
            back_re.astype(jnp.bfloat16), "seq", split_axis=1, concat_axis=2, tiled=True
        ).astype(back_re.dtype),
        lax.all_to_all(
            back_im.astype(jnp.bfloat16), "seq", split_axis=1, concat_axis=2, tiled=True
        ).astype(back_im.dtype),
    )
    back_re, back_im = cross_section(back_re, back_im, -1.0)
    sig_re = kern_re * back_re + kern_im * back_im
    sig_im = kern_re * back_im - kern_im * back_re
    tap_re = jnp.sum(gate_re * back_re + gate_im * back_im, axis=0, keepdims=True)
    tap_im = jnp.sum(gate_re * back_im - gate_im * back_re, axis=0, keepdims=True)
    sig_re, sig_im = cross_section(sig_re, sig_im, 1.0)
    tap_re, tap_im = cross_section(tap_re, tap_im, 1.0)
    sig_re, sig_im, tap_re, tap_im = (
        lax.all_to_all(
            sig_re.astype(jnp.bfloat16), "seq", split_axis=2, concat_axis=1, tiled=True
        ).astype(sig_re.dtype),
        lax.all_to_all(
            sig_im.astype(jnp.bfloat16), "seq", split_axis=2, concat_axis=1, tiled=True
        ).astype(sig_im.dtype),
        lax.all_to_all(
            tap_re.astype(jnp.bfloat16), "seq", split_axis=2, concat_axis=1, tiled=True
        ).astype(tap_re.dtype),
        lax.all_to_all(
            tap_im.astype(jnp.bfloat16), "seq", split_axis=2, concat_axis=1, tiled=True
        ).astype(tap_im.dtype),
    )
    grad_gated = local_inverse(sig_re, sig_im, shard_index, whole_len) + skip_gain * grad_long
    grad_taps_eff = local_inverse(tap_re, tap_im, shard_index, whole_len)[0]
    tanh_val = jnp.tanh(raw_taps / THRESH)
    grad_kernel = (grad_taps_eff * tanh_val * tanh_val)[:, None, :]
    grad_kernel = lax.psum(grad_kernel.astype(jnp.bfloat16), "rows").astype(jnp.float32)
    grad_skip = jnp.sum(grad_long * gated, axis=(0, 1))
    grad_short = jnp.concatenate(
        [grad_query, grad_gated * values * mask_rows, grad_gated * keys * mask_rows], axis=2
    )
    grad_tap_rows = jnp.stack(
        [
            jnp.sum(grad_short * proj_now, axis=(0, 1)),
            jnp.sum(grad_short * proj_one * same_one, axis=(0, 1)),
            jnp.sum(grad_short * proj_two * same_two, axis=(0, 1)),
        ]
    )
    inner_term = short_taps[1] * grad_short * same_one + later(
        short_taps[2] * grad_short * same_two, at_end
    )
    grad_proj = short_taps[0] * grad_short + later(inner_term, at_end)
    grad_proj = grad_proj.reshape(tokens, 3 * width).astype(jnp.bfloat16)
    grad_inp = trans_times(normed_one, grad_proj)
    grad_norm_one = times_trans(grad_proj, in_proj)
    unused_one, norm_back_one = jax.vjp(norm_scale, flat_in, gain_mix)
    grad_first, grad_gain_one = norm_back_one(grad_norm_one)
    grad_flat = grad_mid + grad_first
    mask_flat = mask_rows.reshape(tokens, 1)
    stat_sums = jnp.stack(
        [
            jnp.sum(mask_flat * flat_out * flat_out),
            jnp.sum(mask_flat * mixer_out * mixer_out),
            jnp.sum(mask_flat * mlp_out * mlp_out),
            jnp.sum(mask_flat),
        ]
    )
    grad_gain_one, grad_gain_two, grad_tap_rows, grad_skip, stat_sums = lax.psum(
        (grad_gain_one, grad_gain_two, grad_tap_rows, grad_skip, stat_sums), ("rows", "seq")
    )
    rms_stats = jnp.sqrt(stat_sums[:3] / (jnp.maximum(stat_sums[3], 1.0) * width))
    shares = (
        lax.psum_scatter(grad_inp, "seq", scatter_dimension=0, tiled=True),
        lax.psum_scatter(grad_outp, "seq", scatter_dimension=0, tiled=True),
        lax.psum_scatter(grad_up, "seq", scatter_dimension=0, tiled=True),
        lax.psum_scatter(grad_down, "seq", scatter_dimension=0, tiled=True),
    )
    grad_inp, grad_outp, grad_up, grad_down = (
        lax.psum(shares[0].astype(jnp.bfloat16), "rows").astype(jnp.float32),
        lax.psum(shares[1].astype(jnp.bfloat16), "rows").astype(jnp.float32),
        lax.psum(shares[2].astype(jnp.bfloat16), "rows").astype(jnp.float32),
        lax.psum(shares[3].astype(jnp.bfloat16), "rows").astype(jnp.float32),
    )
    return (
        flat_out.reshape(block_in.shape),
        grad_flat.reshape(block_in.shape),
        grad_gain_one,
        grad_inp,
        grad_tap_rows,
        grad_kernel,
        grad_skip,
        grad_outp,
        grad_gain_two,
        grad_up,
        grad_down,
        rms_stats,
    )


MESH = pl.DeviceIdType.MESH
F32 = jnp.float32
BF16 = jnp.bfloat16
VMEM_BYTES = 62 * 1024 * 1024
C0 = math.sqrt(2.0 / math.pi)
C1 = 0.044715
ALL = slice(None)


def dot_nn(a, b):
    return lax.dot_general(a, b, (((1,), (0,)), ((), ())), preferred_element_type=F32)


def dot_nt(a, b):
    return lax.dot_general(a, b, (((1,), (1,)), ((), ())), preferred_element_type=F32)


def fft_points(re, im, sign):
    n = len(re)
    if n == 1:
        return re, im
    even_r, even_i = fft_points(re[0::2], im[0::2], sign)
    odd_r, odd_i = fft_points(re[1::2], im[1::2], sign)
    out_r, out_i = [None] * n, [None] * n
    for k in range(n // 2):
        if k == 0:
            turn_r, turn_i = odd_r[0], odd_i[0]
        elif 4 * k == n:
            if sign > 0:
                out_r[k], out_i[k] = even_r[k] - odd_i[k], even_i[k] + odd_r[k]
                out_r[k + n // 2], out_i[k + n // 2] = even_r[k] + odd_i[k], even_i[k] - odd_r[k]
            else:
                out_r[k], out_i[k] = even_r[k] + odd_i[k], even_i[k] - odd_r[k]
                out_r[k + n // 2], out_i[k + n // 2] = even_r[k] - odd_i[k], even_i[k] + odd_r[k]
            continue
        else:
            cos, sin = math.cos(2 * math.pi * k / n), sign * math.sin(2 * math.pi * k / n)
            turn_r = cos * odd_r[k] - sin * odd_i[k]
            turn_i = cos * odd_i[k] + sin * odd_r[k]
        out_r[k], out_i[k] = even_r[k] + turn_r, even_i[k] + turn_i
        out_r[k + n // 2], out_i[k + n // 2] = even_r[k] - turn_r, even_i[k] - turn_i
    return out_r, out_i


def spectrum_tables(blocks, phases):
    length = blocks * phases
    k = 2 * np.arange(blocks)[None, :] + 1
    angle = 2.0 * np.pi * np.arange(blocks)[:, None] * k / (4.0 * blocks)
    table = np.concatenate([np.cos(angle), -np.sin(angle)], axis=1)
    turn = 2.0 * np.pi * np.arange(phases)[:, None] * k / (4.0 * length)
    turns = np.stack([np.cos(turn), np.sin(turn)], axis=1)[:, :, None, :]
    return jnp.asarray(table, F32), jnp.asarray(np.broadcast_to(turns, (phases, 2, 8, blocks)), F32)


def place():
    row, seq = lax.axis_index("rows"), lax.axis_index("seq")
    return lax.div(row, 2), lax.rem(row, 2), lax.div(seq, 4), lax.rem(lax.div(seq, 2), 2), lax.rem(seq, 2)


def partner(axis):
    y, c, zh, zl, x = place()
    if axis == "core":
        return {"rows": 2 * y + 1 - c}
    if axis == "y":
        return {"rows": 2 * (1 - y) + c}
    if axis == "x":
        return {"seq": 4 * zh + 2 * zl + 1 - x}
    if axis == "zl":
        return {"seq": 4 * zh + 2 * (1 - zl) + x}
    return {"seq": 4 * (1 - zh) + 2 * zl + x}


def remote(src, dst, send_sem, recv_sem, target):
    return pltpu.make_async_remote_copy(
        src_ref=src, dst_ref=dst, send_sem=send_sem, recv_sem=recv_sem, device_id=target, device_id_type=MESH,
    )


def exchange(src, dst, send_sem, recv_sem, axis):
    return remote(src, dst, send_sem, recv_sem, partner(axis))


def greet(n):
    me = lax.axis_index("seq")
    barrier = pltpu.get_barrier_semaphore()
    for j in range(1, n):
        pl.semaphore_signal(barrier, inc=1, device_id={"seq": lax.rem(me + j, n)}, device_id_type=MESH)
    for axis in ("core", "y"):
        pl.semaphore_signal(barrier, inc=1, device_id=partner(axis), device_id_type=MESH)
    return barrier, n + 1


def aligned(index, size):
    return pl.ds(pl.multiple_of(index * size, size), size)


class Post:
    def __init__(self, n, source, target, sems):
        self.n, self.source, self.target, self.sems = n, source, target, sems

    def copies(self, sender):
        me = lax.axis_index("seq")
        for j in range(1, self.n):
            peer = lax.rem(me + j, self.n)
            come = sender(peer, me)
            yield remote(
                self.source(peer), self.target(come), self.sems.at[0, j], self.sems.at[1, come], {"seq": peer}
            )

    def start(self):
        me = lax.axis_index("seq")
        for copy in self.copies(lambda peer, me: me):
            copy.start()
        self.target(me)[...] = self.source(me)[...]

    def arrive(self):
        for copy in self.copies(lambda peer, me: peer):
            copy.wait_recv()

    def drain(self):
        for copy in self.copies(lambda peer, me: me):
            copy.wait_send()


def over_groups(each, blocks, body):
    for lane in range(0, blocks, 128):
        def step(g, carry):
            body(pl.multiple_of(g * 16, 16), lane)
            return carry
        lax.fori_loop(0, each // 16, step, 0)


def matmul_rows(out, left, right, size=256):
    for at in range(0, out.shape[0], size):
        out[at:at + size, :] = left(at, size, right)


def load_phases(spec, n, each, at, lane, half):
    re = [spec[pl.ds(p * each + at, 8), lane:lane + 128] for p in range(n)]
    im = [spec[pl.ds(p * each + at, 8), half + lane:half + lane + 128] for p in range(n)]
    return re, im


def turn_phases(re, im, turns, lane, sign):
    out_r, out_i = [re[0]], [im[0]]
    for p in range(1, len(re)):
        cos, sin = turns[p, 0, :, lane:lane + 128], turns[p, 1, :, lane:lane + 128]
        if sign > 0:
            out_r.append(re[p] * cos - im[p] * sin)
            out_i.append(im[p] * cos + re[p] * sin)
        else:
            out_r.append(re[p] * cos + im[p] * sin)
            out_i.append(im[p] * cos - re[p] * sin)
    return out_r, out_i


def by_halves(n, each, blocks, spec, work, stores, kept=None):
    def group(at, lane):
        halves = []
        if kept is not None:
            loaded = [
                [kept[pl.ds(k * each + at, 16), part + lane:part + lane + 128].astype(F32) for k in range(n)]
                for part in (0, blocks)
            ]
        for half in (0, 8):
            re, im = load_phases(spec, n, each, at + half, lane, blocks)
            old = None if kept is None else [[value[half:half + 8] for value in part] for part in loaded]
            halves.append(work(re, im, at + half, lane, old))
        for target, first, second in zip(stores, *halves):
            for k in range(n):
                for part in range(2):
                    value = jnp.concatenate([first[part][k], second[part][k]], axis=0).astype(BF16)
                    target[pl.ds(k * each + at, 16), part * blocks + lane:part * blocks + lane + 128] = value

    over_groups(each, blocks, group)


def to_lanes(source, table, spec):
    for at in range(0, spec.shape[0], 256):
        spec[at:at + 256, :] = dot_nn(source(at, 256), table[...])


def from_lanes(fin, table, size, store):
    for at in range(0, fin.shape[0], size):
        store(at, dot_nt(fin[at:at + size, :], table[...]) * (2.0 / fin.shape[1] / (fin.shape[0] // size)))


def over_rows(total, size, body):
    def step(i, carry):
        body(aligned(i, size))
        return carry
    lax.fori_loop(0, total // size, step, 0)


def over_lanes(width, body):
    def step(i, carry):
        body(aligned(i, 128))
        return carry
    lax.fori_loop(0, width // 128, step, 0)


def strided(ref, rows, start, lane, wide):
    return ref[pl.ds(start * wide + lane, rows, stride=wide), :]


def turn_rows(value, amount):
    return pltpu.roll(value, amount % value.shape[0], 0)


def front_kernel(
    n, chunk,
    x_far, cot_far, taps_far, short_taps, skip, gain_mix, gain_mlp, segments, valid, w_in_far, w_out_far, w_up_far, w_down_far,
    table_wide, turns,
    out_far, mid_out, turned_out, saved_out, same_out, spec_taps_out, spec_gate_out, back_out,
    share_up_out, share_down_out, share_out_out, vectors, small,
    marks, marks_got, x, cot, cot_low, near, land, taps_sent, taps_got,
    table, query, saved, same, gate_sent, gate_got, long_sent, long_got, back_sent, back_got,
    w_out, w_up, w_down, fetch, keep, near_sems, mark_sems, tap_sems, gate_sems, long_sems, back_sems,
):
    me = lax.axis_index("seq")
    y, c, zh, zl, xbit = place()
    rows, blocks = query.shape[0], query.shape[1]
    width, hidden = w_up.shape
    each, wide, step = width // n, width // 128, blocks // 2
    at_top = jnp.logical_and(zh == 0, zl == 0)
    barrier, told = greet(n)
    for row, vector in ((9, skip), (10, gain_mix), (11, gain_mlp)):
        small[row, :] = vector[...]
    gain_one, gain_two = small[10:11, :], small[11:12, :]
    table[...] = table_wide[...].astype(BF16)

    fetch_out = pltpu.make_async_copy(w_out_far, w_out, fetch.at[0])
    fetch_up = pltpu.make_async_copy(w_up_far, w_up, fetch.at[1])
    fetch_down = pltpu.make_async_copy(w_down_far, w_down, fetch.at[2])
    post_marks = Post(n, lambda d: marks, lambda p: marks_got.at[p], mark_sems)
    posts_gate = [
        Post(n, lambda e, r=r: gate_sent.at[r, aligned(e, each)], lambda p, r=r: gate_got.at[r, aligned(p, each)], gate_sems.at[r])
        for r in range(rows)
    ]
    posts_long = [
        Post(n, lambda p, r=r: long_sent.at[r, aligned(p, each)], lambda e, r=r: long_got.at[r, aligned(e, each)], long_sems.at[r])
        for r in range(rows)
    ]
    posts_back = [
        Post(n, lambda e, r=r: back_sent.at[r, aligned(e, each)], lambda p, r=r: back_got.at[r, aligned(p, each)], back_sems.at[r])
        for r in range(rows)
    ]

    def far_copy(r, h):
        part = slice(h * step, (h + 1) * step)
        target = {"seq": lax.rem(me + 2, n)}
        return remote(near.at[0, r, part], land.at[1, r, part], near_sems.at[0, 0, r, h], near_sems.at[0, 1, r, h], target)

    def side_copy(r, h, source):
        part = slice(h * step, (h + 1) * step)
        return exchange(source.at[r, part], land.at[0, r, part], near_sems.at[1, 0, r, h], near_sems.at[1, 1, r, h], "x")

    def tap_copy(e):
        return remote(taps_sent.at[aligned(e, each)], taps_got.at[aligned(me, each)], tap_sems.at[0, lax.rem(e, 2)], tap_sems.at[1, me], {"seq": e})

    def tap_spread(axis):
        at = 2 if axis == "core" else 3
        return exchange(taps_got, taps_got, tap_sems.at[at, 0], tap_sems.at[at, 1], axis)

    chosen_chunk = jnp.logical_and(zh == y, zl == c)

    def front(x_in, cot_in, taps, w_in, proj, turned, gate_wide, fin, spec, spec_taps, spec_gate):
        first = [
            pltpu.make_async_copy(src, dst, fetch.at[3 + i])
            for i, (src, dst) in enumerate(((x_far, x_in), (taps_far, taps), (w_in_far, w_in), (cot_far, cot_in)))
        ]
        for copy in first + [fetch_out, fetch_up, fetch_down]:
            copy.start()
        marks[...] = jnp.zeros_like(marks)
        for r in range(rows):
            marks[r:r + 1, :] = segments[r].astype(F32)
            marks[rows + r:rows + r + 1, :] = valid[r].astype(F32)
        for k in range(3):
            small[3 * k:3 * k + 3, :] = short_taps[:, k * width:(k + 1) * width]
        small[12:16, :] = jnp.zeros((4, width), F32)
        first[0].wait()

        def norm_row(r):
            for at in range(r * blocks, (r + 1) * blocks, 128):
                parts = [strided(x_in, 128, at, j, wide) for j in range(wide)]
                total = sum(jnp.sum(part * part, axis=-1, keepdims=True) for part in parts)
                scale = lax.rsqrt(total * (1.0 / width) + EPS)
                for j, part in enumerate(parts):
                    lanes = slice(j * 128, (j + 1) * 128)
                    x[at:at + 128, lanes] = part
                    near[0, r, at - r * blocks:at - r * blocks + 128, lanes] = (part * scale * gain_one[:, lanes]).astype(BF16)

        def send_near(r):
            for h in range(2):
                far_copy(r, h).start()

            @pl.when(xbit == 0)
            def _():
                for h in range(2):
                    side_copy(r, h, near.at[0]).start()

        def hand_on(r):
            @pl.when(xbit == 1)
            def _():
                for h in range(2):
                    far_copy(r, h).wait_recv()
                    side_copy(r, h, land.at[1]).start()

        norm_row(0)
        pl.semaphore_wait(barrier, told)
        send_near(0)
        post_marks.start()
        norm_row(1)
        send_near(1)
        first[1].wait()
        for j in range(wide):
            raw = strided(taps, blocks, 0, j, wide)
            low = raw - THRESH * jnp.tanh(raw * (1.0 / THRESH))
            taps_sent[j * 128:(j + 1) * 128, :] = low.T.astype(BF16)
        for xd in range(2):
            target = 4 * y + 2 * c + xd

            @pl.when(target != me)
            def _():
                tap_copy(target).start()

            @pl.when(target == me)
            def _():
                taps_got[aligned(me, each)] = taps_sent[aligned(me, each)]

        first[2].wait()

        def project(r, j):
            for k in (1, 2, 0):
                for at in range(0, width, 256):
                    cols = slice(k * width + at, k * width + at + 256)
                    proj[r, j, k, :, at:at + 256] = dot_nn(near[j, r], w_in[:, cols]).astype(BF16)

        project(0, 0)
        hand_on(0)
        first[3].wait()
        for r in range(rows):
            for j in range(wide):
                cot[r * blocks:(r + 1) * blocks, j * 128:(j + 1) * 128] = strided(cot_in, blocks, r * blocks, j, wide)
            cot_low[r] = cot[r * blocks:(r + 1) * blocks, :].astype(BF16)
        post_marks.arrive()
        lane = lax.broadcasted_iota(jnp.int32, (rows, blocks), 1)
        now = marks[0:rows, :]
        found = []
        for j in (1, 2):
            before = marks_got[lax.rem(me + n - j, n), 0:rows, :]
            wrapped = me < j
            before = jnp.where(wrapped, pltpu.roll(before, 1, 1), before)
            kept = jnp.logical_and(before == now, jnp.logical_or(jnp.logical_not(wrapped), lane > 0))
            found.append(kept.astype(F32))
        columns = jnp.concatenate(found + [marks[rows:2 * rows, :], jnp.zeros((2, blocks), F32)], axis=0).T
        for s in range(3):
            for r in range(rows):
                same[s, r] = jnp.broadcast_to(columns[:, s * rows + r:s * rows + r + 1], (blocks, 128))

        def chunk_row(r):
            @pl.when(xbit == 0)
            def _():
                for h in range(2):
                    far_copy(r, h).wait_recv()

            for h in range(2):
                side_copy(r, h, near.at[0]).wait_recv()
            for j in (1, 2):
                wrapped = jnp.logical_and(at_top, xbit == 0) if j == 1 else at_top

                @pl.when(wrapped)
                def _():
                    near[j, r] = turn_rows(land[j - 1, r].astype(F32), 1).astype(BF16)

                @pl.when(jnp.logical_not(wrapped))
                def _():
                    near[j, r] = land[j - 1, r]

                project(r, j)

            def lanes_step(lanes):
                def rows_step(here):
                    masks = [same[s, r, here, :] for s in range(3)]
                    value = []
                    for k in range(3):
                        total = small[3 * k:3 * k + 1, lanes] * proj[r, 0, k, here, lanes].astype(F32)
                        total += small[3 * k + 1:3 * k + 2, lanes] * (proj[r, 1, k, here, lanes].astype(F32) * masks[0])
                        total += small[3 * k + 2:3 * k + 3, lanes] * (proj[r, 2, k, here, lanes].astype(F32) * masks[1])
                        value.append(total)
                    query[r, here, lanes] = value[0]
                    keys, values = value[1] * masks[2], value[2] * masks[2]
                    gate = value[1] * values
                    saved[0, r, here, lanes] = keys.astype(BF16)
                    saved[1, r, here, lanes] = values.astype(BF16)
                    saved[2, r, here, lanes] = gate.astype(BF16)
                    gate_wide[here, lanes] = gate

                over_rows(blocks, 64, rows_step)

            over_lanes(width, lanes_step)
            gate_sent[r] = gate_wide[...].T.astype(BF16)
            posts_gate[r].start()

        chunk_row(0)
        project(1, 0)
        hand_on(1)

        @pl.when(chosen_chunk)
        def _():
            for p in range(n):
                @pl.when(me != p)
                def _():
                    remote(
                        taps_sent.at[aligned(me, each)], taps_got.at[p * each:(p + 1) * each],
                        tap_sems.at[0, 0], tap_sems.at[1, p], {"seq": p},
                    ).wait_recv()
            tap_spread("core").start()

        @pl.when(jnp.logical_and(zh == y, zl != c))
        def _():
            tap_spread("core").wait_recv()

        @pl.when(zh == y)
        def _():
            tap_spread("y").start()

        chunk_row(1)

        @pl.when(zh != y)
        def _():
            tap_spread("y").wait_recv()

        to_lanes(lambda at, size: taps_got[at:at + size], table, spec)

        def taps_group(at, lane):
            re, im = load_phases(spec, n, each, at, lane, blocks)
            re, im = turn_phases(re, im, turns, lane, -1)
            re, im = fft_points(re, im, -1)
            for k in range(n):
                spec_taps[pl.ds(k * each + at, 8), lane:lane + 128] = re[k]
                spec_taps[pl.ds(k * each + at, 8), blocks + lane:blocks + lane + 128] = im[k]

        def both_halves(at, lane):
            taps_group(at, lane)
            taps_group(at + 8, lane)

        over_groups(each, blocks, both_halves)
        keeps = [pltpu.make_async_copy(spec_taps, spec_taps_out, keep.at[0])]
        keeps[0].start()

        for r in range(rows):
            posts_gate[r].arrive()
            to_lanes(lambda at, size: gate_got[r, at:at + size], table, spec)

            def work(re, im, at, lane, kept):
                re, im = turn_phases(re, im, turns, lane, -1)
                re, im = fft_points(re, im, -1)
                tap_r, tap_i = load_phases(spec_taps, n, each, at, lane, blocks)
                out_r = [re[k] * tap_r[k] - im[k] * tap_i[k] for k in range(n)]
                out_i = [re[k] * tap_i[k] + im[k] * tap_r[k] for k in range(n)]
                out_r, out_i = fft_points(out_r, out_i, 1)
                out_r, out_i = turn_phases(out_r, out_i, turns, lane, 1)
                return (re, im), (out_r, out_i)

            by_halves(n, each, blocks, spec, work, (spec_gate.at[r], fin))

            def store(at, value):
                long_sent[r, at:at + value.shape[0]] = value.astype(BF16)

            from_lanes(fin, table, each, store)
            posts_long[r].start()
        for j in range(3):
            for r in range(rows):
                value = near[j, r].astype(F32)
                if j > 0:
                    value = value * same[j - 1, r, :, 0:1]
                turned[j, :, r * blocks:(r + 1) * blocks] = value.T.astype(BF16)
        keeps += [
            pltpu.make_async_copy(turned, turned_out, keep.at[1]),
            pltpu.make_async_copy(spec_gate, spec_gate_out, keep.at[2]),
        ]
        for copy in keeps[1:]:
            copy.start()
        for copy in keeps:
            copy.wait()

    pl.run_scoped(
        front,
        pltpu.VMEM(x_far.shape, F32),
        pltpu.VMEM(cot_far.shape, F32),
        pltpu.VMEM(taps_far.shape, F32),
        pltpu.VMEM(w_in_far.shape, BF16),
        pltpu.VMEM((rows, 3, 3, blocks, width), BF16),
        pltpu.VMEM(turned_out.shape, BF16),
        pltpu.VMEM((blocks, width), F32),
        pltpu.VMEM((width, 2 * blocks), BF16),
        pltpu.VMEM((width, 2 * blocks), F32),
        pltpu.VMEM((width, 2 * blocks), F32),
        pltpu.VMEM(spec_gate_out.shape, BF16),
    )
    keep_same = pltpu.make_async_copy(same.at[0:2], same_out, keep.at[3])
    keep_same.start()

    def middle(act, grad_act, resid, long_out, acc_out, acc_back, normed, turned, turned_cot, mixed, mix_back, up, down, out, whole_out, mid):
        vectors[...] = jnp.zeros_like(vectors)
        fetch_out.wait()
        for r in range(rows):
            tokens = slice(r * blocks, (r + 1) * blocks)
            posts_long[r].arrive()
            gated = saved[2, r].astype(F32)
            long_out[...] = long_got[r].astype(F32).T + small[9:10, :] * gated
            low = (query[r] * long_out[...]).astype(BF16)
            mixer = dot_nn(low, w_out[...])
            mixed[r] = low.T
            mask = same[2, r, :, 0:1]
            vectors[1:2, :] += jnp.sum(mixer * mixer * mask, axis=0, keepdims=True)
            state = x[tokens, :] + mixer
            resid[...] = state
            scale = lax.rsqrt(jnp.mean(state * state, axis=-1, keepdims=True) + EPS)
            normed[...] = (state * scale * gain_two).astype(BF16)
            acc_out[...] = jnp.zeros_like(acc_out)
            acc_back[...] = jnp.zeros_like(acc_back)
            if r == 0:
                fetch_up.wait()
                fetch_down.wait()

            def hidden_step(j, carry):
                cols = aligned(j, chunk)
                up_val = dot_nn(normed[...], w_up[:, cols])
                square = up_val * up_val
                tanh = jnp.tanh(up_val * (C0 + (C0 * C1) * square))
                half = 0.5 * (1.0 + tanh)
                act_low = (up_val * half).astype(BF16)
                slope = half + (0.5 * up_val) * (1.0 - tanh * tanh) * (C0 + (3.0 * C0 * C1) * square)
                act[tokens, cols] = act_low
                acc_out[...] += dot_nn(act_low, w_down[cols, :])
                grad = dot_nt(cot_low[r], w_down[cols, :])
                grad_low = (grad * slope).astype(BF16)
                grad_act[tokens, cols] = grad_low
                acc_back[...] += dot_nt(grad_low, w_up[:, cols])
                return carry

            lax.fori_loop(0, hidden // chunk, hidden_step, 0)
            state = resid[...]
            scale = lax.rsqrt(jnp.mean(state * state, axis=-1, keepdims=True) + EPS)
            grad = acc_back[...]
            vectors[4:5, :] += jnp.sum(grad * state * scale, axis=0, keepdims=True)
            scaled = grad * gain_two
            shift = jnp.mean(scaled * state, axis=-1, keepdims=True) * (scale * scale * scale)
            grad_mid = cot[tokens, :] + (scaled * scale - state * shift)
            mix_back[r] = grad_mid.astype(BF16)
            grad_prod = dot_nt(mix_back[r], w_out[...])
            grad_long = grad_prod * query[r]
            back_sent[r] = grad_long.T.astype(BF16)
            posts_back[r].start()
            saved[3, r] = grad_long.astype(BF16)
            saved[4, r] = (grad_prod * long_out[...]).astype(BF16)
            vectors[5:6, :] += jnp.sum(grad_long * saved[2, r].astype(F32), axis=0, keepdims=True)
            mlp = acc_out[...]
            vectors[2:3, :] += jnp.sum(mlp * mlp * mask, axis=0, keepdims=True)
            whole = resid[...] + mlp
            vectors[0:1, :] += jnp.sum(whole * whole * mask, axis=0, keepdims=True)
            vectors[3:4, :] += jnp.broadcast_to(jnp.sum(mask, axis=0, keepdims=True) * (1.0 / width), (1, width))
            for j in range(wide):
                place_at = pl.ds(r * blocks * wide + j, blocks, stride=wide)
                whole_out[place_at, :] = whole[:, j * 128:(j + 1) * 128]
                mid[place_at, :] = grad_mid[:, j * 128:(j + 1) * 128]
            turned[:, tokens] = normed[...].T
            turned_cot[:, tokens] = cot_low[r].T

        kept = [
            pltpu.make_async_copy(src, dst, keep.at[4 + i])
            for i, (src, dst) in enumerate(((saved, saved_out), (whole_out, out_far), (mid, mid_out)))
        ]
        for copy in kept:
            copy.start()
        side, quarter, part = each // 2, width // 4, hidden // n

        def put_rows(share, half, lanes, value):
            for s in range(n):
                for core in range(2):
                    low = (2 * s + core) * side
                    share[s // 4, (s // 2) % 2, s % 2, core, half, :, lanes] = value[low:low + side]

        for half in range(2):
            for low in range(0, hidden // 2, chunk):
                cols = slice(half * (hidden // 2) + low, half * (hidden // 2) + low + chunk)
                put_rows(up, half, slice(low, low + chunk), dot_nn(turned[...], grad_act[:, cols]).astype(BF16))
        kept.append(pltpu.make_async_copy(up, share_up_out, keep.at[7]))
        kept[-1].start()
        for s in range(n):
            value = dot_nn(turned_cot[...], act[:, s * part:(s + 1) * part]).astype(BF16)
            for core in range(2):
                for half in range(2):
                    low = (2 * core + half) * quarter
                    down[s // 4, (s // 2) % 2, s % 2, core, half] = value[low:low + quarter]
        kept.append(pltpu.make_async_copy(down, share_down_out, keep.at[8]))
        kept[-1].start()
        for half in range(2):
            low = half * (width // 2)
            value = sum(dot_nn(mixed[r], mix_back[r, :, low:low + width // 2]) for r in range(rows)).astype(BF16)
            put_rows(out, half, ALL, value)
        kept.append(pltpu.make_async_copy(out, share_out_out, keep.at[9]))
        kept[-1].start()
        for r in range(rows):
            posts_back[r].arrive()
        kept.append(pltpu.make_async_copy(back_got, back_out, keep.at[10]))
        kept[-1].start()
        for copy in kept:
            copy.wait()

    pl.run_scoped(
        middle,
        pltpu.VMEM((rows * blocks, hidden), BF16),
        pltpu.VMEM((rows * blocks, hidden), BF16),
        pltpu.VMEM((blocks, width), F32),
        pltpu.VMEM((blocks, width), F32),
        pltpu.VMEM((blocks, width), F32),
        pltpu.VMEM((blocks, width), F32),
        pltpu.VMEM((blocks, width), BF16),
        pltpu.VMEM((width, rows * blocks), BF16),
        pltpu.VMEM((width, rows * blocks), BF16),
        pltpu.VMEM((rows, width, blocks), BF16),
        pltpu.VMEM((rows, blocks, width), BF16),
        pltpu.VMEM(share_up_out.shape, BF16),
        pltpu.VMEM(share_down_out.shape, BF16),
        pltpu.VMEM(share_out_out.shape, BF16),
        pltpu.VMEM(x_far.shape, F32),
        pltpu.VMEM(x_far.shape, F32),
    )
    keep_same.wait()
    for post in [post_marks] + posts_gate + posts_long + posts_back:
        post.drain()
    for r in range(rows):
        for h in range(2):
            far_copy(r, h).wait_send()
            side_copy(r, h, near.at[0]).wait_send()
    for xd in range(2):
        target = 4 * y + 2 * c + xd

        @pl.when(target != me)
        def _():
            tap_copy(target).wait_send()

    @pl.when(chosen_chunk)
    def _():
        tap_spread("core").wait_send()

    @pl.when(zh == y)
    def _():
        tap_spread("y").wait_send()


class Tree:
    def __init__(self, order, share, own, parts, gathered, sems):
        self.order = ("core",) + order + ("zl", "zh", "back_y", "back_core")
        self.share, self.own, self.parts, self.gathered, self.sems = share, own, parts, gathered, sems
        self.started = []

    def copies(self, step):
        y, c, zh, zl, x = place()
        axis = self.order[step]
        parts, gathered = self.parts, self.gathered
        own = self.share.at[:, :, :, c] if self.own is None else self.own
        second = self.order[1]
        if axis == "core":
            src, dst = self.share.at[:, :, :, 1 - c], parts[0]
        elif axis == "y":
            src = own.at[:, :, :, 1 - y] if second == "y" else own.at[:, :, x, 1 - y]
            dst = parts[step]
        elif axis == "x":
            src = own.at[:, :, 1 - x] if second == "x" else own.at[:, :, 1 - x, y]
            dst = parts[step]
        elif axis == "zl":
            src, dst = own.at[:, 1 - zl, x, y], parts[3]
        elif axis == "zh":
            src, dst = own.at[1 - zh, zl, x, y], parts[4]
        elif axis == "back_y":
            src = dst = gathered.at[c, y]
        else:
            src = dst = gathered.at[c]
        return exchange(src, dst, self.sems.at[0, step], self.sems.at[1, step], axis.replace("back_", ""))

    def start(self, step):
        self.copies(step).start()
        self.started.append(step)

    def mine(self, a, b, d, e):
        c = place()[1]
        return (self.share, (a, b, d, c, e)) if self.own is None else (self.own, (a, b, d, e))

    def add(self, where, part):
        rows = self.share.shape[-2]
        size = 48 if rows % 48 == 0 else rows
        own, where = self.mine(*where)

        def body(i, carry):
            here = aligned(i, size)
            own[where + (here, ALL)] = own[where + (here, ALL)] + part[0][part[1] + (here, ALL)]
            return carry

        lax.fori_loop(0, rows // size, body, 0)

    def finish(self, step):
        y, c, zh, zl, x = place()
        axis = self.order[step]
        self.copies(step).wait_recv()
        second = self.order[1]
        two = range(2)
        if axis == "core":
            for a in two:
                for b in two:
                    for d in two:
                        for e in two:
                            self.add((a, b, d, e), (self.parts[0], (a, b, d, e)))
        elif axis in ("x", "y"):
            for a in two:
                for b in two:
                    if step == 2:
                        self.add((a, b, x, y), (self.parts[2], (a, b)))
                    else:
                        for d in two:
                            self.add((a, b, d, y) if second == "y" else (a, b, x, d), (self.parts[1], (a, b, d)))
        elif axis == "zl":
            for a in two:
                self.add((a, zl, x, y), (self.parts[3], (a,)))
        elif axis == "zh":
            own, where = self.mine(zh, zl, x, y)
            self.gathered[c, y] = own[where] + self.parts[4][...]
        if step + 1 < len(self.order):
            self.start(step + 1)

    def drain(self):
        for step in self.started:
            self.copies(step).wait_send()


def tree_scratch(r, l):
    shapes = [(2, 2, 2, 2, r, l)] * 2 + [(2, 2, 2, r, l), (2, 2, r, l), (2, r, l), (r, l)]
    return [pltpu.VMEM(shape, BF16) for shape in shapes] + [pltpu.SemaphoreType.DMA((2, 7))]


def back_kernel(
    n,
    back_far, spec_taps_far, spec_gate_far, table_wide, turns, share_up, share_down, share_out, saved_far, turned_far,
    same_far, w_in_far, small, sums_in, x_far, mid_far,
    grad_flat, got_up, got_down, got_out, got_in0, got_in1, got_in2, tap_all, vectors,
    table, gate_sent, gate_got, hand, side_got, land, gate_sems, hand_sems, fetch,
    tap_own, tap_got, tap_half, tap_part, tap_sems, tap_send, tap_recv,
    vector_got, vector_sems,
    *tree_refs,
):
    me = lax.axis_index("seq")
    y, c, zh, zl, xbit = place()
    rows, width, blocks = gate_got.shape
    each, wide = width // n, width // 128
    side = each // 2
    at_end = jnp.logical_and(zh == 1, zl == 1)
    barrier, told = greet(n)
    gain_one = small[10:11, :]
    table[...] = table_wide[...].astype(BF16)

    trees, at = {}, 0
    for name, share, order in (("up", share_up, ("y", "x")), ("down", share_down, ("x", "y")), ("out", share_out, ("y", "x"))):
        got = dict(up=got_up, down=got_down, out=got_out)[name]
        trees[name] = Tree(order, share, tree_refs[at], tree_refs[at + 1:at + 6], got, tree_refs[at + 6])
        at += 7
    for name, order in (("in0", ("y", "x")), ("in1", ("x", "y")), ("in2", ("y", "x"))):
        got = dict(in0=got_in0, in1=got_in1, in2=got_in2)[name]
        trees[name] = Tree(order, None, None, tree_refs[at:at + 5], got, tree_refs[at + 5])
        at += 6
    early = ("up", "down", "out")
    posts_gate = [
        Post(n, lambda p, r=r: gate_sent.at[r, aligned(p, each)], lambda e, r=r: gate_got.at[r, aligned(e, each)], gate_sems.at[r])
        for r in range(rows)
    ]

    def side_copy(r):
        return exchange(hand.at[0, r], side_got.at[r], hand_sems.at[0, 0, r], hand_sems.at[0, 1, r], "x")

    def far_copy(r):
        target = {"seq": lax.rem(me + n - 2, n)}
        return remote(hand.at[1, r], land.at[r], hand_sems.at[1, 0, r], hand_sems.at[1, 1, r], target)

    def tap_core():
        return exchange(tap_own.at[1 - c], tap_got, tap_sems.at[0, 0], tap_sems.at[1, 0], "core")

    def tap_y():
        return exchange(tap_own.at[c, 1 - y], tap_half, tap_sems.at[0, 1], tap_sems.at[1, 1], "y")

    def tap_copy(q, there):
        return remote(tap_part.at[q], tap_all.at[c, there], tap_send.at[q], tap_recv.at[there], {"seq": 4 * y + q})

    def tap_back_y():
        return exchange(tap_all.at[c], tap_all.at[c], tap_sems.at[0, 2], tap_sems.at[1, 2], "y")

    def tap_back_core():
        return exchange(tap_all.at[c], tap_all.at[c], tap_sems.at[0, 3], tap_sems.at[1, 3], "core")

    home = zh == y
    own_halves = [
        pltpu.make_async_copy(trees[name].share.at[:, :, :, c], trees[name].own, fetch.at[i]) for i, name in enumerate(early)
    ]

    def conv_phase(back, spec_taps, spec_gate, fin, spec, spec_sum):
        near = [
            pltpu.make_async_copy(src, dst, fetch.at[3 + i])
            for i, (src, dst) in enumerate(((back_far, back), (spec_taps_far, spec_taps), (spec_gate_far, spec_gate)))
        ]
        for copy in near + own_halves:
            copy.start()
        pl.semaphore_wait(barrier, told)
        for name in early:
            trees[name].start(0)
        for copy in near:
            copy.wait()
        for r in range(rows):
            to_lanes(lambda at, size: back[r, at:at + size], table, spec)

            def work(re, im, at, lane, kept):
                re, im = turn_phases(re, im, turns, lane, -1)
                re, im = fft_points(re, im, -1)
                tap_r, tap_i = load_phases(spec_taps, n, each, at, lane, blocks)
                gate_r, gate_i = kept
                out_r, out_i = [], []
                for k in range(n):
                    here = pl.ds(k * each + at, 8)
                    lanes, other = slice(lane, lane + 128), slice(blocks + lane, blocks + lane + 128)
                    old_r, old_i = gate_r[k], gate_i[k]
                    sum_r, sum_i = old_r * re[k] + old_i * im[k], old_r * im[k] - old_i * re[k]
                    if r == 0:
                        spec_sum[here, lanes] = sum_r
                        spec_sum[here, other] = sum_i
                    else:
                        spec_sum[here, lanes] += sum_r
                        spec_sum[here, other] += sum_i
                    out_r.append(tap_r[k] * re[k] + tap_i[k] * im[k])
                    out_i.append(tap_r[k] * im[k] - tap_i[k] * re[k])
                out_r, out_i = fft_points(out_r, out_i, 1)
                return (turn_phases(out_r, out_i, turns, lane, 1),)

            by_halves(n, each, blocks, spec, work, (fin,), spec_gate.at[r])

            def store(at, value):
                gate_sent[r, at:at + value.shape[0]] = value.astype(BF16)

            from_lanes(fin, table, each, store)
            posts_gate[r].start()
        for i, name in enumerate(early):
            own_halves[i].wait()
            trees[name].finish(0)

        def work_taps(re, im, at, lane, kept):
            re, im = fft_points(re, im, 1)
            return (turn_phases(re, im, turns, lane, 1),)

        by_halves(n, each, blocks, spec_sum, work_taps, (fin,))

        def store_taps(at, value):
            p = at // each
            for half in range(2):
                tap_own[half, p // 4, p % 4] = value[half * side:(half + 1) * side].astype(BF16)

        from_lanes(fin, table, each, store_taps)
        tap_core().start()

    pl.run_scoped(
        conv_phase,
        pltpu.VMEM((rows, width, blocks), BF16),
        pltpu.VMEM((width, 2 * blocks), F32),
        pltpu.VMEM((rows, width, 2 * blocks), BF16),
        pltpu.VMEM((width, 2 * blocks), BF16),
        pltpu.VMEM((width, 2 * blocks), F32),
        pltpu.VMEM((width, 2 * blocks), F32),
    )

    def token_phase(saved, turned, same, w_in, x, gate_back, short, part_proj, grad_norm, share0, share1, share2):
        for k, share in enumerate((share0, share1, share2)):
            trees["in%d" % k].share = share
        near = [
            pltpu.make_async_copy(src, dst, fetch.at[6 + i])
            for i, (src, dst) in enumerate((
                (saved_far, saved), (same_far, same), (w_in_far, w_in), (turned_far, turned),
                (x_far, x), (mid_far, grad_flat),
            ))
        ]
        for copy in near:
            copy.start()
        tap_core().wait_recv()
        for half in range(2):
            for q in range(4):
                tap_own[c, half, q] = tap_own[c, half, q] + tap_got[half, q]
        tap_y().start()
        vectors[...] = jnp.zeros_like(vectors)
        for copy in near[:2]:
            copy.wait()

        def token_row(r):
            tokens = slice(r * blocks, (r + 1) * blocks)
            posts_gate[r].arrive()
            gate_back[...] = gate_got[r].astype(F32).T

            def lanes_step(lanes):
                skip = small[9:10, lanes]

                def rows_step(here):
                    there = pl.ds(pl.multiple_of(r * blocks + here.start, 64), here.size)
                    grad = gate_back[here, lanes] + skip * saved[3, r, here, lanes].astype(F32)
                    short[there, lanes] = saved[4, r, here, lanes]
                    second = pl.ds(pl.multiple_of(lanes.start + width, 128), 128)
                    third = pl.ds(pl.multiple_of(lanes.start + 2 * width, 128), 128)
                    short[there, second] = (grad * saved[1, r, here, lanes].astype(F32)).astype(BF16)
                    short[there, third] = (grad * saved[0, r, here, lanes].astype(F32)).astype(BF16)

                over_rows(blocks, 64, rows_step)

            over_lanes(width, lanes_step)

        def spread(r, j):
            def lanes_step(lanes):
                def rows_step(here):
                    there = pl.ds(pl.multiple_of(r * blocks + here.start, 64), here.size)
                    for k in range(3):
                        cols = pl.ds(pl.multiple_of(lanes.start + k * width, 128), 128)
                        value = short[there, cols].astype(F32) * small[3 * k + j:3 * k + j + 1, lanes]
                        if j > 0:
                            value = value * same[j - 1, r, here, :]
                        part_proj[here, cols] = value.astype(BF16)

                over_rows(blocks, 64, rows_step)

            over_lanes(width, lanes_step)
            return dot_nt(part_proj[...], w_in[...])

        def send_hand(r):
            hand[0, r] = spread(r, 1).astype(BF16)
            side_copy(r).start()
            hand[1, r] = spread(r, 2).astype(BF16)

            @pl.when(xbit == 0)
            def _():
                far_copy(r).start()

        def hand_on(r):
            @pl.when(xbit == 1)
            def _():
                side_copy(r).wait_recv()
                hand[1, r] = (hand[1, r].astype(F32) + side_got[r].astype(F32)).astype(BF16)
                far_copy(r).start()

        def weight_part(k):
            share = trees["in%d" % k].share
            for half in range(2):
                low = k * width + half * (width // 2)
                cols = slice(low, low + width // 2)
                lanes = slice(half * (width // 2), (half + 1) * (width // 2))
                total = None
                for j in range(3):
                    value = dot_nn(turned[j], short[:, cols])
                    vectors[3 * k + j:3 * k + j + 1, lanes] = jnp.sum(value * w_in[:, cols].astype(F32), axis=0, keepdims=True)
                    value = value * small[3 * k + j:3 * k + j + 1, lanes]
                    total = value if total is None else total + value
                total = total.astype(BF16)
                for s in range(n):
                    for core in range(2):
                        block = (2 * s + core) * side
                        share[s // 4, (s // 2) % 2, s % 2, core, half] = total[block:block + side]
            trees["in%d" % k].start(0)

        def last_row(r):
            tokens = slice(r * blocks, (r + 1) * blocks)

            @pl.when(xbit == 0)
            def _():
                side_copy(r).wait_recv()
                grad_norm[r] += side_got[r].astype(F32)

            far_copy(r).wait_recv()
            late = land[r].astype(F32)

            @pl.when(at_end)
            def _():
                grad_norm[r] += turn_rows(late, blocks - 1)

            @pl.when(jnp.logical_not(at_end))
            def _():
                grad_norm[r] += late

            grad = grad_norm[r]
            parts = [strided(x, blocks, r * blocks, j, wide) for j in range(wide)]
            total = sum(jnp.sum(part * part, axis=-1, keepdims=True) for part in parts)
            scale = lax.rsqrt(total * (1.0 / width) + EPS)
            inner = 0.0
            scaled = []
            for j, part in enumerate(parts):
                lanes = slice(j * 128, (j + 1) * 128)
                piece = grad[:, lanes]
                vectors[10:11, lanes] += jnp.sum(piece * part * scale, axis=0, keepdims=True)
                scaled.append(piece * gain_one[:, lanes])
                inner += jnp.sum(scaled[j] * part, axis=-1, keepdims=True)
            shift = inner * (1.0 / width) * (scale * scale * scale)
            for j, part in enumerate(parts):
                place_at = pl.ds(r * blocks * wide + j, blocks, stride=wide)
                grad_flat[place_at, :] += scaled[j] * scale - part * shift

        token_row(0)
        near[2].wait()
        send_hand(0)
        trees["up"].finish(1)
        trees["out"].finish(1)
        token_row(1)
        send_hand(1)
        hand_on(0)
        trees["down"].finish(1)
        tap_y().wait_recv()
        for q in range(4):
            tap_part[q] = tap_own[c, y, q] + tap_half[q]
        for q in range(4):
            @pl.when(4 * y + q != me)
            def _():
                tap_copy(q, me).start()

            @pl.when(4 * y + q == me)
            def _():
                tap_all[c, me] = tap_part[q]

        near[3].wait()
        weight_part(0)
        hand_on(1)
        trees["up"].finish(2)
        trees["out"].finish(2)
        weight_part(1)
        weight_part(2)
        trees["in0"].finish(0)
        trees["in1"].finish(0)
        trees["in2"].finish(0)
        for r in range(rows):
            grad_norm[r] = spread(r, 0)
        trees["up"].finish(3)
        trees["out"].finish(3)
        trees["down"].finish(2)
        for copy in near[4:6]:
            copy.wait()
        last_row(0)
        trees["up"].finish(4)
        trees["out"].finish(4)

        @pl.when(home)
        def _():
            for j in range(1, n):
                peer = lax.rem(me + j, n)
                remote(tap_part.at[0], tap_all.at[c, peer], tap_send.at[0], tap_recv.at[peer], {"seq": peer}).wait_recv()
            tap_back_y().start()

        last_row(1)
        vectors[9:10, :] = sums_in[5:6, :]
        vectors[11:12, :] = sums_in[4:5, :]
        vectors[12:16, :] = sums_in[0:4, :]

        def vector_copy(step):
            axis = ("core", "y", "x", "zl", "zh")[step]
            return exchange(vectors, vector_got.at[step], vector_sems.at[0, step], vector_sems.at[1, step], axis)

        def vector_finish(step):
            vector_copy(step).wait()
            vectors[...] += vector_got[step]
            if step < 4:
                vector_copy(step + 1).start()

        vector_copy(0).start()
        trees["in0"].finish(1)
        trees["in1"].finish(1)
        trees["down"].finish(3)
        trees["up"].finish(5)
        trees["out"].finish(5)
        vector_finish(0)
        trees["in2"].finish(1)

        @pl.when(jnp.logical_not(home))
        def _():
            tap_back_y().wait_recv()

        tap_back_core().start()
        trees["down"].finish(4)
        trees["in0"].finish(2)
        trees["in1"].finish(2)
        vector_finish(1)
        trees["in2"].finish(2)
        trees["down"].finish(5)
        trees["in0"].finish(3)
        trees["in1"].finish(3)
        trees["up"].finish(6)
        trees["out"].finish(6)
        vector_finish(2)
        trees["in2"].finish(3)
        trees["in0"].finish(4)
        trees["in1"].finish(4)
        trees["down"].finish(6)
        vector_finish(3)
        trees["in2"].finish(4)
        trees["in0"].finish(5)
        trees["in1"].finish(5)
        vector_finish(4)
        trees["in2"].finish(5)
        trees["in0"].finish(6)
        trees["in1"].finish(6)
        tap_back_core().wait_recv()
        trees["in2"].finish(6)

        for tree in trees.values():
            tree.drain()
        for post in posts_gate:
            post.drain()
        for r in range(rows):
            side_copy(r).wait_send()
            far_copy(r).wait_send()
        tap_core().wait_send()
        tap_y().wait_send()
        for q in range(4):
            @pl.when(4 * y + q != me)
            def _():
                tap_copy(q, me).wait_send()

        @pl.when(home)
        def _():
            tap_back_y().wait_send()

        tap_back_core().wait_send()

    pl.run_scoped(
        token_phase,
        pltpu.VMEM(saved_far.shape, BF16),
        pltpu.VMEM(turned_far.shape, BF16),
        pltpu.VMEM(same_far.shape, F32),
        pltpu.VMEM(w_in_far.shape, BF16),
        pltpu.VMEM(x_far.shape, F32),
        pltpu.VMEM((blocks, width), F32),
        pltpu.VMEM((rows * blocks, 3 * width), BF16),
        pltpu.VMEM((blocks, 3 * width), BF16),
        pltpu.VMEM((rows, blocks, width), F32),
        *[pltpu.VMEM((2, 2, 2, 2, 2, side, width // 2), BF16)] * 3,
    )


def last_kernel(
    block_in, flat_in, got_up, got_down, got_out, got_in0, got_in1, got_in2, tap_all, taps, vectors,
    out, grad_flat, gain_mix, grad_in, grad_taps, grad_kernel, grad_skip, grad_out, gain_mlp, grad_up, grad_down, rms,
):
    out[...] = block_in[...]
    grad_flat[...] = flat_in[...]
    width = vectors.shape[1]
    side, wide, blocks = got_out.shape[2], width // 128, tap_all.shape[3]
    for got, target, low in (
        (got_up, grad_up, 0), (got_out, grad_out, 0), (got_in0, grad_in, 0), (got_in1, grad_in, width), (got_in2, grad_in, 2 * width),
    ):
        l = got.shape[3]
        for half in range(2):
            for core in range(2):
                target[core * side:(core + 1) * side, low + half * l:low + (half + 1) * l] = got[core, half].astype(F32)
    grad_down[...] = got_down[...].reshape(width, grad_down.shape[0]).astype(F32).T
    value = jnp.concatenate(
        [tap_all[core, s] for s in range(tap_all.shape[1]) for core in range(2)], axis=0
    ).astype(F32).T
    for j in range(wide):
        place_at = pl.ds(j, blocks, stride=wide)
        tanh = jnp.tanh(taps[place_at, :] * (1.0 / THRESH))
        grad_kernel[place_at, :] = value[:, j * 128:(j + 1) * 128] * (tanh * tanh)
    for k in range(3):
        grad_taps[:, k * width:(k + 1) * width] = vectors[3 * k:3 * k + 3, :]
    for target, row in ((grad_skip, 9), (gain_mix, 10), (gain_mlp, 11)):
        target[...] = vectors[row, :]
    total = jnp.sum(vectors[12:16, :], axis=1, keepdims=True)
    found = jnp.sqrt(total / (jnp.maximum(total[3:4, :], 1.0) * width))
    for i in range(3):
        rms[i] = found[i, 0]


def call(body, outs, scratch, inputs, collective_id, far=(), far_outs=()):
    return pl.pallas_call(
        body,
        out_shape=tuple(jax.ShapeDtypeStruct(*out) for out in outs),
        in_specs=[pl.BlockSpec(memory_space=pl.ANY if i in far else pltpu.VMEM) for i in range(len(inputs))],
        out_specs=tuple(pl.BlockSpec(memory_space=pl.ANY if i in far_outs else pltpu.VMEM) for i in range(len(outs))),
        scratch_shapes=scratch,
        compiler_params=pltpu.CompilerParams(
            vmem_limit_bytes=VMEM_BYTES, collective_id=collective_id, has_side_effects=True
        ),
    )(*inputs)


def local(
    block_in, segment_ids, valid_mask, cotangent, gain_mix, in_proj, short_taps, long_kernel,
    skip_gain, out_proj, gain_mlp, up_proj, down_proj,
):
    rows, blocks, _, width = block_in.shape
    hidden = up_proj.shape[1]
    n = lax.axis_size("seq")
    each = width // n
    tokens = rows * blocks
    side, wide = each // 2, width // 128
    chunk = 512
    x = block_in.reshape(tokens * wide, 128)
    cot = cotangent.reshape(tokens * wide, 128)
    raw = long_kernel.reshape(blocks * wide, 128)
    segments = segment_ids.reshape(rows, 1, blocks)
    valid = valid_mask.reshape(rows, 1, blocks)
    table, turns = spectrum_tables(blocks, n)
    dma = pltpu.SemaphoreType.DMA
    bits = (2, 2, 2, 2, 2)
    up_shape = bits + (side, hidden // 2)
    down_shape = bits + (width // 4, hidden // n)
    out_shape = bits + (side, width // 2)
    low = lambda *shape: pltpu.VMEM(shape, BF16)
    full = lambda *shape: pltpu.VMEM(shape, F32)

    (block_out, mid, turned, saved, same, spec_taps, spec_gate, back, share_up, share_down, share_out, sums, small) = call(
        functools.partial(front_kernel, n, chunk),
        [
            (x.shape, F32),
            (x.shape, F32),
            ((3, width, tokens), BF16),
            ((5, rows, blocks, width), BF16),
            ((2, rows, blocks, 128), F32),
            ((width, 2 * blocks), F32),
            ((rows, width, 2 * blocks), BF16),
            ((rows, width, blocks), BF16),
            (up_shape, BF16),
            (down_shape, BF16),
            (out_shape, BF16),
            ((8, width), F32),
            ((16, width), F32),
        ],
        [
            full(8, blocks), full(n, 8, blocks), full(tokens, width), full(tokens, width), low(rows, blocks, width),
            low(3, rows, blocks, width), low(2, rows, blocks, width), low(width, blocks), low(width, blocks),
            low(*table.shape), full(rows, blocks, width), low(5, rows, blocks, width), full(3, rows, blocks, 128),
            low(rows, width, blocks), low(rows, width, blocks), low(rows, width, blocks), low(rows, width, blocks),
            low(rows, width, blocks), low(rows, width, blocks),
            low(width, width), low(width, hidden), low(hidden, width),
            dma((7,)), dma((11,)), dma((2, 2, rows, 2)), dma((2, n)), dma((4, n)),
            dma((rows, 2, n)), dma((rows, 2, n)), dma((rows, 2, n)),
        ],
        (x, cot, raw, short_taps, skip_gain, gain_mix, gain_mlp, segments, valid, in_proj, out_proj, up_proj, down_proj, table, turns),
        1,
        far=(0, 1, 2, 9, 10, 11, 12),
        far_outs=range(11),
    )

    trees = []
    for shape in (up_shape, down_shape, out_shape):
        trees += tree_scratch(*shape[5:])
    for _ in range(3):
        trees += tree_scratch(*out_shape[5:])[1:]
    quarter = (4, side, blocks)
    up_got, down_got, out_got = [(2, 2) + shape[5:] for shape in (up_shape, down_shape, out_shape)]
    grad_flat, *gathered, taps_back, vectors = call(
        functools.partial(back_kernel, n),
        [
            (x.shape, F32),
            (up_got, BF16), (down_got, BF16), (out_got, BF16), (out_got, BF16), (out_got, BF16), (out_got, BF16),
            ((2, n, side, blocks), BF16),
            ((16, width), F32),
        ],
        [
            low(*table.shape), low(rows, width, blocks), low(rows, width, blocks),
            low(2, rows, blocks, width), low(rows, blocks, width), low(rows, blocks, width),
            dma((rows, 2, n)), dma((2, 2, rows)), dma((13,)),
            low(2, 2, *quarter), low(2, *quarter), low(*quarter), low(*quarter),
            dma((2, 4)), dma((4,)), dma((n,)),
            full(5, 16, width), dma((2, 5)),
        ] + trees,
        (
            back, spec_taps, spec_gate, table, turns, share_up, share_down, share_out, saved, turned,
            same, in_proj, small, sums, x, mid,
        ),
        2,
        far=(0, 1, 2, 5, 6, 7, 8, 9, 10, 11, 14, 15),
    )

    inputs = (block_out, grad_flat, *gathered, taps_back, raw, vectors)
    near = pl.BlockSpec(memory_space=pltpu.VMEM)
    outs = [
        x.shape, x.shape, (width,), (each, 3 * width), (3, 3 * width), raw.shape, (width,), (each, width), (width,),
        (each, hidden), (hidden // n, width), (3,),
    ]
    results = pl.pallas_call(
        last_kernel,
        out_shape=tuple(jax.ShapeDtypeStruct(shape, F32) for shape in outs),
        in_specs=[near] * len(inputs),
        out_specs=(near,) * 11 + (pl.BlockSpec(memory_space=pltpu.SMEM),),
        compiler_params=pltpu.CompilerParams(vmem_limit_bytes=VMEM_BYTES),
    )(*inputs)
    shapes = {0: block_in.shape, 1: block_in.shape, 5: long_kernel.shape}
    return tuple(value.reshape(shapes.get(i, value.shape)) for i, value in enumerate(results))


def chosen(block_in, *rest):
    rows, blocks, _, width = block_in.shape
    n = lax.axis_size("seq")
    fits = blocks % (32 * n) == 0 and width % (32 * n) == 0 and n == 8 and rows == 2 and lax.axis_size("rows") == 4
    return (local if fits else general_local)(block_in, *rest)


def solution(mesh):
    return jax.shard_map(
        chosen,
        mesh=mesh,
        in_specs=(
            P("rows", None, "seq", None),
            P("rows", None, "seq"),
            P("rows", None, "seq"),
            P("rows", None, "seq", None),
            P(),
            P(),
            P(),
            P(None, "seq", None),
            P(),
            P(),
            P(),
            P(),
            P(),
        ),
        out_specs=(
            P("rows", None, "seq", None),
            P("rows", None, "seq", None),
            P(),
            P("seq", None),
            P(),
            P(None, "seq", None),
            P(),
            P("seq", None),
            P(),
            P("seq", None),
            P("seq", None),
            P(),
        ),
        check_vma=False,
    )
```

```python
import functools
import itertools
import math

import jax
import jax.numpy as jnp
import numpy as np
from jax import lax
from jax.experimental import pallas as pl
from jax.experimental.pallas import tpu as pltpu
from jax.sharding import PartitionSpec as P

EPS = 1e-05
THRESH = 0.003
HIGH = lax.Precision.HIGHEST


def shortened(x):

    def short(part):
        return part.astype(jnp.bfloat16) if part.dtype == jnp.float32 else part

    return jax.tree.map(short, x)


def passed_along(block, axis, distance):
    devices = range(lax.axis_size(axis))
    route = [((i - distance) % len(devices), i) for i in devices]
    return lax.ppermute(block, axis, route)


def norm_scale(value, gain):
    return value * lax.rsqrt(jnp.mean(value * value, axis=-1, keepdims=True) + EPS) * gain


def angle_tables(left_count, right_count, period):
    left_idx = jnp.arange(left_count, dtype=jnp.int32)[:, None]
    right_idx = jnp.arange(right_count, dtype=jnp.int32)[None, :]
    phase = (left_idx * right_idx % period).astype(jnp.float32) * (2.0 * math.pi / period)
    return (jnp.cos(phase), jnp.sin(phase))


def twiddle_tables(shard_index, spec_len, whole_len):
    turned = shard_index * jnp.arange(spec_len, dtype=jnp.int32) % whole_len
    phase = turned.astype(jnp.float32) * (2.0 * math.pi / whole_len)
    return (jnp.cos(phase)[None, :, None], jnp.sin(phase)[None, :, None])


def local_forward(signal, shard_index, whole_len):
    blocks = signal.shape[1]
    cos_table, sin_table = angle_tables(blocks, 2 * blocks, 2 * blocks)
    real_part = jnp.einsum("rjd,jk->rkd", signal, cos_table, precision=HIGH)
    imag_part = -jnp.einsum("rjd,jk->rkd", signal, sin_table, precision=HIGH)
    cos_twid, sin_twid = twiddle_tables(shard_index, 2 * blocks, whole_len)
    out_real = real_part * cos_twid + imag_part * sin_twid
    out_imag = imag_part * cos_twid - real_part * sin_twid
    return (out_real[:, :, None, :], out_imag[:, :, None, :])


def cross_section(real_part, imag_part, direction):
    count = real_part.shape[2]
    cos_table, sin_table = angle_tables(count, count, count)
    re_cos = jnp.einsum("rcpd,pm->rcmd", real_part, cos_table, precision=HIGH)
    re_sin = jnp.einsum("rcpd,pm->rcmd", real_part, sin_table, precision=HIGH)
    im_cos = jnp.einsum("rcpd,pm->rcmd", imag_part, cos_table, precision=HIGH)
    im_sin = jnp.einsum("rcpd,pm->rcmd", imag_part, sin_table, precision=HIGH)
    return (re_cos - direction * im_sin, im_cos + direction * re_sin)


def local_inverse(real_part, imag_part, shard_index, whole_len):
    real_part = real_part[:, :, 0, :]
    imag_part = imag_part[:, :, 0, :]
    spec_len = real_part.shape[1]
    cos_twid, sin_twid = twiddle_tables(shard_index, spec_len, whole_len)
    turned_re = real_part * cos_twid - imag_part * sin_twid
    turned_im = imag_part * cos_twid + real_part * sin_twid
    cos_table, sin_table = angle_tables(spec_len, spec_len // 2, spec_len)
    result = jnp.einsum("rkd,kj->rjd", turned_re, cos_table, precision=HIGH)
    result = result - jnp.einsum("rkd,kj->rjd", turned_im, sin_table, precision=HIGH)
    return result / whole_len


def earlier(members, at_start):
    received = jax.tree.map(
        lambda part, own: part.astype(own.dtype),
        passed_along(shortened(members), "seq", 1),
        members,
    )
    placed = []
    for member in received:
        rolled = jnp.concatenate([jnp.zeros_like(member[:, :1]), member[:, :-1]], axis=1)
        placed.append(jnp.where(at_start, rolled, member))
    return tuple(placed)


def later(member, at_end):
    received = passed_along(member.astype(jnp.bfloat16), "seq", -1).astype(member.dtype)
    rolled = jnp.concatenate([received[:, 1:], jnp.zeros_like(received[:, :1])], axis=1)
    return jnp.where(at_end, rolled, received)


def times_trans(left, right):
    return lax.dot_general(
        left, right, (((1,), (1,)), ((), ())), preferred_element_type=jnp.float32
    )


def trans_times(left, right):
    return lax.dot_general(
        left, right, (((0,), (0,)), ((), ())), preferred_element_type=jnp.float32
    )


def general_local(
    block_in,
    segment_ids,
    valid_mask,
    cotangent,
    gain_mix,
    in_proj,
    short_taps,
    long_kernel,
    skip_gain,
    out_proj,
    gain_mlp,
    up_proj,
    down_proj,
):
    batch_rows = block_in.shape[0]
    blocks = block_in.shape[1]
    width = block_in.shape[3]
    shard_count = lax.axis_size("seq")
    shard_index = lax.axis_index("seq")
    whole_len = 2 * blocks * shard_count
    tokens = batch_rows * blocks
    at_start = shard_index == 0
    at_end = shard_index == shard_count - 1
    flat_in = block_in.reshape(tokens, width)
    mask_rows = valid_mask[:, :, 0].astype(jnp.float32)[:, :, None]
    normed_one = norm_scale(flat_in, gain_mix).astype(jnp.bfloat16)
    proj_low = jnp.dot(normed_one, in_proj, preferred_element_type=jnp.float32).astype(jnp.bfloat16)
    proj_low = proj_low.reshape(batch_rows, blocks, 3 * width)
    seg_low = segment_ids[:, :, 0].astype(jnp.bfloat16)[:, :, None]
    prev_one = earlier((proj_low, seg_low), at_start)
    prev_two = earlier(prev_one, at_start)
    same_one = (prev_one[1] == seg_low).astype(jnp.float32)
    same_two = (prev_two[1] == seg_low).astype(jnp.float32)
    proj_now = proj_low.astype(jnp.float32)
    proj_one = prev_one[0].astype(jnp.float32)
    proj_two = prev_two[0].astype(jnp.float32)
    conv_short = (
        short_taps[0] * proj_now
        + short_taps[1] * proj_one * same_one
        + short_taps[2] * proj_two * same_two
    )
    query = conv_short[:, :, :width]
    keys = conv_short[:, :, width : 2 * width]
    values = conv_short[:, :, 2 * width :]
    gated = keys * values * mask_rows
    raw_taps = long_kernel[:, 0, :]
    taps_eff = raw_taps - THRESH * jnp.tanh(raw_taps / THRESH)
    kern_re, kern_im = local_forward(taps_eff[None], shard_index, whole_len)
    kern_re, kern_im = (
        lax.all_to_all(
            kern_re.astype(jnp.bfloat16), "seq", split_axis=1, concat_axis=2, tiled=True
        ).astype(kern_re.dtype),
        lax.all_to_all(
            kern_im.astype(jnp.bfloat16), "seq", split_axis=1, concat_axis=2, tiled=True
        ).astype(kern_im.dtype),
    )
    kern_re, kern_im = cross_section(kern_re, kern_im, -1.0)
    gate_re, gate_im = local_forward(gated, shard_index, whole_len)
    gate_re, gate_im = (
        lax.all_to_all(
            gate_re.astype(jnp.bfloat16), "seq", split_axis=1, concat_axis=2, tiled=True
        ).astype(gate_re.dtype),
        lax.all_to_all(
            gate_im.astype(jnp.bfloat16), "seq", split_axis=1, concat_axis=2, tiled=True
        ).astype(gate_im.dtype),
    )
    gate_re, gate_im = cross_section(gate_re, gate_im, -1.0)
    prod_re = gate_re * kern_re - gate_im * kern_im
    prod_im = gate_re * kern_im + gate_im * kern_re
    prod_re, prod_im = cross_section(prod_re, prod_im, 1.0)
    prod_re, prod_im = (
        lax.all_to_all(
            prod_re.astype(jnp.bfloat16), "seq", split_axis=2, concat_axis=1, tiled=True
        ).astype(prod_re.dtype),
        lax.all_to_all(
            prod_im.astype(jnp.bfloat16), "seq", split_axis=2, concat_axis=1, tiled=True
        ).astype(prod_im.dtype),
    )
    long_out = local_inverse(prod_re, prod_im, shard_index, whole_len) + skip_gain * gated
    mixer_low = (query * long_out).reshape(tokens, width).astype(jnp.bfloat16)
    mixer_out = jnp.dot(mixer_low, out_proj, preferred_element_type=jnp.float32)
    resid_mid = flat_in + mixer_out
    normed_two = norm_scale(resid_mid, gain_mlp).astype(jnp.bfloat16)
    up_val = jnp.dot(normed_two, up_proj, preferred_element_type=jnp.float32)
    act_low = jax.nn.gelu(up_val).astype(jnp.bfloat16)
    mlp_out = jnp.dot(act_low, down_proj, preferred_element_type=jnp.float32)
    flat_out = resid_mid + mlp_out
    grad_out = cotangent.reshape(tokens, width)
    grad_mlp = grad_out.astype(jnp.bfloat16)
    grad_down = trans_times(act_low, grad_mlp)
    grad_act = times_trans(grad_mlp, down_proj)
    unused_val, gelu_back = jax.vjp(jax.nn.gelu, up_val)
    grad_upval = gelu_back(grad_act)[0].astype(jnp.bfloat16)
    grad_up = trans_times(normed_two, grad_upval)
    grad_norm_two = times_trans(grad_upval, up_proj)
    unused_two, norm_back_two = jax.vjp(norm_scale, resid_mid, gain_mlp)
    grad_resid, grad_gain_two = norm_back_two(grad_norm_two)
    grad_mid = grad_out + grad_resid
    grad_mix = grad_mid.astype(jnp.bfloat16)
    grad_outp = trans_times(mixer_low, grad_mix)
    grad_prod = times_trans(grad_mix, out_proj).reshape(batch_rows, blocks, width)
    grad_query = grad_prod * long_out
    grad_long = grad_prod * query
    back_re, back_im = local_forward(grad_long, shard_index, whole_len)
    back_re, back_im = (
        lax.all_to_all(
            back_re.astype(jnp.bfloat16), "seq", split_axis=1, concat_axis=2, tiled=True
        ).astype(back_re.dtype),
        lax.all_to_all(
            back_im.astype(jnp.bfloat16), "seq", split_axis=1, concat_axis=2, tiled=True
        ).astype(back_im.dtype),
    )
    back_re, back_im = cross_section(back_re, back_im, -1.0)
    sig_re = kern_re * back_re + kern_im * back_im
    sig_im = kern_re * back_im - kern_im * back_re
    tap_re = jnp.sum(gate_re * back_re + gate_im * back_im, axis=0, keepdims=True)
    tap_im = jnp.sum(gate_re * back_im - gate_im * back_re, axis=0, keepdims=True)
    sig_re, sig_im = cross_section(sig_re, sig_im, 1.0)
    tap_re, tap_im = cross_section(tap_re, tap_im, 1.0)
    sig_re, sig_im, tap_re, tap_im = (
        lax.all_to_all(
            sig_re.astype(jnp.bfloat16), "seq", split_axis=2, concat_axis=1, tiled=True
        ).astype(sig_re.dtype),
        lax.all_to_all(
            sig_im.astype(jnp.bfloat16), "seq", split_axis=2, concat_axis=1, tiled=True
        ).astype(sig_im.dtype),
        lax.all_to_all(
            tap_re.astype(jnp.bfloat16), "seq", split_axis=2, concat_axis=1, tiled=True
        ).astype(tap_re.dtype),
        lax.all_to_all(
            tap_im.astype(jnp.bfloat16), "seq", split_axis=2, concat_axis=1, tiled=True
        ).astype(tap_im.dtype),
    )
    grad_gated = local_inverse(sig_re, sig_im, shard_index, whole_len) + skip_gain * grad_long
    grad_taps_eff = local_inverse(tap_re, tap_im, shard_index, whole_len)[0]
    tanh_val = jnp.tanh(raw_taps / THRESH)
    grad_kernel = (grad_taps_eff * tanh_val * tanh_val)[:, None, :]
    grad_kernel = lax.psum(grad_kernel.astype(jnp.bfloat16), "rows").astype(jnp.float32)
    grad_skip = jnp.sum(grad_long * gated, axis=(0, 1))
    grad_short = jnp.concatenate(
        [grad_query, grad_gated * values * mask_rows, grad_gated * keys * mask_rows], axis=2
    )
    grad_tap_rows = jnp.stack(
        [
            jnp.sum(grad_short * proj_now, axis=(0, 1)),
            jnp.sum(grad_short * proj_one * same_one, axis=(0, 1)),
            jnp.sum(grad_short * proj_two * same_two, axis=(0, 1)),
        ]
    )
    inner_term = short_taps[1] * grad_short * same_one + later(
        short_taps[2] * grad_short * same_two, at_end
    )
    grad_proj = short_taps[0] * grad_short + later(inner_term, at_end)
    grad_proj = grad_proj.reshape(tokens, 3 * width).astype(jnp.bfloat16)
    grad_inp = trans_times(normed_one, grad_proj)
    grad_norm_one = times_trans(grad_proj, in_proj)
    unused_one, norm_back_one = jax.vjp(norm_scale, flat_in, gain_mix)
    grad_first, grad_gain_one = norm_back_one(grad_norm_one)
    grad_flat = grad_mid + grad_first
    mask_flat = mask_rows.reshape(tokens, 1)
    stat_sums = jnp.stack(
        [
            jnp.sum(mask_flat * flat_out * flat_out),
            jnp.sum(mask_flat * mixer_out * mixer_out),
            jnp.sum(mask_flat * mlp_out * mlp_out),
            jnp.sum(mask_flat),
        ]
    )
    grad_gain_one, grad_gain_two, grad_tap_rows, grad_skip, stat_sums = lax.psum(
        (grad_gain_one, grad_gain_two, grad_tap_rows, grad_skip, stat_sums), ("rows", "seq")
    )
    rms_stats = jnp.sqrt(stat_sums[:3] / (jnp.maximum(stat_sums[3], 1.0) * width))
    shares = (
        lax.psum_scatter(grad_inp, "seq", scatter_dimension=0, tiled=True),
        lax.psum_scatter(grad_outp, "seq", scatter_dimension=0, tiled=True),
        lax.psum_scatter(grad_up, "seq", scatter_dimension=0, tiled=True),
        lax.psum_scatter(grad_down, "seq", scatter_dimension=0, tiled=True),
    )
    grad_inp, grad_outp, grad_up, grad_down = (
        lax.psum(shares[0].astype(jnp.bfloat16), "rows").astype(jnp.float32),
        lax.psum(shares[1].astype(jnp.bfloat16), "rows").astype(jnp.float32),
        lax.psum(shares[2].astype(jnp.bfloat16), "rows").astype(jnp.float32),
        lax.psum(shares[3].astype(jnp.bfloat16), "rows").astype(jnp.float32),
    )
    return (
        flat_out.reshape(block_in.shape),
        grad_flat.reshape(block_in.shape),
        grad_gain_one,
        grad_inp,
        grad_tap_rows,
        grad_kernel,
        grad_skip,
        grad_outp,
        grad_gain_two,
        grad_up,
        grad_down,
        rms_stats,
    )


MESH = pl.DeviceIdType.MESH
F32 = jnp.float32
BF16 = jnp.bfloat16
VMEM_BYTES = 62 * 1024 * 1024
C0 = math.sqrt(2.0 / math.pi)
C1 = 0.044715
ALL = slice(None)
YX, XY = ("y", "x", "zl", "zh"), ("x", "y", "zl", "zh")
ZY = ("zl", "y", "x", "zh")
ORDERS = (YX, XY, YX, ZY, YX, YX, YX, ZY)


def dot_nn(a, b):
    return lax.dot_general(a, b, (((1,), (0,)), ((), ())), preferred_element_type=F32)


def dot_nt(a, b):
    return lax.dot_general(a, b, (((1,), (1,)), ((), ())), preferred_element_type=F32)


def fft_points(re, im, sign):
    n = len(re)
    if n == 1:
        return re, im
    even_r, even_i = fft_points(re[0::2], im[0::2], sign)
    odd_r, odd_i = fft_points(re[1::2], im[1::2], sign)
    out_r, out_i = [None] * n, [None] * n
    for k in range(n // 2):
        if k == 0:
            turn_r, turn_i = odd_r[0], odd_i[0]
        elif 4 * k == n:
            if sign > 0:
                out_r[k], out_i[k] = even_r[k] - odd_i[k], even_i[k] + odd_r[k]
                out_r[k + n // 2], out_i[k + n // 2] = even_r[k] + odd_i[k], even_i[k] - odd_r[k]
            else:
                out_r[k], out_i[k] = even_r[k] + odd_i[k], even_i[k] - odd_r[k]
                out_r[k + n // 2], out_i[k + n // 2] = even_r[k] - odd_i[k], even_i[k] + odd_r[k]
            continue
        else:
            cos, sin = math.cos(2 * math.pi * k / n), sign * math.sin(2 * math.pi * k / n)
            turn_r = cos * odd_r[k] - sin * odd_i[k]
            turn_i = cos * odd_i[k] + sin * odd_r[k]
        out_r[k], out_i[k] = even_r[k] + turn_r, even_i[k] + turn_i
        out_r[k + n // 2], out_i[k + n // 2] = even_r[k] - turn_r, even_i[k] - turn_i
    return out_r, out_i


def spectrum_tables(blocks, phases):
    length = blocks * phases
    k = 2 * np.arange(blocks)[None, :] + 1
    angle = 2.0 * np.pi * np.arange(blocks)[:, None] * k / (4.0 * blocks)
    table = np.concatenate([np.cos(angle), -np.sin(angle)], axis=1)
    turn = 2.0 * np.pi * np.arange(phases)[:, None] * k / (4.0 * length)
    turns = np.stack([np.cos(turn), np.sin(turn)], axis=1)[:, :, None, :]
    return jnp.asarray(table, F32), jnp.asarray(np.broadcast_to(turns, (phases, 2, 8, blocks)), F32)


def place():
    row, seq = lax.axis_index("rows"), lax.axis_index("seq")
    return lax.div(row, 2), lax.rem(row, 2), lax.div(seq, 4), lax.rem(lax.div(seq, 2), 2), lax.rem(seq, 2)


def partner(axis):
    y, c, zh, zl, x = place()
    if axis == "core":
        return {"rows": 2 * y + 1 - c}
    if axis == "y":
        return {"rows": 2 * (1 - y) + c}
    if axis == "x":
        return {"seq": 4 * zh + 2 * zl + 1 - x}
    if axis == "zl":
        return {"seq": 4 * zh + 2 * (1 - zl) + x}
    return {"seq": 4 * (1 - zh) + 2 * zl + x}


def remote(src, dst, send_sem, recv_sem, target):
    return pltpu.make_async_remote_copy(
        src_ref=src, dst_ref=dst, send_sem=send_sem, recv_sem=recv_sem, device_id=target, device_id_type=MESH,
    )


def exchange(src, dst, send_sem, recv_sem, axis):
    return remote(src, dst, send_sem, recv_sem, partner(axis))


def greet(n):
    me = lax.axis_index("seq")
    barrier = pltpu.get_barrier_semaphore()
    for j in range(1, n):
        pl.semaphore_signal(barrier, inc=1, device_id={"seq": lax.rem(me + j, n)}, device_id_type=MESH)
    for axis in ("core", "y"):
        pl.semaphore_signal(barrier, inc=1, device_id=partner(axis), device_id_type=MESH)
    return barrier, n + 1


def aligned(index, size):
    return pl.ds(pl.multiple_of(index * size, size), size)


class Post:
    def __init__(self, n, source, target, sems):
        self.n, self.source, self.target, self.sems = n, source, target, sems

    def copies(self, sender):
        me = lax.axis_index("seq")
        for j in range(1, self.n):
            peer = lax.rem(me + j, self.n)
            come = sender(peer, me)
            yield remote(
                self.source(peer), self.target(come), self.sems.at[0, j], self.sems.at[1, come], {"seq": peer}
            )

    def start(self):
        me = lax.axis_index("seq")
        for copy in self.copies(lambda peer, me: me):
            copy.start()
        self.target(me)[...] = self.source(me)[...]

    def arrive(self):
        for copy in self.copies(lambda peer, me: peer):
            copy.wait_recv()

    def drain(self):
        for copy in self.copies(lambda peer, me: me):
            copy.wait_send()


def over_groups(each, blocks, body):
    for lane in range(0, blocks, 128):
        def step(g, carry):
            body(pl.multiple_of(g * 16, 16), lane)
            return carry
        lax.fori_loop(0, each // 16, step, 0)


def matmul_rows(out, left, right, size=256):
    for at in range(0, out.shape[0], size):
        out[at:at + size, :] = left(at, size, right)


def load_phases(spec, n, each, at, lane, half):
    re = [spec[pl.ds(p * each + at, 8), lane:lane + 128] for p in range(n)]
    im = [spec[pl.ds(p * each + at, 8), half + lane:half + lane + 128] for p in range(n)]
    return re, im


def turn_phases(re, im, turns, lane, sign):
    out_r, out_i = [re[0]], [im[0]]
    for p in range(1, len(re)):
        cos, sin = turns[p, 0, :, lane:lane + 128], turns[p, 1, :, lane:lane + 128]
        if sign > 0:
            out_r.append(re[p] * cos - im[p] * sin)
            out_i.append(im[p] * cos + re[p] * sin)
        else:
            out_r.append(re[p] * cos + im[p] * sin)
            out_i.append(im[p] * cos - re[p] * sin)
    return out_r, out_i


def by_halves(n, each, blocks, spec, work, stores, kept=None):
    def group(at, lane):
        halves = []
        if kept is not None:
            loaded = [
                [kept[pl.ds(k * each + at, 16), part + lane:part + lane + 128].astype(F32) for k in range(n)]
                for part in (0, blocks)
            ]
        for half in (0, 8):
            re, im = load_phases(spec, n, each, at + half, lane, blocks)
            old = None if kept is None else [[value[half:half + 8] for value in part] for part in loaded]
            halves.append(work(re, im, at + half, lane, old))
        for target, first, second in zip(stores, *halves):
            for k in range(n):
                for part in range(2):
                    value = jnp.concatenate([first[part][k], second[part][k]], axis=0).astype(BF16)
                    target[pl.ds(k * each + at, 16), part * blocks + lane:part * blocks + lane + 128] = value

    over_groups(each, blocks, group)


def to_lanes(source, table, spec):
    for at in range(0, spec.shape[0], 256):
        spec[at:at + 256, :] = dot_nn(source(at, 256), table[...])


def from_lanes(fin, table, size, store):
    for at in range(0, fin.shape[0], size):
        store(at, dot_nt(fin[at:at + size, :], table[...]) * (2.0 / fin.shape[1] / (fin.shape[0] // size)))


def over_rows(total, size, body):
    def step(i, carry):
        body(aligned(i, size))
        return carry
    lax.fori_loop(0, total // size, step, 0)


def over_lanes(width, body):
    def step(i, carry):
        body(aligned(i, 128))
        return carry
    lax.fori_loop(0, width // 128, step, 0)


def strided(ref, rows, start, lane, wide):
    return ref[pl.ds(start * wide + lane, rows, stride=wide), :]


def turn_rows(value, amount):
    return pltpu.roll(value, amount % value.shape[0], 0)


class Tree:
    def __init__(self, order, share, own, parts, gathered, sems):
        self.order = order + ("back_y", "back_core")
        self.share, self.own, self.parts, self.gathered, self.sems = share, own, parts, gathered, sems
        self.done = 0
        self.started = []

    def half(self, step, bit):
        y, c, zh, zl, x = place()
        here = dict(zh=zh, zl=zl, x=x, y=y)
        settled = self.order[:step]
        return tuple(here[a] if a in settled else (bit(here[a]) if a == self.order[step] else ALL) for a in ("zh", "zl", "x", "y"))

    def block(self, index):
        c = place()[1]
        return (self.share, index[:3] + (c,) + index[3:]) if self.own is None else (self.own, index)

    def copies(self, step):
        y, c, zh, zl, x = place()
        axis = self.order[step]
        gathered = self.gathered
        if axis == "core":
            src = self.share.at[:, :, :, 1 - c]
        elif axis == "back_y":
            src = gathered.at[c, y]
        elif axis == "back_core":
            src = gathered.at[c]
        else:
            ref, index = self.block(self.half(step, lambda bit: 1 - bit))
            src = ref.at[index]
        dst = src if axis.startswith("back") else self.parts[step]
        return exchange(src, dst, self.sems.at[0, step], self.sems.at[1, step], axis.replace("back_", ""))

    def start(self):
        self.copies(self.done).start()
        self.started.append(self.done)

    def add(self, index, part, at, target=None):
        own, index = self.block(index)
        size = 48

        def body(i, carry):
            here = aligned(i, size)
            value = own[index + (here, ALL)] + part[at + (here, ALL)]
            if target is None:
                own[index + (here, ALL)] = value
            else:
                target[here, :] = value
            return carry

        lax.fori_loop(0, part.shape[-2] // size, body, 0)

    def finish(self, go=True):
        y, c, zh, zl, x = place()
        step = self.done
        axis = self.order[step]
        self.copies(step).wait_recv()
        if not axis.startswith("back"):
            index = (ALL,) * 4 if axis == "core" else self.half(step, lambda bit: bit)
            free = [i for i, entry in enumerate(index) if entry is ALL or isinstance(entry, slice)]
            last = self.order[step + 1] == "back_y"
            for bits in itertools.product(range(2), repeat=len(free)):
                full = list(index)
                for i, bit in zip(free, bits):
                    full[i] = bit
                self.add(tuple(full), self.parts[step], bits, self.gathered.at[c, y] if last else None)
        self.done += 1
        if go and self.done < len(self.order):
            self.start()

    def drain(self):
        for step in self.started:
            self.copies(step).wait_send()


def tree_scratch(r, l):
    shapes = [(2, 2, 2, 2, r, l), (2, 2, 2, r, l), (2, 2, r, l), (2, r, l), (r, l)]
    return [pltpu.VMEM(shape, BF16) for shape in shapes] + [pltpu.SemaphoreType.DMA((2, 7))]


def whole_kernel(
    n, chunk,
    x_far, cot_far, taps_far, short_taps, skip, gain_mix, gain_mlp, segments, valid, w_in_far, w_out_far, w_up_far, w_down_far,
    table_wide, turns,
    out_far, flat_far, mid_far, turned_far, spec_taps_far, spec_gate_far,
    got_ua, got_ub, got_da, got_db, got_out, got_in0, got_in1, got_in2, tap_all, vectors,
    small, table, marks, marks_got, land, taps_got, query, saved, same, sent_one, sent_two, got_one, got_two, hand,
    tap_own, tap_got, tap_half, tap_part, vector_got,
    fetch, keep, near_sems, mark_sems, tap_sems, gate_sems, long_sems, back_sems, gated_sems, hand_sems,
    pair_sems, home_sems, home_send, home_recv, vector_sems,
    *tree_refs,
):
    me = lax.axis_index("seq")
    y, c, zh, zl, xbit = place()
    rows, blocks = query.shape[0], query.shape[1]
    width, hidden = w_up_far.shape
    each, wide, step = width // n, width // 128, blocks // 2
    side, linear = each // 2, blocks * wide
    at_top = jnp.logical_and(zh == 0, zl == 0)
    at_end = jnp.logical_and(zh == 1, zl == 1)
    chosen_chunk = jnp.logical_and(zh == y, zl == c)
    home = zh == y
    barrier, told = greet(n)
    for row, vector in ((9, skip), (10, gain_mix), (11, gain_mlp)):
        small[row, :] = vector[...]
    gain_one, gain_two = small[10:11, :], small[11:12, :]
    table[...] = table_wide[...].astype(BF16)

    trees, at = {}, 0
    for name, got, order in zip(("ua", "ub", "da", "db", "out"), (got_ua, got_ub, got_da, got_db, got_out), ORDERS):
        trees[name] = Tree(order, None, tree_refs[at], tree_refs[at + 1:at + 5], got, tree_refs[at + 5])
        at += 6
    for name, got, order in (("in0", got_in0, ORDERS[5]), ("in1", got_in1, ORDERS[6]), ("in2", got_in2, ORDERS[7])):
        trees[name] = Tree(("core",) + order, None, None, tree_refs[at:at + 5], got, tree_refs[at + 5])
        at += 6

    post_marks = Post(n, lambda d: marks, lambda p: marks_got.at[p], mark_sems)

    def posts(sent, got, sems):
        return [
            Post(n, lambda e, r=r: sent.at[r, aligned(e, each)], lambda p, r=r: got.at[r, aligned(p, each)], sems.at[r])
            for r in range(rows)
        ]

    posts_gate = posts(sent_one, got_one, gate_sems)
    posts_long = posts(sent_two, got_two, long_sems)
    posts_back = posts(sent_one, got_one, back_sems)
    posts_gated = posts(sent_two, got_two, gated_sems)

    def near_far(r, h, source):
        part = slice(h * step, (h + 1) * step)
        target = {"seq": lax.rem(me + 2, n)}
        return remote(source.at[r, part], land.at[1, r, part], near_sems.at[0, 0, r, h], near_sems.at[0, 1, r, h], target)

    def near_side(r, h, source):
        part = slice(h * step, (h + 1) * step)
        return exchange(source.at[r, part], land.at[0, r, part], near_sems.at[1, 0, r, h], near_sems.at[1, 1, r, h], "x")

    def tap_copy(e, taps_sent):
        return remote(taps_sent.at[aligned(e, each)], taps_got.at[aligned(me, each)], tap_sems.at[0, lax.rem(e, 2)], tap_sems.at[1, me], {"seq": e})

    def tap_spread(axis):
        at = 2 if axis == "core" else 3
        return exchange(taps_got, taps_got, tap_sems.at[at, 0], tap_sems.at[at, 1], axis)

    def side_copy(r):
        return exchange(hand.at[0, r], land.at[0, r], hand_sems.at[0, 0, r], hand_sems.at[0, 1, r], "x")

    def far_copy(r):
        target = {"seq": lax.rem(me + n - 2, n)}
        return remote(hand.at[1, r], land.at[1, r], hand_sems.at[1, 0, r], hand_sems.at[1, 1, r], target)

    def tap_core():
        return exchange(tap_own.at[1 - c], tap_got, home_sems.at[0, 0], home_sems.at[1, 0], "core")

    def tap_y():
        return exchange(tap_own.at[c, 1 - y], tap_half, home_sems.at[0, 1], home_sems.at[1, 1], "y")

    def home_copy(q, there):
        return remote(tap_part.at[q], tap_all.at[c, there], home_send.at[q], home_recv.at[there], {"seq": 4 * y + q})

    def tap_back_y():
        return exchange(tap_all.at[c], tap_all.at[c], home_sems.at[0, 2], home_sems.at[1, 2], "y")

    def tap_back_core():
        return exchange(tap_all.at[c], tap_all.at[c], home_sems.at[0, 3], home_sems.at[1, 3], "core")

    def front(near, x_in, taps, taps_sent, w_in, proj, turned, gate_wide, fin, spec, spec_taps, spec_gate):
        first = [
            pltpu.make_async_copy(src, dst, fetch.at[i])
            for i, (src, dst) in enumerate(((x_far, x_in), (taps_far, taps), (w_in_far, w_in)))
        ]
        for copy in first:
            copy.start()
        marks[...] = jnp.zeros_like(marks)
        for r in range(rows):
            marks[r:r + 1, :] = segments[r].astype(F32)
            marks[rows + r:rows + r + 1, :] = valid[r].astype(F32)
        for k in range(3):
            small[3 * k:3 * k + 3, :] = short_taps[:, k * width:(k + 1) * width]
        small[12:16, :] = jnp.zeros((4, width), F32)
        first[0].wait()

        def norm_row(r):
            for at in range(r * blocks, (r + 1) * blocks, 128):
                parts = [strided(x_in, 128, at, j, wide) for j in range(wide)]
                total = sum(jnp.sum(part * part, axis=-1, keepdims=True) for part in parts)
                scale = lax.rsqrt(total * (1.0 / width) + EPS)
                for j, part in enumerate(parts):
                    lanes = slice(j * 128, (j + 1) * 128)
                    near[0, r, at - r * blocks:at - r * blocks + 128, lanes] = (part * scale * gain_one[:, lanes]).astype(BF16)

        def send_near(r):
            for h in range(2):
                near_far(r, h, near.at[0]).start()

            @pl.when(xbit == 0)
            def _():
                for h in range(2):
                    near_side(r, h, near.at[0]).start()

        def hand_on(r):
            @pl.when(xbit == 1)
            def _():
                for h in range(2):
                    near_far(r, h, near.at[0]).wait_recv()
                    near_side(r, h, land.at[1]).start()

        norm_row(0)
        pl.semaphore_wait(barrier, told)
        send_near(0)
        post_marks.start()
        norm_row(1)
        send_near(1)
        first[1].wait()
        for j in range(wide):
            raw = strided(taps, blocks, 0, j, wide)
            low = raw - THRESH * jnp.tanh(raw * (1.0 / THRESH))
            taps_sent[j * 128:(j + 1) * 128, :] = low.T.astype(BF16)
        for xd in range(2):
            target = 4 * y + 2 * c + xd

            @pl.when(target != me)
            def _():
                tap_copy(target, taps_sent).start()

            @pl.when(target == me)
            def _():
                taps_got[aligned(me, each)] = taps_sent[aligned(me, each)]

        first[2].wait()

        def project(r, j):
            for k in (1, 2, 0):
                for at in range(0, width, 256):
                    cols = slice(k * width + at, k * width + at + 256)
                    proj[j, k, :, at:at + 256] = dot_nn(near[j, r], w_in[:, cols]).astype(BF16)

        project(0, 0)
        hand_on(0)
        post_marks.arrive()
        lane = lax.broadcasted_iota(jnp.int32, (rows, blocks), 1)
        now = marks[0:rows, :]
        found = []
        for j in (1, 2):
            before = marks_got[lax.rem(me + n - j, n), 0:rows, :]
            wrapped = me < j
            before = jnp.where(wrapped, pltpu.roll(before, 1, 1), before)
            kept = jnp.logical_and(before == now, jnp.logical_or(jnp.logical_not(wrapped), lane > 0))
            found.append(kept.astype(F32))
        columns = jnp.concatenate(found + [marks[rows:2 * rows, :], jnp.zeros((2, blocks), F32)], axis=0).T
        for s in range(3):
            for r in range(rows):
                same[s, r] = jnp.broadcast_to(columns[:, s * rows + r:s * rows + r + 1], (blocks, 128))

        def chunk_row(r):
            @pl.when(xbit == 0)
            def _():
                for h in range(2):
                    near_far(r, h, near.at[0]).wait_recv()

            for h in range(2):
                near_side(r, h, near.at[0]).wait_recv()
            for j in (1, 2):
                wrapped = jnp.logical_and(at_top, xbit == 0) if j == 1 else at_top

                @pl.when(wrapped)
                def _():
                    near[j, r] = turn_rows(land[j - 1, r].astype(F32), 1).astype(BF16)

                @pl.when(jnp.logical_not(wrapped))
                def _():
                    near[j, r] = land[j - 1, r]

                project(r, j)

            def lanes_step(lanes):
                def rows_step(here):
                    masks = [same[s, r, here, :] for s in range(3)]
                    value = []
                    for k in range(3):
                        total = small[3 * k:3 * k + 1, lanes] * proj[0, k, here, lanes].astype(F32)
                        total += small[3 * k + 1:3 * k + 2, lanes] * (proj[1, k, here, lanes].astype(F32) * masks[0])
                        total += small[3 * k + 2:3 * k + 3, lanes] * (proj[2, k, here, lanes].astype(F32) * masks[1])
                        value.append(total)
                    query[r, here, lanes] = value[0]
                    keys, values = value[1] * masks[2], value[2] * masks[2]
                    gate = value[1] * values
                    saved[0, r, here, lanes] = keys.astype(BF16)
                    saved[1, r, here, lanes] = values.astype(BF16)
                    saved[2, r, here, lanes] = gate.astype(BF16)
                    gate_wide[here, lanes] = gate

                over_rows(blocks, 64, rows_step)

            over_lanes(width, lanes_step)
            sent_one[r] = gate_wide[...].T.astype(BF16)
            posts_gate[r].start()

        chunk_row(0)
        project(1, 0)
        hand_on(1)

        @pl.when(chosen_chunk)
        def _():
            for p in range(n):
                @pl.when(me != p)
                def _():
                    remote(
                        taps_sent.at[aligned(me, each)], taps_got.at[p * each:(p + 1) * each],
                        tap_sems.at[0, 0], tap_sems.at[1, p], {"seq": p},
                    ).wait_recv()
            tap_spread("core").start()

        @pl.when(jnp.logical_and(zh == y, zl != c))
        def _():
            tap_spread("core").wait_recv()

        @pl.when(zh == y)
        def _():
            tap_spread("y").start()

        chunk_row(1)

        @pl.when(zh != y)
        def _():
            tap_spread("y").wait_recv()

        to_lanes(lambda at, size: taps_got[at:at + size], table, spec)

        def taps_group(at, lane):
            re, im = load_phases(spec, n, each, at, lane, blocks)
            re, im = turn_phases(re, im, turns, lane, -1)
            re, im = fft_points(re, im, -1)
            for k in range(n):
                spec_taps[pl.ds(k * each + at, 8), lane:lane + 128] = re[k]
                spec_taps[pl.ds(k * each + at, 8), blocks + lane:blocks + lane + 128] = im[k]

        def both_halves(at, lane):
            taps_group(at, lane)
            taps_group(at + 8, lane)

        over_groups(each, blocks, both_halves)
        keeps = [pltpu.make_async_copy(spec_taps, spec_taps_far, keep.at[0])]
        keeps[0].start()

        for r in range(rows):
            posts_gate[r].arrive()
            to_lanes(lambda at, size: got_one[r, at:at + size], table, spec)

            def work(re, im, at, lane, kept):
                re, im = turn_phases(re, im, turns, lane, -1)
                re, im = fft_points(re, im, -1)
                tap_r, tap_i = load_phases(spec_taps, n, each, at, lane, blocks)
                out_r = [re[k] * tap_r[k] - im[k] * tap_i[k] for k in range(n)]
                out_i = [re[k] * tap_i[k] + im[k] * tap_r[k] for k in range(n)]
                out_r, out_i = fft_points(out_r, out_i, 1)
                out_r, out_i = turn_phases(out_r, out_i, turns, lane, 1)
                return (re, im), (out_r, out_i)

            by_halves(n, each, blocks, spec, work, (spec_gate.at[r], fin))

            def store(at, value):
                sent_two[r, at:at + value.shape[0]] = value.astype(BF16)

            from_lanes(fin, table, each, store)
            posts_long[r].start()
        for j in range(3):
            for r in range(rows):
                value = near[j, r].astype(F32)
                if j > 0:
                    value = value * same[j - 1, r, :, 0:1]
                turned[j, :, r * blocks:(r + 1) * blocks] = value.T.astype(BF16)
        keeps += [
            pltpu.make_async_copy(turned, turned_far, keep.at[1]),
            pltpu.make_async_copy(spec_gate, spec_gate_far, keep.at[2]),
        ]
        for copy in keeps[1:]:
            copy.start()
        for copy in keeps:
            copy.wait()
        for r in range(rows):
            for h in range(2):
                near_far(r, h, near.at[0]).wait_send()
                near_side(r, h, near.at[0]).wait_send()
        for xd in range(2):
            target = 4 * y + 2 * c + xd

            @pl.when(target != me)
            def _():
                tap_copy(target, taps_sent).wait_send()

    pl.run_scoped(
        front,
        pltpu.VMEM((3, rows, blocks, width), BF16),
        pltpu.VMEM(x_far.shape, F32),
        pltpu.VMEM(taps_far.shape, F32),
        pltpu.VMEM((width, blocks), BF16),
        pltpu.VMEM(w_in_far.shape, BF16),
        pltpu.VMEM((3, 3, blocks, width), BF16),
        pltpu.VMEM(turned_far.shape, BF16),
        pltpu.VMEM((blocks, width), F32),
        pltpu.VMEM((width, 2 * blocks), BF16),
        pltpu.VMEM((width, 2 * blocks), F32),
        pltpu.VMEM((width, 2 * blocks), F32),
        pltpu.VMEM(spec_gate_far.shape, BF16),
    )

    def middle(act, grad_act, turned, turned_cot, mixed, mix_back):
        def mlp(w_out, w_up, w_down, x, cot, cot_near, cot_low, resid, long_out, acc_out, acc_back, normed, whole_out, mid):
            vectors[...] = jnp.zeros_like(vectors)
            kept = []
            first = [
                pltpu.make_async_copy(src, dst, fetch.at[i])
                for i, (src, dst) in enumerate(((w_out_far, w_out), (x_far, x), (cot_far, cot), (w_up_far, w_up), (w_down_far, w_down)))
            ]
            for copy in first:
                copy.start()
            first[0].wait()
            for r in range(rows):
                tokens = slice(r * blocks, (r + 1) * blocks)
                posts_long[r].arrive()
                gated = saved[2, r].astype(F32)
                long_out[...] = got_two[r].astype(F32).T + small[9:10, :] * gated
                low = (query[r] * long_out[...]).astype(BF16)
                mixer = dot_nn(low, w_out[...])
                mixed[r] = low.T
                mask = same[2, r, :, 0:1]
                vectors[13:14, :] += jnp.sum(mixer * mixer * mask, axis=0, keepdims=True)
                if r == 0:
                    first[1].wait()
                    first[2].wait()
                for j in range(wide):
                    lanes = slice(j * 128, (j + 1) * 128)
                    resid[:, lanes] = strided(x, blocks, r * blocks, j, wide) + mixer[:, lanes]
                    cot_near[:, lanes] = strided(cot, blocks, r * blocks, j, wide)
                cot_low[...] = cot_near[...].astype(BF16)
                state = resid[...]
                scale = lax.rsqrt(jnp.mean(state * state, axis=-1, keepdims=True) + EPS)
                normed[...] = (state * scale * gain_two).astype(BF16)
                acc_out[...] = jnp.zeros_like(acc_out)
                acc_back[...] = jnp.zeros_like(acc_back)
                if r == 0:
                    first[3].wait()
                    first[4].wait()

                def hidden_step(j, carry):
                    cols = aligned(j, chunk)
                    up_val = dot_nn(normed[...], w_up[:, cols])
                    square = up_val * up_val
                    tanh = jnp.tanh(up_val * (C0 + (C0 * C1) * square))
                    half = 0.5 * (1.0 + tanh)
                    act_low = (up_val * half).astype(BF16)
                    slope = half + (0.5 * up_val) * (1.0 - tanh * tanh) * (C0 + (3.0 * C0 * C1) * square)
                    act[tokens, cols] = act_low
                    acc_out[...] += dot_nn(act_low, w_down[cols, :])
                    grad = dot_nt(cot_low[...], w_down[cols, :])
                    grad_low = (grad * slope).astype(BF16)
                    grad_act[tokens, cols] = grad_low
                    acc_back[...] += dot_nt(grad_low, w_up[:, cols])
                    return carry

                lax.fori_loop(0, hidden // chunk, hidden_step, 0)
                state = resid[...]
                scale = lax.rsqrt(jnp.mean(state * state, axis=-1, keepdims=True) + EPS)
                grad = acc_back[...]
                vectors[11:12, :] += jnp.sum(grad * state * scale, axis=0, keepdims=True)
                scaled = grad * gain_two
                shift = jnp.mean(scaled * state, axis=-1, keepdims=True) * (scale * scale * scale)
                grad_mid = cot_near[...] + (scaled * scale - state * shift)
                mix_back[r] = grad_mid.astype(BF16)
                grad_prod = dot_nt(mix_back[r], w_out[...])
                grad_long = grad_prod * query[r]
                posts_gate[r].drain()
                sent_one[r] = grad_long.T.astype(BF16)
                posts_back[r].start()
                saved[3, r] = grad_long.astype(BF16)
                vectors[9:10, :] += jnp.sum(grad_long * saved[2, r].astype(F32), axis=0, keepdims=True)
                saved[2, r] = (grad_prod * long_out[...]).astype(BF16)
                mlp = acc_out[...]
                vectors[14:15, :] += jnp.sum(mlp * mlp * mask, axis=0, keepdims=True)
                whole = resid[...] + mlp
                vectors[12:13, :] += jnp.sum(whole * whole * mask, axis=0, keepdims=True)
                vectors[15:16, :] += jnp.broadcast_to(jnp.sum(mask, axis=0, keepdims=True) * (1.0 / width), (1, width))
                if r > 0:
                    for copy in kept:
                        copy.wait()
                    kept.clear()
                for j in range(wide):
                    place_at = pl.ds(j, blocks, stride=wide)
                    whole_out[place_at, :] = whole[:, j * 128:(j + 1) * 128]
                    mid[place_at, :] = grad_mid[:, j * 128:(j + 1) * 128]
                part_rows = slice(r * blocks * wide, (r + 1) * blocks * wide)
                for i, (src, dst) in enumerate(((whole_out, out_far), (mid, mid_far))):
                    kept.append(pltpu.make_async_copy(src, dst.at[part_rows], keep.at[3 + i]))
                    kept[-1].start()
                turned[:, tokens] = normed[...].T
                turned_cot[:, tokens] = cot_low[...].T

            for copy in kept:
                copy.wait()

        pl.run_scoped(
            mlp,
            pltpu.VMEM(w_out_far.shape, BF16),
            pltpu.VMEM(w_up_far.shape, BF16),
            pltpu.VMEM(w_down_far.shape, BF16),
            pltpu.VMEM(x_far.shape, F32),
            pltpu.VMEM(x_far.shape, F32),
            pltpu.VMEM((blocks, width), F32),
            pltpu.VMEM((blocks, width), BF16),
            *[pltpu.VMEM((blocks, width), F32)] * 4,
            pltpu.VMEM((blocks, width), BF16),
            *[pltpu.VMEM((linear, 128), F32)] * 2,
        )

        def sums(up_a, up_b, down_a, down_b, out, spec_taps, spec_gate, fin, spec, spec_sum):
            near = [
                pltpu.make_async_copy(src, dst, fetch.at[i])
                for i, (src, dst) in enumerate(((spec_taps_far, spec_taps), (spec_gate_far, spec_gate)))
            ]
            for copy in near:
                copy.start()
            quarter, part = width // 4, hidden // n
            pairs = [(share, trees[name].own) for name, share in zip(("ua", "ub", "da", "db", "out"), (up_a, up_b, down_a, down_b, out))]

            def pair_copy(i):
                return exchange(pairs[i][0].at[:, :, :, 1 - c], pairs[i][1], pair_sems.at[0, i], pair_sems.at[1, i], "core")

            def put_rows(share, half, lanes, value):
                for s in range(n):
                    for core in range(2):
                        low = (2 * s + core) * side
                        share[s // 4, (s // 2) % 2, s % 2, core, half, :, lanes] = value[low:low + side]

            def add_pair(i):
                share, pair = pairs[i]
                pair_copy(i).wait_recv()
                size = 48
                for a in range(2):
                    for b in range(2):
                        for d in range(2):
                            for e in range(2):
                                def body(k, carry):
                                    here = aligned(k, size)
                                    pair[a, b, d, e, here, :] = pair[a, b, d, e, here, :] + share[a, b, d, c, e, here, :]
                                    return carry
                                lax.fori_loop(0, pair.shape[4] // size, body, 0)


            def conv_row(r):
                posts_back[r].arrive()
                to_lanes(lambda at, size: got_one[r, at:at + size], table, spec)

                def work(re, im, at, lane, kept):
                    re, im = turn_phases(re, im, turns, lane, -1)
                    re, im = fft_points(re, im, -1)
                    tap_r, tap_i = load_phases(spec_taps, n, each, at, lane, blocks)
                    gate_r, gate_i = kept
                    out_r, out_i = [], []
                    for k in range(n):
                        here = pl.ds(k * each + at, 8)
                        lanes, other = slice(lane, lane + 128), slice(blocks + lane, blocks + lane + 128)
                        old_r, old_i = gate_r[k], gate_i[k]
                        sum_r, sum_i = old_r * re[k] + old_i * im[k], old_r * im[k] - old_i * re[k]
                        if r == 0:
                            spec_sum[here, lanes] = sum_r
                            spec_sum[here, other] = sum_i
                        else:
                            spec_sum[here, lanes] += sum_r
                            spec_sum[here, other] += sum_i
                        out_r.append(tap_r[k] * re[k] + tap_i[k] * im[k])
                        out_i.append(tap_r[k] * im[k] - tap_i[k] * re[k])
                    out_r, out_i = fft_points(out_r, out_i, 1)
                    return (turn_phases(out_r, out_i, turns, lane, 1),)

                by_halves(n, each, blocks, spec, work, (fin,), spec_gate.at[r])

                posts_long[r].drain()

                def store(at, value):
                    sent_two[r, at:at + value.shape[0]] = value.astype(BF16)

                from_lanes(fin, table, each, store)
                posts_gated[r].start()
            for i, share in enumerate((up_a, up_b)):
                for half in range(2):
                    low = half * (hidden // 2) + i * (hidden // 4)
                    value = dot_nn(turned[...], grad_act[:, low:low + hidden // 4]).astype(BF16)
                    put_rows(share, half, ALL, value)
                pair_copy(i).start()
            for s in range(n):
                value = dot_nn(turned_cot[...], act[:, s * part:(s + 1) * part]).astype(BF16)
                for core in range(2):
                    for half in range(2):
                        low = (2 * core + half) * quarter
                        down_a[s // 4, (s // 2) % 2, s % 2, core, half] = value[low:low + quarter // 2]
                        down_b[s // 4, (s // 2) % 2, s % 2, core, half] = value[low + quarter // 2:low + quarter]
            pair_copy(2).start()
            pair_copy(3).start()
            for half in range(2):
                low = half * (width // 2)
                value = sum(dot_nn(mixed[r], mix_back[r, :, low:low + width // 2]) for r in range(rows)).astype(BF16)
                put_rows(out, half, ALL, value)
            pair_copy(4).start()
            add_pair(0)
            trees["ua"].start()
            add_pair(1)
            trees["ub"].start()
            add_pair(3)
            trees["db"].start()
            add_pair(2)
            trees["da"].start()
            add_pair(4)
            for copy in near:
                copy.wait()
            conv_row(0)
            conv_row(1)

            def work_taps(re, im, at, lane, kept):
                re, im = fft_points(re, im, 1)
                return (turn_phases(re, im, turns, lane, 1),)

            by_halves(n, each, blocks, spec_sum, work_taps, (fin,))

            def store_taps(at, value):
                p = at // each
                for half in range(2):
                    tap_own[half, p // 4, p % 4] = value[half * side:(half + 1) * side].astype(BF16)

            from_lanes(fin, table, each, store_taps)
            tap_core().start()
            for i in range(5):
                pair_copy(i).wait_send()

        pl.run_scoped(
            sums,
            *[pltpu.VMEM(trees[name].own.shape[:3] + (2,) + trees[name].own.shape[3:], BF16) for name in ("ua", "ub", "da", "db", "out")],
            pltpu.VMEM((width, 2 * blocks), F32),
            pltpu.VMEM((rows, width, 2 * blocks), BF16),
            pltpu.VMEM((width, 2 * blocks), BF16),
            pltpu.VMEM((width, 2 * blocks), F32),
            pltpu.VMEM((width, 2 * blocks), F32),
        )

    pl.run_scoped(
        middle,
        pltpu.VMEM((rows * blocks, hidden), BF16),
        pltpu.VMEM((rows * blocks, hidden), BF16),
        pltpu.VMEM((width, rows * blocks), BF16),
        pltpu.VMEM((width, rows * blocks), BF16),
        pltpu.VMEM((rows, width, blocks), BF16),
        pltpu.VMEM((rows, blocks, width), BF16),
    )

    def token_phase(turned, w_in, x, mid, gate_back, short, part_proj, grad_norm, gain_lanes, share0, share1, share2):
        for k, share in enumerate((share0, share1, share2)):
            trees["in%d" % k].share = share
        near = [
            pltpu.make_async_copy(src, dst, fetch.at[i])
            for i, (src, dst) in enumerate((
                (w_in_far, w_in), (turned_far, turned), (x_far, x), (mid_far, mid),
            ))
        ]
        for copy in near:
            copy.start()
        tap_core().wait_recv()
        for half in range(2):
            for q in range(4):
                tap_own[c, half, q] = tap_own[c, half, q] + tap_got[half, q]
        tap_y().start()

        def token_row(r):
            tokens = slice(r * blocks, (r + 1) * blocks)
            posts_gated[r].arrive()
            gate_back[...] = got_two[r].astype(F32).T

            def lanes_step(lanes):
                skip = small[9:10, lanes]

                def rows_step(here):
                    there = pl.ds(pl.multiple_of(r * blocks + here.start, 64), here.size)
                    grad = gate_back[here, lanes] + skip * saved[3, r, here, lanes].astype(F32)
                    short[there, lanes] = saved[2, r, here, lanes]
                    second = pl.ds(pl.multiple_of(lanes.start + width, 128), 128)
                    third = pl.ds(pl.multiple_of(lanes.start + 2 * width, 128), 128)
                    short[there, second] = (grad * saved[1, r, here, lanes].astype(F32)).astype(BF16)
                    short[there, third] = (grad * saved[0, r, here, lanes].astype(F32)).astype(BF16)

                over_rows(blocks, 64, rows_step)

            over_lanes(width, lanes_step)

        def spread(r, j):
            def lanes_step(lanes):
                def rows_step(here):
                    there = pl.ds(pl.multiple_of(r * blocks + here.start, 64), here.size)
                    for k in range(3):
                        cols = pl.ds(pl.multiple_of(lanes.start + k * width, 128), 128)
                        value = short[there, cols].astype(F32) * small[3 * k + j:3 * k + j + 1, lanes]
                        if j > 0:
                            value = value * same[j - 1, r, here, :]
                        part_proj[here, cols] = value.astype(BF16)

                over_rows(blocks, 64, rows_step)

            over_lanes(width, lanes_step)
            return dot_nt(part_proj[...], w_in[...])

        def send_hand(r):
            hand[0, r] = spread(r, 1).astype(BF16)
            side_copy(r).start()
            hand[1, r] = spread(r, 2).astype(BF16)

            @pl.when(xbit == 0)
            def _():
                far_copy(r).start()

        def hand_on(r):
            @pl.when(xbit == 1)
            def _():
                side_copy(r).wait_recv()
                hand[1, r] = (hand[1, r].astype(F32) + land[0, r].astype(F32)).astype(BF16)
                far_copy(r).start()

        def weight_part(k):
            share = trees["in%d" % k].share
            for half in range(2):
                low = k * width + half * (width // 2)
                cols = slice(low, low + width // 2)
                lanes = slice(half * (width // 2), (half + 1) * (width // 2))
                total = None
                for j in range(3):
                    value = dot_nn(turned[j], short[:, cols])
                    vectors[3 * k + j:3 * k + j + 1, lanes] = jnp.sum(value * w_in[:, cols].astype(F32), axis=0, keepdims=True)
                    value = value * small[3 * k + j:3 * k + j + 1, lanes]
                    total = value if total is None else total + value
                product = total * w_in[:, cols].astype(F32)
                gain_lanes[...] += sum(product[:, at:at + 128] for at in range(0, width // 2, 128))
                total = total.astype(BF16)
                for s in range(n):
                    for core in range(2):
                        block = (2 * s + core) * side
                        share[s // 4, (s // 2) % 2, s % 2, core, half] = total[block:block + side]
            trees["in%d" % k].start()

        def last_row(r):
            tokens = slice(r * blocks, (r + 1) * blocks)

            @pl.when(xbit == 0)
            def _():
                side_copy(r).wait_recv()
                grad_norm[r] += land[0, r].astype(F32)

            far_copy(r).wait_recv()
            late = land[1, r].astype(F32)

            @pl.when(at_end)
            def _():
                grad_norm[r] += turn_rows(late, blocks - 1)

            @pl.when(jnp.logical_not(at_end))
            def _():
                grad_norm[r] += late

            grad = grad_norm[r]
            parts = [strided(x, blocks, r * blocks, j, wide) for j in range(wide)]
            total = sum(jnp.sum(part * part, axis=-1, keepdims=True) for part in parts)
            scale = lax.rsqrt(total * (1.0 / width) + EPS)
            inner = 0.0
            scaled = []
            for j, part in enumerate(parts):
                lanes = slice(j * 128, (j + 1) * 128)
                piece = grad[:, lanes]
                scaled.append(piece * gain_one[:, lanes])
                inner += jnp.sum(scaled[j] * part, axis=-1, keepdims=True)
            shift = inner * (1.0 / width) * (scale * scale * scale)
            for j, part in enumerate(parts):
                place_at = pl.ds(r * linear + j, blocks, stride=wide)
                mid[place_at, :] += scaled[j] * scale - part * shift
            done = slice(r * linear, (r + 1) * linear)
            ready.append(pltpu.make_async_copy(mid.at[done], flat_far.at[done], keep.at[r]))
            ready[-1].start()

        def tap_home():
            tap_y().wait_recv()
            for q in range(4):
                tap_part[q] = tap_own[c, y, q] + tap_half[q]
            for q in range(4):
                @pl.when(4 * y + q != me)
                def _():
                    home_copy(q, me).start()

                @pl.when(4 * y + q == me)
                def _():
                    tap_all[c, me] = tap_part[q]

        def tap_return():
            @pl.when(home)
            def _():
                for j in range(1, n):
                    peer = lax.rem(me + j, n)
                    remote(tap_part.at[0], tap_all.at[c, peer], home_send.at[0], home_recv.at[peer], {"seq": peer}).wait_recv()
                tap_back_y().start()

        def tap_share():
            @pl.when(jnp.logical_not(home))
            def _():
                tap_back_y().wait_recv()

            tap_back_core().start()

        def vector_copy(step):
            axis = ("core", "y", "x", "zl", "zh")[step]
            return exchange(vectors, vector_got.at[step], vector_sems.at[0, step], vector_sems.at[1, step], axis)

        def vector_start():
            vectors[10:11, :] = jnp.sum(gain_lanes[...].T, axis=0, keepdims=True) / gain_one
            vector_copy(0).start()

        def vector_finish(step):
            vector_copy(step).wait()
            vectors[...] += vector_got[step]
            if step < 4:
                vector_copy(step + 1).start()

        def whole_norm():
            for r in range(rows):
                grad_norm[r] = spread(r, 0)
            for copy in near[2:4]:
                copy.wait()

        ready = []
        gain_lanes[...] = jnp.zeros_like(gain_lanes)
        near[0].wait()
        trees["ua"].finish()
        trees["ub"].finish()
        token_row(0)
        send_hand(0)
        trees["db"].finish()
        tap_home()
        token_row(1)
        send_hand(1)
        trees["ua"].finish()
        near[1].wait()
        weight_part(0)
        hand_on(0)
        trees["da"].finish()
        trees['out'].start()
        weight_part(1)
        weight_part(2)
        vector_start()
        tap_return()
        trees["in0"].finish()
        trees["in1"].finish()
        trees["in2"].finish()
        hand_on(1)
        trees["ub"].finish()
        trees["db"].finish()
        whole_norm()
        tap_share()
        trees["ua"].finish()
        last_row(0)
        vector_finish(0)
        trees["da"].finish()
        trees["in0"].finish()
        trees["in1"].finish()
        trees["in2"].finish()
        vector_finish(1)
        trees["ub"].finish()
        trees["db"].finish()
        trees["out"].finish()
        last_row(1)
        vector_finish(2)
        trees["da"].finish()
        rest = ["db", "ub", "out", "in0", "in1", "in2", "ua", "da"]
        step = 3
        while any(trees[name].done < len(trees[name].order) for name in rest):
            for name in rest:
                if trees[name].done < len(trees[name].order):
                    trees[name].finish()
            if step < 5:
                vector_finish(step)
                step += 1
        tap_back_core().wait_recv()
        for copy in ready:
            copy.wait()

        for tree in trees.values():
            tree.drain()
        for post in [post_marks] + posts_back + posts_gated:
            post.drain()
        for r in range(rows):
            side_copy(r).wait_send()
            far_copy(r).wait_send()
        tap_core().wait_send()
        tap_y().wait_send()
        for q in range(4):
            @pl.when(4 * y + q != me)
            def _():
                home_copy(q, me).wait_send()

        @pl.when(home)
        def _():
            tap_back_y().wait_send()

        tap_back_core().wait_send()

        @pl.when(chosen_chunk)
        def _():
            tap_spread("core").wait_send()

        @pl.when(zh == y)
        def _():
            tap_spread("y").wait_send()

    pl.run_scoped(
        token_phase,
        pltpu.VMEM(turned_far.shape, BF16),
        pltpu.VMEM(w_in_far.shape, BF16),
        pltpu.VMEM(x_far.shape, F32),
        pltpu.VMEM(x_far.shape, F32),
        pltpu.VMEM((blocks, width), F32),
        pltpu.VMEM((rows * blocks, 3 * width), BF16),
        pltpu.VMEM((blocks, 3 * width), BF16),
        pltpu.VMEM((rows, blocks, width), F32),
        pltpu.VMEM((width, 128), F32),
        *[pltpu.VMEM((2, 2, 2, 2, 2, side, width // 2), BF16)] * 3,
    )


def last_kernel(
    block_in, flat_in, got_ua, got_ub, got_da, got_db, got_out, got_in0, got_in1, got_in2, tap_all, taps, vectors,
    out, grad_flat, gain_mix, grad_in, grad_taps, grad_kernel, grad_skip, grad_out, gain_mlp, grad_up, grad_down, rms,
):
    out[...] = block_in[...]
    grad_flat[...] = flat_in[...]
    width = vectors.shape[1]
    side, wide, blocks = got_out.shape[2], width // 128, tap_all.shape[3]
    half_up = grad_up.shape[1] // 2
    for got, target, low, skip in (
        (got_ua, grad_up, 0, half_up), (got_ub, grad_up, half_up // 2, half_up), (got_out, grad_out, 0, width // 2),
        (got_in0, grad_in, 0, width // 2), (got_in1, grad_in, width, width // 2), (got_in2, grad_in, 2 * width, width // 2),
    ):
        l = got.shape[3]
        for half in range(2):
            for core in range(2):
                at = low + half * skip
                target[core * side:(core + 1) * side, at:at + l] = got[core, half].astype(F32)
    grad_down[...] = jnp.concatenate(
        [got[core, half] for core in range(2) for half in range(2) for got in (got_da, got_db)], axis=0
    ).astype(F32).T
    value = jnp.concatenate(
        [tap_all[core, s] for s in range(tap_all.shape[1]) for core in range(2)], axis=0
    ).astype(F32).T
    for j in range(wide):
        place_at = pl.ds(j, blocks, stride=wide)
        tanh = jnp.tanh(taps[place_at, :] * (1.0 / THRESH))
        grad_kernel[place_at, :] = value[:, j * 128:(j + 1) * 128] * (tanh * tanh)
    for k in range(3):
        grad_taps[:, k * width:(k + 1) * width] = vectors[3 * k:3 * k + 3, :]
    for target, row in ((grad_skip, 9), (gain_mix, 10), (gain_mlp, 11)):
        target[...] = vectors[row, :]
    total = jnp.sum(vectors[12:16, :], axis=1, keepdims=True)
    found = jnp.sqrt(total / (jnp.maximum(total[3:4, :], 1.0) * width))
    for i in range(3):
        rms[i] = found[i, 0]


def call(body, outs, scratch, inputs, collective_id, far=(), far_outs=()):
    return pl.pallas_call(
        body,
        out_shape=tuple(jax.ShapeDtypeStruct(*out) for out in outs),
        in_specs=[pl.BlockSpec(memory_space=pl.ANY if i in far else pltpu.VMEM) for i in range(len(inputs))],
        out_specs=tuple(pl.BlockSpec(memory_space=pl.ANY if i in far_outs else pltpu.VMEM) for i in range(len(outs))),
        scratch_shapes=scratch,
        compiler_params=pltpu.CompilerParams(
            vmem_limit_bytes=VMEM_BYTES, collective_id=collective_id, has_side_effects=True
        ),
    )(*inputs)


def local(
    block_in, segment_ids, valid_mask, cotangent, gain_mix, in_proj, short_taps, long_kernel,
    skip_gain, out_proj, gain_mlp, up_proj, down_proj,
):
    rows, blocks, _, width = block_in.shape
    hidden = up_proj.shape[1]
    n = lax.axis_size("seq")
    each = width // n
    tokens = rows * blocks
    side, wide = each // 2, width // 128
    chunk = 512
    x = block_in.reshape(tokens * wide, 128)
    cot = cotangent.reshape(tokens * wide, 128)
    raw = long_kernel.reshape(blocks * wide, 128)
    segments = segment_ids.reshape(rows, 1, blocks)
    valid = valid_mask.reshape(rows, 1, blocks)
    table, turns = spectrum_tables(blocks, n)
    dma = pltpu.SemaphoreType.DMA
    bits = (2, 2, 2, 2, 2)
    up_shape = bits[1:] + (side, hidden // 4)
    down_shape = bits[1:] + (width // 8, hidden // n)
    out_shape = bits[1:] + (side, width // 2)
    own_shapes = (up_shape, up_shape, down_shape, down_shape, out_shape)
    low = lambda *shape: pltpu.VMEM(shape, BF16)
    full = lambda *shape: pltpu.VMEM(shape, F32)

    trees = []
    for shape in own_shapes:
        trees += tree_scratch(*shape[4:])
    for _ in range(3):
        trees += tree_scratch(*out_shape[4:])
    gots = [(2, 2) + shape[4:] for shape in own_shapes + (out_shape,) * 3]
    quarter = (4, side, blocks)
    pair = (rows, 2, n)
    block_out, grad_flat, _, _, _, _, *gathered, taps_back, vectors = call(
        functools.partial(whole_kernel, n, chunk),
        [
            (x.shape, F32),
            (x.shape, F32),
            (x.shape, F32),
            ((3, width, tokens), BF16),
            ((width, 2 * blocks), F32),
            ((rows, width, 2 * blocks), BF16),
            *[(shape, BF16) for shape in gots],
            ((2, n, side, blocks), BF16),
            ((16, width), F32),
        ],
        [
            full(16, width), low(*table.shape), full(8, blocks), full(n, 8, blocks), low(2, rows, blocks, width), low(width, blocks),
            full(rows, blocks, width), low(4, rows, blocks, width), full(3, rows, blocks, 128),
            low(rows, width, blocks), low(rows, width, blocks), low(rows, width, blocks), low(rows, width, blocks),
            low(2, rows, blocks, width),
            low(2, 2, *quarter), low(2, *quarter), low(*quarter), low(*quarter), full(5, 16, width),
            dma((5,)), dma((5,)), dma((2, 2, rows, 2)), dma((2, n)), dma((4, n)),
            dma(pair), dma(pair), dma(pair), dma(pair), dma((2, 2, rows)),
            dma((2, 5)), dma((2, 4)), dma((4,)), dma((n,)), dma((2, 5)),
        ] + trees,
        (x, cot, raw, short_taps, skip_gain, gain_mix, gain_mlp, segments, valid, in_proj, out_proj, up_proj, down_proj, table, turns),
        1,
        far=(0, 1, 2, 9, 10, 11, 12),
        far_outs=range(6),
    )
    inputs = (block_out, grad_flat, *gathered, taps_back, raw, vectors)
    near = pl.BlockSpec(memory_space=pltpu.VMEM)
    outs = [
        x.shape, x.shape, (width,), (each, 3 * width), (3, 3 * width), raw.shape, (width,), (each, width), (width,),
        (each, hidden), (hidden // n, width), (3,),
    ]
    results = pl.pallas_call(
        last_kernel,
        out_shape=tuple(jax.ShapeDtypeStruct(shape, F32) for shape in outs),
        in_specs=[near] * len(inputs),
        out_specs=(near,) * 11 + (pl.BlockSpec(memory_space=pltpu.SMEM),),
        compiler_params=pltpu.CompilerParams(vmem_limit_bytes=VMEM_BYTES),
    )(*inputs)
    shapes = {0: block_in.shape, 1: block_in.shape, 5: long_kernel.shape}
    return tuple(value.reshape(shapes.get(i, value.shape)) for i, value in enumerate(results))


def chosen(block_in, *rest):
    rows, blocks, _, width = block_in.shape
    n = lax.axis_size("seq")
    fits = blocks % (32 * n) == 0 and width % (32 * n) == 0 and n == 8 and rows == 2 and lax.axis_size("rows") == 4
    return (local if fits else general_local)(block_in, *rest)


def solution(mesh):
    return jax.shard_map(
        chosen,
        mesh=mesh,
        in_specs=(
            P("rows", None, "seq", None),
            P("rows", None, "seq"),
            P("rows", None, "seq"),
            P("rows", None, "seq", None),
            P(),
            P(),
            P(),
            P(None, "seq", None),
            P(),
            P(),
            P(),
            P(),
            P(),
        ),
        out_specs=(
            P("rows", None, "seq", None),
            P("rows", None, "seq", None),
            P(),
            P("seq", None),
            P(),
            P(None, "seq", None),
            P(),
            P("seq", None),
            P(),
            P("seq", None),
            P("seq", None),
            P(),
        ),
        check_vma=False,
    )
```

```python
import functools
import itertools
import math

import jax
import jax.numpy as jnp
import numpy as np
from jax import lax
from jax.experimental import pallas as pl
from jax.experimental.pallas import tpu as pltpu
from jax.sharding import PartitionSpec as P

EPS = 1e-05
THRESH = 0.003
HIGH = lax.Precision.HIGHEST


def shortened(x):

    def short(part):
        return part.astype(jnp.bfloat16) if part.dtype == jnp.float32 else part

    return jax.tree.map(short, x)


def passed_along(block, axis, distance):
    devices = range(lax.axis_size(axis))
    route = [((i - distance) % len(devices), i) for i in devices]
    return lax.ppermute(block, axis, route)


def norm_scale(value, gain):
    return value * lax.rsqrt(jnp.mean(value * value, axis=-1, keepdims=True) + EPS) * gain


def angle_tables(left_count, right_count, period):
    left_idx = jnp.arange(left_count, dtype=jnp.int32)[:, None]
    right_idx = jnp.arange(right_count, dtype=jnp.int32)[None, :]
    phase = (left_idx * right_idx % period).astype(jnp.float32) * (2.0 * math.pi / period)
    return (jnp.cos(phase), jnp.sin(phase))


def twiddle_tables(shard_index, spec_len, whole_len):
    turned = shard_index * jnp.arange(spec_len, dtype=jnp.int32) % whole_len
    phase = turned.astype(jnp.float32) * (2.0 * math.pi / whole_len)
    return (jnp.cos(phase)[None, :, None], jnp.sin(phase)[None, :, None])


def local_forward(signal, shard_index, whole_len):
    blocks = signal.shape[1]
    cos_table, sin_table = angle_tables(blocks, 2 * blocks, 2 * blocks)
    real_part = jnp.einsum("rjd,jk->rkd", signal, cos_table, precision=HIGH)
    imag_part = -jnp.einsum("rjd,jk->rkd", signal, sin_table, precision=HIGH)
    cos_twid, sin_twid = twiddle_tables(shard_index, 2 * blocks, whole_len)
    out_real = real_part * cos_twid + imag_part * sin_twid
    out_imag = imag_part * cos_twid - real_part * sin_twid
    return (out_real[:, :, None, :], out_imag[:, :, None, :])


def cross_section(real_part, imag_part, direction):
    count = real_part.shape[2]
    cos_table, sin_table = angle_tables(count, count, count)
    re_cos = jnp.einsum("rcpd,pm->rcmd", real_part, cos_table, precision=HIGH)
    re_sin = jnp.einsum("rcpd,pm->rcmd", real_part, sin_table, precision=HIGH)
    im_cos = jnp.einsum("rcpd,pm->rcmd", imag_part, cos_table, precision=HIGH)
    im_sin = jnp.einsum("rcpd,pm->rcmd", imag_part, sin_table, precision=HIGH)
    return (re_cos - direction * im_sin, im_cos + direction * re_sin)


def local_inverse(real_part, imag_part, shard_index, whole_len):
    real_part = real_part[:, :, 0, :]
    imag_part = imag_part[:, :, 0, :]
    spec_len = real_part.shape[1]
    cos_twid, sin_twid = twiddle_tables(shard_index, spec_len, whole_len)
    turned_re = real_part * cos_twid - imag_part * sin_twid
    turned_im = imag_part * cos_twid + real_part * sin_twid
    cos_table, sin_table = angle_tables(spec_len, spec_len // 2, spec_len)
    result = jnp.einsum("rkd,kj->rjd", turned_re, cos_table, precision=HIGH)
    result = result - jnp.einsum("rkd,kj->rjd", turned_im, sin_table, precision=HIGH)
    return result / whole_len


def earlier(members, at_start):
    received = jax.tree.map(
        lambda part, own: part.astype(own.dtype),
        passed_along(shortened(members), "seq", 1),
        members,
    )
    placed = []
    for member in received:
        rolled = jnp.concatenate([jnp.zeros_like(member[:, :1]), member[:, :-1]], axis=1)
        placed.append(jnp.where(at_start, rolled, member))
    return tuple(placed)


def later(member, at_end):
    received = passed_along(member.astype(jnp.bfloat16), "seq", -1).astype(member.dtype)
    rolled = jnp.concatenate([received[:, 1:], jnp.zeros_like(received[:, :1])], axis=1)
    return jnp.where(at_end, rolled, received)


def times_trans(left, right):
    return lax.dot_general(
        left, right, (((1,), (1,)), ((), ())), preferred_element_type=jnp.float32
    )


def trans_times(left, right):
    return lax.dot_general(
        left, right, (((0,), (0,)), ((), ())), preferred_element_type=jnp.float32
    )


def general_local(
    block_in,
    segment_ids,
    valid_mask,
    cotangent,
    gain_mix,
    in_proj,
    short_taps,
    long_kernel,
    skip_gain,
    out_proj,
    gain_mlp,
    up_proj,
    down_proj,
):
    batch_rows = block_in.shape[0]
    blocks = block_in.shape[1]
    width = block_in.shape[3]
    shard_count = lax.axis_size("seq")
    shard_index = lax.axis_index("seq")
    whole_len = 2 * blocks * shard_count
    tokens = batch_rows * blocks
    at_start = shard_index == 0
    at_end = shard_index == shard_count - 1
    flat_in = block_in.reshape(tokens, width)
    mask_rows = valid_mask[:, :, 0].astype(jnp.float32)[:, :, None]
    normed_one = norm_scale(flat_in, gain_mix).astype(jnp.bfloat16)
    proj_low = jnp.dot(normed_one, in_proj, preferred_element_type=jnp.float32).astype(jnp.bfloat16)
    proj_low = proj_low.reshape(batch_rows, blocks, 3 * width)
    seg_low = segment_ids[:, :, 0].astype(jnp.bfloat16)[:, :, None]
    prev_one = earlier((proj_low, seg_low), at_start)
    prev_two = earlier(prev_one, at_start)
    same_one = (prev_one[1] == seg_low).astype(jnp.float32)
    same_two = (prev_two[1] == seg_low).astype(jnp.float32)
    proj_now = proj_low.astype(jnp.float32)
    proj_one = prev_one[0].astype(jnp.float32)
    proj_two = prev_two[0].astype(jnp.float32)
    conv_short = (
        short_taps[0] * proj_now
        + short_taps[1] * proj_one * same_one
        + short_taps[2] * proj_two * same_two
    )
    query = conv_short[:, :, :width]
    keys = conv_short[:, :, width : 2 * width]
    values = conv_short[:, :, 2 * width :]
    gated = keys * values * mask_rows
    raw_taps = long_kernel[:, 0, :]
    taps_eff = raw_taps - THRESH * jnp.tanh(raw_taps / THRESH)
    kern_re, kern_im = local_forward(taps_eff[None], shard_index, whole_len)
    kern_re, kern_im = (
        lax.all_to_all(
            kern_re.astype(jnp.bfloat16), "seq", split_axis=1, concat_axis=2, tiled=True
        ).astype(kern_re.dtype),
        lax.all_to_all(
            kern_im.astype(jnp.bfloat16), "seq", split_axis=1, concat_axis=2, tiled=True
        ).astype(kern_im.dtype),
    )
    kern_re, kern_im = cross_section(kern_re, kern_im, -1.0)
    gate_re, gate_im = local_forward(gated, shard_index, whole_len)
    gate_re, gate_im = (
        lax.all_to_all(
            gate_re.astype(jnp.bfloat16), "seq", split_axis=1, concat_axis=2, tiled=True
        ).astype(gate_re.dtype),
        lax.all_to_all(
            gate_im.astype(jnp.bfloat16), "seq", split_axis=1, concat_axis=2, tiled=True
        ).astype(gate_im.dtype),
    )
    gate_re, gate_im = cross_section(gate_re, gate_im, -1.0)
    prod_re = gate_re * kern_re - gate_im * kern_im
    prod_im = gate_re * kern_im + gate_im * kern_re
    prod_re, prod_im = cross_section(prod_re, prod_im, 1.0)
    prod_re, prod_im = (
        lax.all_to_all(
            prod_re.astype(jnp.bfloat16), "seq", split_axis=2, concat_axis=1, tiled=True
        ).astype(prod_re.dtype),
        lax.all_to_all(
            prod_im.astype(jnp.bfloat16), "seq", split_axis=2, concat_axis=1, tiled=True
        ).astype(prod_im.dtype),
    )
    long_out = local_inverse(prod_re, prod_im, shard_index, whole_len) + skip_gain * gated
    mixer_low = (query * long_out).reshape(tokens, width).astype(jnp.bfloat16)
    mixer_out = jnp.dot(mixer_low, out_proj, preferred_element_type=jnp.float32)
    resid_mid = flat_in + mixer_out
    normed_two = norm_scale(resid_mid, gain_mlp).astype(jnp.bfloat16)
    up_val = jnp.dot(normed_two, up_proj, preferred_element_type=jnp.float32)
    act_low = jax.nn.gelu(up_val).astype(jnp.bfloat16)
    mlp_out = jnp.dot(act_low, down_proj, preferred_element_type=jnp.float32)
    flat_out = resid_mid + mlp_out
    grad_out = cotangent.reshape(tokens, width)
    grad_mlp = grad_out.astype(jnp.bfloat16)
    grad_down = trans_times(act_low, grad_mlp)
    grad_act = times_trans(grad_mlp, down_proj)
    unused_val, gelu_back = jax.vjp(jax.nn.gelu, up_val)
    grad_upval = gelu_back(grad_act)[0].astype(jnp.bfloat16)
    grad_up = trans_times(normed_two, grad_upval)
    grad_norm_two = times_trans(grad_upval, up_proj)
    unused_two, norm_back_two = jax.vjp(norm_scale, resid_mid, gain_mlp)
    grad_resid, grad_gain_two = norm_back_two(grad_norm_two)
    grad_mid = grad_out + grad_resid
    grad_mix = grad_mid.astype(jnp.bfloat16)
    grad_outp = trans_times(mixer_low, grad_mix)
    grad_prod = times_trans(grad_mix, out_proj).reshape(batch_rows, blocks, width)
    grad_query = grad_prod * long_out
    grad_long = grad_prod * query
    back_re, back_im = local_forward(grad_long, shard_index, whole_len)
    back_re, back_im = (
        lax.all_to_all(
            back_re.astype(jnp.bfloat16), "seq", split_axis=1, concat_axis=2, tiled=True
        ).astype(back_re.dtype),
        lax.all_to_all(
            back_im.astype(jnp.bfloat16), "seq", split_axis=1, concat_axis=2, tiled=True
        ).astype(back_im.dtype),
    )
    back_re, back_im = cross_section(back_re, back_im, -1.0)
    sig_re = kern_re * back_re + kern_im * back_im
    sig_im = kern_re * back_im - kern_im * back_re
    tap_re = jnp.sum(gate_re * back_re + gate_im * back_im, axis=0, keepdims=True)
    tap_im = jnp.sum(gate_re * back_im - gate_im * back_re, axis=0, keepdims=True)
    sig_re, sig_im = cross_section(sig_re, sig_im, 1.0)
    tap_re, tap_im = cross_section(tap_re, tap_im, 1.0)
    sig_re, sig_im, tap_re, tap_im = (
        lax.all_to_all(
            sig_re.astype(jnp.bfloat16), "seq", split_axis=2, concat_axis=1, tiled=True
        ).astype(sig_re.dtype),
        lax.all_to_all(
            sig_im.astype(jnp.bfloat16), "seq", split_axis=2, concat_axis=1, tiled=True
        ).astype(sig_im.dtype),
        lax.all_to_all(
            tap_re.astype(jnp.bfloat16), "seq", split_axis=2, concat_axis=1, tiled=True
        ).astype(tap_re.dtype),
        lax.all_to_all(
            tap_im.astype(jnp.bfloat16), "seq", split_axis=2, concat_axis=1, tiled=True
        ).astype(tap_im.dtype),
    )
    grad_gated = local_inverse(sig_re, sig_im, shard_index, whole_len) + skip_gain * grad_long
    grad_taps_eff = local_inverse(tap_re, tap_im, shard_index, whole_len)[0]
    tanh_val = jnp.tanh(raw_taps / THRESH)
    grad_kernel = (grad_taps_eff * tanh_val * tanh_val)[:, None, :]
    grad_kernel = lax.psum(grad_kernel.astype(jnp.bfloat16), "rows").astype(jnp.float32)
    grad_skip = jnp.sum(grad_long * gated, axis=(0, 1))
    grad_short = jnp.concatenate(
        [grad_query, grad_gated * values * mask_rows, grad_gated * keys * mask_rows], axis=2
    )
    grad_tap_rows = jnp.stack(
        [
            jnp.sum(grad_short * proj_now, axis=(0, 1)),
            jnp.sum(grad_short * proj_one * same_one, axis=(0, 1)),
            jnp.sum(grad_short * proj_two * same_two, axis=(0, 1)),
        ]
    )
    inner_term = short_taps[1] * grad_short * same_one + later(
        short_taps[2] * grad_short * same_two, at_end
    )
    grad_proj = short_taps[0] * grad_short + later(inner_term, at_end)
    grad_proj = grad_proj.reshape(tokens, 3 * width).astype(jnp.bfloat16)
    grad_inp = trans_times(normed_one, grad_proj)
    grad_norm_one = times_trans(grad_proj, in_proj)
    unused_one, norm_back_one = jax.vjp(norm_scale, flat_in, gain_mix)
    grad_first, grad_gain_one = norm_back_one(grad_norm_one)
    grad_flat = grad_mid + grad_first
    mask_flat = mask_rows.reshape(tokens, 1)
    stat_sums = jnp.stack(
        [
            jnp.sum(mask_flat * flat_out * flat_out),
            jnp.sum(mask_flat * mixer_out * mixer_out),
            jnp.sum(mask_flat * mlp_out * mlp_out),
            jnp.sum(mask_flat),
        ]
    )
    grad_gain_one, grad_gain_two, grad_tap_rows, grad_skip, stat_sums = lax.psum(
        (grad_gain_one, grad_gain_two, grad_tap_rows, grad_skip, stat_sums), ("rows", "seq")
    )
    rms_stats = jnp.sqrt(stat_sums[:3] / (jnp.maximum(stat_sums[3], 1.0) * width))
    shares = (
        lax.psum_scatter(grad_inp, "seq", scatter_dimension=0, tiled=True),
        lax.psum_scatter(grad_outp, "seq", scatter_dimension=0, tiled=True),
        lax.psum_scatter(grad_up, "seq", scatter_dimension=0, tiled=True),
        lax.psum_scatter(grad_down, "seq", scatter_dimension=0, tiled=True),
    )
    grad_inp, grad_outp, grad_up, grad_down = (
        lax.psum(shares[0].astype(jnp.bfloat16), "rows").astype(jnp.float32),
        lax.psum(shares[1].astype(jnp.bfloat16), "rows").astype(jnp.float32),
        lax.psum(shares[2].astype(jnp.bfloat16), "rows").astype(jnp.float32),
        lax.psum(shares[3].astype(jnp.bfloat16), "rows").astype(jnp.float32),
    )
    return (
        flat_out.reshape(block_in.shape),
        grad_flat.reshape(block_in.shape),
        grad_gain_one,
        grad_inp,
        grad_tap_rows,
        grad_kernel,
        grad_skip,
        grad_outp,
        grad_gain_two,
        grad_up,
        grad_down,
        rms_stats,
    )


MESH = pl.DeviceIdType.MESH
F32 = jnp.float32
BF16 = jnp.bfloat16
VMEM_BYTES = 62 * 1024 * 1024
C0 = math.sqrt(2.0 / math.pi)
C1 = 0.044715
ALL = slice(None)
ORDERS = (
    ("y", "zl", "x", "zh"),
    ("y", "zl", "x", "zh"),
    ("x", "y", "zl", "zh"),
    ("y", "x", "zl", "zh"),
    ("y", "x", "zl", "zh"),
    ("y", "x", "zl", "zh"),
    ("y", "zl", "x", "zh"),
    ("x", "y", "zl", "zh"),
)


def dot_nn(a, b):
    return lax.dot_general(a, b, (((1,), (0,)), ((), ())), preferred_element_type=F32)


def dot_nt(a, b):
    return lax.dot_general(a, b, (((1,), (1,)), ((), ())), preferred_element_type=F32)


def fft_points(re, im, sign):
    n = len(re)
    if n == 1:
        return re, im
    even_r, even_i = fft_points(re[0::2], im[0::2], sign)
    odd_r, odd_i = fft_points(re[1::2], im[1::2], sign)
    out_r, out_i = [None] * n, [None] * n
    for k in range(n // 2):
        if k == 0:
            turn_r, turn_i = odd_r[0], odd_i[0]
        elif 4 * k == n:
            if sign > 0:
                out_r[k], out_i[k] = even_r[k] - odd_i[k], even_i[k] + odd_r[k]
                out_r[k + n // 2], out_i[k + n // 2] = even_r[k] + odd_i[k], even_i[k] - odd_r[k]
            else:
                out_r[k], out_i[k] = even_r[k] + odd_i[k], even_i[k] - odd_r[k]
                out_r[k + n // 2], out_i[k + n // 2] = even_r[k] - odd_i[k], even_i[k] + odd_r[k]
            continue
        else:
            cos, sin = math.cos(2 * math.pi * k / n), sign * math.sin(2 * math.pi * k / n)
            turn_r = cos * odd_r[k] - sin * odd_i[k]
            turn_i = cos * odd_i[k] + sin * odd_r[k]
        out_r[k], out_i[k] = even_r[k] + turn_r, even_i[k] + turn_i
        out_r[k + n // 2], out_i[k + n // 2] = even_r[k] - turn_r, even_i[k] - turn_i
    return out_r, out_i


def spectrum_tables(blocks, phases):
    length = blocks * phases
    k = 2 * np.arange(blocks)[None, :] + 1
    angle = 2.0 * np.pi * np.arange(blocks)[:, None] * k / (4.0 * blocks)
    table = np.concatenate([np.cos(angle), -np.sin(angle)], axis=1)
    turn = 2.0 * np.pi * np.arange(phases)[:, None] * k / (4.0 * length)
    turns = np.stack([np.cos(turn), np.sin(turn)], axis=1)[:, :, None, :]
    return jnp.asarray(table, F32), jnp.asarray(np.broadcast_to(turns, (phases, 2, 8, blocks)), F32)


def place():
    row, seq = lax.axis_index("rows"), lax.axis_index("seq")
    return lax.div(row, 2), lax.rem(row, 2), lax.div(seq, 4), lax.rem(lax.div(seq, 2), 2), lax.rem(seq, 2)


def partner(axis):
    y, c, zh, zl, x = place()
    if axis == "core":
        return {"rows": 2 * y + 1 - c}
    if axis == "y":
        return {"rows": 2 * (1 - y) + c}
    if axis == "x":
        return {"seq": 4 * zh + 2 * zl + 1 - x}
    if axis == "zl":
        return {"seq": 4 * zh + 2 * (1 - zl) + x}
    return {"seq": 4 * (1 - zh) + 2 * zl + x}


def remote(src, dst, send_sem, recv_sem, target):
    return pltpu.make_async_remote_copy(
        src_ref=src, dst_ref=dst, send_sem=send_sem, recv_sem=recv_sem, device_id=target, device_id_type=MESH,
    )


def exchange(src, dst, send_sem, recv_sem, axis):
    return remote(src, dst, send_sem, recv_sem, partner(axis))


def greet(n):
    me = lax.axis_index("seq")
    barrier = pltpu.get_barrier_semaphore()
    for j in range(1, n):
        pl.semaphore_signal(barrier, inc=1, device_id={"seq": lax.rem(me + j, n)}, device_id_type=MESH)
    for axis in ("core", "y"):
        pl.semaphore_signal(barrier, inc=1, device_id=partner(axis), device_id_type=MESH)
    return barrier, n + 1


def aligned(index, size):
    return pl.ds(pl.multiple_of(index * size, size), size)


class Post:
    def __init__(self, n, source, target, sems):
        self.n, self.source, self.target, self.sems = n, source, target, sems

    def copies(self, sender):
        me = lax.axis_index("seq")
        for j in range(1, self.n):
            peer = lax.rem(me + j, self.n)
            come = sender(peer, me)
            yield remote(
                self.source(peer), self.target(come), self.sems.at[0, j], self.sems.at[1, come], {"seq": peer}
            )

    def start(self):
        me = lax.axis_index("seq")
        for copy in self.copies(lambda peer, me: me):
            copy.start()
        self.target(me)[...] = self.source(me)[...]

    def arrive(self):
        for copy in self.copies(lambda peer, me: peer):
            copy.wait_recv()

    def drain(self):
        for copy in self.copies(lambda peer, me: me):
            copy.wait_send()


def over_groups(each, blocks, body):
    for lane in range(0, blocks, 128):
        def step(g, carry):
            body(pl.multiple_of(g * 16, 16), lane)
            return carry
        lax.fori_loop(0, each // 16, step, 0)


def matmul_rows(out, left, right, size=256):
    for at in range(0, out.shape[0], size):
        out[at:at + size, :] = left(at, size, right)


def load_phases(spec, n, each, at, lane, half):
    re = [spec[pl.ds(p * each + at, 8), lane:lane + 128] for p in range(n)]
    im = [spec[pl.ds(p * each + at, 8), half + lane:half + lane + 128] for p in range(n)]
    return re, im


def turn_phases(re, im, turns, lane, sign):
    out_r, out_i = [re[0]], [im[0]]
    for p in range(1, len(re)):
        cos, sin = turns[p, 0, :, lane:lane + 128], turns[p, 1, :, lane:lane + 128]
        if sign > 0:
            out_r.append(re[p] * cos - im[p] * sin)
            out_i.append(im[p] * cos + re[p] * sin)
        else:
            out_r.append(re[p] * cos + im[p] * sin)
            out_i.append(im[p] * cos - re[p] * sin)
    return out_r, out_i


def by_halves(n, each, blocks, spec, work, stores, kept=None):
    def group(at, lane):
        halves = []
        if kept is not None:
            loaded = [
                [kept[pl.ds(k * each + at, 16), part + lane:part + lane + 128].astype(F32) for k in range(n)]
                for part in (0, blocks)
            ]
        for half in (0, 8):
            re, im = load_phases(spec, n, each, at + half, lane, blocks)
            old = None if kept is None else [[value[half:half + 8] for value in part] for part in loaded]
            halves.append(work(re, im, at + half, lane, old))
        for target, first, second in zip(stores, *halves):
            for k in range(n):
                for part in range(2):
                    value = jnp.concatenate([first[part][k], second[part][k]], axis=0).astype(BF16)
                    target[pl.ds(k * each + at, 16), part * blocks + lane:part * blocks + lane + 128] = value

    over_groups(each, blocks, group)


def to_lanes(source, table, spec):
    for at in range(0, spec.shape[0], 256):
        spec[at:at + 256, :] = dot_nn(source(at, 256), table[...])


def from_lanes(fin, table, size, store):
    for at in range(0, fin.shape[0], size):
        store(at, dot_nt(fin[at:at + size, :], table[...]) * (2.0 / fin.shape[1] / (fin.shape[0] // size)))


def over_rows(total, size, body):
    def step(i, carry):
        body(aligned(i, size))
        return carry
    lax.fori_loop(0, total // size, step, 0)


def over_lanes(width, body):
    def step(i, carry):
        body(aligned(i, 128))
        return carry
    lax.fori_loop(0, width // 128, step, 0)


def strided(ref, rows, start, lane, wide):
    return ref[pl.ds(start * wide + lane, rows, stride=wide), :]


def turn_rows(value, amount):
    return pltpu.roll(value, amount % value.shape[0], 0)


class Tree:
    def __init__(self, order, share, own, parts, gathered, sems):
        self.order = order + ("back_y", "back_core")
        self.share, self.own, self.parts, self.gathered, self.sems = share, own, parts, gathered, sems
        self.done = 0
        self.started = []

    def half(self, step, bit):
        y, c, zh, zl, x = place()
        here = dict(zh=zh, zl=zl, x=x, y=y)
        settled = self.order[:step]
        return tuple(here[a] if a in settled else (bit(here[a]) if a == self.order[step] else ALL) for a in ("zh", "zl", "x", "y"))

    def block(self, index):
        c = place()[1]
        return (self.share, index[:3] + (c,) + index[3:]) if self.own is None else (self.own, index)

    def copies(self, step):
        y, c, zh, zl, x = place()
        axis = self.order[step]
        gathered = self.gathered
        if axis == "core":
            src = self.share.at[:, :, :, 1 - c]
        elif axis == "back_y":
            src = gathered.at[c, y]
        elif axis == "back_core":
            src = gathered.at[c]
        else:
            ref, index = self.block(self.half(step, lambda bit: 1 - bit))
            src = ref.at[index]
        dst = src if axis.startswith("back") else self.parts[step]
        return exchange(src, dst, self.sems.at[0, step], self.sems.at[1, step], axis.replace("back_", ""))

    def start(self):
        self.copies(self.done).start()
        self.started.append(self.done)

    def add(self, index, part, at, target=None):
        own, index = self.block(index)
        size = 48

        def body(i, carry):
            here = aligned(i, size)
            value = own[index + (here, ALL)] + part[at + (here, ALL)]
            if target is None:
                own[index + (here, ALL)] = value
            else:
                target[here, :] = value
            return carry

        lax.fori_loop(0, part.shape[-2] // size, body, 0)

    def finish(self, go=True):
        y, c, zh, zl, x = place()
        step = self.done
        axis = self.order[step]
        self.copies(step).wait_recv()
        if not axis.startswith("back"):
            index = (ALL,) * 4 if axis == "core" else self.half(step, lambda bit: bit)
            free = [i for i, entry in enumerate(index) if entry is ALL or isinstance(entry, slice)]
            last = self.order[step + 1] == "back_y"
            for bits in itertools.product(range(2), repeat=len(free)):
                full = list(index)
                for i, bit in zip(free, bits):
                    full[i] = bit
                self.add(tuple(full), self.parts[step], bits, self.gathered.at[c, y] if last else None)
        self.done += 1
        if go and self.done < len(self.order):
            self.start()

    def drain(self):
        for step in self.started:
            self.copies(step).wait_send()


def tree_scratch(r, l):
    shapes = [(2, 2, 2, 2, r, l), (2, 2, 2, r, l), (2, 2, r, l), (2, r, l), (r, l)]
    return [pltpu.VMEM(shape, BF16) for shape in shapes] + [pltpu.SemaphoreType.DMA((2, 7))]


def whole_kernel(
    n, chunk,
    x_far, cot_far, taps_far, short_taps, skip, gain_mix, gain_mlp, segments, valid, w_in_far, w_out_far, w_up_far, w_down_far,
    table_wide, turns,
    out_far, flat_far, mid_far, turned_far, spec_taps_far, spec_gate_far,
    got_ua, got_ub, got_da, got_db, got_out, got_in0, got_in1, got_in2, tap_all, vectors,
    small, table, marks, marks_got, land, taps_got, query, saved, same, sent_one, sent_two, got_one, got_two, hand,
    tap_own, tap_got, tap_half, tap_part, vector_got,
    fetch, keep, near_sems, mark_sems, tap_sems, gate_sems, long_sems, back_sems, gated_sems, hand_sems,
    pair_sems, home_sems, home_send, home_recv, vector_sems,
    *tree_refs,
):
    me = lax.axis_index("seq")
    y, c, zh, zl, xbit = place()
    rows, blocks = query.shape[0], query.shape[1]
    width, hidden = w_up_far.shape
    each, wide, step = width // n, width // 128, blocks // 2
    side, linear = each // 2, blocks * wide
    at_top = jnp.logical_and(zh == 0, zl == 0)
    at_end = jnp.logical_and(zh == 1, zl == 1)
    chosen_chunk = jnp.logical_and(zh == y, zl == c)
    home = zh == y
    barrier, told = greet(n)
    for row, vector in ((9, skip), (10, gain_mix), (11, gain_mlp)):
        small[row, :] = vector[...]
    gain_one, gain_two = small[10:11, :], small[11:12, :]
    table[...] = table_wide[...].astype(BF16)

    trees, at = {}, 0
    for name, got, order in zip(("ua", "ub", "da", "db", "out"), (got_ua, got_ub, got_da, got_db, got_out), ORDERS):
        trees[name] = Tree(order, None, tree_refs[at], tree_refs[at + 1:at + 5], got, tree_refs[at + 5])
        at += 6
    for name, got, order in (("in0", got_in0, ORDERS[5]), ("in1", got_in1, ORDERS[6]), ("in2", got_in2, ORDERS[7])):
        trees[name] = Tree(("core",) + order, None, None, tree_refs[at:at + 5], got, tree_refs[at + 5])
        at += 6

    post_marks = Post(n, lambda d: marks, lambda p: marks_got.at[p], mark_sems)

    def posts(sent, got, sems):
        return [
            Post(n, lambda e, r=r: sent.at[r, aligned(e, each)], lambda p, r=r: got.at[r, aligned(p, each)], sems.at[r])
            for r in range(rows)
        ]

    posts_gate = posts(sent_one, got_one, gate_sems)
    posts_long = posts(sent_two, got_two, long_sems)
    posts_back = posts(sent_one, got_one, back_sems)
    posts_gated = posts(sent_two, got_two, gated_sems)

    def near_far(r, h, source):
        part = slice(h * step, (h + 1) * step)
        target = {"seq": lax.rem(me + 2, n)}
        return remote(source.at[r, part], land.at[1, r, part], near_sems.at[0, 0, r, h], near_sems.at[0, 1, r, h], target)

    def near_side(r, h, source):
        part = slice(h * step, (h + 1) * step)
        return exchange(source.at[r, part], land.at[0, r, part], near_sems.at[1, 0, r, h], near_sems.at[1, 1, r, h], "x")

    def tap_copy(e, taps_sent):
        return remote(taps_sent.at[aligned(e, each)], taps_got.at[aligned(me, each)], tap_sems.at[0, lax.rem(e, 2)], tap_sems.at[1, me], {"seq": e})

    def tap_spread(axis):
        at = 2 if axis == "core" else 3
        return exchange(taps_got, taps_got, tap_sems.at[at, 0], tap_sems.at[at, 1], axis)

    def side_copy(r):
        return exchange(hand.at[0, r], land.at[0, r], hand_sems.at[0, 0, r], hand_sems.at[0, 1, r], "x")

    def far_copy(r):
        target = {"seq": lax.rem(me + n - 2, n)}
        return remote(hand.at[1, r], land.at[1, r], hand_sems.at[1, 0, r], hand_sems.at[1, 1, r], target)

    def tap_core():
        return exchange(tap_own.at[1 - c], tap_got, home_sems.at[0, 0], home_sems.at[1, 0], "core")

    def tap_y():
        return exchange(tap_own.at[c, 1 - y], tap_half, home_sems.at[0, 1], home_sems.at[1, 1], "y")

    def home_copy(q, there):
        return remote(tap_part.at[q], tap_all.at[c, there], home_send.at[q], home_recv.at[there], {"seq": 4 * y + q})

    def tap_back_y():
        return exchange(tap_all.at[c], tap_all.at[c], home_sems.at[0, 2], home_sems.at[1, 2], "y")

    def tap_back_core():
        return exchange(tap_all.at[c], tap_all.at[c], home_sems.at[0, 3], home_sems.at[1, 3], "core")

    def front(near, x_in, taps, taps_sent, w_in, proj, turned, gate_wide):
        first = [
            pltpu.make_async_copy(src, dst, fetch.at[i])
            for i, (src, dst) in enumerate(((x_far, x_in), (taps_far, taps), (w_in_far, w_in)))
        ]
        for copy in first:
            copy.start()
        marks[...] = jnp.zeros_like(marks)
        for r in range(rows):
            marks[r:r + 1, :] = segments[r].astype(F32)
            marks[rows + r:rows + r + 1, :] = valid[r].astype(F32)
        for k in range(3):
            small[3 * k:3 * k + 3, :] = short_taps[:, k * width:(k + 1) * width]
        small[12:16, :] = jnp.zeros((4, width), F32)
        first[0].wait()

        def norm_row(r):
            for at in range(r * blocks, (r + 1) * blocks, 128):
                parts = [strided(x_in, 128, at, j, wide) for j in range(wide)]
                total = sum(jnp.sum(part * part, axis=-1, keepdims=True) for part in parts)
                scale = lax.rsqrt(total * (1.0 / width) + EPS)
                for j, part in enumerate(parts):
                    lanes = slice(j * 128, (j + 1) * 128)
                    near[0, r, at - r * blocks:at - r * blocks + 128, lanes] = (part * scale * gain_one[:, lanes]).astype(BF16)

        def send_near(r):
            for h in range(2):
                near_far(r, h, near.at[0]).start()

            @pl.when(xbit == 0)
            def _():
                for h in range(2):
                    near_side(r, h, near.at[0]).start()

        def hand_on(r):
            @pl.when(xbit == 1)
            def _():
                for h in range(2):
                    near_far(r, h, near.at[0]).wait_recv()
                    near_side(r, h, land.at[1]).start()

        norm_row(0)
        pl.semaphore_wait(barrier, told)
        send_near(0)
        post_marks.start()
        norm_row(1)
        send_near(1)
        first[1].wait()
        for j in range(wide):
            raw = strided(taps, blocks, 0, j, wide)
            low = raw - THRESH * jnp.tanh(raw * (1.0 / THRESH))
            taps_sent[j * 128:(j + 1) * 128, :] = low.T.astype(BF16)
        for xd in range(2):
            target = 4 * y + 2 * c + xd

            @pl.when(target != me)
            def _():
                tap_copy(target, taps_sent).start()

            @pl.when(target == me)
            def _():
                taps_got[aligned(me, each)] = taps_sent[aligned(me, each)]

        first[2].wait()

        def project(r, j):
            for k in (1, 2, 0):
                for at in range(0, width, 256):
                    cols = slice(k * width + at, k * width + at + 256)
                    proj[j, k, :, at:at + 256] = dot_nn(near[j, r], w_in[:, cols]).astype(BF16)

        project(0, 0)
        hand_on(0)
        post_marks.arrive()
        lane = lax.broadcasted_iota(jnp.int32, (rows, blocks), 1)
        now = marks[0:rows, :]
        found = []
        for j in (1, 2):
            before = marks_got[lax.rem(me + n - j, n), 0:rows, :]
            wrapped = me < j
            before = jnp.where(wrapped, pltpu.roll(before, 1, 1), before)
            kept = jnp.logical_and(before == now, jnp.logical_or(jnp.logical_not(wrapped), lane > 0))
            found.append(kept.astype(F32))
        columns = jnp.concatenate(found + [marks[rows:2 * rows, :], jnp.zeros((2, blocks), F32)], axis=0).T
        for s in range(3):
            for r in range(rows):
                same[s, r] = jnp.broadcast_to(columns[:, s * rows + r:s * rows + r + 1], (blocks, 128))

        def chunk_row(r):
            @pl.when(xbit == 0)
            def _():
                for h in range(2):
                    near_far(r, h, near.at[0]).wait_recv()

            for h in range(2):
                near_side(r, h, near.at[0]).wait_recv()
            for j in (1, 2):
                wrapped = jnp.logical_and(at_top, xbit == 0) if j == 1 else at_top

                @pl.when(wrapped)
                def _():
                    near[j, r] = turn_rows(land[j - 1, r].astype(F32), 1).astype(BF16)

                @pl.when(jnp.logical_not(wrapped))
                def _():
                    near[j, r] = land[j - 1, r]

                project(r, j)

            def lanes_step(lanes):
                def rows_step(here):
                    masks = [same[s, r, here, :] for s in range(3)]
                    value = []
                    for k in range(3):
                        total = small[3 * k:3 * k + 1, lanes] * proj[0, k, here, lanes].astype(F32)
                        total += small[3 * k + 1:3 * k + 2, lanes] * (proj[1, k, here, lanes].astype(F32) * masks[0])
                        total += small[3 * k + 2:3 * k + 3, lanes] * (proj[2, k, here, lanes].astype(F32) * masks[1])
                        value.append(total)
                    query[r, here, lanes] = value[0]
                    keys, values = value[1] * masks[2], value[2] * masks[2]
                    gate = value[1] * values
                    saved[0, r, here, lanes] = keys.astype(BF16)
                    saved[1, r, here, lanes] = values.astype(BF16)
                    saved[2, r, here, lanes] = gate.astype(BF16)
                    gate_wide[here, lanes] = gate

                over_rows(blocks, 64, rows_step)

            over_lanes(width, lanes_step)
            sent_one[r] = gate_wide[...].T.astype(BF16)
            posts_gate[r].start()

        chunk_row(0)
        project(1, 0)
        hand_on(1)

        @pl.when(chosen_chunk)
        def _():
            for p in range(n):
                @pl.when(me != p)
                def _():
                    remote(
                        taps_sent.at[aligned(me, each)], taps_got.at[p * each:(p + 1) * each],
                        tap_sems.at[0, 0], tap_sems.at[1, p], {"seq": p},
                    ).wait_recv()
            tap_spread("core").start()

        @pl.when(jnp.logical_and(zh == y, zl != c))
        def _():
            tap_spread("core").wait_recv()

        @pl.when(zh == y)
        def _():
            tap_spread("y").start()

        chunk_row(1)

        for j in range(3):
            for r in range(rows):
                value = near[j, r].astype(F32)
                if j > 0:
                    value = value * same[j - 1, r, :, 0:1]
                turned[j, :, r * blocks:(r + 1) * blocks] = value.T.astype(BF16)
        kept = pltpu.make_async_copy(turned, turned_far, keep.at[2])
        kept.start()
        for r in range(rows):
            for h in range(2):
                near_far(r, h, near.at[0]).wait_send()
                near_side(r, h, near.at[0]).wait_send()
        for xd in range(2):
            target = 4 * y + 2 * c + xd

            @pl.when(target != me)
            def _():
                tap_copy(target, taps_sent).wait_send()

        kept.wait()

    pl.run_scoped(
        front,
        pltpu.VMEM((3, rows, blocks, width), BF16),
        pltpu.VMEM(x_far.shape, F32),
        pltpu.VMEM(taps_far.shape, F32),
        pltpu.VMEM((width, blocks), BF16),
        pltpu.VMEM(w_in_far.shape, BF16),
        pltpu.VMEM((3, 3, blocks, width), BF16),
        pltpu.VMEM(turned_far.shape, BF16),
        pltpu.VMEM((blocks, width), F32),
    )

    def conv(fin, spec, spec_taps, spec_gate):
        @pl.when(zh != y)
        def _():
            tap_spread("y").wait_recv()

        to_lanes(lambda at, size: taps_got[at:at + size], table, spec)

        def taps_group(at, lane):
            re, im = load_phases(spec, n, each, at, lane, blocks)
            re, im = turn_phases(re, im, turns, lane, -1)
            re, im = fft_points(re, im, -1)
            for k in range(n):
                spec_taps[pl.ds(k * each + at, 8), lane:lane + 128] = re[k]
                spec_taps[pl.ds(k * each + at, 8), blocks + lane:blocks + lane + 128] = im[k]

        def both_halves(at, lane):
            taps_group(at, lane)
            taps_group(at + 8, lane)

        over_groups(each, blocks, both_halves)
        keeps = [pltpu.make_async_copy(spec_taps, spec_taps_far, keep.at[0])]
        keeps[0].start()

        for r in range(rows):
            posts_gate[r].arrive()
            to_lanes(lambda at, size: got_one[r, at:at + size], table, spec)

            def work(re, im, at, lane, kept):
                re, im = turn_phases(re, im, turns, lane, -1)
                re, im = fft_points(re, im, -1)
                tap_r, tap_i = load_phases(spec_taps, n, each, at, lane, blocks)
                out_r = [re[k] * tap_r[k] - im[k] * tap_i[k] for k in range(n)]
                out_i = [re[k] * tap_i[k] + im[k] * tap_r[k] for k in range(n)]
                out_r, out_i = fft_points(out_r, out_i, 1)
                out_r, out_i = turn_phases(out_r, out_i, turns, lane, 1)
                return (re, im), (out_r, out_i)

            by_halves(n, each, blocks, spec, work, (spec_gate.at[r], fin))

            def store(at, value):
                sent_two[r, at:at + value.shape[0]] = value.astype(BF16)

            from_lanes(fin, table, each, store)
            posts_long[r].start()
        keeps.append(pltpu.make_async_copy(spec_gate, spec_gate_far, keep.at[1]))
        keeps[1].start()
        for copy in keeps:
            copy.wait()

    def middle(act, grad_act, turned, turned_cot, mixed, mix_back):
        def mlp(first, w_out, w_up, w_down, x, cot, cot_near, cot_low, resid, long_out, acc_out, acc_back, normed, whole_out, mid):
            vectors[...] = jnp.zeros_like(vectors)
            kept = []
            first[0].wait()
            for r in range(rows):
                tokens = slice(r * blocks, (r + 1) * blocks)
                posts_long[r].arrive()
                gated = saved[2, r].astype(F32)
                long_out[...] = got_two[r].astype(F32).T + small[9:10, :] * gated
                low = (query[r] * long_out[...]).astype(BF16)
                mixer = dot_nn(low, w_out[...])
                mixed[r] = low.T
                mask = same[2, r, :, 0:1]
                vectors[13:14, :] += jnp.sum(mixer * mixer * mask, axis=0, keepdims=True)
                if r == 0:
                    first[1].wait()
                    first[2].wait()
                for j in range(wide):
                    lanes = slice(j * 128, (j + 1) * 128)
                    resid[:, lanes] = strided(x, blocks, r * blocks, j, wide) + mixer[:, lanes]
                    cot_near[:, lanes] = strided(cot, blocks, r * blocks, j, wide)
                cot_low[...] = cot_near[...].astype(BF16)
                state = resid[...]
                scale = lax.rsqrt(jnp.mean(state * state, axis=-1, keepdims=True) + EPS)
                normed[...] = (state * scale * gain_two).astype(BF16)
                acc_out[...] = jnp.zeros_like(acc_out)
                acc_back[...] = jnp.zeros_like(acc_back)
                if r == 0:
                    first[3].wait()
                    first[4].wait()

                def hidden_step(j, carry):
                    cols = aligned(j, chunk)
                    up_val = dot_nn(normed[...], w_up[:, cols])
                    square = up_val * up_val
                    tanh = jnp.tanh(up_val * (C0 + (C0 * C1) * square))
                    half = 0.5 * (1.0 + tanh)
                    act_low = (up_val * half).astype(BF16)
                    slope = half + (0.5 * up_val) * (1.0 - tanh * tanh) * (C0 + (3.0 * C0 * C1) * square)
                    act[tokens, cols] = act_low
                    acc_out[...] += dot_nn(act_low, w_down[cols, :])
                    grad = dot_nt(cot_low[...], w_down[cols, :])
                    grad_low = (grad * slope).astype(BF16)
                    grad_act[tokens, cols] = grad_low
                    acc_back[...] += dot_nt(grad_low, w_up[:, cols])
                    return carry

                lax.fori_loop(0, hidden // chunk, hidden_step, 0)
                state = resid[...]
                scale = lax.rsqrt(jnp.mean(state * state, axis=-1, keepdims=True) + EPS)
                grad = acc_back[...]
                vectors[11:12, :] += jnp.sum(grad * state * scale, axis=0, keepdims=True)
                scaled = grad * gain_two
                shift = jnp.mean(scaled * state, axis=-1, keepdims=True) * (scale * scale * scale)
                grad_mid = cot_near[...] + (scaled * scale - state * shift)
                mix_back[r] = grad_mid.astype(BF16)
                grad_prod = dot_nt(mix_back[r], w_out[...])
                grad_long = grad_prod * query[r]
                posts_gate[r].drain()
                sent_one[r] = grad_long.T.astype(BF16)
                posts_back[r].start()
                saved[3, r] = grad_long.astype(BF16)
                vectors[9:10, :] += jnp.sum(grad_long * saved[2, r].astype(F32), axis=0, keepdims=True)
                saved[2, r] = (grad_prod * long_out[...]).astype(BF16)
                mlp = acc_out[...]
                vectors[14:15, :] += jnp.sum(mlp * mlp * mask, axis=0, keepdims=True)
                whole = resid[...] + mlp
                vectors[12:13, :] += jnp.sum(whole * whole * mask, axis=0, keepdims=True)
                vectors[15:16, :] += jnp.broadcast_to(jnp.sum(mask, axis=0, keepdims=True) * (1.0 / width), (1, width))
                if r > 0:
                    for copy in kept:
                        copy.wait()
                    kept.clear()
                for j in range(wide):
                    place_at = pl.ds(j, blocks, stride=wide)
                    whole_out[place_at, :] = whole[:, j * 128:(j + 1) * 128]
                    mid[place_at, :] = grad_mid[:, j * 128:(j + 1) * 128]
                part_rows = slice(r * blocks * wide, (r + 1) * blocks * wide)
                for i, (src, dst) in enumerate(((whole_out, out_far), (mid, mid_far))):
                    kept.append(pltpu.make_async_copy(src, dst.at[part_rows], keep.at[3 + i]))
                    kept[-1].start()
                turned[:, tokens] = normed[...].T
                turned_cot[:, tokens] = cot_low[...].T

            for copy in kept:
                copy.wait()

        def fetched(w_out, w_up, w_down, x, cot):
            first = [
                pltpu.make_async_copy(src, dst, fetch.at[i])
                for i, (src, dst) in enumerate(((w_out_far, w_out), (x_far, x), (cot_far, cot), (w_up_far, w_up), (w_down_far, w_down)))
            ]
            for copy in first:
                copy.start()
            pl.run_scoped(
                conv,
                pltpu.VMEM((width, 2 * blocks), BF16),
                pltpu.VMEM((width, 2 * blocks), F32),
                pltpu.VMEM((width, 2 * blocks), F32),
                pltpu.VMEM(spec_gate_far.shape, BF16),
            )
            pl.run_scoped(
                functools.partial(mlp, first, w_out, w_up, w_down, x, cot),
                pltpu.VMEM((blocks, width), F32),
                pltpu.VMEM((blocks, width), BF16),
                *[pltpu.VMEM((blocks, width), F32)] * 4,
                pltpu.VMEM((blocks, width), BF16),
                *[pltpu.VMEM((linear, 128), F32)] * 2,
            )

        pl.run_scoped(
            fetched,
            pltpu.VMEM(w_out_far.shape, BF16),
            pltpu.VMEM(w_up_far.shape, BF16),
            pltpu.VMEM(w_down_far.shape, BF16),
            pltpu.VMEM(x_far.shape, F32),
            pltpu.VMEM(x_far.shape, F32),
        )

        def sums(up_a, up_b, down_a, down_b, out, spec_taps, spec_gate, fin, spec, spec_sum):
            near = [
                pltpu.make_async_copy(src, dst, fetch.at[i])
                for i, (src, dst) in enumerate(((spec_taps_far, spec_taps), (spec_gate_far, spec_gate)))
            ]
            for copy in near:
                copy.start()
            quarter, part = width // 4, hidden // n
            pairs = [(share, trees[name].own) for name, share in zip(("ua", "ub", "da", "db", "out"), (up_a, up_b, down_a, down_b, out))]

            def pair_copy(i):
                return exchange(pairs[i][0].at[:, :, :, 1 - c], pairs[i][1], pair_sems.at[0, i], pair_sems.at[1, i], "core")

            def put_rows(share, half, lanes, value):
                for s in range(n):
                    for core in range(2):
                        low = (2 * s + core) * side
                        share[s // 4, (s // 2) % 2, s % 2, core, half, :, lanes] = value[low:low + side]

            def add_pair(i):
                share, pair = pairs[i]
                pair_copy(i).wait_recv()
                size = 48
                for a in range(2):
                    for b in range(2):
                        for d in range(2):
                            for e in range(2):
                                def body(k, carry):
                                    here = aligned(k, size)
                                    pair[a, b, d, e, here, :] = pair[a, b, d, e, here, :] + share[a, b, d, c, e, here, :]
                                    return carry
                                lax.fori_loop(0, pair.shape[4] // size, body, 0)


            def conv_row(r):
                posts_back[r].arrive()
                to_lanes(lambda at, size: got_one[r, at:at + size], table, spec)

                def work(re, im, at, lane, kept):
                    re, im = turn_phases(re, im, turns, lane, -1)
                    re, im = fft_points(re, im, -1)
                    tap_r, tap_i = load_phases(spec_taps, n, each, at, lane, blocks)
                    gate_r, gate_i = kept
                    out_r, out_i = [], []
                    for k in range(n):
                        here = pl.ds(k * each + at, 8)
                        lanes, other = slice(lane, lane + 128), slice(blocks + lane, blocks + lane + 128)
                        old_r, old_i = gate_r[k], gate_i[k]
                        sum_r, sum_i = old_r * re[k] + old_i * im[k], old_r * im[k] - old_i * re[k]
                        if r == 0:
                            spec_sum[here, lanes] = sum_r
                            spec_sum[here, other] = sum_i
                        else:
                            spec_sum[here, lanes] += sum_r
                            spec_sum[here, other] += sum_i
                        out_r.append(tap_r[k] * re[k] + tap_i[k] * im[k])
                        out_i.append(tap_r[k] * im[k] - tap_i[k] * re[k])
                    out_r, out_i = fft_points(out_r, out_i, 1)
                    return (turn_phases(out_r, out_i, turns, lane, 1),)

                by_halves(n, each, blocks, spec, work, (fin,), spec_gate.at[r])

                posts_long[r].drain()

                def store(at, value):
                    sent_two[r, at:at + value.shape[0]] = value.astype(BF16)

                from_lanes(fin, table, each, store)
                posts_gated[r].start()
            def up_part(i):
                for half in range(2):
                    low = half * (hidden // 2) + i * (hidden // 4)
                    value = dot_nn(turned[...], grad_act[:, low:low + hidden // 4]).astype(BF16)
                    put_rows((up_a, up_b)[i], half, ALL, value)
                pair_copy(i).start()

            def down_parts():
                for s in range(n):
                    value = dot_nn(turned_cot[...], act[:, s * part:(s + 1) * part]).astype(BF16)
                    for core in range(2):
                        for half in range(2):
                            low = (2 * core + half) * quarter
                            down_a[s // 4, (s // 2) % 2, s % 2, core, half] = value[low:low + quarter // 2]
                            down_b[s // 4, (s // 2) % 2, s % 2, core, half] = value[low + quarter // 2:low + quarter]
                pair_copy(2).start()
                pair_copy(3).start()

            def out_part():
                for half in range(2):
                    low = half * (width // 2)
                    value = sum(dot_nn(mixed[r], mix_back[r, :, low:low + width // 2]) for r in range(rows)).astype(BF16)
                    put_rows(out, half, ALL, value)
                pair_copy(4).start()

            def tap_row():
                def work_taps(re, im, at, lane, kept):
                    re, im = fft_points(re, im, 1)
                    return (turn_phases(re, im, turns, lane, 1),)

                by_halves(n, each, blocks, spec_sum, work_taps, (fin,))

                def store_taps(at, value):
                    p = at // each
                    for half in range(2):
                        tap_own[half, p // 4, p % 4] = value[half * side:(half + 1) * side].astype(BF16)

                from_lanes(fin, table, each, store_taps)
                tap_core().start()

            up_part(0)
            up_part(1)
            add_pair(0)
            trees["ua"].start()
            for copy in near:
                copy.wait()
            conv_row(0)
            down_parts()
            conv_row(1)
            add_pair(1)
            tap_row()
            trees["ub"].start()
            add_pair(2)
            trees["da"].start()
            out_part()
            add_pair(4)
            add_pair(3)
            for i in range(5):
                pair_copy(i).wait_send()

        pl.run_scoped(
            sums,
            *[pltpu.VMEM(trees[name].own.shape[:3] + (2,) + trees[name].own.shape[3:], BF16) for name in ("ua", "ub", "da", "db", "out")],
            pltpu.VMEM((width, 2 * blocks), F32),
            pltpu.VMEM((rows, width, 2 * blocks), BF16),
            pltpu.VMEM((width, 2 * blocks), BF16),
            pltpu.VMEM((width, 2 * blocks), F32),
            pltpu.VMEM((width, 2 * blocks), F32),
        )

    pl.run_scoped(
        middle,
        pltpu.VMEM((rows * blocks, hidden), BF16),
        pltpu.VMEM((rows * blocks, hidden), BF16),
        pltpu.VMEM((width, rows * blocks), BF16),
        pltpu.VMEM((width, rows * blocks), BF16),
        pltpu.VMEM((rows, width, blocks), BF16),
        pltpu.VMEM((rows, blocks, width), BF16),
    )

    def token_phase(turned, w_in, x, mid, gate_back, short, part_proj, grad_norm, gain_lanes, share0, share1, share2):
        for k, share in enumerate((share0, share1, share2)):
            trees["in%d" % k].share = share
        near = [
            pltpu.make_async_copy(src, dst, fetch.at[i])
            for i, (src, dst) in enumerate((
                (w_in_far, w_in), (turned_far, turned), (x_far, x), (mid_far, mid),
            ))
        ]
        for copy in near:
            copy.start()
        tap_core().wait_recv()
        for half in range(2):
            for q in range(4):
                tap_own[c, half, q] = tap_own[c, half, q] + tap_got[half, q]
        tap_y().start()

        def token_row(r):
            tokens = slice(r * blocks, (r + 1) * blocks)
            posts_gated[r].arrive()
            gate_back[...] = got_two[r].astype(F32).T

            def lanes_step(lanes):
                skip = small[9:10, lanes]

                def rows_step(here):
                    there = pl.ds(pl.multiple_of(r * blocks + here.start, 64), here.size)
                    grad = gate_back[here, lanes] + skip * saved[3, r, here, lanes].astype(F32)
                    short[there, lanes] = saved[2, r, here, lanes]
                    second = pl.ds(pl.multiple_of(lanes.start + width, 128), 128)
                    third = pl.ds(pl.multiple_of(lanes.start + 2 * width, 128), 128)
                    short[there, second] = (grad * saved[1, r, here, lanes].astype(F32)).astype(BF16)
                    short[there, third] = (grad * saved[0, r, here, lanes].astype(F32)).astype(BF16)

                over_rows(blocks, 64, rows_step)

            over_lanes(width, lanes_step)

        def spread(r, j):
            def lanes_step(lanes):
                def rows_step(here):
                    there = pl.ds(pl.multiple_of(r * blocks + here.start, 64), here.size)
                    for k in range(3):
                        cols = pl.ds(pl.multiple_of(lanes.start + k * width, 128), 128)
                        value = short[there, cols].astype(F32) * small[3 * k + j:3 * k + j + 1, lanes]
                        if j > 0:
                            value = value * same[j - 1, r, here, :]
                        part_proj[here, cols] = value.astype(BF16)

                over_rows(blocks, 64, rows_step)

            over_lanes(width, lanes_step)
            return dot_nt(part_proj[...], w_in[...])

        def send_hand(r):
            hand[0, r] = spread(r, 1).astype(BF16)
            side_copy(r).start()
            hand[1, r] = spread(r, 2).astype(BF16)

            @pl.when(xbit == 0)
            def _():
                far_copy(r).start()

        def hand_on(r):
            @pl.when(xbit == 1)
            def _():
                side_copy(r).wait_recv()
                hand[1, r] = (hand[1, r].astype(F32) + land[0, r].astype(F32)).astype(BF16)
                far_copy(r).start()

        def weight_part(k):
            share = trees["in%d" % k].share
            for half in range(2):
                low = k * width + half * (width // 2)
                cols = slice(low, low + width // 2)
                lanes = slice(half * (width // 2), (half + 1) * (width // 2))
                total = None
                for j in range(3):
                    value = dot_nn(turned[j], short[:, cols])
                    vectors[3 * k + j:3 * k + j + 1, lanes] = jnp.sum(value * w_in[:, cols].astype(F32), axis=0, keepdims=True)
                    value = value * small[3 * k + j:3 * k + j + 1, lanes]
                    total = value if total is None else total + value
                product = total * w_in[:, cols].astype(F32)
                gain_lanes[...] += sum(product[:, at:at + 128] for at in range(0, width // 2, 128))
                total = total.astype(BF16)
                for s in range(n):
                    for core in range(2):
                        block = (2 * s + core) * side
                        share[s // 4, (s // 2) % 2, s % 2, core, half] = total[block:block + side]
            trees["in%d" % k].start()

        def last_row(r):
            tokens = slice(r * blocks, (r + 1) * blocks)

            @pl.when(xbit == 0)
            def _():
                side_copy(r).wait_recv()
                grad_norm[r] += land[0, r].astype(F32)

            far_copy(r).wait_recv()
            late = land[1, r].astype(F32)

            @pl.when(at_end)
            def _():
                grad_norm[r] += turn_rows(late, blocks - 1)

            @pl.when(jnp.logical_not(at_end))
            def _():
                grad_norm[r] += late

            grad = grad_norm[r]
            parts = [strided(x, blocks, r * blocks, j, wide) for j in range(wide)]
            total = sum(jnp.sum(part * part, axis=-1, keepdims=True) for part in parts)
            scale = lax.rsqrt(total * (1.0 / width) + EPS)
            inner = 0.0
            scaled = []
            for j, part in enumerate(parts):
                lanes = slice(j * 128, (j + 1) * 128)
                piece = grad[:, lanes]
                scaled.append(piece * gain_one[:, lanes])
                inner += jnp.sum(scaled[j] * part, axis=-1, keepdims=True)
            shift = inner * (1.0 / width) * (scale * scale * scale)
            for j, part in enumerate(parts):
                place_at = pl.ds(r * linear + j, blocks, stride=wide)
                mid[place_at, :] += scaled[j] * scale - part * shift
            done = slice(r * linear, (r + 1) * linear)
            ready.append(pltpu.make_async_copy(mid.at[done], flat_far.at[done], keep.at[r]))
            ready[-1].start()

        def tap_home():
            tap_y().wait_recv()
            for q in range(4):
                tap_part[q] = tap_own[c, y, q] + tap_half[q]
            for q in range(4):
                @pl.when(4 * y + q != me)
                def _():
                    home_copy(q, me).start()

                @pl.when(4 * y + q == me)
                def _():
                    tap_all[c, me] = tap_part[q]

        def tap_return():
            @pl.when(home)
            def _():
                for j in range(1, n):
                    peer = lax.rem(me + j, n)
                    remote(tap_part.at[0], tap_all.at[c, peer], home_send.at[0], home_recv.at[peer], {"seq": peer}).wait_recv()
                tap_back_y().start()

        def tap_share():
            @pl.when(jnp.logical_not(home))
            def _():
                tap_back_y().wait_recv()

            tap_back_core().start()

        def vector_copy(step):
            axis = ("core", "y", "x", "zl", "zh")[step]
            return exchange(vectors, vector_got.at[step], vector_sems.at[0, step], vector_sems.at[1, step], axis)

        def vector_start():
            vectors[10:11, :] = jnp.sum(gain_lanes[...].T, axis=0, keepdims=True) / gain_one
            vector_copy(0).start()

        def vector_finish(step):
            vector_copy(step).wait()
            vectors[...] += vector_got[step]
            if step < 4:
                vector_copy(step + 1).start()

        def whole_norm():
            for r in range(rows):
                grad_norm[r] = spread(r, 0)
            for copy in near[2:4]:
                copy.wait()

        ready = []
        gain_lanes[...] = jnp.zeros_like(gain_lanes)
        trees["ua"].finish()
        trees["db"].start()
        token_row(0)
        near[0].wait()
        send_hand(0)
        trees["ub"].finish()
        tap_home()
        trees["da"].finish()
        token_row(1)
        send_hand(1)
        trees["ua"].finish()
        near[1].wait()
        weight_part(0)
        hand_on(0)
        trees["in0"].finish()
        weight_part(1)
        weight_part(2)
        hand_on(1)
        trees["db"].finish()
        whole_norm()
        trees["da"].finish()
        trees["in1"].finish()
        vector_start()
        trees["ua"].finish()
        trees["in2"].finish()
        trees["in0"].finish()
        trees["out"].start()
        trees["ub"].finish()
        trees["db"].finish()
        vector_finish(0)
        trees["da"].finish()
        trees["in2"].finish()
        trees["in1"].finish()
        tap_return()
        trees["db"].finish()
        trees["in0"].finish()
        trees["out"].finish()
        trees["ub"].finish()
        trees["in1"].finish()
        last_row(0)
        trees["out"].finish()
        trees["da"].finish()
        vector_finish(1)
        trees["in0"].finish()
        trees["in2"].finish()
        trees["db"].finish()
        trees["in1"].finish()
        last_row(1)
        trees["out"].finish()
        trees["ua"].finish()
        trees["ub"].finish()
        vector_finish(2)
        trees["da"].finish()
        tap_share()
        trees["in2"].finish()
        trees["db"].finish()
        trees["in0"].finish()
        trees["in1"].finish()
        trees["out"].finish()
        trees["ua"].finish()
        trees["ub"].finish()
        trees["in2"].finish()
        vector_finish(3)
        tap_back_core().wait_recv()
        trees["in0"].finish()
        trees["db"].finish()
        trees["in1"].finish()
        trees["ub"].finish()
        trees["out"].finish()
        trees["in0"].finish()
        trees["ua"].finish()
        trees["in2"].finish()
        vector_finish(4)
        trees["in1"].finish()
        trees["out"].finish()
        trees["da"].finish()
        trees["in2"].finish()
        for copy in ready:
            copy.wait()

        for tree in trees.values():
            tree.drain()
        for post in [post_marks] + posts_back + posts_gated:
            post.drain()
        for r in range(rows):
            side_copy(r).wait_send()
            far_copy(r).wait_send()
        tap_core().wait_send()
        tap_y().wait_send()
        for q in range(4):
            @pl.when(4 * y + q != me)
            def _():
                home_copy(q, me).wait_send()

        @pl.when(home)
        def _():
            tap_back_y().wait_send()

        tap_back_core().wait_send()

        @pl.when(chosen_chunk)
        def _():
            tap_spread("core").wait_send()

        @pl.when(zh == y)
        def _():
            tap_spread("y").wait_send()

    pl.run_scoped(
        token_phase,
        pltpu.VMEM(turned_far.shape, BF16),
        pltpu.VMEM(w_in_far.shape, BF16),
        pltpu.VMEM(x_far.shape, F32),
        pltpu.VMEM(x_far.shape, F32),
        pltpu.VMEM((blocks, width), F32),
        pltpu.VMEM((rows * blocks, 3 * width), BF16),
        pltpu.VMEM((blocks, 3 * width), BF16),
        pltpu.VMEM((rows, blocks, width), F32),
        pltpu.VMEM((width, 128), F32),
        *[pltpu.VMEM((2, 2, 2, 2, 2, side, width // 2), BF16)] * 3,
    )


def last_kernel(
    block_in, flat_in, got_ua, got_ub, got_da, got_db, got_out, got_in0, got_in1, got_in2, tap_all, taps, vectors,
    out, grad_flat, gain_mix, grad_in, grad_taps, grad_kernel, grad_skip, grad_out, gain_mlp, grad_up, grad_down, rms,
):
    out[...] = block_in[...]
    grad_flat[...] = flat_in[...]
    width = vectors.shape[1]
    side, wide, blocks = got_out.shape[2], width // 128, tap_all.shape[3]
    half_up = grad_up.shape[1] // 2
    for got, target, low, skip in (
        (got_ua, grad_up, 0, half_up), (got_ub, grad_up, half_up // 2, half_up), (got_out, grad_out, 0, width // 2),
        (got_in0, grad_in, 0, width // 2), (got_in1, grad_in, width, width // 2), (got_in2, grad_in, 2 * width, width // 2),
    ):
        l = got.shape[3]
        for half in range(2):
            for core in range(2):
                at = low + half * skip
                target[core * side:(core + 1) * side, at:at + l] = got[core, half].astype(F32)
    grad_down[...] = jnp.concatenate(
        [got[core, half] for core in range(2) for half in range(2) for got in (got_da, got_db)], axis=0
    ).astype(F32).T
    value = jnp.concatenate(
        [tap_all[core, s] for s in range(tap_all.shape[1]) for core in range(2)], axis=0
    ).astype(F32).T
    for j in range(wide):
        place_at = pl.ds(j, blocks, stride=wide)
        tanh = jnp.tanh(taps[place_at, :] * (1.0 / THRESH))
        grad_kernel[place_at, :] = value[:, j * 128:(j + 1) * 128] * (tanh * tanh)
    for k in range(3):
        grad_taps[:, k * width:(k + 1) * width] = vectors[3 * k:3 * k + 3, :]
    for target, row in ((grad_skip, 9), (gain_mix, 10), (gain_mlp, 11)):
        target[...] = vectors[row, :]
    total = jnp.sum(vectors[12:16, :], axis=1, keepdims=True)
    found = jnp.sqrt(total / (jnp.maximum(total[3:4, :], 1.0) * width))
    for i in range(3):
        rms[i] = found[i, 0]


def call(body, outs, scratch, inputs, collective_id, far=(), far_outs=()):
    return pl.pallas_call(
        body,
        out_shape=tuple(jax.ShapeDtypeStruct(*out) for out in outs),
        in_specs=[pl.BlockSpec(memory_space=pl.ANY if i in far else pltpu.VMEM) for i in range(len(inputs))],
        out_specs=tuple(pl.BlockSpec(memory_space=pl.ANY if i in far_outs else pltpu.VMEM) for i in range(len(outs))),
        scratch_shapes=scratch,
        compiler_params=pltpu.CompilerParams(
            vmem_limit_bytes=VMEM_BYTES, collective_id=collective_id, has_side_effects=True
        ),
    )(*inputs)


def local(
    block_in, segment_ids, valid_mask, cotangent, gain_mix, in_proj, short_taps, long_kernel,
    skip_gain, out_proj, gain_mlp, up_proj, down_proj,
):
    rows, blocks, _, width = block_in.shape
    hidden = up_proj.shape[1]
    n = lax.axis_size("seq")
    each = width // n
    tokens = rows * blocks
    side, wide = each // 2, width // 128
    chunk = 512
    x = block_in.reshape(tokens * wide, 128)
    cot = cotangent.reshape(tokens * wide, 128)
    raw = long_kernel.reshape(blocks * wide, 128)
    segments = segment_ids.reshape(rows, 1, blocks)
    valid = valid_mask.reshape(rows, 1, blocks)
    table, turns = spectrum_tables(blocks, n)
    dma = pltpu.SemaphoreType.DMA
    bits = (2, 2, 2, 2, 2)
    up_shape = bits[1:] + (side, hidden // 4)
    down_shape = bits[1:] + (width // 8, hidden // n)
    out_shape = bits[1:] + (side, width // 2)
    own_shapes = (up_shape, up_shape, down_shape, down_shape, out_shape)
    low = lambda *shape: pltpu.VMEM(shape, BF16)
    full = lambda *shape: pltpu.VMEM(shape, F32)

    trees = []
    for shape in own_shapes:
        trees += tree_scratch(*shape[4:])
    for _ in range(3):
        trees += tree_scratch(*out_shape[4:])
    gots = [(2, 2) + shape[4:] for shape in own_shapes + (out_shape,) * 3]
    quarter = (4, side, blocks)
    pair = (rows, 2, n)
    block_out, grad_flat, _, _, _, _, *gathered, taps_back, vectors = call(
        functools.partial(whole_kernel, n, chunk),
        [
            (x.shape, F32),
            (x.shape, F32),
            (x.shape, F32),
            ((3, width, tokens), BF16),
            ((width, 2 * blocks), F32),
            ((rows, width, 2 * blocks), BF16),
            *[(shape, BF16) for shape in gots],
            ((2, n, side, blocks), BF16),
            ((16, width), F32),
        ],
        [
            full(16, width), low(*table.shape), full(8, blocks), full(n, 8, blocks), low(2, rows, blocks, width), low(width, blocks),
            full(rows, blocks, width), low(4, rows, blocks, width), full(3, rows, blocks, 128),
            low(rows, width, blocks), low(rows, width, blocks), low(rows, width, blocks), low(rows, width, blocks),
            low(2, rows, blocks, width),
            low(2, 2, *quarter), low(2, *quarter), low(*quarter), low(*quarter), full(5, 16, width),
            dma((5,)), dma((5,)), dma((2, 2, rows, 2)), dma((2, n)), dma((4, n)),
            dma(pair), dma(pair), dma(pair), dma(pair), dma((2, 2, rows)),
            dma((2, 5)), dma((2, 4)), dma((4,)), dma((n,)), dma((2, 5)),
        ] + trees,
        (x, cot, raw, short_taps, skip_gain, gain_mix, gain_mlp, segments, valid, in_proj, out_proj, up_proj, down_proj, table, turns),
        1,
        far=(0, 1, 2, 9, 10, 11, 12),
        far_outs=range(6),
    )
    inputs = (block_out, grad_flat, *gathered, taps_back, raw, vectors)
    near = pl.BlockSpec(memory_space=pltpu.VMEM)
    outs = [
        x.shape, x.shape, (width,), (each, 3 * width), (3, 3 * width), raw.shape, (width,), (each, width), (width,),
        (each, hidden), (hidden // n, width), (3,),
    ]
    results = pl.pallas_call(
        last_kernel,
        out_shape=tuple(jax.ShapeDtypeStruct(shape, F32) for shape in outs),
        in_specs=[near] * len(inputs),
        out_specs=(near,) * 11 + (pl.BlockSpec(memory_space=pltpu.SMEM),),
        compiler_params=pltpu.CompilerParams(vmem_limit_bytes=VMEM_BYTES),
    )(*inputs)
    shapes = {0: block_in.shape, 1: block_in.shape, 5: long_kernel.shape}
    return tuple(value.reshape(shapes.get(i, value.shape)) for i, value in enumerate(results))


def chosen(block_in, *rest):
    rows, blocks, _, width = block_in.shape
    n = lax.axis_size("seq")
    fits = blocks % (32 * n) == 0 and width % (32 * n) == 0 and n == 8 and rows == 2 and lax.axis_size("rows") == 4
    return (local if fits else general_local)(block_in, *rest)


def solution(mesh):
    return jax.shard_map(
        chosen,
        mesh=mesh,
        in_specs=(
            P("rows", None, "seq", None),
            P("rows", None, "seq"),
            P("rows", None, "seq"),
            P("rows", None, "seq", None),
            P(),
            P(),
            P(),
            P(None, "seq", None),
            P(),
            P(),
            P(),
            P(),
            P(),
        ),
        out_specs=(
            P("rows", None, "seq", None),
            P("rows", None, "seq", None),
            P(),
            P("seq", None),
            P(),
            P(None, "seq", None),
            P(),
            P("seq", None),
            P(),
            P("seq", None),
            P("seq", None),
            P(),
        ),
        check_vma=False,
    )
```

```python
import functools
import itertools
import math

import jax
import jax.numpy as jnp
import numpy as np
from jax import lax
from jax.experimental import pallas as pl
from jax.experimental.pallas import tpu as pltpu
from jax.sharding import PartitionSpec as P

EPS = 1e-05
THRESH = 0.003
HIGH = lax.Precision.HIGHEST


def shortened(x):

    def short(part):
        return part.astype(jnp.bfloat16) if part.dtype == jnp.float32 else part

    return jax.tree.map(short, x)


def passed_along(block, axis, distance):
    devices = range(lax.axis_size(axis))
    route = [((i - distance) % len(devices), i) for i in devices]
    return lax.ppermute(block, axis, route)


def norm_scale(value, gain):
    return value * lax.rsqrt(jnp.mean(value * value, axis=-1, keepdims=True) + EPS) * gain


def angle_tables(left_count, right_count, period):
    left_idx = jnp.arange(left_count, dtype=jnp.int32)[:, None]
    right_idx = jnp.arange(right_count, dtype=jnp.int32)[None, :]
    phase = (left_idx * right_idx % period).astype(jnp.float32) * (2.0 * math.pi / period)
    return (jnp.cos(phase), jnp.sin(phase))


def twiddle_tables(shard_index, spec_len, whole_len):
    turned = shard_index * jnp.arange(spec_len, dtype=jnp.int32) % whole_len
    phase = turned.astype(jnp.float32) * (2.0 * math.pi / whole_len)
    return (jnp.cos(phase)[None, :, None], jnp.sin(phase)[None, :, None])


def local_forward(signal, shard_index, whole_len):
    blocks = signal.shape[1]
    cos_table, sin_table = angle_tables(blocks, 2 * blocks, 2 * blocks)
    real_part = jnp.einsum("rjd,jk->rkd", signal, cos_table, precision=HIGH)
    imag_part = -jnp.einsum("rjd,jk->rkd", signal, sin_table, precision=HIGH)
    cos_twid, sin_twid = twiddle_tables(shard_index, 2 * blocks, whole_len)
    out_real = real_part * cos_twid + imag_part * sin_twid
    out_imag = imag_part * cos_twid - real_part * sin_twid
    return (out_real[:, :, None, :], out_imag[:, :, None, :])


def cross_section(real_part, imag_part, direction):
    count = real_part.shape[2]
    cos_table, sin_table = angle_tables(count, count, count)
    re_cos = jnp.einsum("rcpd,pm->rcmd", real_part, cos_table, precision=HIGH)
    re_sin = jnp.einsum("rcpd,pm->rcmd", real_part, sin_table, precision=HIGH)
    im_cos = jnp.einsum("rcpd,pm->rcmd", imag_part, cos_table, precision=HIGH)
    im_sin = jnp.einsum("rcpd,pm->rcmd", imag_part, sin_table, precision=HIGH)
    return (re_cos - direction * im_sin, im_cos + direction * re_sin)


def local_inverse(real_part, imag_part, shard_index, whole_len):
    real_part = real_part[:, :, 0, :]
    imag_part = imag_part[:, :, 0, :]
    spec_len = real_part.shape[1]
    cos_twid, sin_twid = twiddle_tables(shard_index, spec_len, whole_len)
    turned_re = real_part * cos_twid - imag_part * sin_twid
    turned_im = imag_part * cos_twid + real_part * sin_twid
    cos_table, sin_table = angle_tables(spec_len, spec_len // 2, spec_len)
    result = jnp.einsum("rkd,kj->rjd", turned_re, cos_table, precision=HIGH)
    result = result - jnp.einsum("rkd,kj->rjd", turned_im, sin_table, precision=HIGH)
    return result / whole_len


def earlier(members, at_start):
    received = jax.tree.map(
        lambda part, own: part.astype(own.dtype),
        passed_along(shortened(members), "seq", 1),
        members,
    )
    placed = []
    for member in received:
        rolled = jnp.concatenate([jnp.zeros_like(member[:, :1]), member[:, :-1]], axis=1)
        placed.append(jnp.where(at_start, rolled, member))
    return tuple(placed)


def later(member, at_end):
    received = passed_along(member.astype(jnp.bfloat16), "seq", -1).astype(member.dtype)
    rolled = jnp.concatenate([received[:, 1:], jnp.zeros_like(received[:, :1])], axis=1)
    return jnp.where(at_end, rolled, received)


def times_trans(left, right):
    return lax.dot_general(
        left, right, (((1,), (1,)), ((), ())), preferred_element_type=jnp.float32
    )


def trans_times(left, right):
    return lax.dot_general(
        left, right, (((0,), (0,)), ((), ())), preferred_element_type=jnp.float32
    )


def general_local(
    block_in,
    segment_ids,
    valid_mask,
    cotangent,
    gain_mix,
    in_proj,
    short_taps,
    long_kernel,
    skip_gain,
    out_proj,
    gain_mlp,
    up_proj,
    down_proj,
):
    batch_rows = block_in.shape[0]
    blocks = block_in.shape[1]
    width = block_in.shape[3]
    shard_count = lax.axis_size("seq")
    shard_index = lax.axis_index("seq")
    whole_len = 2 * blocks * shard_count
    tokens = batch_rows * blocks
    at_start = shard_index == 0
    at_end = shard_index == shard_count - 1
    flat_in = block_in.reshape(tokens, width)
    mask_rows = valid_mask[:, :, 0].astype(jnp.float32)[:, :, None]
    normed_one = norm_scale(flat_in, gain_mix).astype(jnp.bfloat16)
    proj_low = jnp.dot(normed_one, in_proj, preferred_element_type=jnp.float32).astype(jnp.bfloat16)
    proj_low = proj_low.reshape(batch_rows, blocks, 3 * width)
    seg_low = segment_ids[:, :, 0].astype(jnp.bfloat16)[:, :, None]
    prev_one = earlier((proj_low, seg_low), at_start)
    prev_two = earlier(prev_one, at_start)
    same_one = (prev_one[1] == seg_low).astype(jnp.float32)
    same_two = (prev_two[1] == seg_low).astype(jnp.float32)
    proj_now = proj_low.astype(jnp.float32)
    proj_one = prev_one[0].astype(jnp.float32)
    proj_two = prev_two[0].astype(jnp.float32)
    conv_short = (
        short_taps[0] * proj_now
        + short_taps[1] * proj_one * same_one
        + short_taps[2] * proj_two * same_two
    )
    query = conv_short[:, :, :width]
    keys = conv_short[:, :, width : 2 * width]
    values = conv_short[:, :, 2 * width :]
    gated = keys * values * mask_rows
    raw_taps = long_kernel[:, 0, :]
    taps_eff = raw_taps - THRESH * jnp.tanh(raw_taps / THRESH)
    kern_re, kern_im = local_forward(taps_eff[None], shard_index, whole_len)
    kern_re, kern_im = (
        lax.all_to_all(
            kern_re.astype(jnp.bfloat16), "seq", split_axis=1, concat_axis=2, tiled=True
        ).astype(kern_re.dtype),
        lax.all_to_all(
            kern_im.astype(jnp.bfloat16), "seq", split_axis=1, concat_axis=2, tiled=True
        ).astype(kern_im.dtype),
    )
    kern_re, kern_im = cross_section(kern_re, kern_im, -1.0)
    gate_re, gate_im = local_forward(gated, shard_index, whole_len)
    gate_re, gate_im = (
        lax.all_to_all(
            gate_re.astype(jnp.bfloat16), "seq", split_axis=1, concat_axis=2, tiled=True
        ).astype(gate_re.dtype),
        lax.all_to_all(
            gate_im.astype(jnp.bfloat16), "seq", split_axis=1, concat_axis=2, tiled=True
        ).astype(gate_im.dtype),
    )
    gate_re, gate_im = cross_section(gate_re, gate_im, -1.0)
    prod_re = gate_re * kern_re - gate_im * kern_im
    prod_im = gate_re * kern_im + gate_im * kern_re
    prod_re, prod_im = cross_section(prod_re, prod_im, 1.0)
    prod_re, prod_im = (
        lax.all_to_all(
            prod_re.astype(jnp.bfloat16), "seq", split_axis=2, concat_axis=1, tiled=True
        ).astype(prod_re.dtype),
        lax.all_to_all(
            prod_im.astype(jnp.bfloat16), "seq", split_axis=2, concat_axis=1, tiled=True
        ).astype(prod_im.dtype),
    )
    long_out = local_inverse(prod_re, prod_im, shard_index, whole_len) + skip_gain * gated
    mixer_low = (query * long_out).reshape(tokens, width).astype(jnp.bfloat16)
    mixer_out = jnp.dot(mixer_low, out_proj, preferred_element_type=jnp.float32)
    resid_mid = flat_in + mixer_out
    normed_two = norm_scale(resid_mid, gain_mlp).astype(jnp.bfloat16)
    up_val = jnp.dot(normed_two, up_proj, preferred_element_type=jnp.float32)
    act_low = jax.nn.gelu(up_val).astype(jnp.bfloat16)
    mlp_out = jnp.dot(act_low, down_proj, preferred_element_type=jnp.float32)
    flat_out = resid_mid + mlp_out
    grad_out = cotangent.reshape(tokens, width)
    grad_mlp = grad_out.astype(jnp.bfloat16)
    grad_down = trans_times(act_low, grad_mlp)
    grad_act = times_trans(grad_mlp, down_proj)
    unused_val, gelu_back = jax.vjp(jax.nn.gelu, up_val)
    grad_upval = gelu_back(grad_act)[0].astype(jnp.bfloat16)
    grad_up = trans_times(normed_two, grad_upval)
    grad_norm_two = times_trans(grad_upval, up_proj)
    unused_two, norm_back_two = jax.vjp(norm_scale, resid_mid, gain_mlp)
    grad_resid, grad_gain_two = norm_back_two(grad_norm_two)
    grad_mid = grad_out + grad_resid
    grad_mix = grad_mid.astype(jnp.bfloat16)
    grad_outp = trans_times(mixer_low, grad_mix)
    grad_prod = times_trans(grad_mix, out_proj).reshape(batch_rows, blocks, width)
    grad_query = grad_prod * long_out
    grad_long = grad_prod * query
    back_re, back_im = local_forward(grad_long, shard_index, whole_len)
    back_re, back_im = (
        lax.all_to_all(
            back_re.astype(jnp.bfloat16), "seq", split_axis=1, concat_axis=2, tiled=True
        ).astype(back_re.dtype),
        lax.all_to_all(
            back_im.astype(jnp.bfloat16), "seq", split_axis=1, concat_axis=2, tiled=True
        ).astype(back_im.dtype),
    )
    back_re, back_im = cross_section(back_re, back_im, -1.0)
    sig_re = kern_re * back_re + kern_im * back_im
    sig_im = kern_re * back_im - kern_im * back_re
    tap_re = jnp.sum(gate_re * back_re + gate_im * back_im, axis=0, keepdims=True)
    tap_im = jnp.sum(gate_re * back_im - gate_im * back_re, axis=0, keepdims=True)
    sig_re, sig_im = cross_section(sig_re, sig_im, 1.0)
    tap_re, tap_im = cross_section(tap_re, tap_im, 1.0)
    sig_re, sig_im, tap_re, tap_im = (
        lax.all_to_all(
            sig_re.astype(jnp.bfloat16), "seq", split_axis=2, concat_axis=1, tiled=True
        ).astype(sig_re.dtype),
        lax.all_to_all(
            sig_im.astype(jnp.bfloat16), "seq", split_axis=2, concat_axis=1, tiled=True
        ).astype(sig_im.dtype),
        lax.all_to_all(
            tap_re.astype(jnp.bfloat16), "seq", split_axis=2, concat_axis=1, tiled=True
        ).astype(tap_re.dtype),
        lax.all_to_all(
            tap_im.astype(jnp.bfloat16), "seq", split_axis=2, concat_axis=1, tiled=True
        ).astype(tap_im.dtype),
    )
    grad_gated = local_inverse(sig_re, sig_im, shard_index, whole_len) + skip_gain * grad_long
    grad_taps_eff = local_inverse(tap_re, tap_im, shard_index, whole_len)[0]
    tanh_val = jnp.tanh(raw_taps / THRESH)
    grad_kernel = (grad_taps_eff * tanh_val * tanh_val)[:, None, :]
    grad_kernel = lax.psum(grad_kernel.astype(jnp.bfloat16), "rows").astype(jnp.float32)
    grad_skip = jnp.sum(grad_long * gated, axis=(0, 1))
    grad_short = jnp.concatenate(
        [grad_query, grad_gated * values * mask_rows, grad_gated * keys * mask_rows], axis=2
    )
    grad_tap_rows = jnp.stack(
        [
            jnp.sum(grad_short * proj_now, axis=(0, 1)),
            jnp.sum(grad_short * proj_one * same_one, axis=(0, 1)),
            jnp.sum(grad_short * proj_two * same_two, axis=(0, 1)),
        ]
    )
    inner_term = short_taps[1] * grad_short * same_one + later(
        short_taps[2] * grad_short * same_two, at_end
    )
    grad_proj = short_taps[0] * grad_short + later(inner_term, at_end)
    grad_proj = grad_proj.reshape(tokens, 3 * width).astype(jnp.bfloat16)
    grad_inp = trans_times(normed_one, grad_proj)
    grad_norm_one = times_trans(grad_proj, in_proj)
    unused_one, norm_back_one = jax.vjp(norm_scale, flat_in, gain_mix)
    grad_first, grad_gain_one = norm_back_one(grad_norm_one)
    grad_flat = grad_mid + grad_first
    mask_flat = mask_rows.reshape(tokens, 1)
    stat_sums = jnp.stack(
        [
            jnp.sum(mask_flat * flat_out * flat_out),
            jnp.sum(mask_flat * mixer_out * mixer_out),
            jnp.sum(mask_flat * mlp_out * mlp_out),
            jnp.sum(mask_flat),
        ]
    )
    grad_gain_one, grad_gain_two, grad_tap_rows, grad_skip, stat_sums = lax.psum(
        (grad_gain_one, grad_gain_two, grad_tap_rows, grad_skip, stat_sums), ("rows", "seq")
    )
    rms_stats = jnp.sqrt(stat_sums[:3] / (jnp.maximum(stat_sums[3], 1.0) * width))
    shares = (
        lax.psum_scatter(grad_inp, "seq", scatter_dimension=0, tiled=True),
        lax.psum_scatter(grad_outp, "seq", scatter_dimension=0, tiled=True),
        lax.psum_scatter(grad_up, "seq", scatter_dimension=0, tiled=True),
        lax.psum_scatter(grad_down, "seq", scatter_dimension=0, tiled=True),
    )
    grad_inp, grad_outp, grad_up, grad_down = (
        lax.psum(shares[0].astype(jnp.bfloat16), "rows").astype(jnp.float32),
        lax.psum(shares[1].astype(jnp.bfloat16), "rows").astype(jnp.float32),
        lax.psum(shares[2].astype(jnp.bfloat16), "rows").astype(jnp.float32),
        lax.psum(shares[3].astype(jnp.bfloat16), "rows").astype(jnp.float32),
    )
    return (
        flat_out.reshape(block_in.shape),
        grad_flat.reshape(block_in.shape),
        grad_gain_one,
        grad_inp,
        grad_tap_rows,
        grad_kernel,
        grad_skip,
        grad_outp,
        grad_gain_two,
        grad_up,
        grad_down,
        rms_stats,
    )


MESH = pl.DeviceIdType.MESH
F32 = jnp.float32
BF16 = jnp.bfloat16
VMEM_BYTES = 62 * 1024 * 1024
C0 = math.sqrt(2.0 / math.pi)
C1 = 0.044715
ALL = slice(None)
ORDERS = (
    ("y", "zl", "x", "zh"),
    ("y", "zl", "x", "zh"),
    ("x", "y", "zl", "zh"),
    ("y", "x", "zl", "zh"),
    ("y", "x", "zl", "zh"),
    ("y", "x", "zl", "zh"),
    ("y", "zl", "x", "zh"),
    ("x", "y", "zl", "zh"),
)


def dot_nn(a, b):
    return lax.dot_general(a, b, (((1,), (0,)), ((), ())), preferred_element_type=F32)


def dot_nt(a, b):
    return lax.dot_general(a, b, (((1,), (1,)), ((), ())), preferred_element_type=F32)


def fft_points(re, im, sign):
    n = len(re)
    if n == 1:
        return re, im
    even_r, even_i = fft_points(re[0::2], im[0::2], sign)
    odd_r, odd_i = fft_points(re[1::2], im[1::2], sign)
    out_r, out_i = [None] * n, [None] * n
    for k in range(n // 2):
        if k == 0:
            turn_r, turn_i = odd_r[0], odd_i[0]
        elif 4 * k == n:
            if sign > 0:
                out_r[k], out_i[k] = even_r[k] - odd_i[k], even_i[k] + odd_r[k]
                out_r[k + n // 2], out_i[k + n // 2] = even_r[k] + odd_i[k], even_i[k] - odd_r[k]
            else:
                out_r[k], out_i[k] = even_r[k] + odd_i[k], even_i[k] - odd_r[k]
                out_r[k + n // 2], out_i[k + n // 2] = even_r[k] - odd_i[k], even_i[k] + odd_r[k]
            continue
        else:
            cos, sin = math.cos(2 * math.pi * k / n), sign * math.sin(2 * math.pi * k / n)
            turn_r = cos * odd_r[k] - sin * odd_i[k]
            turn_i = cos * odd_i[k] + sin * odd_r[k]
        out_r[k], out_i[k] = even_r[k] + turn_r, even_i[k] + turn_i
        out_r[k + n // 2], out_i[k + n // 2] = even_r[k] - turn_r, even_i[k] - turn_i
    return out_r, out_i


def spectrum_tables(blocks, phases):
    length = blocks * phases
    k = 2 * np.arange(blocks)[None, :] + 1
    angle = 2.0 * np.pi * np.arange(blocks)[:, None] * k / (4.0 * blocks)
    table = np.concatenate([np.cos(angle), -np.sin(angle)], axis=1)
    turn = 2.0 * np.pi * np.arange(phases)[:, None] * k / (4.0 * length)
    turns = np.stack([np.cos(turn), np.sin(turn)], axis=1)[:, :, None, :]
    return jnp.asarray(table, F32), jnp.asarray(np.broadcast_to(turns, (phases, 2, 8, blocks)), F32)


def place():
    row, seq = lax.axis_index("rows"), lax.axis_index("seq")
    return lax.div(row, 2), lax.rem(row, 2), lax.div(seq, 4), lax.rem(lax.div(seq, 2), 2), lax.rem(seq, 2)


def partner(axis):
    y, c, zh, zl, x = place()
    if axis == "core":
        return {"rows": 2 * y + 1 - c}
    if axis == "y":
        return {"rows": 2 * (1 - y) + c}
    if axis == "x":
        return {"seq": 4 * zh + 2 * zl + 1 - x}
    if axis == "zl":
        return {"seq": 4 * zh + 2 * (1 - zl) + x}
    return {"seq": 4 * (1 - zh) + 2 * zl + x}


def remote(src, dst, send_sem, recv_sem, target):
    return pltpu.make_async_remote_copy(
        src_ref=src, dst_ref=dst, send_sem=send_sem, recv_sem=recv_sem, device_id=target, device_id_type=MESH,
    )


def exchange(src, dst, send_sem, recv_sem, axis):
    return remote(src, dst, send_sem, recv_sem, partner(axis))


def greet(n):
    me = lax.axis_index("seq")
    barrier = pltpu.get_barrier_semaphore()
    for j in range(1, n):
        pl.semaphore_signal(barrier, inc=1, device_id={"seq": lax.rem(me + j, n)}, device_id_type=MESH)
    for axis in ("core", "y"):
        pl.semaphore_signal(barrier, inc=1, device_id=partner(axis), device_id_type=MESH)
    return barrier, n + 1


def aligned(index, size):
    return pl.ds(pl.multiple_of(index * size, size), size)


class Post:
    def __init__(self, n, source, target, sems):
        self.n, self.source, self.target, self.sems = n, source, target, sems

    def copies(self, sender):
        me = lax.axis_index("seq")
        for j in range(1, self.n):
            peer = lax.rem(me + j, self.n)
            come = sender(peer, me)
            yield remote(
                self.source(peer), self.target(come), self.sems.at[0, j], self.sems.at[1, come], {"seq": peer}
            )

    def start(self):
        me = lax.axis_index("seq")
        for copy in self.copies(lambda peer, me: me):
            copy.start()
        self.target(me)[...] = self.source(me)[...]

    def arrive(self):
        for copy in self.copies(lambda peer, me: peer):
            copy.wait_recv()

    def drain(self):
        for copy in self.copies(lambda peer, me: me):
            copy.wait_send()


def over_groups(each, blocks, body):
    for lane in range(0, blocks, 128):
        def step(g, carry):
            body(pl.multiple_of(g * 16, 16), lane)
            return carry
        lax.fori_loop(0, each // 16, step, 0)


def matmul_rows(out, left, right, size=256):
    for at in range(0, out.shape[0], size):
        out[at:at + size, :] = left(at, size, right)


def load_phases(spec, n, each, at, lane, half):
    re = [spec[pl.ds(p * each + at, 8), lane:lane + 128] for p in range(n)]
    im = [spec[pl.ds(p * each + at, 8), half + lane:half + lane + 128] for p in range(n)]
    return re, im


def turn_phases(re, im, turns, lane, sign):
    out_r, out_i = [re[0]], [im[0]]
    for p in range(1, len(re)):
        cos, sin = turns[p, 0, :, lane:lane + 128], turns[p, 1, :, lane:lane + 128]
        if sign > 0:
            out_r.append(re[p] * cos - im[p] * sin)
            out_i.append(im[p] * cos + re[p] * sin)
        else:
            out_r.append(re[p] * cos + im[p] * sin)
            out_i.append(im[p] * cos - re[p] * sin)
    return out_r, out_i


def by_halves(n, each, blocks, spec, work, stores, kept=None):
    def group(at, lane):
        halves = []
        if kept is not None:
            loaded = [
                [kept[pl.ds(k * each + at, 16), part + lane:part + lane + 128].astype(F32) for k in range(n)]
                for part in (0, blocks)
            ]
        for half in (0, 8):
            re, im = load_phases(spec, n, each, at + half, lane, blocks)
            old = None if kept is None else [[value[half:half + 8] for value in part] for part in loaded]
            halves.append(work(re, im, at + half, lane, old))
        for target, first, second in zip(stores, *halves):
            for k in range(n):
                for part in range(2):
                    value = jnp.concatenate([first[part][k], second[part][k]], axis=0).astype(BF16)
                    target[pl.ds(k * each + at, 16), part * blocks + lane:part * blocks + lane + 128] = value

    over_groups(each, blocks, group)


def to_lanes(source, table, spec):
    for at in range(0, spec.shape[0], 256):
        spec[at:at + 256, :] = dot_nn(source(at, 256), table[...])


def from_lanes(fin, table, size, store):
    for at in range(0, fin.shape[0], size):
        store(at, dot_nt(fin[at:at + size, :], table[...]) * (2.0 / fin.shape[1] / (fin.shape[0] // size)))


def over_rows(total, size, body):
    def step(i, carry):
        body(aligned(i, size))
        return carry
    lax.fori_loop(0, total // size, step, 0)


def over_lanes(width, body):
    def step(i, carry):
        body(aligned(i, 128))
        return carry
    lax.fori_loop(0, width // 128, step, 0)


def strided(ref, rows, start, lane, wide):
    return ref[pl.ds(start * wide + lane, rows, stride=wide), :]


def turn_rows(value, amount):
    return pltpu.roll(value, amount % value.shape[0], 0)


class Tree:
    def __init__(self, order, share, own, parts, gathered, sems):
        self.order = order + ("back_y", "back_core")
        self.share, self.own, self.parts, self.gathered, self.sems = share, own, parts, gathered, sems
        self.done = 0
        self.started = []

    def half(self, step, bit):
        y, c, zh, zl, x = place()
        here = dict(zh=zh, zl=zl, x=x, y=y)
        settled = self.order[:step]
        return tuple(here[a] if a in settled else (bit(here[a]) if a == self.order[step] else ALL) for a in ("zh", "zl", "x", "y"))

    def block(self, index):
        c = place()[1]
        return (self.share, index[:3] + (c,) + index[3:]) if self.own is None else (self.own, index)

    def copies(self, step):
        y, c, zh, zl, x = place()
        axis = self.order[step]
        gathered = self.gathered
        if axis == "core":
            src = self.share.at[:, :, :, 1 - c]
        elif axis == "back_y":
            src = gathered.at[c, y]
        elif axis == "back_core":
            src = gathered.at[c]
        else:
            ref, index = self.block(self.half(step, lambda bit: 1 - bit))
            src = ref.at[index]
        dst = src if axis.startswith("back") else self.parts[step]
        return exchange(src, dst, self.sems.at[0, step], self.sems.at[1, step], axis.replace("back_", ""))

    def start(self):
        self.copies(self.done).start()
        self.started.append(self.done)

    def add(self, index, part, at, target=None):
        own, index = self.block(index)
        size = 48

        def body(i, carry):
            here = aligned(i, size)
            value = own[index + (here, ALL)] + part[at + (here, ALL)]
            if target is None:
                own[index + (here, ALL)] = value
            else:
                target[here, :] = value
            return carry

        lax.fori_loop(0, part.shape[-2] // size, body, 0)

    def finish(self, go=True):
        y, c, zh, zl, x = place()
        step = self.done
        axis = self.order[step]
        self.copies(step).wait_recv()
        if not axis.startswith("back"):
            index = (ALL,) * 4 if axis == "core" else self.half(step, lambda bit: bit)
            free = [i for i, entry in enumerate(index) if entry is ALL or isinstance(entry, slice)]
            last = self.order[step + 1] == "back_y"
            for bits in itertools.product(range(2), repeat=len(free)):
                full = list(index)
                for i, bit in zip(free, bits):
                    full[i] = bit
                self.add(tuple(full), self.parts[step], bits, self.gathered.at[c, y] if last else None)
        self.done += 1
        if go and self.done < len(self.order):
            self.start()

    def drain(self):
        for step in self.started:
            self.copies(step).wait_send()


def tree_scratch(r, l):
    shapes = [(2, 2, 2, 2, r, l), (2, 2, 2, r, l), (2, 2, r, l), (2, r, l), (r, l)]
    return [pltpu.VMEM(shape, BF16) for shape in shapes] + [pltpu.SemaphoreType.DMA((2, 7))]


def whole_kernel(
    n, chunk,
    x_far, cot_far, taps_far, short_taps, skip, gain_mix, gain_mlp, segments, valid, w_in_far, w_out_far, w_up_far, w_down_far,
    table_wide, turns,
    out_far, flat_far, mid_far, turned_far, spec_taps_far, spec_gate_far,
    got_ua, got_ub, got_da, got_db, got_out, got_in0, got_in1, got_in2, tap_all, vectors,
    small, table, marks, marks_got, land, taps_got, query, saved, same, sent_one, sent_two, got_one, got_two, hand,
    tap_own, tap_got, tap_half, tap_part, vector_got,
    fetch, keep, near_sems, mark_sems, tap_sems, gate_sems, long_sems, back_sems, gated_sems, hand_sems,
    pair_sems, home_sems, home_send, home_recv, vector_sems,
    *tree_refs,
):
    me = lax.axis_index("seq")
    y, c, zh, zl, xbit = place()
    rows, blocks = query.shape[0], query.shape[1]
    width, hidden = w_up_far.shape
    each, wide, step = width // n, width // 128, blocks // 2
    side, linear = each // 2, blocks * wide
    at_top = jnp.logical_and(zh == 0, zl == 0)
    at_end = jnp.logical_and(zh == 1, zl == 1)
    chosen_chunk = jnp.logical_and(zh == y, zl == c)
    home = zh == y
    barrier, told = greet(n)
    for row, vector in ((9, skip), (10, gain_mix), (11, gain_mlp)):
        small[row, :] = vector[...]
    gain_one, gain_two = small[10:11, :], small[11:12, :]
    table[...] = table_wide[...].astype(BF16)

    trees, at = {}, 0
    for name, got, order in zip(("ua", "ub", "da", "db", "out"), (got_ua, got_ub, got_da, got_db, got_out), ORDERS):
        trees[name] = Tree(order, None, tree_refs[at], tree_refs[at + 1:at + 5], got, tree_refs[at + 5])
        at += 6
    for name, got, order in (("in0", got_in0, ORDERS[5]), ("in1", got_in1, ORDERS[6]), ("in2", got_in2, ORDERS[7])):
        trees[name] = Tree(("core",) + order, None, None, tree_refs[at:at + 5], got, tree_refs[at + 5])
        at += 6

    post_marks = Post(n, lambda d: marks, lambda p: marks_got.at[p], mark_sems)

    def posts(sent, got, sems):
        return [
            Post(n, lambda e, r=r: sent.at[r, aligned(e, each)], lambda p, r=r: got.at[r, aligned(p, each)], sems.at[r])
            for r in range(rows)
        ]

    posts_gate = posts(sent_one, got_one, gate_sems)
    posts_long = posts(sent_two, got_two, long_sems)
    posts_back = posts(sent_one, got_one, back_sems)
    posts_gated = posts(sent_two, got_two, gated_sems)

    def near_far(r, h, source):
        part = slice(h * step, (h + 1) * step)
        target = {"seq": lax.rem(me + 2, n)}
        return remote(source.at[r, part], land.at[1, r, part], near_sems.at[0, 0, r, h], near_sems.at[0, 1, r, h], target)

    def near_side(r, h, source):
        part = slice(h * step, (h + 1) * step)
        return exchange(source.at[r, part], land.at[0, r, part], near_sems.at[1, 0, r, h], near_sems.at[1, 1, r, h], "x")

    def tap_copy(e, taps_sent):
        return remote(taps_sent.at[aligned(e, each)], taps_got.at[aligned(me, each)], tap_sems.at[0, lax.rem(e, 2)], tap_sems.at[1, me], {"seq": e})

    def tap_spread(axis):
        at = 2 if axis == "core" else 3
        return exchange(taps_got, taps_got, tap_sems.at[at, 0], tap_sems.at[at, 1], axis)

    def side_copy(r):
        return exchange(hand.at[0, r], land.at[0, r], hand_sems.at[0, 0, r], hand_sems.at[0, 1, r], "x")

    def far_copy(r):
        target = {"seq": lax.rem(me + n - 2, n)}
        return remote(hand.at[1, r], land.at[1, r], hand_sems.at[1, 0, r], hand_sems.at[1, 1, r], target)

    def tap_core():
        return exchange(tap_own.at[1 - c], tap_got, home_sems.at[0, 0], home_sems.at[1, 0], "core")

    def tap_y():
        return exchange(tap_own.at[c, 1 - y], tap_half, home_sems.at[0, 1], home_sems.at[1, 1], "y")

    def home_copy(q, there):
        return remote(tap_part.at[q], tap_all.at[c, there], home_send.at[q], home_recv.at[there], {"seq": 4 * y + q})

    def tap_back_y():
        return exchange(tap_all.at[c], tap_all.at[c], home_sems.at[0, 2], home_sems.at[1, 2], "y")

    def tap_back_core():
        return exchange(tap_all.at[c], tap_all.at[c], home_sems.at[0, 3], home_sems.at[1, 3], "core")

    def front(near, x_in, taps, taps_sent, w_in, proj, turned, gate_wide):
        first = [
            pltpu.make_async_copy(src, dst, fetch.at[i])
            for i, (src, dst) in enumerate(((x_far, x_in), (taps_far, taps), (w_in_far, w_in)))
        ]
        for copy in first:
            copy.start()
        marks[...] = jnp.zeros_like(marks)
        for r in range(rows):
            marks[r:r + 1, :] = segments[r].astype(F32)
            marks[rows + r:rows + r + 1, :] = valid[r].astype(F32)
        for k in range(3):
            small[3 * k:3 * k + 3, :] = short_taps[:, k * width:(k + 1) * width]
        small[12:16, :] = jnp.zeros((4, width), F32)
        first[0].wait()

        def norm_row(r):
            for at in range(r * blocks, (r + 1) * blocks, 128):
                parts = [strided(x_in, 128, at, j, wide) for j in range(wide)]
                total = sum(jnp.sum(part * part, axis=-1, keepdims=True) for part in parts)
                scale = lax.rsqrt(total * (1.0 / width) + EPS)
                for j, part in enumerate(parts):
                    lanes = slice(j * 128, (j + 1) * 128)
                    near[0, r, at - r * blocks:at - r * blocks + 128, lanes] = (part * scale * gain_one[:, lanes]).astype(BF16)

        def send_near(r):
            for h in range(2):
                near_far(r, h, near.at[0]).start()

            @pl.when(xbit == 0)
            def _():
                for h in range(2):
                    near_side(r, h, near.at[0]).start()

        def hand_on(r):
            @pl.when(xbit == 1)
            def _():
                for h in range(2):
                    near_far(r, h, near.at[0]).wait_recv()
                    near_side(r, h, land.at[1]).start()

        norm_row(0)
        pl.semaphore_wait(barrier, told)
        send_near(0)
        post_marks.start()
        norm_row(1)
        send_near(1)
        first[1].wait()
        for j in range(wide):
            raw = strided(taps, blocks, 0, j, wide)
            low = raw - THRESH * jnp.tanh(raw * (1.0 / THRESH))
            taps_sent[j * 128:(j + 1) * 128, :] = low.T.astype(BF16)
        for xd in range(2):
            target = 4 * y + 2 * c + xd

            @pl.when(target != me)
            def _():
                tap_copy(target, taps_sent).start()

            @pl.when(target == me)
            def _():
                taps_got[aligned(me, each)] = taps_sent[aligned(me, each)]

        first[2].wait()

        def project(r, j):
            for k in (1, 2, 0):
                for at in range(0, width, 256):
                    cols = slice(k * width + at, k * width + at + 256)
                    proj[j, k, :, at:at + 256] = dot_nn(near[j, r], w_in[:, cols]).astype(BF16)

        project(0, 0)
        hand_on(0)
        post_marks.arrive()
        lane = lax.broadcasted_iota(jnp.int32, (rows, blocks), 1)
        now = marks[0:rows, :]
        found = []
        for j in (1, 2):
            before = marks_got[lax.rem(me + n - j, n), 0:rows, :]
            wrapped = me < j
            before = jnp.where(wrapped, pltpu.roll(before, 1, 1), before)
            kept = jnp.logical_and(before == now, jnp.logical_or(jnp.logical_not(wrapped), lane > 0))
            found.append(kept.astype(F32))
        columns = jnp.concatenate(found + [marks[rows:2 * rows, :], jnp.zeros((2, blocks), F32)], axis=0).T
        for s in range(3):
            for r in range(rows):
                same[s, r] = jnp.broadcast_to(columns[:, s * rows + r:s * rows + r + 1], (blocks, 128))

        def chunk_row(r):
            @pl.when(xbit == 0)
            def _():
                for h in range(2):
                    near_far(r, h, near.at[0]).wait_recv()

            for h in range(2):
                near_side(r, h, near.at[0]).wait_recv()
            for j in (1, 2):
                wrapped = jnp.logical_and(at_top, xbit == 0) if j == 1 else at_top

                @pl.when(wrapped)
                def _():
                    near[j, r] = turn_rows(land[j - 1, r].astype(F32), 1).astype(BF16)

                @pl.when(jnp.logical_not(wrapped))
                def _():
                    near[j, r] = land[j - 1, r]

                project(r, j)

            def lanes_step(lanes):
                def rows_step(here):
                    masks = [same[s, r, here, :] for s in range(3)]
                    value = []
                    for k in range(3):
                        total = small[3 * k:3 * k + 1, lanes] * proj[0, k, here, lanes].astype(F32)
                        total += small[3 * k + 1:3 * k + 2, lanes] * (proj[1, k, here, lanes].astype(F32) * masks[0])
                        total += small[3 * k + 2:3 * k + 3, lanes] * (proj[2, k, here, lanes].astype(F32) * masks[1])
                        value.append(total)
                    query[r, here, lanes] = value[0]
                    keys, values = value[1] * masks[2], value[2] * masks[2]
                    gate = value[1] * values
                    saved[0, r, here, lanes] = keys.astype(BF16)
                    saved[1, r, here, lanes] = values.astype(BF16)
                    saved[2, r, here, lanes] = gate.astype(BF16)
                    gate_wide[here, lanes] = gate

                over_rows(blocks, 64, rows_step)

            over_lanes(width, lanes_step)
            sent_one[r] = gate_wide[...].T.astype(BF16)
            posts_gate[r].start()

        chunk_row(0)
        project(1, 0)
        hand_on(1)

        @pl.when(chosen_chunk)
        def _():
            for p in range(n):
                @pl.when(me != p)
                def _():
                    remote(
                        taps_sent.at[aligned(me, each)], taps_got.at[p * each:(p + 1) * each],
                        tap_sems.at[0, 0], tap_sems.at[1, p], {"seq": p},
                    ).wait_recv()
            tap_spread("core").start()

        @pl.when(jnp.logical_and(zh == y, zl != c))
        def _():
            tap_spread("core").wait_recv()

        @pl.when(zh == y)
        def _():
            tap_spread("y").start()

        chunk_row(1)

        for j in range(3):
            for r in range(rows):
                value = near[j, r].astype(F32)
                if j > 0:
                    value = value * same[j - 1, r, :, 0:1]
                turned[j, :, r * blocks:(r + 1) * blocks] = value.T.astype(BF16)
        kept = pltpu.make_async_copy(turned, turned_far, keep.at[2])
        kept.start()
        for r in range(rows):
            for h in range(2):
                near_far(r, h, near.at[0]).wait_send()
                near_side(r, h, near.at[0]).wait_send()
        for xd in range(2):
            target = 4 * y + 2 * c + xd

            @pl.when(target != me)
            def _():
                tap_copy(target, taps_sent).wait_send()

        kept.wait()

    pl.run_scoped(
        front,
        pltpu.VMEM((3, rows, blocks, width), BF16),
        pltpu.VMEM(x_far.shape, F32),
        pltpu.VMEM(taps_far.shape, F32),
        pltpu.VMEM((width, blocks), BF16),
        pltpu.VMEM(w_in_far.shape, BF16),
        pltpu.VMEM((3, 3, blocks, width), BF16),
        pltpu.VMEM(turned_far.shape, BF16),
        pltpu.VMEM((blocks, width), F32),
    )

    def conv(fin, spec, spec_taps, spec_gate):
        @pl.when(zh != y)
        def _():
            tap_spread("y").wait_recv()

        to_lanes(lambda at, size: taps_got[at:at + size], table, spec)

        def taps_group(at, lane):
            re, im = load_phases(spec, n, each, at, lane, blocks)
            re, im = turn_phases(re, im, turns, lane, -1)
            re, im = fft_points(re, im, -1)
            for k in range(n):
                spec_taps[pl.ds(k * each + at, 8), lane:lane + 128] = re[k]
                spec_taps[pl.ds(k * each + at, 8), blocks + lane:blocks + lane + 128] = im[k]

        def both_halves(at, lane):
            taps_group(at, lane)
            taps_group(at + 8, lane)

        over_groups(each, blocks, both_halves)
        keeps = [pltpu.make_async_copy(spec_taps, spec_taps_far, keep.at[0])]
        keeps[0].start()

        for r in range(rows):
            posts_gate[r].arrive()
            to_lanes(lambda at, size: got_one[r, at:at + size], table, spec)

            def work(re, im, at, lane, kept):
                re, im = turn_phases(re, im, turns, lane, -1)
                re, im = fft_points(re, im, -1)
                tap_r, tap_i = load_phases(spec_taps, n, each, at, lane, blocks)
                out_r = [re[k] * tap_r[k] - im[k] * tap_i[k] for k in range(n)]
                out_i = [re[k] * tap_i[k] + im[k] * tap_r[k] for k in range(n)]
                out_r, out_i = fft_points(out_r, out_i, 1)
                out_r, out_i = turn_phases(out_r, out_i, turns, lane, 1)
                return (re, im), (out_r, out_i)

            by_halves(n, each, blocks, spec, work, (spec_gate.at[r], fin))

            def store(at, value):
                sent_two[r, at:at + value.shape[0]] = value.astype(BF16)

            from_lanes(fin, table, each, store)
            posts_long[r].start()
        keeps.append(pltpu.make_async_copy(spec_gate, spec_gate_far, keep.at[1]))
        keeps[1].start()
        for copy in keeps:
            copy.wait()

    def middle(act, grad_act, turned, turned_cot, mixed, mix_back):
        def mlp(first, w_out, w_up, w_down, x, cot, cot_near, cot_low, resid, long_out, acc_out, acc_back, normed, whole_out, mid):
            vectors[...] = jnp.zeros_like(vectors)
            kept = []
            first[0].wait()
            for r in range(rows):
                tokens = slice(r * blocks, (r + 1) * blocks)
                posts_long[r].arrive()
                gated = saved[2, r].astype(F32)
                long_out[...] = got_two[r].astype(F32).T + small[9:10, :] * gated
                low = (query[r] * long_out[...]).astype(BF16)
                mixer = dot_nn(low, w_out[...])
                mixed[r] = low.T
                mask = same[2, r, :, 0:1]
                vectors[13:14, :] += jnp.sum(mixer * mixer * mask, axis=0, keepdims=True)
                first[1].wait()
                first[2].wait()
                for j in range(wide):
                    lanes = slice(j * 128, (j + 1) * 128)
                    resid[:, lanes] = strided(x, blocks, 0, j, wide) + mixer[:, lanes]
                    cot_near[:, lanes] = strided(cot, blocks, 0, j, wide)
                if r + 1 < rows:
                    after = slice((r + 1) * linear, (r + 2) * linear)
                    for i, (src, dst) in ((1, (x_far, x)), (2, (cot_far, cot))):
                        first[i] = pltpu.make_async_copy(src.at[after], dst, fetch.at[i])
                        first[i].start()
                cot_low[...] = cot_near[...].astype(BF16)
                state = resid[...]
                scale = lax.rsqrt(jnp.mean(state * state, axis=-1, keepdims=True) + EPS)
                normed[...] = (state * scale * gain_two).astype(BF16)
                acc_out[...] = jnp.zeros_like(acc_out)
                acc_back[...] = jnp.zeros_like(acc_back)
                if r == 0:
                    first[3].wait()
                    first[4].wait()

                def hidden_step(j, carry):
                    cols = aligned(j, chunk)
                    up_val = dot_nn(normed[...], w_up[:, cols])
                    square = up_val * up_val
                    tanh = jnp.tanh(up_val * (C0 + (C0 * C1) * square))
                    half = 0.5 * (1.0 + tanh)
                    act_low = (up_val * half).astype(BF16)
                    slope = half + (0.5 * up_val) * (1.0 - tanh * tanh) * (C0 + (3.0 * C0 * C1) * square)
                    act[tokens, cols] = act_low
                    acc_out[...] += dot_nn(act_low, w_down[cols, :])
                    grad = dot_nt(cot_low[...], w_down[cols, :])
                    grad_low = (grad * slope).astype(BF16)
                    grad_act[tokens, cols] = grad_low
                    acc_back[...] += dot_nt(grad_low, w_up[:, cols])
                    return carry

                lax.fori_loop(0, hidden // chunk, hidden_step, 0, unroll=4)
                state = resid[...]
                scale = lax.rsqrt(jnp.mean(state * state, axis=-1, keepdims=True) + EPS)
                grad = acc_back[...]
                vectors[11:12, :] += jnp.sum(grad * state * scale, axis=0, keepdims=True)
                scaled = grad * gain_two
                shift = jnp.mean(scaled * state, axis=-1, keepdims=True) * (scale * scale * scale)
                grad_mid = cot_near[...] + (scaled * scale - state * shift)
                mix_back[r] = grad_mid.astype(BF16)
                grad_prod = dot_nt(mix_back[r], w_out[...])
                grad_long = grad_prod * query[r]
                posts_gate[r].drain()
                sent_one[r] = grad_long.T.astype(BF16)
                posts_back[r].start()
                saved[3, r] = grad_long.astype(BF16)
                vectors[9:10, :] += jnp.sum(grad_long * saved[2, r].astype(F32), axis=0, keepdims=True)
                saved[2, r] = (grad_prod * long_out[...]).astype(BF16)
                mlp = acc_out[...]
                vectors[14:15, :] += jnp.sum(mlp * mlp * mask, axis=0, keepdims=True)
                whole = resid[...] + mlp
                vectors[12:13, :] += jnp.sum(whole * whole * mask, axis=0, keepdims=True)
                vectors[15:16, :] += jnp.broadcast_to(jnp.sum(mask, axis=0, keepdims=True) * (1.0 / width), (1, width))
                if r > 0:
                    for copy in kept:
                        copy.wait()
                    kept.clear()
                for j in range(wide):
                    place_at = pl.ds(j, blocks, stride=wide)
                    whole_out[place_at, :] = whole[:, j * 128:(j + 1) * 128]
                    mid[place_at, :] = grad_mid[:, j * 128:(j + 1) * 128]
                part_rows = slice(r * blocks * wide, (r + 1) * blocks * wide)
                for i, (src, dst) in enumerate(((whole_out, out_far), (mid, mid_far))):
                    kept.append(pltpu.make_async_copy(src, dst.at[part_rows], keep.at[3 + i]))
                    kept[-1].start()
                turned[:, tokens] = normed[...].T
                turned_cot[:, tokens] = cot_low[...].T

            for copy in kept:
                copy.wait()

        def fetched(w_out, w_up, w_down, x, cot):
            first = [
                pltpu.make_async_copy(src, dst, fetch.at[i])
                for i, (src, dst) in enumerate((
                    (w_out_far, w_out), (x_far.at[0:linear], x), (cot_far.at[0:linear], cot), (w_up_far, w_up), (w_down_far, w_down),
                ))
            ]
            for copy in first:
                copy.start()
            pl.run_scoped(
                conv,
                pltpu.VMEM((width, 2 * blocks), BF16),
                pltpu.VMEM((width, 2 * blocks), F32),
                pltpu.VMEM((width, 2 * blocks), F32),
                pltpu.VMEM(spec_gate_far.shape, BF16),
            )
            pl.run_scoped(
                functools.partial(mlp, first, w_out, w_up, w_down, x, cot),
                pltpu.VMEM((blocks, width), F32),
                pltpu.VMEM((blocks, width), BF16),
                *[pltpu.VMEM((blocks, width), F32)] * 4,
                pltpu.VMEM((blocks, width), BF16),
                *[pltpu.VMEM((linear, 128), F32)] * 2,
            )

        pl.run_scoped(
            fetched,
            pltpu.VMEM(w_out_far.shape, BF16),
            pltpu.VMEM(w_up_far.shape, BF16),
            pltpu.VMEM(w_down_far.shape, BF16),
            pltpu.VMEM((linear, 128), F32),
            pltpu.VMEM((linear, 128), F32),
        )

        def sums(up_a, up_b, down_a, down_b, out, spec_taps, spec_gate, fin, spec, spec_sum):
            near = [
                pltpu.make_async_copy(src, dst, fetch.at[i])
                for i, (src, dst) in enumerate(((spec_taps_far, spec_taps), (spec_gate_far, spec_gate)))
            ]
            for copy in near:
                copy.start()
            quarter, part = width // 4, hidden // n
            pairs = [(share, trees[name].own) for name, share in zip(("ua", "ub", "da", "db", "out"), (up_a, up_b, down_a, down_b, out))]

            def pair_copy(i):
                return exchange(pairs[i][0].at[:, :, :, 1 - c], pairs[i][1], pair_sems.at[0, i], pair_sems.at[1, i], "core")

            def put_rows(share, half, lanes, value):
                for s in range(n):
                    for core in range(2):
                        low = (2 * s + core) * side
                        share[s // 4, (s // 2) % 2, s % 2, core, half, :, lanes] = value[low:low + side]

            def add_pair(i):
                share, pair = pairs[i]
                pair_copy(i).wait_recv()
                size = 48
                for a in range(2):
                    for b in range(2):
                        for d in range(2):
                            for e in range(2):
                                def body(k, carry):
                                    here = aligned(k, size)
                                    pair[a, b, d, e, here, :] = pair[a, b, d, e, here, :] + share[a, b, d, c, e, here, :]
                                    return carry
                                lax.fori_loop(0, pair.shape[4] // size, body, 0)


            def conv_row(r):
                posts_back[r].arrive()
                to_lanes(lambda at, size: got_one[r, at:at + size], table, spec)

                def work(re, im, at, lane, kept):
                    re, im = turn_phases(re, im, turns, lane, -1)
                    re, im = fft_points(re, im, -1)
                    tap_r, tap_i = load_phases(spec_taps, n, each, at, lane, blocks)
                    gate_r, gate_i = kept
                    out_r, out_i = [], []
                    for k in range(n):
                        here = pl.ds(k * each + at, 8)
                        lanes, other = slice(lane, lane + 128), slice(blocks + lane, blocks + lane + 128)
                        old_r, old_i = gate_r[k], gate_i[k]
                        sum_r, sum_i = old_r * re[k] + old_i * im[k], old_r * im[k] - old_i * re[k]
                        if r == 0:
                            spec_sum[here, lanes] = sum_r
                            spec_sum[here, other] = sum_i
                        else:
                            spec_sum[here, lanes] += sum_r
                            spec_sum[here, other] += sum_i
                        out_r.append(tap_r[k] * re[k] + tap_i[k] * im[k])
                        out_i.append(tap_r[k] * im[k] - tap_i[k] * re[k])
                    out_r, out_i = fft_points(out_r, out_i, 1)
                    return (turn_phases(out_r, out_i, turns, lane, 1),)

                by_halves(n, each, blocks, spec, work, (fin,), spec_gate.at[r])

                posts_long[r].drain()

                def store(at, value):
                    sent_two[r, at:at + value.shape[0]] = value.astype(BF16)

                from_lanes(fin, table, each, store)
                posts_gated[r].start()
            def up_part(i):
                for half in range(2):
                    low = half * (hidden // 2) + i * (hidden // 4)
                    value = dot_nn(turned[...], grad_act[:, low:low + hidden // 4]).astype(BF16)
                    put_rows((up_a, up_b)[i], half, ALL, value)
                pair_copy(i).start()

            def down_parts():
                for s in range(n):
                    value = dot_nn(turned_cot[...], act[:, s * part:(s + 1) * part]).astype(BF16)
                    for core in range(2):
                        for half in range(2):
                            low = (2 * core + half) * quarter
                            down_a[s // 4, (s // 2) % 2, s % 2, core, half] = value[low:low + quarter // 2]
                            down_b[s // 4, (s // 2) % 2, s % 2, core, half] = value[low + quarter // 2:low + quarter]
                pair_copy(2).start()
                pair_copy(3).start()

            def out_part():
                for half in range(2):
                    low = half * (width // 2)
                    value = sum(dot_nn(mixed[r], mix_back[r, :, low:low + width // 2]) for r in range(rows)).astype(BF16)
                    put_rows(out, half, ALL, value)
                pair_copy(4).start()

            def tap_row():
                def work_taps(re, im, at, lane, kept):
                    re, im = fft_points(re, im, 1)
                    return (turn_phases(re, im, turns, lane, 1),)

                by_halves(n, each, blocks, spec_sum, work_taps, (fin,))

                def store_taps(at, value):
                    p = at // each
                    for half in range(2):
                        tap_own[half, p // 4, p % 4] = value[half * side:(half + 1) * side].astype(BF16)

                from_lanes(fin, table, each, store_taps)
                tap_core().start()

            up_part(0)
            up_part(1)
            add_pair(0)
            trees["ua"].start()
            for copy in near:
                copy.wait()
            conv_row(0)
            down_parts()
            conv_row(1)
            add_pair(1)
            tap_row()
            trees["ub"].start()
            add_pair(2)
            trees["da"].start()
            out_part()
            add_pair(4)
            add_pair(3)
            for i in range(5):
                pair_copy(i).wait_send()

        pl.run_scoped(
            sums,
            *[pltpu.VMEM(trees[name].own.shape[:3] + (2,) + trees[name].own.shape[3:], BF16) for name in ("ua", "ub", "da", "db", "out")],
            pltpu.VMEM((width, 2 * blocks), F32),
            pltpu.VMEM((rows, width, 2 * blocks), BF16),
            pltpu.VMEM((width, 2 * blocks), BF16),
            pltpu.VMEM((width, 2 * blocks), F32),
            pltpu.VMEM((width, 2 * blocks), F32),
        )

    pl.run_scoped(
        middle,
        pltpu.VMEM((rows * blocks, hidden), BF16),
        pltpu.VMEM((rows * blocks, hidden), BF16),
        pltpu.VMEM((width, rows * blocks), BF16),
        pltpu.VMEM((width, rows * blocks), BF16),
        pltpu.VMEM((rows, width, blocks), BF16),
        pltpu.VMEM((rows, blocks, width), BF16),
    )

    def token_phase(turned, w_in, x, mid, gate_back, short, part_proj, grad_norm, gain_lanes, share0, share1, share2):
        for k, share in enumerate((share0, share1, share2)):
            trees["in%d" % k].share = share
        near = [
            pltpu.make_async_copy(src, dst, fetch.at[i])
            for i, (src, dst) in enumerate((
                (w_in_far, w_in), (turned_far, turned), (x_far, x), (mid_far, mid),
            ))
        ]
        for copy in near:
            copy.start()
        tap_core().wait_recv()
        for half in range(2):
            for q in range(4):
                tap_own[c, half, q] = tap_own[c, half, q] + tap_got[half, q]
        tap_y().start()

        def token_row(r):
            tokens = slice(r * blocks, (r + 1) * blocks)
            posts_gated[r].arrive()
            gate_back[...] = got_two[r].astype(F32).T

            def lanes_step(lanes):
                skip = small[9:10, lanes]

                def rows_step(here):
                    there = pl.ds(pl.multiple_of(r * blocks + here.start, 64), here.size)
                    grad = gate_back[here, lanes] + skip * saved[3, r, here, lanes].astype(F32)
                    short[there, lanes] = saved[2, r, here, lanes]
                    second = pl.ds(pl.multiple_of(lanes.start + width, 128), 128)
                    third = pl.ds(pl.multiple_of(lanes.start + 2 * width, 128), 128)
                    short[there, second] = (grad * saved[1, r, here, lanes].astype(F32)).astype(BF16)
                    short[there, third] = (grad * saved[0, r, here, lanes].astype(F32)).astype(BF16)

                over_rows(blocks, 64, rows_step)

            over_lanes(width, lanes_step)

        def spread(r, j):
            def lanes_step(lanes):
                def rows_step(here):
                    there = pl.ds(pl.multiple_of(r * blocks + here.start, 64), here.size)
                    for k in range(3):
                        cols = pl.ds(pl.multiple_of(lanes.start + k * width, 128), 128)
                        value = short[there, cols].astype(F32) * small[3 * k + j:3 * k + j + 1, lanes]
                        if j > 0:
                            value = value * same[j - 1, r, here, :]
                        part_proj[here, cols] = value.astype(BF16)

                over_rows(blocks, 64, rows_step)

            over_lanes(width, lanes_step)
            return dot_nt(part_proj[...], w_in[...])

        def send_hand(r):
            hand[0, r] = spread(r, 1).astype(BF16)
            side_copy(r).start()
            hand[1, r] = spread(r, 2).astype(BF16)

            @pl.when(xbit == 0)
            def _():
                far_copy(r).start()

        def hand_on(r):
            @pl.when(xbit == 1)
            def _():
                side_copy(r).wait_recv()
                hand[1, r] = (hand[1, r].astype(F32) + land[0, r].astype(F32)).astype(BF16)
                far_copy(r).start()

        def weight_part(k):
            share = trees["in%d" % k].share
            for half in range(2):
                low = k * width + half * (width // 2)
                cols = slice(low, low + width // 2)
                lanes = slice(half * (width // 2), (half + 1) * (width // 2))
                total = None
                for j in range(3):
                    value = dot_nn(turned[j], short[:, cols])
                    vectors[3 * k + j:3 * k + j + 1, lanes] = jnp.sum(value * w_in[:, cols].astype(F32), axis=0, keepdims=True)
                    value = value * small[3 * k + j:3 * k + j + 1, lanes]
                    total = value if total is None else total + value
                product = total * w_in[:, cols].astype(F32)
                gain_lanes[...] += sum(product[:, at:at + 128] for at in range(0, width // 2, 128))
                total = total.astype(BF16)
                for s in range(n):
                    for core in range(2):
                        block = (2 * s + core) * side
                        share[s // 4, (s // 2) % 2, s % 2, core, half] = total[block:block + side]
            trees["in%d" % k].start()

        def last_row(r):
            tokens = slice(r * blocks, (r + 1) * blocks)

            @pl.when(xbit == 0)
            def _():
                side_copy(r).wait_recv()
                grad_norm[r] += land[0, r].astype(F32)

            far_copy(r).wait_recv()
            late = land[1, r].astype(F32)

            @pl.when(at_end)
            def _():
                grad_norm[r] += turn_rows(late, blocks - 1)

            @pl.when(jnp.logical_not(at_end))
            def _():
                grad_norm[r] += late

            grad = grad_norm[r]
            parts = [strided(x, blocks, r * blocks, j, wide) for j in range(wide)]
            total = sum(jnp.sum(part * part, axis=-1, keepdims=True) for part in parts)
            scale = lax.rsqrt(total * (1.0 / width) + EPS)
            inner = 0.0
            scaled = []
            for j, part in enumerate(parts):
                lanes = slice(j * 128, (j + 1) * 128)
                piece = grad[:, lanes]
                scaled.append(piece * gain_one[:, lanes])
                inner += jnp.sum(scaled[j] * part, axis=-1, keepdims=True)
            shift = inner * (1.0 / width) * (scale * scale * scale)
            for j, part in enumerate(parts):
                place_at = pl.ds(r * linear + j, blocks, stride=wide)
                mid[place_at, :] += scaled[j] * scale - part * shift
            done = slice(r * linear, (r + 1) * linear)
            ready.append(pltpu.make_async_copy(mid.at[done], flat_far.at[done], keep.at[r]))
            ready[-1].start()

        def tap_home():
            tap_y().wait_recv()
            for q in range(4):
                tap_part[q] = tap_own[c, y, q] + tap_half[q]
            for q in range(4):
                @pl.when(4 * y + q != me)
                def _():
                    home_copy(q, me).start()

                @pl.when(4 * y + q == me)
                def _():
                    tap_all[c, me] = tap_part[q]

        def tap_return():
            @pl.when(home)
            def _():
                for j in range(1, n):
                    peer = lax.rem(me + j, n)
                    remote(tap_part.at[0], tap_all.at[c, peer], home_send.at[0], home_recv.at[peer], {"seq": peer}).wait_recv()
                tap_back_y().start()

        def tap_share():
            @pl.when(jnp.logical_not(home))
            def _():
                tap_back_y().wait_recv()

            tap_back_core().start()

        def vector_copy(step):
            axis = ("core", "y", "x", "zl", "zh")[step]
            return exchange(vectors, vector_got.at[step], vector_sems.at[0, step], vector_sems.at[1, step], axis)

        def vector_start():
            vectors[10:11, :] = jnp.sum(gain_lanes[...].T, axis=0, keepdims=True) / gain_one
            vector_copy(0).start()

        def vector_finish(step):
            vector_copy(step).wait()
            vectors[...] += vector_got[step]
            if step < 4:
                vector_copy(step + 1).start()

        def whole_norm():
            for r in range(rows):
                grad_norm[r] = spread(r, 0)
            for copy in near[2:4]:
                copy.wait()

        ready = []
        gain_lanes[...] = jnp.zeros_like(gain_lanes)
        trees["ua"].finish()
        trees["db"].start()
        token_row(0)
        near[0].wait()
        send_hand(0)
        trees["ub"].finish()
        tap_home()
        trees["da"].finish()
        token_row(1)
        send_hand(1)
        trees["ua"].finish()
        near[1].wait()
        weight_part(0)
        hand_on(0)
        trees["in0"].finish()
        weight_part(1)
        weight_part(2)
        hand_on(1)
        trees["db"].finish()
        whole_norm()
        trees["da"].finish()
        trees["in1"].finish()
        vector_start()
        trees["ua"].finish()
        trees["in2"].finish()
        trees["in0"].finish()
        trees["out"].start()
        trees["ub"].finish()
        trees["db"].finish()
        vector_finish(0)
        trees["da"].finish()
        trees["in2"].finish()
        trees["in1"].finish()
        tap_return()
        trees["db"].finish()
        trees["in0"].finish()
        trees["out"].finish()
        trees["ub"].finish()
        trees["in1"].finish()
        last_row(0)
        trees["out"].finish()
        trees["da"].finish()
        vector_finish(1)
        trees["in0"].finish()
        trees["in2"].finish()
        trees["db"].finish()
        trees["in1"].finish()
        last_row(1)
        trees["out"].finish()
        trees["ua"].finish()
        trees["ub"].finish()
        vector_finish(2)
        trees["da"].finish()
        tap_share()
        trees["in2"].finish()
        trees["db"].finish()
        trees["in0"].finish()
        trees["in1"].finish()
        trees["out"].finish()
        trees["ua"].finish()
        trees["ub"].finish()
        trees["in2"].finish()
        vector_finish(3)
        tap_back_core().wait_recv()
        trees["in0"].finish()
        trees["db"].finish()
        trees["in1"].finish()
        trees["ub"].finish()
        trees["out"].finish()
        trees["in0"].finish()
        trees["ua"].finish()
        trees["in2"].finish()
        vector_finish(4)
        trees["in1"].finish()
        trees["out"].finish()
        trees["da"].finish()
        trees["in2"].finish()
        for copy in ready:
            copy.wait()

        for tree in trees.values():
            tree.drain()
        for post in [post_marks] + posts_back + posts_gated:
            post.drain()
        for r in range(rows):
            side_copy(r).wait_send()
            far_copy(r).wait_send()
        tap_core().wait_send()
        tap_y().wait_send()
        for q in range(4):
            @pl.when(4 * y + q != me)
            def _():
                home_copy(q, me).wait_send()

        @pl.when(home)
        def _():
            tap_back_y().wait_send()

        tap_back_core().wait_send()

        @pl.when(chosen_chunk)
        def _():
            tap_spread("core").wait_send()

        @pl.when(zh == y)
        def _():
            tap_spread("y").wait_send()

    pl.run_scoped(
        token_phase,
        pltpu.VMEM(turned_far.shape, BF16),
        pltpu.VMEM(w_in_far.shape, BF16),
        pltpu.VMEM(x_far.shape, F32),
        pltpu.VMEM(x_far.shape, F32),
        pltpu.VMEM((blocks, width), F32),
        pltpu.VMEM((rows * blocks, 3 * width), BF16),
        pltpu.VMEM((blocks, 3 * width), BF16),
        pltpu.VMEM((rows, blocks, width), F32),
        pltpu.VMEM((width, 128), F32),
        *[pltpu.VMEM((2, 2, 2, 2, 2, side, width // 2), BF16)] * 3,
    )


def last_kernel(
    block_in, flat_in, got_ua, got_ub, got_da, got_db, got_out, got_in0, got_in1, got_in2, tap_all, taps, vectors,
    out, grad_flat, gain_mix, grad_in, grad_taps, grad_kernel, grad_skip, grad_out, gain_mlp, grad_up, grad_down, rms,
):
    out[...] = block_in[...]
    grad_flat[...] = flat_in[...]
    width = vectors.shape[1]
    side, wide, blocks = got_out.shape[2], width // 128, tap_all.shape[3]
    half_up = grad_up.shape[1] // 2
    for got, target, low, skip in (
        (got_ua, grad_up, 0, half_up), (got_ub, grad_up, half_up // 2, half_up), (got_out, grad_out, 0, width // 2),
        (got_in0, grad_in, 0, width // 2), (got_in1, grad_in, width, width // 2), (got_in2, grad_in, 2 * width, width // 2),
    ):
        l = got.shape[3]
        for half in range(2):
            for core in range(2):
                at = low + half * skip
                target[core * side:(core + 1) * side, at:at + l] = got[core, half].astype(F32)
    grad_down[...] = jnp.concatenate(
        [got[core, half] for core in range(2) for half in range(2) for got in (got_da, got_db)], axis=0
    ).astype(F32).T
    value = jnp.concatenate(
        [tap_all[core, s] for s in range(tap_all.shape[1]) for core in range(2)], axis=0
    ).astype(F32).T
    for j in range(wide):
        place_at = pl.ds(j, blocks, stride=wide)
        tanh = jnp.tanh(taps[place_at, :] * (1.0 / THRESH))
        grad_kernel[place_at, :] = value[:, j * 128:(j + 1) * 128] * (tanh * tanh)
    for k in range(3):
        grad_taps[:, k * width:(k + 1) * width] = vectors[3 * k:3 * k + 3, :]
    for target, row in ((grad_skip, 9), (gain_mix, 10), (gain_mlp, 11)):
        target[...] = vectors[row, :]
    total = jnp.sum(vectors[12:16, :], axis=1, keepdims=True)
    found = jnp.sqrt(total / (jnp.maximum(total[3:4, :], 1.0) * width))
    for i in range(3):
        rms[i] = found[i, 0]


def call(body, outs, scratch, inputs, collective_id, far=(), far_outs=()):
    return pl.pallas_call(
        body,
        out_shape=tuple(jax.ShapeDtypeStruct(*out) for out in outs),
        in_specs=[pl.BlockSpec(memory_space=pl.ANY if i in far else pltpu.VMEM) for i in range(len(inputs))],
        out_specs=tuple(pl.BlockSpec(memory_space=pl.ANY if i in far_outs else pltpu.VMEM) for i in range(len(outs))),
        scratch_shapes=scratch,
        compiler_params=pltpu.CompilerParams(
            vmem_limit_bytes=VMEM_BYTES, collective_id=collective_id, has_side_effects=True
        ),
    )(*inputs)


def local(
    block_in, segment_ids, valid_mask, cotangent, gain_mix, in_proj, short_taps, long_kernel,
    skip_gain, out_proj, gain_mlp, up_proj, down_proj,
):
    rows, blocks, _, width = block_in.shape
    hidden = up_proj.shape[1]
    n = lax.axis_size("seq")
    each = width // n
    tokens = rows * blocks
    side, wide = each // 2, width // 128
    chunk = 768
    x = block_in.reshape(tokens * wide, 128)
    cot = cotangent.reshape(tokens * wide, 128)
    raw = long_kernel.reshape(blocks * wide, 128)
    segments = segment_ids.reshape(rows, 1, blocks)
    valid = valid_mask.reshape(rows, 1, blocks)
    table, turns = spectrum_tables(blocks, n)
    dma = pltpu.SemaphoreType.DMA
    bits = (2, 2, 2, 2, 2)
    up_shape = bits[1:] + (side, hidden // 4)
    down_shape = bits[1:] + (width // 8, hidden // n)
    out_shape = bits[1:] + (side, width // 2)
    own_shapes = (up_shape, up_shape, down_shape, down_shape, out_shape)
    low = lambda *shape: pltpu.VMEM(shape, BF16)
    full = lambda *shape: pltpu.VMEM(shape, F32)

    trees = []
    for shape in own_shapes:
        trees += tree_scratch(*shape[4:])
    for _ in range(3):
        trees += tree_scratch(*out_shape[4:])
    gots = [(2, 2) + shape[4:] for shape in own_shapes + (out_shape,) * 3]
    quarter = (4, side, blocks)
    pair = (rows, 2, n)
    block_out, grad_flat, _, _, _, _, *gathered, taps_back, vectors = call(
        functools.partial(whole_kernel, n, chunk),
        [
            (x.shape, F32),
            (x.shape, F32),
            (x.shape, F32),
            ((3, width, tokens), BF16),
            ((width, 2 * blocks), F32),
            ((rows, width, 2 * blocks), BF16),
            *[(shape, BF16) for shape in gots],
            ((2, n, side, blocks), BF16),
            ((16, width), F32),
        ],
        [
            full(16, width), low(*table.shape), full(8, blocks), full(n, 8, blocks), low(2, rows, blocks, width), low(width, blocks),
            full(rows, blocks, width), low(4, rows, blocks, width), full(3, rows, blocks, 128),
            low(rows, width, blocks), low(rows, width, blocks), low(rows, width, blocks), low(rows, width, blocks),
            low(2, rows, blocks, width),
            low(2, 2, *quarter), low(2, *quarter), low(*quarter), low(*quarter), full(5, 16, width),
            dma((5,)), dma((5,)), dma((2, 2, rows, 2)), dma((2, n)), dma((4, n)),
            dma(pair), dma(pair), dma(pair), dma(pair), dma((2, 2, rows)),
            dma((2, 5)), dma((2, 4)), dma((4,)), dma((n,)), dma((2, 5)),
        ] + trees,
        (x, cot, raw, short_taps, skip_gain, gain_mix, gain_mlp, segments, valid, in_proj, out_proj, up_proj, down_proj, table, turns),
        1,
        far=(0, 1, 2, 9, 10, 11, 12),
        far_outs=range(6),
    )
    inputs = (block_out, grad_flat, *gathered, taps_back, raw, vectors)
    near = pl.BlockSpec(memory_space=pltpu.VMEM)
    outs = [
        x.shape, x.shape, (width,), (each, 3 * width), (3, 3 * width), raw.shape, (width,), (each, width), (width,),
        (each, hidden), (hidden // n, width), (3,),
    ]
    results = pl.pallas_call(
        last_kernel,
        out_shape=tuple(jax.ShapeDtypeStruct(shape, F32) for shape in outs),
        in_specs=[near] * len(inputs),
        out_specs=(near,) * 11 + (pl.BlockSpec(memory_space=pltpu.SMEM),),
        compiler_params=pltpu.CompilerParams(vmem_limit_bytes=VMEM_BYTES),
    )(*inputs)
    shapes = {0: block_in.shape, 1: block_in.shape, 5: long_kernel.shape}
    return tuple(value.reshape(shapes.get(i, value.shape)) for i, value in enumerate(results))


def chosen(block_in, *rest):
    rows, blocks, _, width = block_in.shape
    n = lax.axis_size("seq")
    fits = blocks % (32 * n) == 0 and width % (32 * n) == 0 and n == 8 and rows == 2 and lax.axis_size("rows") == 4
    return (local if fits else general_local)(block_in, *rest)


def solution(mesh):
    return jax.shard_map(
        chosen,
        mesh=mesh,
        in_specs=(
            P("rows", None, "seq", None),
            P("rows", None, "seq"),
            P("rows", None, "seq"),
            P("rows", None, "seq", None),
            P(),
            P(),
            P(),
            P(None, "seq", None),
            P(),
            P(),
            P(),
            P(),
            P(),
        ),
        out_specs=(
            P("rows", None, "seq", None),
            P("rows", None, "seq", None),
            P(),
            P("seq", None),
            P(),
            P(None, "seq", None),
            P(),
            P("seq", None),
            P(),
            P("seq", None),
            P("seq", None),
            P(),
        ),
        check_vma=False,
    )
```

```python
import functools
import itertools
import math

import jax
import jax.numpy as jnp
import numpy as np
from jax import lax
from jax.experimental import pallas as pl
from jax.experimental.pallas import tpu as pltpu
from jax.sharding import PartitionSpec as P

EPS = 1e-05
THRESH = 0.003
HIGH = lax.Precision.HIGHEST


def shortened(x):

    def short(part):
        return part.astype(jnp.bfloat16) if part.dtype == jnp.float32 else part

    return jax.tree.map(short, x)


def passed_along(block, axis, distance):
    devices = range(lax.axis_size(axis))
    route = [((i - distance) % len(devices), i) for i in devices]
    return lax.ppermute(block, axis, route)


def norm_scale(value, gain):
    return value * lax.rsqrt(jnp.mean(value * value, axis=-1, keepdims=True) + EPS) * gain


def angle_tables(left_count, right_count, period):
    left_idx = jnp.arange(left_count, dtype=jnp.int32)[:, None]
    right_idx = jnp.arange(right_count, dtype=jnp.int32)[None, :]
    phase = (left_idx * right_idx % period).astype(jnp.float32) * (2.0 * math.pi / period)
    return (jnp.cos(phase), jnp.sin(phase))


def twiddle_tables(shard_index, spec_len, whole_len):
    turned = shard_index * jnp.arange(spec_len, dtype=jnp.int32) % whole_len
    phase = turned.astype(jnp.float32) * (2.0 * math.pi / whole_len)
    return (jnp.cos(phase)[None, :, None], jnp.sin(phase)[None, :, None])


def local_forward(signal, shard_index, whole_len):
    blocks = signal.shape[1]
    cos_table, sin_table = angle_tables(blocks, 2 * blocks, 2 * blocks)
    real_part = jnp.einsum("rjd,jk->rkd", signal, cos_table, precision=HIGH)
    imag_part = -jnp.einsum("rjd,jk->rkd", signal, sin_table, precision=HIGH)
    cos_twid, sin_twid = twiddle_tables(shard_index, 2 * blocks, whole_len)
    out_real = real_part * cos_twid + imag_part * sin_twid
    out_imag = imag_part * cos_twid - real_part * sin_twid
    return (out_real[:, :, None, :], out_imag[:, :, None, :])


def cross_section(real_part, imag_part, direction):
    count = real_part.shape[2]
    cos_table, sin_table = angle_tables(count, count, count)
    re_cos = jnp.einsum("rcpd,pm->rcmd", real_part, cos_table, precision=HIGH)
    re_sin = jnp.einsum("rcpd,pm->rcmd", real_part, sin_table, precision=HIGH)
    im_cos = jnp.einsum("rcpd,pm->rcmd", imag_part, cos_table, precision=HIGH)
    im_sin = jnp.einsum("rcpd,pm->rcmd", imag_part, sin_table, precision=HIGH)
    return (re_cos - direction * im_sin, im_cos + direction * re_sin)


def local_inverse(real_part, imag_part, shard_index, whole_len):
    real_part = real_part[:, :, 0, :]
    imag_part = imag_part[:, :, 0, :]
    spec_len = real_part.shape[1]
    cos_twid, sin_twid = twiddle_tables(shard_index, spec_len, whole_len)
    turned_re = real_part * cos_twid - imag_part * sin_twid
    turned_im = imag_part * cos_twid + real_part * sin_twid
    cos_table, sin_table = angle_tables(spec_len, spec_len // 2, spec_len)
    result = jnp.einsum("rkd,kj->rjd", turned_re, cos_table, precision=HIGH)
    result = result - jnp.einsum("rkd,kj->rjd", turned_im, sin_table, precision=HIGH)
    return result / whole_len


def earlier(members, at_start):
    received = jax.tree.map(
        lambda part, own: part.astype(own.dtype),
        passed_along(shortened(members), "seq", 1),
        members,
    )
    placed = []
    for member in received:
        rolled = jnp.concatenate([jnp.zeros_like(member[:, :1]), member[:, :-1]], axis=1)
        placed.append(jnp.where(at_start, rolled, member))
    return tuple(placed)


def later(member, at_end):
    received = passed_along(member.astype(jnp.bfloat16), "seq", -1).astype(member.dtype)
    rolled = jnp.concatenate([received[:, 1:], jnp.zeros_like(received[:, :1])], axis=1)
    return jnp.where(at_end, rolled, received)


def times_trans(left, right):
    return lax.dot_general(
        left, right, (((1,), (1,)), ((), ())), preferred_element_type=jnp.float32
    )


def trans_times(left, right):
    return lax.dot_general(
        left, right, (((0,), (0,)), ((), ())), preferred_element_type=jnp.float32
    )


def general_local(
    block_in,
    segment_ids,
    valid_mask,
    cotangent,
    gain_mix,
    in_proj,
    short_taps,
    long_kernel,
    skip_gain,
    out_proj,
    gain_mlp,
    up_proj,
    down_proj,
):
    batch_rows = block_in.shape[0]
    blocks = block_in.shape[1]
    width = block_in.shape[3]
    shard_count = lax.axis_size("seq")
    shard_index = lax.axis_index("seq")
    whole_len = 2 * blocks * shard_count
    tokens = batch_rows * blocks
    at_start = shard_index == 0
    at_end = shard_index == shard_count - 1
    flat_in = block_in.reshape(tokens, width)
    mask_rows = valid_mask[:, :, 0].astype(jnp.float32)[:, :, None]
    normed_one = norm_scale(flat_in, gain_mix).astype(jnp.bfloat16)
    proj_low = jnp.dot(normed_one, in_proj, preferred_element_type=jnp.float32).astype(jnp.bfloat16)
    proj_low = proj_low.reshape(batch_rows, blocks, 3 * width)
    seg_low = segment_ids[:, :, 0].astype(jnp.bfloat16)[:, :, None]
    prev_one = earlier((proj_low, seg_low), at_start)
    prev_two = earlier(prev_one, at_start)
    same_one = (prev_one[1] == seg_low).astype(jnp.float32)
    same_two = (prev_two[1] == seg_low).astype(jnp.float32)
    proj_now = proj_low.astype(jnp.float32)
    proj_one = prev_one[0].astype(jnp.float32)
    proj_two = prev_two[0].astype(jnp.float32)
    conv_short = (
        short_taps[0] * proj_now
        + short_taps[1] * proj_one * same_one
        + short_taps[2] * proj_two * same_two
    )
    query = conv_short[:, :, :width]
    keys = conv_short[:, :, width : 2 * width]
    values = conv_short[:, :, 2 * width :]
    gated = keys * values * mask_rows
    raw_taps = long_kernel[:, 0, :]
    taps_eff = raw_taps - THRESH * jnp.tanh(raw_taps / THRESH)
    kern_re, kern_im = local_forward(taps_eff[None], shard_index, whole_len)
    kern_re, kern_im = (
        lax.all_to_all(
            kern_re.astype(jnp.bfloat16), "seq", split_axis=1, concat_axis=2, tiled=True
        ).astype(kern_re.dtype),
        lax.all_to_all(
            kern_im.astype(jnp.bfloat16), "seq", split_axis=1, concat_axis=2, tiled=True
        ).astype(kern_im.dtype),
    )
    kern_re, kern_im = cross_section(kern_re, kern_im, -1.0)
    gate_re, gate_im = local_forward(gated, shard_index, whole_len)
    gate_re, gate_im = (
        lax.all_to_all(
            gate_re.astype(jnp.bfloat16), "seq", split_axis=1, concat_axis=2, tiled=True
        ).astype(gate_re.dtype),
        lax.all_to_all(
            gate_im.astype(jnp.bfloat16), "seq", split_axis=1, concat_axis=2, tiled=True
        ).astype(gate_im.dtype),
    )
    gate_re, gate_im = cross_section(gate_re, gate_im, -1.0)
    prod_re = gate_re * kern_re - gate_im * kern_im
    prod_im = gate_re * kern_im + gate_im * kern_re
    prod_re, prod_im = cross_section(prod_re, prod_im, 1.0)
    prod_re, prod_im = (
        lax.all_to_all(
            prod_re.astype(jnp.bfloat16), "seq", split_axis=2, concat_axis=1, tiled=True
        ).astype(prod_re.dtype),
        lax.all_to_all(
            prod_im.astype(jnp.bfloat16), "seq", split_axis=2, concat_axis=1, tiled=True
        ).astype(prod_im.dtype),
    )
    long_out = local_inverse(prod_re, prod_im, shard_index, whole_len) + skip_gain * gated
    mixer_low = (query * long_out).reshape(tokens, width).astype(jnp.bfloat16)
    mixer_out = jnp.dot(mixer_low, out_proj, preferred_element_type=jnp.float32)
    resid_mid = flat_in + mixer_out
    normed_two = norm_scale(resid_mid, gain_mlp).astype(jnp.bfloat16)
    up_val = jnp.dot(normed_two, up_proj, preferred_element_type=jnp.float32)
    act_low = jax.nn.gelu(up_val).astype(jnp.bfloat16)
    mlp_out = jnp.dot(act_low, down_proj, preferred_element_type=jnp.float32)
    flat_out = resid_mid + mlp_out
    grad_out = cotangent.reshape(tokens, width)
    grad_mlp = grad_out.astype(jnp.bfloat16)
    grad_down = trans_times(act_low, grad_mlp)
    grad_act = times_trans(grad_mlp, down_proj)
    unused_val, gelu_back = jax.vjp(jax.nn.gelu, up_val)
    grad_upval = gelu_back(grad_act)[0].astype(jnp.bfloat16)
    grad_up = trans_times(normed_two, grad_upval)
    grad_norm_two = times_trans(grad_upval, up_proj)
    unused_two, norm_back_two = jax.vjp(norm_scale, resid_mid, gain_mlp)
    grad_resid, grad_gain_two = norm_back_two(grad_norm_two)
    grad_mid = grad_out + grad_resid
    grad_mix = grad_mid.astype(jnp.bfloat16)
    grad_outp = trans_times(mixer_low, grad_mix)
    grad_prod = times_trans(grad_mix, out_proj).reshape(batch_rows, blocks, width)
    grad_query = grad_prod * long_out
    grad_long = grad_prod * query
    back_re, back_im = local_forward(grad_long, shard_index, whole_len)
    back_re, back_im = (
        lax.all_to_all(
            back_re.astype(jnp.bfloat16), "seq", split_axis=1, concat_axis=2, tiled=True
        ).astype(back_re.dtype),
        lax.all_to_all(
            back_im.astype(jnp.bfloat16), "seq", split_axis=1, concat_axis=2, tiled=True
        ).astype(back_im.dtype),
    )
    back_re, back_im = cross_section(back_re, back_im, -1.0)
    sig_re = kern_re * back_re + kern_im * back_im
    sig_im = kern_re * back_im - kern_im * back_re
    tap_re = jnp.sum(gate_re * back_re + gate_im * back_im, axis=0, keepdims=True)
    tap_im = jnp.sum(gate_re * back_im - gate_im * back_re, axis=0, keepdims=True)
    sig_re, sig_im = cross_section(sig_re, sig_im, 1.0)
    tap_re, tap_im = cross_section(tap_re, tap_im, 1.0)
    sig_re, sig_im, tap_re, tap_im = (
        lax.all_to_all(
            sig_re.astype(jnp.bfloat16), "seq", split_axis=2, concat_axis=1, tiled=True
        ).astype(sig_re.dtype),
        lax.all_to_all(
            sig_im.astype(jnp.bfloat16), "seq", split_axis=2, concat_axis=1, tiled=True
        ).astype(sig_im.dtype),
        lax.all_to_all(
            tap_re.astype(jnp.bfloat16), "seq", split_axis=2, concat_axis=1, tiled=True
        ).astype(tap_re.dtype),
        lax.all_to_all(
            tap_im.astype(jnp.bfloat16), "seq", split_axis=2, concat_axis=1, tiled=True
        ).astype(tap_im.dtype),
    )
    grad_gated = local_inverse(sig_re, sig_im, shard_index, whole_len) + skip_gain * grad_long
    grad_taps_eff = local_inverse(tap_re, tap_im, shard_index, whole_len)[0]
    tanh_val = jnp.tanh(raw_taps / THRESH)
    grad_kernel = (grad_taps_eff * tanh_val * tanh_val)[:, None, :]
    grad_kernel = lax.psum(grad_kernel.astype(jnp.bfloat16), "rows").astype(jnp.float32)
    grad_skip = jnp.sum(grad_long * gated, axis=(0, 1))
    grad_short = jnp.concatenate(
        [grad_query, grad_gated * values * mask_rows, grad_gated * keys * mask_rows], axis=2
    )
    grad_tap_rows = jnp.stack(
        [
            jnp.sum(grad_short * proj_now, axis=(0, 1)),
            jnp.sum(grad_short * proj_one * same_one, axis=(0, 1)),
            jnp.sum(grad_short * proj_two * same_two, axis=(0, 1)),
        ]
    )
    inner_term = short_taps[1] * grad_short * same_one + later(
        short_taps[2] * grad_short * same_two, at_end
    )
    grad_proj = short_taps[0] * grad_short + later(inner_term, at_end)
    grad_proj = grad_proj.reshape(tokens, 3 * width).astype(jnp.bfloat16)
    grad_inp = trans_times(normed_one, grad_proj)
    grad_norm_one = times_trans(grad_proj, in_proj)
    unused_one, norm_back_one = jax.vjp(norm_scale, flat_in, gain_mix)
    grad_first, grad_gain_one = norm_back_one(grad_norm_one)
    grad_flat = grad_mid + grad_first
    mask_flat = mask_rows.reshape(tokens, 1)
    stat_sums = jnp.stack(
        [
            jnp.sum(mask_flat * flat_out * flat_out),
            jnp.sum(mask_flat * mixer_out * mixer_out),
            jnp.sum(mask_flat * mlp_out * mlp_out),
            jnp.sum(mask_flat),
        ]
    )
    grad_gain_one, grad_gain_two, grad_tap_rows, grad_skip, stat_sums = lax.psum(
        (grad_gain_one, grad_gain_two, grad_tap_rows, grad_skip, stat_sums), ("rows", "seq")
    )
    rms_stats = jnp.sqrt(stat_sums[:3] / (jnp.maximum(stat_sums[3], 1.0) * width))
    shares = (
        lax.psum_scatter(grad_inp, "seq", scatter_dimension=0, tiled=True),
        lax.psum_scatter(grad_outp, "seq", scatter_dimension=0, tiled=True),
        lax.psum_scatter(grad_up, "seq", scatter_dimension=0, tiled=True),
        lax.psum_scatter(grad_down, "seq", scatter_dimension=0, tiled=True),
    )
    grad_inp, grad_outp, grad_up, grad_down = (
        lax.psum(shares[0].astype(jnp.bfloat16), "rows").astype(jnp.float32),
        lax.psum(shares[1].astype(jnp.bfloat16), "rows").astype(jnp.float32),
        lax.psum(shares[2].astype(jnp.bfloat16), "rows").astype(jnp.float32),
        lax.psum(shares[3].astype(jnp.bfloat16), "rows").astype(jnp.float32),
    )
    return (
        flat_out.reshape(block_in.shape),
        grad_flat.reshape(block_in.shape),
        grad_gain_one,
        grad_inp,
        grad_tap_rows,
        grad_kernel,
        grad_skip,
        grad_outp,
        grad_gain_two,
        grad_up,
        grad_down,
        rms_stats,
    )


MESH = pl.DeviceIdType.MESH
F32 = jnp.float32
BF16 = jnp.bfloat16
VMEM_BYTES = 62 * 1024 * 1024
C0 = math.sqrt(2.0 / math.pi)
C1 = 0.044715
ALL = slice(None)
ORDERS = (
    ("y", "zl", "x", "zh"),
    ("y", "zl", "x", "zh"),
    ("x", "y", "zl", "zh"),
    ("y", "x", "zl", "zh"),
    ("y", "x", "zl", "zh"),
    ("y", "x", "zl", "zh"),
    ("y", "zl", "x", "zh"),
    ("x", "y", "zl", "zh"),
)


def dot_nn(a, b):
    return lax.dot_general(a, b, (((1,), (0,)), ((), ())), preferred_element_type=F32)


def dot_nt(a, b):
    return lax.dot_general(a, b, (((1,), (1,)), ((), ())), preferred_element_type=F32)


def fft_points(re, im, sign):
    n = len(re)
    if n == 1:
        return re, im
    even_r, even_i = fft_points(re[0::2], im[0::2], sign)
    odd_r, odd_i = fft_points(re[1::2], im[1::2], sign)
    out_r, out_i = [None] * n, [None] * n
    for k in range(n // 2):
        if k == 0:
            turn_r, turn_i = odd_r[0], odd_i[0]
        elif 4 * k == n:
            if sign > 0:
                out_r[k], out_i[k] = even_r[k] - odd_i[k], even_i[k] + odd_r[k]
                out_r[k + n // 2], out_i[k + n // 2] = even_r[k] + odd_i[k], even_i[k] - odd_r[k]
            else:
                out_r[k], out_i[k] = even_r[k] + odd_i[k], even_i[k] - odd_r[k]
                out_r[k + n // 2], out_i[k + n // 2] = even_r[k] - odd_i[k], even_i[k] + odd_r[k]
            continue
        else:
            cos, sin = math.cos(2 * math.pi * k / n), sign * math.sin(2 * math.pi * k / n)
            turn_r = cos * odd_r[k] - sin * odd_i[k]
            turn_i = cos * odd_i[k] + sin * odd_r[k]
        out_r[k], out_i[k] = even_r[k] + turn_r, even_i[k] + turn_i
        out_r[k + n // 2], out_i[k + n // 2] = even_r[k] - turn_r, even_i[k] - turn_i
    return out_r, out_i


def spectrum_tables(blocks, phases):
    length = blocks * phases
    k = 2 * np.arange(blocks)[None, :] + 1
    angle = 2.0 * np.pi * np.arange(blocks)[:, None] * k / (4.0 * blocks)
    table = np.concatenate([np.cos(angle), -np.sin(angle)], axis=1)
    turn = 2.0 * np.pi * np.arange(phases)[:, None] * k / (4.0 * length)
    turns = np.stack([np.cos(turn), np.sin(turn)], axis=1)[:, :, None, :]
    return jnp.asarray(table, F32), jnp.asarray(np.broadcast_to(turns, (phases, 2, 8, blocks)), F32)


def place():
    row, seq = lax.axis_index("rows"), lax.axis_index("seq")
    return lax.div(row, 2), lax.rem(row, 2), lax.div(seq, 4), lax.rem(lax.div(seq, 2), 2), lax.rem(seq, 2)


def partner(axis):
    y, c, zh, zl, x = place()
    if axis == "core":
        return {"rows": 2 * y + 1 - c}
    if axis == "y":
        return {"rows": 2 * (1 - y) + c}
    if axis == "x":
        return {"seq": 4 * zh + 2 * zl + 1 - x}
    if axis == "zl":
        return {"seq": 4 * zh + 2 * (1 - zl) + x}
    return {"seq": 4 * (1 - zh) + 2 * zl + x}


def remote(src, dst, send_sem, recv_sem, target):
    return pltpu.make_async_remote_copy(
        src_ref=src, dst_ref=dst, send_sem=send_sem, recv_sem=recv_sem, device_id=target, device_id_type=MESH,
    )


def exchange(src, dst, send_sem, recv_sem, axis):
    return remote(src, dst, send_sem, recv_sem, partner(axis))


def greet(n):
    me = lax.axis_index("seq")
    barrier = pltpu.get_barrier_semaphore()
    for j in range(1, n):
        pl.semaphore_signal(barrier, inc=1, device_id={"seq": lax.rem(me + j, n)}, device_id_type=MESH)
    for axis in ("core", "y"):
        pl.semaphore_signal(barrier, inc=1, device_id=partner(axis), device_id_type=MESH)
    return barrier, n + 1


def aligned(index, size):
    return pl.ds(pl.multiple_of(index * size, size), size)


class Post:
    def __init__(self, n, source, target, sems):
        self.n, self.source, self.target, self.sems = n, source, target, sems

    def copies(self, sender):
        me = lax.axis_index("seq")
        for j in range(1, self.n):
            peer = lax.rem(me + j, self.n)
            come = sender(peer, me)
            yield remote(
                self.source(peer), self.target(come), self.sems.at[0, j], self.sems.at[1, come], {"seq": peer}
            )

    def start(self):
        me = lax.axis_index("seq")
        for copy in self.copies(lambda peer, me: me):
            copy.start()
        self.target(me)[...] = self.source(me)[...]

    def arrive(self):
        for copy in self.copies(lambda peer, me: peer):
            copy.wait_recv()

    def drain(self):
        for copy in self.copies(lambda peer, me: me):
            copy.wait_send()


def over_groups(each, blocks, body):
    for lane in range(0, blocks, 128):
        def step(g, carry):
            body(pl.multiple_of(g * 16, 16), lane)
            return carry
        lax.fori_loop(0, each // 16, step, 0)


def matmul_rows(out, left, right, size=256):
    for at in range(0, out.shape[0], size):
        out[at:at + size, :] = left(at, size, right)


def load_phases(spec, n, each, at, lane, half):
    re = [spec[pl.ds(p * each + at, 8), lane:lane + 128] for p in range(n)]
    im = [spec[pl.ds(p * each + at, 8), half + lane:half + lane + 128] for p in range(n)]
    return re, im


def turn_phases(re, im, turns, lane, sign):
    out_r, out_i = [re[0]], [im[0]]
    for p in range(1, len(re)):
        cos, sin = turns[p, 0, :, lane:lane + 128], turns[p, 1, :, lane:lane + 128]
        if sign > 0:
            out_r.append(re[p] * cos - im[p] * sin)
            out_i.append(im[p] * cos + re[p] * sin)
        else:
            out_r.append(re[p] * cos + im[p] * sin)
            out_i.append(im[p] * cos - re[p] * sin)
    return out_r, out_i


def by_halves(n, each, blocks, spec, work, stores, kept=None):
    def group(at, lane):
        halves = []
        if kept is not None:
            loaded = [
                [kept[pl.ds(k * each + at, 16), part + lane:part + lane + 128].astype(F32) for k in range(n)]
                for part in (0, blocks)
            ]
        for half in (0, 8):
            re, im = load_phases(spec, n, each, at + half, lane, blocks)
            old = None if kept is None else [[value[half:half + 8] for value in part] for part in loaded]
            halves.append(work(re, im, at + half, lane, old))
        for target, first, second in zip(stores, *halves):
            for k in range(n):
                for part in range(2):
                    value = jnp.concatenate([first[part][k], second[part][k]], axis=0).astype(BF16)
                    target[pl.ds(k * each + at, 16), part * blocks + lane:part * blocks + lane + 128] = value

    over_groups(each, blocks, group)


def to_lanes(source, table, spec):
    for at in range(0, spec.shape[0], 256):
        spec[at:at + 256, :] = dot_nn(source(at, 256), table[...])


def from_lanes(fin, table, size, store):
    for at in range(0, fin.shape[0], size):
        store(at, dot_nt(fin[at:at + size, :], table[...]) * (2.0 / fin.shape[1] / (fin.shape[0] // size)))


def over_rows(total, size, body):
    def step(i, carry):
        body(aligned(i, size))
        return carry
    lax.fori_loop(0, total // size, step, 0)


def over_lanes(width, body):
    def step(i, carry):
        body(aligned(i, 128))
        return carry
    lax.fori_loop(0, width // 128, step, 0)


def strided(ref, rows, start, lane, wide):
    return ref[pl.ds(start * wide + lane, rows, stride=wide), :]


def turn_rows(value, amount):
    return pltpu.roll(value, amount % value.shape[0], 0)


class Tree:
    def __init__(self, order, share, own, parts, gathered, sems):
        self.order = order + ("back_y", "back_core")
        self.share, self.own, self.parts, self.gathered, self.sems = share, own, parts, gathered, sems
        self.done = 0
        self.started = []

    def half(self, step, bit):
        y, c, zh, zl, x = place()
        here = dict(zh=zh, zl=zl, x=x, y=y)
        settled = self.order[:step]
        return tuple(here[a] if a in settled else (bit(here[a]) if a == self.order[step] else ALL) for a in ("zh", "zl", "x", "y"))

    def block(self, index):
        c = place()[1]
        return (self.share, index[:3] + (c,) + index[3:]) if self.own is None else (self.own, index)

    def copies(self, step):
        y, c, zh, zl, x = place()
        axis = self.order[step]
        gathered = self.gathered
        if axis == "core":
            src = self.share.at[:, :, :, 1 - c]
        elif axis == "back_y":
            src = gathered.at[c, y]
        elif axis == "back_core":
            src = gathered.at[c]
        else:
            ref, index = self.block(self.half(step, lambda bit: 1 - bit))
            src = ref.at[index]
        dst = src if axis.startswith("back") else self.parts[step]
        return exchange(src, dst, self.sems.at[0, step], self.sems.at[1, step], axis.replace("back_", ""))

    def start(self):
        self.copies(self.done).start()
        self.started.append(self.done)

    def add(self, index, part, at, target=None):
        own, index = self.block(index)
        size = 48

        def body(i, carry):
            here = aligned(i, size)
            value = own[index + (here, ALL)] + part[at + (here, ALL)]
            if target is None:
                own[index + (here, ALL)] = value
            else:
                target[here, :] = value
            return carry

        lax.fori_loop(0, part.shape[-2] // size, body, 0)

    def finish(self, go=True):
        y, c, zh, zl, x = place()
        step = self.done
        axis = self.order[step]
        self.copies(step).wait_recv()
        if not axis.startswith("back"):
            index = (ALL,) * 4 if axis == "core" else self.half(step, lambda bit: bit)
            free = [i for i, entry in enumerate(index) if entry is ALL or isinstance(entry, slice)]
            last = self.order[step + 1] == "back_y"
            for bits in itertools.product(range(2), repeat=len(free)):
                full = list(index)
                for i, bit in zip(free, bits):
                    full[i] = bit
                self.add(tuple(full), self.parts[step], bits, self.gathered.at[c, y] if last else None)
        self.done += 1
        if go and self.done < len(self.order):
            self.start()

    def drain(self):
        for step in self.started:
            self.copies(step).wait_send()


def tree_scratch(r, l):
    shapes = [(2, 2, 2, 2, r, l), (2, 2, 2, r, l), (2, 2, r, l), (2, r, l), (r, l)]
    return [pltpu.VMEM(shape, BF16) for shape in shapes] + [pltpu.SemaphoreType.DMA((2, 7))]


def whole_kernel(
    n, chunk,
    x_far, cot_far, taps_far, short_taps, skip, gain_mix, gain_mlp, segments, valid, w_in_far, w_out_far, w_up_far, w_down_far,
    table_wide, turns,
    out_far, flat_far, mid_far, turned_far, spec_taps_far, spec_gate_far,
    got_ua, got_ub, got_da, got_db, got_out, got_in0, got_in1, got_in2, tap_all, vectors,
    small, table, marks, marks_got, land, taps_got, query, saved, same, sent_one, sent_two, got_one, got_two, hand,
    tap_own, tap_got, tap_half, tap_part, vector_got,
    fetch, keep, near_sems, mark_sems, tap_sems, gate_sems, long_sems, back_sems, gated_sems, hand_sems,
    pair_sems, home_sems, home_send, home_recv, vector_sems,
    *tree_refs,
):
    me = lax.axis_index("seq")
    y, c, zh, zl, xbit = place()
    rows, blocks = query.shape[0], query.shape[1]
    width, hidden = w_up_far.shape
    each, wide, step = width // n, width // 128, blocks // 2
    side, linear = each // 2, blocks * wide
    at_top = jnp.logical_and(zh == 0, zl == 0)
    at_end = jnp.logical_and(zh == 1, zl == 1)
    chosen_chunk = jnp.logical_and(zh == y, zl == c)
    home = zh == y
    barrier, told = greet(n)
    for row, vector in ((9, skip), (10, gain_mix), (11, gain_mlp)):
        small[row, :] = vector[...]
    gain_one, gain_two = small[10:11, :], small[11:12, :]
    table[...] = table_wide[...].astype(BF16)

    trees, at = {}, 0
    for name, got, order in zip(("ua", "ub", "da", "db", "out"), (got_ua, got_ub, got_da, got_db, got_out), ORDERS):
        trees[name] = Tree(order, None, tree_refs[at], tree_refs[at + 1:at + 5], got, tree_refs[at + 5])
        at += 6
    for name, got, order in (("in0", got_in0, ORDERS[5]), ("in1", got_in1, ORDERS[6]), ("in2", got_in2, ORDERS[7])):
        trees[name] = Tree(("core",) + order, None, None, tree_refs[at:at + 5], got, tree_refs[at + 5])
        at += 6

    post_marks = Post(n, lambda d: marks, lambda p: marks_got.at[p], mark_sems)

    def posts(sent, got, sems):
        return [
            Post(n, lambda e, r=r: sent.at[r, aligned(e, each)], lambda p, r=r: got.at[r, aligned(p, each)], sems.at[r])
            for r in range(rows)
        ]

    posts_gate = posts(sent_one, got_one, gate_sems)
    posts_long = posts(sent_two, got_two, long_sems)
    posts_back = posts(sent_one, got_one, back_sems)
    posts_gated = posts(sent_two, got_two, gated_sems)

    def near_far(r, h, source):
        part = slice(h * step, (h + 1) * step)
        target = {"seq": lax.rem(me + 2, n)}
        return remote(source.at[r, part], land.at[1, r, part], near_sems.at[0, 0, r, h], near_sems.at[0, 1, r, h], target)

    def near_side(r, h, source):
        part = slice(h * step, (h + 1) * step)
        return exchange(source.at[r, part], land.at[0, r, part], near_sems.at[1, 0, r, h], near_sems.at[1, 1, r, h], "x")

    def tap_copy(e, taps_sent):
        return remote(taps_sent.at[aligned(e, each)], taps_got.at[aligned(me, each)], tap_sems.at[0, lax.rem(e, 2)], tap_sems.at[1, me], {"seq": e})

    def tap_spread(axis):
        at = 2 if axis == "core" else 3
        return exchange(taps_got, taps_got, tap_sems.at[at, 0], tap_sems.at[at, 1], axis)

    def side_copy(r):
        return exchange(hand.at[0, r], land.at[0, r], hand_sems.at[0, 0, r], hand_sems.at[0, 1, r], "x")

    def far_copy(r):
        target = {"seq": lax.rem(me + n - 2, n)}
        return remote(hand.at[1, r], land.at[1, r], hand_sems.at[1, 0, r], hand_sems.at[1, 1, r], target)

    def tap_core():
        return exchange(tap_own.at[1 - c], tap_got, home_sems.at[0, 0], home_sems.at[1, 0], "core")

    def tap_y():
        return exchange(tap_own.at[c, 1 - y], tap_half, home_sems.at[0, 1], home_sems.at[1, 1], "y")

    def home_copy(q, there):
        return remote(tap_part.at[q], tap_all.at[c, there], home_send.at[q], home_recv.at[there], {"seq": 4 * y + q})

    def tap_back_y():
        return exchange(tap_all.at[c], tap_all.at[c], home_sems.at[0, 2], home_sems.at[1, 2], "y")

    def tap_back_core():
        return exchange(tap_all.at[c], tap_all.at[c], home_sems.at[0, 3], home_sems.at[1, 3], "core")

    def front(near, x_in, taps, taps_sent, w_in, proj, turned, gate_wide):
        first = [
            pltpu.make_async_copy(src, dst, fetch.at[i])
            for i, (src, dst) in enumerate(((x_far, x_in), (taps_far, taps), (w_in_far, w_in)))
        ]
        for copy in first:
            copy.start()
        marks[...] = jnp.zeros_like(marks)
        for r in range(rows):
            marks[r:r + 1, :] = segments[r].astype(F32)
            marks[rows + r:rows + r + 1, :] = valid[r].astype(F32)
        for k in range(3):
            small[3 * k:3 * k + 3, :] = short_taps[:, k * width:(k + 1) * width]
        small[12:16, :] = jnp.zeros((4, width), F32)
        first[0].wait()

        def norm_row(r):
            for at in range(r * blocks, (r + 1) * blocks, 128):
                parts = [strided(x_in, 128, at, j, wide) for j in range(wide)]
                total = sum(jnp.sum(part * part, axis=-1, keepdims=True) for part in parts)
                scale = lax.rsqrt(total * (1.0 / width) + EPS)
                for j, part in enumerate(parts):
                    lanes = slice(j * 128, (j + 1) * 128)
                    near[0, r, at - r * blocks:at - r * blocks + 128, lanes] = (part * scale * gain_one[:, lanes]).astype(BF16)

        def send_near(r):
            for h in range(2):
                near_far(r, h, near.at[0]).start()

            @pl.when(xbit == 0)
            def _():
                for h in range(2):
                    near_side(r, h, near.at[0]).start()

        def hand_on(r):
            @pl.when(xbit == 1)
            def _():
                for h in range(2):
                    near_far(r, h, near.at[0]).wait_recv()
                    near_side(r, h, land.at[1]).start()

        norm_row(0)
        pl.semaphore_wait(barrier, told)
        send_near(0)
        post_marks.start()
        norm_row(1)
        send_near(1)
        first[1].wait()
        for j in range(wide):
            raw = strided(taps, blocks, 0, j, wide)
            low = raw - THRESH * jnp.tanh(raw * (1.0 / THRESH))
            taps_sent[j * 128:(j + 1) * 128, :] = low.T.astype(BF16)
        for xd in range(2):
            target = 4 * y + 2 * c + xd

            @pl.when(target != me)
            def _():
                tap_copy(target, taps_sent).start()

            @pl.when(target == me)
            def _():
                taps_got[aligned(me, each)] = taps_sent[aligned(me, each)]

        first[2].wait()

        def project(r, j):
            for k in (1, 2, 0):
                for at in range(0, width, 256):
                    cols = slice(k * width + at, k * width + at + 256)
                    proj[j, k, :, at:at + 256] = dot_nn(near[j, r], w_in[:, cols]).astype(BF16)

        project(0, 0)
        hand_on(0)
        post_marks.arrive()
        lane = lax.broadcasted_iota(jnp.int32, (rows, blocks), 1)
        now = marks[0:rows, :]
        found = []
        for j in (1, 2):
            before = marks_got[lax.rem(me + n - j, n), 0:rows, :]
            wrapped = me < j
            before = jnp.where(wrapped, pltpu.roll(before, 1, 1), before)
            kept = jnp.logical_and(before == now, jnp.logical_or(jnp.logical_not(wrapped), lane > 0))
            found.append(kept.astype(F32))
        columns = jnp.concatenate(found + [marks[rows:2 * rows, :], jnp.zeros((2, blocks), F32)], axis=0).T
        for s in range(3):
            for r in range(rows):
                same[s, r] = jnp.broadcast_to(columns[:, s * rows + r:s * rows + r + 1], (blocks, 128))

        def chunk_row(r):
            @pl.when(xbit == 0)
            def _():
                for h in range(2):
                    near_far(r, h, near.at[0]).wait_recv()

            for h in range(2):
                near_side(r, h, near.at[0]).wait_recv()
            for j in (1, 2):
                wrapped = jnp.logical_and(at_top, xbit == 0) if j == 1 else at_top

                @pl.when(wrapped)
                def _():
                    near[j, r] = turn_rows(land[j - 1, r].astype(F32), 1).astype(BF16)

                @pl.when(jnp.logical_not(wrapped))
                def _():
                    near[j, r] = land[j - 1, r]

                project(r, j)

            def lanes_step(lanes):
                def rows_step(here):
                    masks = [same[s, r, here, :] for s in range(3)]
                    value = []
                    for k in range(3):
                        total = small[3 * k:3 * k + 1, lanes] * proj[0, k, here, lanes].astype(F32)
                        total += small[3 * k + 1:3 * k + 2, lanes] * (proj[1, k, here, lanes].astype(F32) * masks[0])
                        total += small[3 * k + 2:3 * k + 3, lanes] * (proj[2, k, here, lanes].astype(F32) * masks[1])
                        value.append(total)
                    query[r, here, lanes] = value[0]
                    keys, values = value[1] * masks[2], value[2] * masks[2]
                    gate = value[1] * values
                    saved[0, r, here, lanes] = keys.astype(BF16)
                    saved[1, r, here, lanes] = values.astype(BF16)
                    saved[2, r, here, lanes] = gate.astype(BF16)
                    gate_wide[here, lanes] = gate

                over_rows(blocks, 64, rows_step)

            over_lanes(width, lanes_step)
            sent_one[r] = gate_wide[...].T.astype(BF16)
            posts_gate[r].start()

        chunk_row(0)
        project(1, 0)
        hand_on(1)

        @pl.when(chosen_chunk)
        def _():
            for p in range(n):
                @pl.when(me != p)
                def _():
                    remote(
                        taps_sent.at[aligned(me, each)], taps_got.at[p * each:(p + 1) * each],
                        tap_sems.at[0, 0], tap_sems.at[1, p], {"seq": p},
                    ).wait_recv()
            tap_spread("core").start()

        @pl.when(jnp.logical_and(zh == y, zl != c))
        def _():
            tap_spread("core").wait_recv()

        @pl.when(zh == y)
        def _():
            tap_spread("y").start()

        chunk_row(1)

        for j in range(3):
            for r in range(rows):
                value = near[j, r].astype(F32)
                if j > 0:
                    value = value * same[j - 1, r, :, 0:1]
                turned[j, :, r * blocks:(r + 1) * blocks] = value.T.astype(BF16)
        kept = pltpu.make_async_copy(turned, turned_far, keep.at[2])
        kept.start()
        for r in range(rows):
            for h in range(2):
                near_far(r, h, near.at[0]).wait_send()
                near_side(r, h, near.at[0]).wait_send()
        for xd in range(2):
            target = 4 * y + 2 * c + xd

            @pl.when(target != me)
            def _():
                tap_copy(target, taps_sent).wait_send()

        kept.wait()

    pl.run_scoped(
        front,
        pltpu.VMEM((3, rows, blocks, width), BF16),
        pltpu.VMEM(x_far.shape, F32),
        pltpu.VMEM(taps_far.shape, F32),
        pltpu.VMEM((width, blocks), BF16),
        pltpu.VMEM(w_in_far.shape, BF16),
        pltpu.VMEM((3, 3, blocks, width), BF16),
        pltpu.VMEM(turned_far.shape, BF16),
        pltpu.VMEM((blocks, width), F32),
    )

    def conv(fin, spec, spec_taps, spec_gate):
        @pl.when(zh != y)
        def _():
            tap_spread("y").wait_recv()

        to_lanes(lambda at, size: taps_got[at:at + size], table, spec)

        def taps_group(at, lane):
            re, im = load_phases(spec, n, each, at, lane, blocks)
            re, im = turn_phases(re, im, turns, lane, -1)
            re, im = fft_points(re, im, -1)
            for k in range(n):
                spec_taps[pl.ds(k * each + at, 8), lane:lane + 128] = re[k]
                spec_taps[pl.ds(k * each + at, 8), blocks + lane:blocks + lane + 128] = im[k]

        def both_halves(at, lane):
            taps_group(at, lane)
            taps_group(at + 8, lane)

        over_groups(each, blocks, both_halves)
        keeps = [pltpu.make_async_copy(spec_taps, spec_taps_far, keep.at[0])]
        keeps[0].start()

        for r in range(rows):
            posts_gate[r].arrive()
            to_lanes(lambda at, size: got_one[r, at:at + size], table, spec)

            def work(re, im, at, lane, kept):
                re, im = turn_phases(re, im, turns, lane, -1)
                re, im = fft_points(re, im, -1)
                tap_r, tap_i = load_phases(spec_taps, n, each, at, lane, blocks)
                out_r = [re[k] * tap_r[k] - im[k] * tap_i[k] for k in range(n)]
                out_i = [re[k] * tap_i[k] + im[k] * tap_r[k] for k in range(n)]
                out_r, out_i = fft_points(out_r, out_i, 1)
                out_r, out_i = turn_phases(out_r, out_i, turns, lane, 1)
                return (re, im), (out_r, out_i)

            by_halves(n, each, blocks, spec, work, (spec_gate.at[r], fin))

            def store(at, value):
                sent_two[r, at:at + value.shape[0]] = value.astype(BF16)

            from_lanes(fin, table, each, store)
            posts_long[r].start()
        keeps.append(pltpu.make_async_copy(spec_gate, spec_gate_far, keep.at[1]))
        keeps[1].start()
        for copy in keeps:
            copy.wait()

    def middle(act, grad_act, turned, turned_cot, mixed, mix_back):
        def mlp(first, w_out, w_up, w_down, x, cot, cot_near, cot_low, resid, long_out, acc_out, acc_back, normed, whole_out, mid):
            vectors[...] = jnp.zeros_like(vectors)
            kept = []
            first[0].wait()
            for r in range(rows):
                tokens = slice(r * blocks, (r + 1) * blocks)
                posts_long[r].arrive()
                gated = saved[2, r].astype(F32)
                long_out[...] = got_two[r].astype(F32).T + small[9:10, :] * gated
                low = (query[r] * long_out[...]).astype(BF16)
                mixer = dot_nn(low, w_out[...])
                mixed[r] = low.T
                mask = same[2, r, :, 0:1]
                vectors[13:14, :] += jnp.sum(mixer * mixer * mask, axis=0, keepdims=True)
                first[1].wait()
                first[2].wait()
                for j in range(wide):
                    lanes = slice(j * 128, (j + 1) * 128)
                    resid[:, lanes] = strided(x, blocks, 0, j, wide) + mixer[:, lanes]
                    cot_near[:, lanes] = strided(cot, blocks, 0, j, wide)
                if r + 1 < rows:
                    after = slice((r + 1) * linear, (r + 2) * linear)
                    for i, (src, dst) in ((1, (x_far, x)), (2, (cot_far, cot))):
                        first[i] = pltpu.make_async_copy(src.at[after], dst, fetch.at[i])
                        first[i].start()
                cot_low[...] = cot_near[...].astype(BF16)
                state = resid[...]
                scale = lax.rsqrt(jnp.mean(state * state, axis=-1, keepdims=True) + EPS)
                normed[...] = (state * scale * gain_two).astype(BF16)
                acc_out[...] = jnp.zeros_like(acc_out)
                acc_back[...] = jnp.zeros_like(acc_back)
                if r == 0:
                    first[3].wait()
                    first[4].wait()

                def hidden_step(j, carry):
                    cols = aligned(j, chunk)
                    up_val = dot_nn(normed[...], w_up[:, cols])
                    square = up_val * up_val
                    tanh = jnp.tanh(up_val * (C0 + (C0 * C1) * square))
                    half = 0.5 * (1.0 + tanh)
                    act_low = (up_val * half).astype(BF16)
                    slope = half + (0.5 * up_val) * (1.0 - tanh * tanh) * (C0 + (3.0 * C0 * C1) * square)
                    act[tokens, cols] = act_low
                    acc_out[...] += dot_nn(act_low, w_down[cols, :])
                    grad = dot_nt(cot_low[...], w_down[cols, :])
                    grad_low = (grad * slope).astype(BF16)
                    grad_act[tokens, cols] = grad_low
                    acc_back[...] += dot_nt(grad_low, w_up[:, cols])
                    return carry

                lax.fori_loop(0, hidden // chunk, hidden_step, 0, unroll=4)
                state = resid[...]
                scale = lax.rsqrt(jnp.mean(state * state, axis=-1, keepdims=True) + EPS)
                grad = acc_back[...]
                scaled = grad * gain_two
                shift = jnp.mean(scaled * state, axis=-1, keepdims=True) * (scale * scale * scale)
                grad_mid = cot_near[...] + (scaled * scale - state * shift)
                mix_back[r] = grad_mid.astype(BF16)
                grad_prod = dot_nt(mix_back[r], w_out[...])
                grad_long = grad_prod * query[r]
                posts_gate[r].drain()
                sent_one[r] = grad_long.T.astype(BF16)
                posts_back[r].start()
                vectors[11:12, :] += jnp.sum(acc_back[...] * resid[...] * scale, axis=0, keepdims=True)
                saved[3, r] = grad_long.astype(BF16)
                vectors[9:10, :] += jnp.sum(grad_long * saved[2, r].astype(F32), axis=0, keepdims=True)
                saved[2, r] = (grad_prod * long_out[...]).astype(BF16)
                mlp = acc_out[...]
                vectors[14:15, :] += jnp.sum(mlp * mlp * mask, axis=0, keepdims=True)
                whole = resid[...] + mlp
                vectors[12:13, :] += jnp.sum(whole * whole * mask, axis=0, keepdims=True)
                vectors[15:16, :] += jnp.broadcast_to(jnp.sum(mask, axis=0, keepdims=True) * (1.0 / width), (1, width))
                if r > 0:
                    for copy in kept:
                        copy.wait()
                    kept.clear()
                for j in range(wide):
                    place_at = pl.ds(j, blocks, stride=wide)
                    whole_out[place_at, :] = whole[:, j * 128:(j + 1) * 128]
                    mid[place_at, :] = grad_mid[:, j * 128:(j + 1) * 128]
                part_rows = slice(r * blocks * wide, (r + 1) * blocks * wide)
                for i, (src, dst) in enumerate(((whole_out, out_far), (mid, mid_far))):
                    kept.append(pltpu.make_async_copy(src, dst.at[part_rows], keep.at[3 + i]))
                    kept[-1].start()
                turned[:, tokens] = normed[...].T
                turned_cot[:, tokens] = cot_low[...].T

            for copy in kept:
                copy.wait()

        def fetched(w_out, w_up, w_down, x, cot):
            first = [
                pltpu.make_async_copy(src, dst, fetch.at[i])
                for i, (src, dst) in enumerate((
                    (w_out_far, w_out), (x_far.at[0:linear], x), (cot_far.at[0:linear], cot), (w_up_far, w_up), (w_down_far, w_down),
                ))
            ]
            for copy in first:
                copy.start()
            pl.run_scoped(
                conv,
                pltpu.VMEM((width, 2 * blocks), BF16),
                pltpu.VMEM((width, 2 * blocks), F32),
                pltpu.VMEM((width, 2 * blocks), F32),
                pltpu.VMEM(spec_gate_far.shape, BF16),
            )
            pl.run_scoped(
                functools.partial(mlp, first, w_out, w_up, w_down, x, cot),
                pltpu.VMEM((blocks, width), F32),
                pltpu.VMEM((blocks, width), BF16),
                *[pltpu.VMEM((blocks, width), F32)] * 4,
                pltpu.VMEM((blocks, width), BF16),
                *[pltpu.VMEM((linear, 128), F32)] * 2,
            )

        pl.run_scoped(
            fetched,
            pltpu.VMEM(w_out_far.shape, BF16),
            pltpu.VMEM(w_up_far.shape, BF16),
            pltpu.VMEM(w_down_far.shape, BF16),
            pltpu.VMEM((linear, 128), F32),
            pltpu.VMEM((linear, 128), F32),
        )

        def sums(up_a, up_b, down_a, down_b, out, spec_taps, spec_gate, fin, spec, spec_sum):
            near = [
                pltpu.make_async_copy(src, dst, fetch.at[i])
                for i, (src, dst) in enumerate(((spec_taps_far, spec_taps), (spec_gate_far, spec_gate)))
            ]
            for copy in near:
                copy.start()
            quarter, part = width // 4, hidden // n
            pairs = [(share, trees[name].own) for name, share in zip(("ua", "ub", "da", "db", "out"), (up_a, up_b, down_a, down_b, out))]

            def pair_copy(i):
                return exchange(pairs[i][0].at[:, :, :, 1 - c], pairs[i][1], pair_sems.at[0, i], pair_sems.at[1, i], "core")

            def put_rows(share, half, lanes, value):
                for s in range(n):
                    for core in range(2):
                        low = (2 * s + core) * side
                        share[s // 4, (s // 2) % 2, s % 2, core, half, :, lanes] = value[low:low + side]

            def add_pair(i):
                share, pair = pairs[i]
                pair_copy(i).wait_recv()
                size = 48
                for a in range(2):
                    for b in range(2):
                        for d in range(2):
                            for e in range(2):
                                def body(k, carry):
                                    here = aligned(k, size)
                                    pair[a, b, d, e, here, :] = pair[a, b, d, e, here, :] + share[a, b, d, c, e, here, :]
                                    return carry
                                lax.fori_loop(0, pair.shape[4] // size, body, 0)


            def conv_row(r):
                posts_back[r].arrive()
                to_lanes(lambda at, size: got_one[r, at:at + size], table, spec)

                def work(re, im, at, lane, kept):
                    re, im = turn_phases(re, im, turns, lane, -1)
                    re, im = fft_points(re, im, -1)
                    tap_r, tap_i = load_phases(spec_taps, n, each, at, lane, blocks)
                    gate_r, gate_i = kept
                    out_r, out_i = [], []
                    for k in range(n):
                        here = pl.ds(k * each + at, 8)
                        lanes, other = slice(lane, lane + 128), slice(blocks + lane, blocks + lane + 128)
                        old_r, old_i = gate_r[k], gate_i[k]
                        sum_r, sum_i = old_r * re[k] + old_i * im[k], old_r * im[k] - old_i * re[k]
                        if r == 0:
                            spec_sum[here, lanes] = sum_r
                            spec_sum[here, other] = sum_i
                        else:
                            spec_sum[here, lanes] += sum_r
                            spec_sum[here, other] += sum_i
                        out_r.append(tap_r[k] * re[k] + tap_i[k] * im[k])
                        out_i.append(tap_r[k] * im[k] - tap_i[k] * re[k])
                    out_r, out_i = fft_points(out_r, out_i, 1)
                    return (turn_phases(out_r, out_i, turns, lane, 1),)

                by_halves(n, each, blocks, spec, work, (fin,), spec_gate.at[r])

                posts_long[r].drain()

                def store(at, value):
                    sent_two[r, at:at + value.shape[0]] = value.astype(BF16)

                from_lanes(fin, table, each, store)
                posts_gated[r].start()
            def up_part(i):
                for half in range(2):
                    low = half * (hidden // 2) + i * (hidden // 4)
                    value = dot_nn(turned[...], grad_act[:, low:low + hidden // 4]).astype(BF16)
                    put_rows((up_a, up_b)[i], half, ALL, value)
                pair_copy(i).start()

            def down_parts():
                for s in range(n):
                    value = dot_nn(turned_cot[...], act[:, s * part:(s + 1) * part]).astype(BF16)
                    for core in range(2):
                        for half in range(2):
                            low = (2 * core + half) * quarter
                            down_a[s // 4, (s // 2) % 2, s % 2, core, half] = value[low:low + quarter // 2]
                            down_b[s // 4, (s // 2) % 2, s % 2, core, half] = value[low + quarter // 2:low + quarter]
                pair_copy(2).start()
                pair_copy(3).start()

            def out_part():
                for half in range(2):
                    low = half * (width // 2)
                    value = sum(dot_nn(mixed[r], mix_back[r, :, low:low + width // 2]) for r in range(rows)).astype(BF16)
                    put_rows(out, half, ALL, value)
                pair_copy(4).start()

            def tap_row():
                def work_taps(re, im, at, lane, kept):
                    re, im = fft_points(re, im, 1)
                    return (turn_phases(re, im, turns, lane, 1),)

                by_halves(n, each, blocks, spec_sum, work_taps, (fin,))

                def store_taps(at, value):
                    p = at // each
                    for half in range(2):
                        tap_own[half, p // 4, p % 4] = value[half * side:(half + 1) * side].astype(BF16)

                from_lanes(fin, table, each, store_taps)
                tap_core().start()

            up_part(0)
            up_part(1)
            add_pair(0)
            trees["ua"].start()
            add_pair(1)
            trees["ub"].start()
            for copy in near:
                copy.wait()
            conv_row(0)
            down_parts()
            conv_row(1)
            tap_row()
            add_pair(2)
            trees["da"].start()
            out_part()
            add_pair(4)
            add_pair(3)
            for i in range(5):
                pair_copy(i).wait_send()

        pl.run_scoped(
            sums,
            *[pltpu.VMEM(trees[name].own.shape[:3] + (2,) + trees[name].own.shape[3:], BF16) for name in ("ua", "ub", "da", "db", "out")],
            pltpu.VMEM((width, 2 * blocks), F32),
            pltpu.VMEM((rows, width, 2 * blocks), BF16),
            pltpu.VMEM((width, 2 * blocks), BF16),
            pltpu.VMEM((width, 2 * blocks), F32),
            pltpu.VMEM((width, 2 * blocks), F32),
        )

    pl.run_scoped(
        middle,
        pltpu.VMEM((rows * blocks, hidden), BF16),
        pltpu.VMEM((rows * blocks, hidden), BF16),
        pltpu.VMEM((width, rows * blocks), BF16),
        pltpu.VMEM((width, rows * blocks), BF16),
        pltpu.VMEM((rows, width, blocks), BF16),
        pltpu.VMEM((rows, blocks, width), BF16),
    )

    def token_phase(turned, w_in, x, mid, gate_back, short, part_proj, grad_norm, gain_lanes, share0, share1, share2):
        for k, share in enumerate((share0, share1, share2)):
            trees["in%d" % k].share = share
        near = [
            pltpu.make_async_copy(src, dst, fetch.at[i])
            for i, (src, dst) in enumerate((
                (w_in_far, w_in), (turned_far, turned), (x_far, x), (mid_far, mid),
            ))
        ]
        for copy in near:
            copy.start()
        tap_core().wait_recv()
        for half in range(2):
            for q in range(4):
                tap_own[c, half, q] = tap_own[c, half, q] + tap_got[half, q]
        tap_y().start()

        def token_row(r):
            tokens = slice(r * blocks, (r + 1) * blocks)
            posts_gated[r].arrive()
            gate_back[...] = got_two[r].astype(F32).T

            def lanes_step(lanes):
                skip = small[9:10, lanes]

                def rows_step(here):
                    there = pl.ds(pl.multiple_of(r * blocks + here.start, 64), here.size)
                    grad = gate_back[here, lanes] + skip * saved[3, r, here, lanes].astype(F32)
                    short[there, lanes] = saved[2, r, here, lanes]
                    second = pl.ds(pl.multiple_of(lanes.start + width, 128), 128)
                    third = pl.ds(pl.multiple_of(lanes.start + 2 * width, 128), 128)
                    short[there, second] = (grad * saved[1, r, here, lanes].astype(F32)).astype(BF16)
                    short[there, third] = (grad * saved[0, r, here, lanes].astype(F32)).astype(BF16)

                over_rows(blocks, 64, rows_step)

            over_lanes(width, lanes_step)

        def spread(r, j):
            def lanes_step(lanes):
                def rows_step(here):
                    there = pl.ds(pl.multiple_of(r * blocks + here.start, 64), here.size)
                    for k in range(3):
                        cols = pl.ds(pl.multiple_of(lanes.start + k * width, 128), 128)
                        value = short[there, cols].astype(F32) * small[3 * k + j:3 * k + j + 1, lanes]
                        if j > 0:
                            value = value * same[j - 1, r, here, :]
                        part_proj[here, cols] = value.astype(BF16)

                over_rows(blocks, 64, rows_step)

            over_lanes(width, lanes_step)
            return dot_nt(part_proj[...], w_in[...])

        def send_hand(r):
            hand[0, r] = spread(r, 1).astype(BF16)
            side_copy(r).start()
            hand[1, r] = spread(r, 2).astype(BF16)

            @pl.when(xbit == 0)
            def _():
                far_copy(r).start()

        def hand_on(r):
            @pl.when(xbit == 1)
            def _():
                side_copy(r).wait_recv()
                hand[1, r] = (hand[1, r].astype(F32) + land[0, r].astype(F32)).astype(BF16)
                far_copy(r).start()

        def weight_part(k):
            share = trees["in%d" % k].share
            for half in range(2):
                low = k * width + half * (width // 2)
                cols = slice(low, low + width // 2)
                lanes = slice(half * (width // 2), (half + 1) * (width // 2))
                total = None
                for j in range(3):
                    value = dot_nn(turned[j], short[:, cols])
                    vectors[3 * k + j:3 * k + j + 1, lanes] = jnp.sum(value * w_in[:, cols].astype(F32), axis=0, keepdims=True)
                    value = value * small[3 * k + j:3 * k + j + 1, lanes]
                    total = value if total is None else total + value
                product = total * w_in[:, cols].astype(F32)
                gain_lanes[...] += sum(product[:, at:at + 128] for at in range(0, width // 2, 128))
                total = total.astype(BF16)
                for s in range(n):
                    for core in range(2):
                        block = (2 * s + core) * side
                        share[s // 4, (s // 2) % 2, s % 2, core, half] = total[block:block + side]
            trees["in%d" % k].start()

        def last_row(r):
            tokens = slice(r * blocks, (r + 1) * blocks)

            @pl.when(xbit == 0)
            def _():
                side_copy(r).wait_recv()
                grad_norm[r] += land[0, r].astype(F32)

            far_copy(r).wait_recv()
            late = land[1, r].astype(F32)

            @pl.when(at_end)
            def _():
                grad_norm[r] += turn_rows(late, blocks - 1)

            @pl.when(jnp.logical_not(at_end))
            def _():
                grad_norm[r] += late

            grad = grad_norm[r]
            parts = [strided(x, blocks, r * blocks, j, wide) for j in range(wide)]
            total = sum(jnp.sum(part * part, axis=-1, keepdims=True) for part in parts)
            scale = lax.rsqrt(total * (1.0 / width) + EPS)
            inner = 0.0
            scaled = []
            for j, part in enumerate(parts):
                lanes = slice(j * 128, (j + 1) * 128)
                piece = grad[:, lanes]
                scaled.append(piece * gain_one[:, lanes])
                inner += jnp.sum(scaled[j] * part, axis=-1, keepdims=True)
            shift = inner * (1.0 / width) * (scale * scale * scale)
            for j, part in enumerate(parts):
                place_at = pl.ds(r * linear + j, blocks, stride=wide)
                mid[place_at, :] += scaled[j] * scale - part * shift
            done = slice(r * linear, (r + 1) * linear)
            ready.append(pltpu.make_async_copy(mid.at[done], flat_far.at[done], keep.at[r]))
            ready[-1].start()

        def tap_home():
            tap_y().wait_recv()
            for q in range(4):
                tap_part[q] = tap_own[c, y, q] + tap_half[q]
            for q in range(4):
                @pl.when(4 * y + q != me)
                def _():
                    home_copy(q, me).start()

                @pl.when(4 * y + q == me)
                def _():
                    tap_all[c, me] = tap_part[q]

        def tap_return():
            @pl.when(home)
            def _():
                for j in range(1, n):
                    peer = lax.rem(me + j, n)
                    remote(tap_part.at[0], tap_all.at[c, peer], home_send.at[0], home_recv.at[peer], {"seq": peer}).wait_recv()
                tap_back_y().start()

        def tap_share():
            @pl.when(jnp.logical_not(home))
            def _():
                tap_back_y().wait_recv()

            tap_back_core().start()

        def vector_copy(step):
            axis = ("core", "y", "x", "zl", "zh")[step]
            return exchange(vectors, vector_got.at[step], vector_sems.at[0, step], vector_sems.at[1, step], axis)

        def vector_start():
            vectors[10:11, :] = jnp.sum(gain_lanes[...].T, axis=0, keepdims=True) / gain_one
            vector_copy(0).start()

        def vector_finish(step):
            vector_copy(step).wait()
            vectors[...] += vector_got[step]
            if step < 4:
                vector_copy(step + 1).start()

        def whole_norm():
            for r in range(rows):
                grad_norm[r] = spread(r, 0)
            for copy in near[2:4]:
                copy.wait()

        ready = []
        gain_lanes[...] = jnp.zeros_like(gain_lanes)
        trees["ua"].finish()
        trees["db"].start()
        token_row(0)
        near[0].wait()
        send_hand(0)
        trees["ub"].finish()
        tap_home()
        trees["da"].finish()
        token_row(1)
        send_hand(1)
        trees["ua"].finish()
        near[1].wait()
        weight_part(0)
        hand_on(0)
        trees["in0"].finish()
        weight_part(1)
        weight_part(2)
        hand_on(1)
        trees["db"].finish()
        whole_norm()
        trees["da"].finish()
        trees["in1"].finish()
        vector_start()
        trees["ua"].finish()
        trees["in2"].finish()
        trees["in0"].finish()
        trees["out"].start()
        trees["ub"].finish()
        trees["db"].finish()
        vector_finish(0)
        trees["da"].finish()
        trees["in2"].finish()
        trees["in1"].finish()
        tap_return()
        trees["db"].finish()
        trees["in0"].finish()
        trees["out"].finish()
        trees["ub"].finish()
        trees["in1"].finish()
        last_row(0)
        trees["out"].finish()
        trees["da"].finish()
        vector_finish(1)
        trees["in0"].finish()
        trees["in2"].finish()
        trees["db"].finish()
        trees["in1"].finish()
        last_row(1)
        trees["out"].finish()
        trees["ua"].finish()
        trees["ub"].finish()
        vector_finish(2)
        trees["da"].finish()
        tap_share()
        trees["in2"].finish()
        trees["db"].finish()
        trees["in0"].finish()
        trees["in1"].finish()
        trees["out"].finish()
        trees["ua"].finish()
        trees["ub"].finish()
        trees["in2"].finish()
        vector_finish(3)
        tap_back_core().wait_recv()
        trees["in0"].finish()
        trees["db"].finish()
        trees["in1"].finish()
        trees["ub"].finish()
        trees["out"].finish()
        trees["in0"].finish()
        trees["ua"].finish()
        trees["in2"].finish()
        vector_finish(4)
        trees["in1"].finish()
        trees["out"].finish()
        trees["da"].finish()
        trees["in2"].finish()
        for copy in ready:
            copy.wait()

        for tree in trees.values():
            tree.drain()
        for post in [post_marks] + posts_back + posts_gated:
            post.drain()
        for r in range(rows):
            side_copy(r).wait_send()
            far_copy(r).wait_send()
        tap_core().wait_send()
        tap_y().wait_send()
        for q in range(4):
            @pl.when(4 * y + q != me)
            def _():
                home_copy(q, me).wait_send()

        @pl.when(home)
        def _():
            tap_back_y().wait_send()

        tap_back_core().wait_send()

        @pl.when(chosen_chunk)
        def _():
            tap_spread("core").wait_send()

        @pl.when(zh == y)
        def _():
            tap_spread("y").wait_send()

    pl.run_scoped(
        token_phase,
        pltpu.VMEM(turned_far.shape, BF16),
        pltpu.VMEM(w_in_far.shape, BF16),
        pltpu.VMEM(x_far.shape, F32),
        pltpu.VMEM(x_far.shape, F32),
        pltpu.VMEM((blocks, width), F32),
        pltpu.VMEM((rows * blocks, 3 * width), BF16),
        pltpu.VMEM((blocks, 3 * width), BF16),
        pltpu.VMEM((rows, blocks, width), F32),
        pltpu.VMEM((width, 128), F32),
        *[pltpu.VMEM((2, 2, 2, 2, 2, side, width // 2), BF16)] * 3,
    )


def last_kernel(
    block_in, flat_in, got_ua, got_ub, got_da, got_db, got_out, got_in0, got_in1, got_in2, tap_all, taps, vectors,
    out, grad_flat, gain_mix, grad_in, grad_taps, grad_kernel, grad_skip, grad_out, gain_mlp, grad_up, grad_down, rms,
):
    out[...] = block_in[...]
    grad_flat[...] = flat_in[...]
    width = vectors.shape[1]
    side, wide, blocks = got_out.shape[2], width // 128, tap_all.shape[3]
    half_up = grad_up.shape[1] // 2
    for got, target, low, skip in (
        (got_ua, grad_up, 0, half_up), (got_ub, grad_up, half_up // 2, half_up), (got_out, grad_out, 0, width // 2),
        (got_in0, grad_in, 0, width // 2), (got_in1, grad_in, width, width // 2), (got_in2, grad_in, 2 * width, width // 2),
    ):
        l = got.shape[3]
        for half in range(2):
            for core in range(2):
                at = low + half * skip
                target[core * side:(core + 1) * side, at:at + l] = got[core, half].astype(F32)
    grad_down[...] = jnp.concatenate(
        [got[core, half] for core in range(2) for half in range(2) for got in (got_da, got_db)], axis=0
    ).astype(F32).T
    value = jnp.concatenate(
        [tap_all[core, s] for s in range(tap_all.shape[1]) for core in range(2)], axis=0
    ).astype(F32).T
    for j in range(wide):
        place_at = pl.ds(j, blocks, stride=wide)
        tanh = jnp.tanh(taps[place_at, :] * (1.0 / THRESH))
        grad_kernel[place_at, :] = value[:, j * 128:(j + 1) * 128] * (tanh * tanh)
    for k in range(3):
        grad_taps[:, k * width:(k + 1) * width] = vectors[3 * k:3 * k + 3, :]
    for target, row in ((grad_skip, 9), (gain_mix, 10), (gain_mlp, 11)):
        target[...] = vectors[row, :]
    total = jnp.sum(vectors[12:16, :], axis=1, keepdims=True)
    found = jnp.sqrt(total / (jnp.maximum(total[3:4, :], 1.0) * width))
    for i in range(3):
        rms[i] = found[i, 0]


def call(body, outs, scratch, inputs, collective_id, far=(), far_outs=()):
    return pl.pallas_call(
        body,
        out_shape=tuple(jax.ShapeDtypeStruct(*out) for out in outs),
        in_specs=[pl.BlockSpec(memory_space=pl.ANY if i in far else pltpu.VMEM) for i in range(len(inputs))],
        out_specs=tuple(pl.BlockSpec(memory_space=pl.ANY if i in far_outs else pltpu.VMEM) for i in range(len(outs))),
        scratch_shapes=scratch,
        compiler_params=pltpu.CompilerParams(
            vmem_limit_bytes=VMEM_BYTES, collective_id=collective_id, has_side_effects=True
        ),
    )(*inputs)


def local(
    block_in, segment_ids, valid_mask, cotangent, gain_mix, in_proj, short_taps, long_kernel,
    skip_gain, out_proj, gain_mlp, up_proj, down_proj,
):
    rows, blocks, _, width = block_in.shape
    hidden = up_proj.shape[1]
    n = lax.axis_size("seq")
    each = width // n
    tokens = rows * blocks
    side, wide = each // 2, width // 128
    chunk = 768
    x = block_in.reshape(tokens * wide, 128)
    cot = cotangent.reshape(tokens * wide, 128)
    raw = long_kernel.reshape(blocks * wide, 128)
    segments = segment_ids.reshape(rows, 1, blocks)
    valid = valid_mask.reshape(rows, 1, blocks)
    table, turns = spectrum_tables(blocks, n)
    dma = pltpu.SemaphoreType.DMA
    bits = (2, 2, 2, 2, 2)
    up_shape = bits[1:] + (side, hidden // 4)
    down_shape = bits[1:] + (width // 8, hidden // n)
    out_shape = bits[1:] + (side, width // 2)
    own_shapes = (up_shape, up_shape, down_shape, down_shape, out_shape)
    low = lambda *shape: pltpu.VMEM(shape, BF16)
    full = lambda *shape: pltpu.VMEM(shape, F32)

    trees = []
    for shape in own_shapes:
        trees += tree_scratch(*shape[4:])
    for _ in range(3):
        trees += tree_scratch(*out_shape[4:])
    gots = [(2, 2) + shape[4:] for shape in own_shapes + (out_shape,) * 3]
    quarter = (4, side, blocks)
    pair = (rows, 2, n)
    block_out, grad_flat, _, _, _, _, *gathered, taps_back, vectors = call(
        functools.partial(whole_kernel, n, chunk),
        [
            (x.shape, F32),
            (x.shape, F32),
            (x.shape, F32),
            ((3, width, tokens), BF16),
            ((width, 2 * blocks), F32),
            ((rows, width, 2 * blocks), BF16),
            *[(shape, BF16) for shape in gots],
            ((2, n, side, blocks), BF16),
            ((16, width), F32),
        ],
        [
            full(16, width), low(*table.shape), full(8, blocks), full(n, 8, blocks), low(2, rows, blocks, width), low(width, blocks),
            full(rows, blocks, width), low(4, rows, blocks, width), full(3, rows, blocks, 128),
            low(rows, width, blocks), low(rows, width, blocks), low(rows, width, blocks), low(rows, width, blocks),
            low(2, rows, blocks, width),
            low(2, 2, *quarter), low(2, *quarter), low(*quarter), low(*quarter), full(5, 16, width),
            dma((5,)), dma((5,)), dma((2, 2, rows, 2)), dma((2, n)), dma((4, n)),
            dma(pair), dma(pair), dma(pair), dma(pair), dma((2, 2, rows)),
            dma((2, 5)), dma((2, 4)), dma((4,)), dma((n,)), dma((2, 5)),
        ] + trees,
        (x, cot, raw, short_taps, skip_gain, gain_mix, gain_mlp, segments, valid, in_proj, out_proj, up_proj, down_proj, table, turns),
        1,
        far=(0, 1, 2, 9, 10, 11, 12),
        far_outs=range(6),
    )
    inputs = (block_out, grad_flat, *gathered, taps_back, raw, vectors)
    near = pl.BlockSpec(memory_space=pltpu.VMEM)
    outs = [
        x.shape, x.shape, (width,), (each, 3 * width), (3, 3 * width), raw.shape, (width,), (each, width), (width,),
        (each, hidden), (hidden // n, width), (3,),
    ]
    results = pl.pallas_call(
        last_kernel,
        out_shape=tuple(jax.ShapeDtypeStruct(shape, F32) for shape in outs),
        in_specs=[near] * len(inputs),
        out_specs=(near,) * 11 + (pl.BlockSpec(memory_space=pltpu.SMEM),),
        compiler_params=pltpu.CompilerParams(vmem_limit_bytes=VMEM_BYTES),
    )(*inputs)
    shapes = {0: block_in.shape, 1: block_in.shape, 5: long_kernel.shape}
    return tuple(value.reshape(shapes.get(i, value.shape)) for i, value in enumerate(results))


def chosen(block_in, *rest):
    rows, blocks, _, width = block_in.shape
    n = lax.axis_size("seq")
    fits = blocks % (32 * n) == 0 and width % (32 * n) == 0 and n == 8 and rows == 2 and lax.axis_size("rows") == 4
    return (local if fits else general_local)(block_in, *rest)


def solution(mesh):
    return jax.shard_map(
        chosen,
        mesh=mesh,
        in_specs=(
            P("rows", None, "seq", None),
            P("rows", None, "seq"),
            P("rows", None, "seq"),
            P("rows", None, "seq", None),
            P(),
            P(),
            P(),
            P(None, "seq", None),
            P(),
            P(),
            P(),
            P(),
            P(),
        ),
        out_specs=(
            P("rows", None, "seq", None),
            P("rows", None, "seq", None),
            P(),
            P("seq", None),
            P(),
            P(None, "seq", None),
            P(),
            P("seq", None),
            P(),
            P("seq", None),
            P("seq", None),
            P(),
        ),
        check_vma=False,
    )
```
